32 devices in a mesh: section: 2 (over x), dp: 16 (over z, y, core).
Axes of the slice: x: 2, y: 2, z: 4, core: 2. Of those that a mesh axis runs over, the one named last changes fastest.
Arguments:
- token_ids: int32 [2, 2, 256, 12], P('section', None, 'dp'), may hold values from 0 to 7679
- resets: int32 [2, 2, 256, 12], P('section', None, 'dp'), may hold values 0 or 1
- targets: int32 [2, 256, 12], P(None, 'dp'), may hold values from 0 to 7679
- embedding: bfloat16 [2, 7680, 620], P('section', 'dp'), may hold values from -6 to 6
- input_gates: bfloat16 [2, 3072, 620], P('section', 'dp'), may hold values from -0.25 to 0.25
- recur_gates: bfloat16 [2, 1024, 3072], P('section', 'dp'), may hold values from -0.1875 to 0.1875
- square: bfloat16 [2, 1024, 1024], P('section', 'dp'), may hold values from -0.1875 to 0.1875
- context_gates: bfloat16 [1024, 3072], P(('section', 'dp')), may hold values from -0.1875 to 0.1875
- deep_embed: bfloat16 [1024, 620], P(('section', 'dp')), may hold values from -0.25 to 0.25
- deep_context: bfloat16 [1024, 1024], P(('section', 'dp')), may hold values from -0.1875 to 0.1875
- softmax_weight: bfloat16 [7680, 512], P(('section', 'dp')), may hold values from -0.25 to 0.25
Outputs:
- total_loss: float32 [], replicated
- embedding_grad: float32 [2, 7680, 620], P('section', 'dp')
- input_gates_grad: float32 [2, 3072, 620], P('section', 'dp')
- recur_gates_grad: float32 [2, 1024, 3072], P('section', 'dp')
- square_grad: float32 [2, 1024, 1024], P('section', 'dp')
- context_gates_grad: float32 [1024, 3072], P(('section', 'dp'))
- deep_embed_grad: float32 [1024, 620], P(('section', 'dp'))
- deep_context_grad: float32 [1024, 1024], P(('section', 'dp'))
- softmax_weight_grad: float32 [7680, 512], P(('section', 'dp'))
The draws below stay inside these ranges and needn't reach their ends.
All inputs are finite; a program needn't handle non-finite values. No bound on the sum of `resets` on one device may be relied on, other than what follows from the above.
Results may differ from the reference program's by a relative error of at most 0.0055.
Values may be sent and summed in bfloat16 or wider, within the bound.
A program may use at most 320 MiB of HBM per device.

```python
import math
from functools import partial
import jax
import jax.numpy as jnp
import numpy as np
from jax import lax

E = 620
H = 1024
M = 512
VOC = 7680
L = 12
MB = 2
ROWS = 256


def place_ends(entries, key, low, high):
    extent = entries.shape
    place = [jax.random.randint(jax.random.fold_in(key, axis), (), 0, extent[axis]) for axis in range(len(extent))]
    entries = entries.at[tuple(place)].set(low)
    longest = extent.index(max(extent))
    place[longest] = (place[longest] + 1) % extent[longest]
    return entries.at[tuple(place)].set(high)


def block_levels(rng, dims, pieces, least, top_value):
    loudness, own = 1.0, jax.random.fold_in(rng, 6)
    for axis_at, shards_of in pieces:
        steps = jnp.exp(jax.random.uniform(jax.random.fold_in(own, axis_at), (shards_of,), jnp.float32, least / len(pieces), top_value / len(pieces)))
        loudness = loudness * jnp.repeat(steps, dims[axis_at] // shards_of).reshape([-1 if axis == axis_at else 1 for axis in range(len(dims))])
    return loudness


def cumulative_ranks(amount, slope):
    weights = [(1 << 20) // math.isqrt(grade ** slope) + 1 for grade in range(1, amount + 1)]
    deviation = 1 + sum(weights) // (1 << 30)
    return np.cumsum(np.array([max(1, weight // deviation) for weight in weights]))


def ranked_ids(own_key, dims, count, lean):
    grid = cumulative_ranks(count, lean)
    lot = jax.random.randint(jax.random.fold_in(own_key, 1), dims, 0, int(grid[count - 1]))
    standing = jnp.searchsorted(jnp.asarray(grid, jnp.int32), lot, side="right")
    return jax.random.permutation(jax.random.fold_in(own_key, 2), count)[standing].astype(jnp.int32)


def bell_draw(stream_key, shape, spread, limit, cuts=(), held_as=jnp.bfloat16):
    result = jax.random.normal(stream_key, shape, jnp.float32) * spread
    if len(cuts) > 0:
        result = block_levels(stream_key, shape, cuts, -0.22, 0.18) * result
    return jnp.clip(result, min=-limit, max=limit).astype(held_as)


def setup_inputs(seed: int = 0) -> dict:
    streams_of = jax.random.split(jax.random.key(seed), 12)
    token_ids = place_ends(ranked_ids(streams_of[0], (2, MB, ROWS, L), VOC, 2), jax.random.fold_in(streams_of[0], 3), 0, VOC - 1).astype(jnp.int32)
    resets = place_ends((jax.random.randint(streams_of[1], (2, MB, ROWS, L), 0, 4) < 1).astype(jnp.int32), jax.random.fold_in(streams_of[1], 1), 0, 1)
    targets = place_ends(ranked_ids(streams_of[2], (MB, ROWS, L), VOC, 2), jax.random.fold_in(streams_of[2], 3), 0, VOC - 1).astype(jnp.int32)
    embedding = bell_draw(streams_of[3], (2, VOC, E), 1.0, 6.0, ((0, 2), (1, 16)))
    input_gates = bell_draw(streams_of[4], (2, 3 * H, E), E ** -0.5, 0.25, ((0, 2), (1, 16)))
    recur_gates = bell_draw(streams_of[5], (2, H, 3 * H), H ** -0.5, 0.1875, ((0, 2), (1, 16)))
    square = bell_draw(streams_of[6], (2, H, H), H ** -0.5, 0.1875, ((0, 2), (1, 16)))
    context_gates = bell_draw(streams_of[7], (H, 3 * H), H ** -0.5, 0.1875, ((0, 32),))
    deep_embed = bell_draw(streams_of[8], (2 * M, E), E ** -0.5, 0.25, ((0, 32),))
    deep_context = bell_draw(streams_of[9], (H, 2 * M), H ** -0.5, 0.1875, ((0, 32),))
    softmax_weight = bell_draw(streams_of[10], (VOC, M), M ** -0.5, 0.25, ((0, 32),))
    return {"token_ids": token_ids, "resets": resets, "targets": targets, "embedding": embedding, "input_gates": input_gates, "recur_gates": recur_gates, "square": square, "context_gates": context_gates, "deep_embed": deep_embed, "deep_context": deep_context, "softmax_weight": softmax_weight}


@jax.custom_vjp
def low(v):
    return lax.optimization_barrier(v.astype(jnp.bfloat16)).astype(jnp.float32)

@jax.custom_vjp
def low_back(v):
    return v

def low_keep(v):
    return (low(v), None)

def low_pass(kept, grad):
    return (grad,)

def back_keep(v):
    return (v, None)

def back_low(kept, grad):
    return (low(grad),)
low.defvjp(low_keep, low_pass)
low_back.defvjp(back_keep, back_low)

def dense_product(first_mat, second_mat):
    return jnp.dot(first_mat, second_mat, precision=lax.Precision.HIGHEST, preferred_element_type=jnp.float32)

def recurrence(inputs, keep_mask, input_weight, recur_weight, context):
    step_count, row_count, in_width = inputs.shape
    hidden = recur_weight.shape[0]
    input_drive = low_back(dense_product(inputs.reshape(step_count * row_count, in_width), input_weight.T))
    input_drive = input_drive.reshape(step_count, row_count, 3 * hidden)

    def advance(current, step_input):
        drive_now, keep_now = step_input
        before = current * keep_now[:, None]
        recurrent = low_back(dense_product(low(before), recur_weight))
        update = jax.nn.sigmoid(drive_now[:, :hidden] + recurrent[:, :hidden] + context[:, :hidden])
        reset_gate = jax.nn.sigmoid(drive_now[:, hidden:2 * hidden] + recurrent[:, hidden:2 * hidden] + context[:, hidden:2 * hidden])
        memory = recurrent[:, 2 * hidden:] + context[:, 2 * hidden:]
        candidate = jnp.tanh(drive_now[:, 2 * hidden:] + reset_gate * memory)
        current = update * before + (1.0 - update) * candidate
        return (current, current)
    return lax.scan(jax.checkpoint(advance), jnp.zeros((row_count, hidden), jnp.float32), (input_drive, keep_mask))

def forward(embedding, input_gates, recur_gates, square, context_gates, deep_embed, deep_context, softmax_weight, token_ids, keep_mask, targets):
    hidden = recur_gates.shape[1]
    unit_count = softmax_weight.shape[1]
    micro_count = token_ids.shape[1]
    row_count = token_ids.shape[2]
    step_count = token_ids.shape[3]
    token_count = step_count * row_count
    block_rows = math.gcd(token_count, 4096)
    total_loss = jnp.zeros((), jnp.float32)
    for batch_index in range(micro_count):
        source = jnp.take(embedding[0], token_ids[0, batch_index].T, axis=0)
        last_state, _ = recurrence(source, keep_mask[0, batch_index].T, input_gates[0], recur_gates[0], jnp.zeros((row_count, 3 * hidden), jnp.float32))
        context = low_back(low(jnp.tanh(low_back(dense_product(low(last_state), square[0])))))
        target_input = jnp.take(embedding[1], token_ids[1, batch_index].T, axis=0)
        ctx_drive = low_back(dense_product(context, context_gates))
        _, states = recurrence(target_input, keep_mask[1, batch_index].T, input_gates[1], recur_gates[1], ctx_drive)
        deep_pre = low_back(dense_product(low(states.reshape(token_count, hidden)), square[1]) + dense_product(target_input.reshape(token_count, -1), deep_embed.T))
        deep_pre = deep_pre.reshape(step_count, row_count, 2 * unit_count) + low_back(dense_product(context, deep_context))[None]
        smooth = low(jnp.logaddexp(deep_pre[..., :unit_count], deep_pre[..., unit_count:])).reshape(token_count, unit_count)
        labels = targets[batch_index].T.reshape(token_count)

        def head_block(block_input):
            block_smooth, block_labels = block_input
            logits = low_back(dense_product(block_smooth, softmax_weight.T))
            log_norm = jax.nn.logsumexp(logits, axis=1)
            picked = jnp.take_along_axis(logits, block_labels[:, None], axis=1)[:, 0]
            return jnp.sum(log_norm - picked)
        block_losses = lax.map(jax.checkpoint(head_block), (smooth.reshape(-1, block_rows, unit_count), labels.reshape(-1, block_rows)))
        total_loss = total_loss + jnp.sum(block_losses)
    return total_loss / (micro_count * row_count)

def reference(token_ids, resets, targets, embedding, input_gates, recur_gates, square, context_gates, deep_embed, deep_context, softmax_weight):
    keep_mask = (1 - resets).astype(jnp.float32)
    weights = tuple((weight_arg.astype(jnp.float32) for weight_arg in (embedding, input_gates, recur_gates, square, context_gates, deep_embed, deep_context, softmax_weight)))
    objective = partial(forward, token_ids=token_ids, keep_mask=keep_mask, targets=targets)
    total_loss, pullback = jax.vjp(objective, *weights)
    gradients = pullback(jnp.ones((), jnp.float32))
    return (total_loss, gradients[0], gradients[1], gradients[2], gradients[3], gradients[4], gradients[5], gradients[6], gradients[7])
```

```python
import functools

import jax
import jax.numpy as jnp
from jax import lax
from jax.experimental import pallas as pl
from jax.experimental.pallas import tpu as pltpu
from jax.sharding import PartitionSpec as P

MESH = pl.DeviceIdType.MESH
ANY = pl.BlockSpec(memory_space=pl.ANY)
VMEM = pl.BlockSpec(memory_space=pltpu.VMEM)
f32 = jnp.float32
bf16 = jnp.bfloat16
VMEM_LIMIT = 60 * 2**20


def nn(a, b):
    return jnp.dot(a, b, preferred_element_type=f32)


def nt(a, b):
    return lax.dot_general(a, b, (((1,), (1,)), ((), ())), preferred_element_type=f32)


def tn(a, b):
    return lax.dot_general(a, b, (((0,), (0,)), ((), ())), preferred_element_type=f32)


def factors(n):
    z = 4 if n % 8 == 0 else 1
    return z, n // (2 * z)


class Place:
    def __init__(self, n):
        self.Z, self.Y = factors(n)
        self.s = lax.axis_index("section")
        d = lax.axis_index("dp")
        self.d = d
        self.c = d % 2
        self.zy = d // 2
        self.y = self.zy % self.Y
        self.z = self.zy // self.Y

    def along_z(self, step):
        return lax.rem(self.z + step + self.Z, self.Z)

    def along_y(self, step):
        return lax.rem(self.y + step + self.Y, self.Y)

    def device(self, z, y, c):
        return (self.s, (z * self.Y + y) * 2 + c)

    def partners(self):
        found = [self.device(self.along_z(k), self.y, self.c) for k in range(1, self.Z)]
        found += [self.device(self.z, self.along_y(k), self.c) for k in range(1, self.Y)]
        return found + [self.device(self.z, self.y, 1 - self.c), (1 - self.s, self.d)]


def greet(devices):
    barrier = pltpu.get_barrier_semaphore()
    for device in devices:
        pl.semaphore_signal(barrier, inc=1, device_id=device, device_id_type=MESH)
    pl.semaphore_wait(barrier, len(devices))


def remote(src, dst, send, recv, device):
    return pltpu.make_async_remote_copy(
        src_ref=src, dst_ref=dst, send_sem=send, recv_sem=recv, device_id=device, device_id_type=MESH
    )


def arrival(ref, sem):
    return pltpu.make_async_copy(ref, ref, sem)


def gather_kernel(n, crossed, *refs):
    count = len(crossed)
    sources, outs = refs[:count], refs[count : 2 * count]
    z_sem, y_sem, c_sem, s_sem, l_sem, x_sem, xs_sem = refs[2 * count :]
    at = Place(n)
    Z, Y = at.Z, at.Y
    greet(at.partners())

    x_copies = []
    for item in range(count):
        if crossed[item]:
            copy = remote(
                sources[item],
                outs[item].at[at.s, at.zy, at.c],
                xs_sem.at[item],
                x_sem.at[item],
                (1 - at.s, at.d),
            )
            copy.start()
            x_copies.append(copy)

    units = []
    for item in range(count):
        if crossed[item]:
            units.append((item, outs[item].at[at.s], sources[item]))
        else:
            units.append((item, outs[item], sources[item]))
    own = len(units)
    for item in range(count):
        if crossed[item]:
            gathered = outs[item].at[1 - at.s]
            units.append((item, gathered, gathered.at[at.zy, at.c]))

    def spread(u, src, zy, z_slot, to_z, to_y):
        gathered = units[u][1]
        dst = gathered.at[zy, at.c]
        if to_z:
            for k in range(1, Z):
                remote(
                    src, dst, s_sem.at[u], z_sem.at[u, k - 1], at.device(at.along_z(k), at.y, at.c)
                ).start()
        if to_y:
            for k in range(1, Y):
                remote(
                    src,
                    dst,
                    s_sem.at[u],
                    y_sem.at[u, z_slot * (Y - 1) + k - 1],
                    at.device(at.z, at.along_y(k), at.c),
                ).start()
        remote(src, dst, s_sem.at[u], c_sem.at[u], at.device(at.z, at.y, 1 - at.c)).start()

    for u, (item, gathered, src) in enumerate(units):
        if u < own:
            pltpu.make_async_copy(src, gathered.at[at.zy, at.c], l_sem.at[u]).start()
        else:
            arrival(src, x_sem.at[item]).wait()
        spread(u, src, at.zy, 0, True, True)
    for u, (item, gathered, _) in enumerate(units):
        for k in range(1, Z):
            zy = at.along_z(-k) * Y + at.y
            block = gathered.at[zy, at.c]
            arrival(block, z_sem.at[u, k - 1]).wait()
            spread(u, block, zy, k, False, True)
        for slot in range(Z):
            for k in range(1, Y):
                zy = at.along_z(-slot) * Y + at.along_y(-k)
                block = gathered.at[zy, at.c]
                arrival(block, y_sem.at[u, slot * (Y - 1) + k - 1]).wait()
                spread(u, block, zy, 0, False, False)
    for u, (item, gathered, src) in enumerate(units):
        if u < own:
            pltpu.make_async_copy(src, gathered.at[at.zy, at.c], l_sem.at[u]).wait()
        theirs = gathered.at[:, 1 - at.c]
        arrival(theirs, c_sem.at[u]).wait()
        most = gathered.at[pl.ds(0, Z * Y - 1)]
        arrival(most, s_sem.at[u]).wait()
        arrival(gathered.at[0, 0], s_sem.at[u]).wait()
    for copy in x_copies:
        copy.wait_send()


def gather(n, arrays, crossed):
    Z, Y = factors(n)
    shapes = []
    for array, over_section in zip(arrays, crossed):
        lead = (2, Z * Y, 2) if over_section else (Z * Y, 2)
        shapes.append(jax.ShapeDtypeStruct(lead + array.shape, array.dtype))
    units = len(arrays) + sum(crossed)
    dma = pltpu.SemaphoreType.DMA
    return pl.pallas_call(
        functools.partial(gather_kernel, n, crossed),
        out_shape=shapes,
        in_specs=[ANY] * len(arrays),
        out_specs=[ANY] * len(arrays),
        scratch_shapes=[
            dma((units, max(Z - 1, 1))),
            dma((units, max(Z * (Y - 1), 1))),
            dma((units,)),
            dma((units,)),
            dma((units,)),
            dma((len(arrays),)),
            dma((len(arrays),)),
        ],
        compiler_params=pltpu.CompilerParams(collective_id=0, has_side_effects=True),
    )(*arrays)


def add_blocks(rows, terms, out, out_type):
    chunk = 16 if rows % 16 == 0 else rows

    def body(i, _):
        part = pl.ds(pl.multiple_of(i * chunk, chunk), chunk)
        total = terms[0][part, :].astype(f32)
        for term in terms[1:]:
            total = total + term[part, :].astype(f32)
        out[part, :] = total.astype(out_type)
        return _

    lax.fori_loop(0, rows // chunk, body, 0)


def scatter_kernel(n, count, *refs):
    sources, outs = refs[:count], refs[count : 2 * count]
    scratch = refs[2 * count :]
    mine, from_c, from_y, from_z = (scratch[k * count : (k + 1) * count] for k in range(4))
    l_sem, cs_sem, cr_sem, ys_sem, yr_sem, zs_sem, zr_sem = scratch[4 * count :]
    at = Place(n)
    Z, Y = at.Z, at.Y
    greet(at.partners()[:-1])

    c_copies, l_copies, y_copies, z_copies = [], [], [], []
    for i in range(count):
        copy = remote(
            sources[i].at[:, 1 - at.c],
            from_c[i],
            cs_sem.at[i],
            cr_sem.at[i],
            at.device(at.z, at.y, 1 - at.c),
        )
        copy.start()
        c_copies.append(copy)
        copy = pltpu.make_async_copy(sources[i].at[:, at.c], mine[i], l_sem.at[i])
        copy.start()
        l_copies.append(copy)

    def after_core(i):
        c_copies[i].wait_recv()
        l_copies[i].wait()
        rows = mine[i].shape[1]
        for k in list(range(1, Y)) + [0]:
            y = at.along_y(k)

            def per_z(z, _):
                zy = z * Y + y
                add_blocks(rows, [mine[i].at[zy], from_c[i].at[zy]], mine[i].at[zy], mine[i].dtype)
                return _

            lax.fori_loop(0, Z, per_z, 0)
            if k:
                for z in range(Z):
                    copy = remote(
                        mine[i].at[z * Y + y],
                        from_y[i].at[k - 1, z],
                        ys_sem.at[i, k - 1, z],
                        yr_sem.at[i, k - 1, z],
                        at.device(at.z, y, at.c),
                    )
                    copy.start()
                    y_copies.append(copy)

    def after_y(i):
        rows = mine[i].shape[1]
        for k in list(range(1, Z)) + [0]:
            z = at.along_z(k)
            block = mine[i].at[z * Y + at.y]
            for j in range(1, Y):
                arrival(from_y[i].at[j - 1, z], yr_sem.at[i, j - 1, z]).wait()
            terms = [block] + [from_y[i].at[j - 1, z] for j in range(1, Y)]
            add_blocks(rows, terms, block, mine[i].dtype)
            if k:
                copy = remote(
                    block,
                    from_z[i].at[k - 1],
                    zs_sem.at[i, k - 1],
                    zr_sem.at[i, k - 1],
                    at.device(z, at.y, at.c),
                )
                copy.start()
                z_copies.append(copy)

    def after_z(i):
        rows = mine[i].shape[1]
        for k in range(1, Z):
            arrival(from_z[i].at[k - 1], zr_sem.at[i, k - 1]).wait()
        terms = [mine[i].at[at.zy]] + [from_z[i].at[k - 1] for k in range(1, Z)]
        add_blocks(rows, terms, outs[i], outs[i].dtype)

    for turn in range(count + 2):
        if turn < count:
            after_core(turn)
        if 0 <= turn - 1 < count:
            after_y(turn - 1)
        if turn - 2 >= 0:
            after_z(turn - 2)
    for copy in c_copies + y_copies + z_copies:
        copy.wait_send()


def scatter(n, arrays):
    Z, Y = factors(n)
    count = len(arrays)
    blocks = [a.shape[-2:] for a in arrays]
    arrays = [a.reshape((Z * Y, 2) + b) for a, b in zip(arrays, blocks)]
    dma = pltpu.SemaphoreType.DMA
    scratch = [pltpu.VMEM((Z * Y,) + b, a.dtype) for a, b in zip(arrays, blocks)]
    scratch += [pltpu.VMEM((Z * Y,) + b, a.dtype) for a, b in zip(arrays, blocks)]
    scratch += [pltpu.VMEM((max(Y - 1, 1), Z) + b, a.dtype) for a, b in zip(arrays, blocks)]
    scratch += [pltpu.VMEM((max(Z - 1, 1),) + b, a.dtype) for a, b in zip(arrays, blocks)]
    return pl.pallas_call(
        functools.partial(scatter_kernel, n, count),
        out_shape=[jax.ShapeDtypeStruct(b, f32) for b in blocks],
        in_specs=[ANY] * count,
        out_specs=[VMEM] * count,
        scratch_shapes=scratch
        + [
            dma((count,)),
            dma((count,)),
            dma((count,)),
            dma((count, max(Y - 1, 1), Z)),
            dma((count, max(Y - 1, 1), Z)),
            dma((count, max(Z - 1, 1))),
            dma((count, max(Z - 1, 1))),
        ],
        compiler_params=pltpu.CompilerParams(
            collective_id=1, has_side_effects=True, vmem_limit_bytes=VMEM_LIMIT
        ),
    )(*arrays)


def forward_kernel(emb, wi, wr, ctx, keep, z_o, r_o, n_o, m_o, p_o, h_o, drive):
    R, H = ctx.shape[0], wr.shape[0]
    drive[...] = nt(emb[...], wi[...])

    def step(t, h):
        rows = pl.ds(pl.multiple_of(t * R, R), R)
        p = h * keep[rows, :]
        p_o[rows, :] = p
        rec = nn(p.astype(bf16), wr[...])
        d = drive[rows, :]
        z = jax.nn.sigmoid(d[:, :H] + rec[:, :H] + ctx[:, :H])
        r = jax.nn.sigmoid(d[:, H : 2 * H] + rec[:, H : 2 * H] + ctx[:, H : 2 * H])
        m = rec[:, 2 * H :] + ctx[:, 2 * H :]
        n = jnp.tanh(d[:, 2 * H :] + r * m)
        h = z * p + (1.0 - z) * n
        z_o[rows, :] = z
        r_o[rows, :] = r
        n_o[rows, :] = n
        m_o[rows, :] = m
        h_o[rows, :] = h.astype(bf16)
        return h

    lax.fori_loop(0, emb.shape[0] // R, step, jnp.zeros((R, H), f32))


def gru_forward(emb, wi, wr, ctx, keep):
    tokens, H = emb.shape[0], wr.shape[0]
    shape = jax.ShapeDtypeStruct
    return pl.pallas_call(
        forward_kernel,
        out_shape=[shape((tokens, H), f32)] * 5 + [shape((tokens, H), bf16)],
        in_specs=[VMEM] * 5,
        out_specs=[VMEM] * 6,
        scratch_shapes=[pltpu.VMEM((tokens, 3 * H), f32)],
        compiler_params=pltpu.CompilerParams(vmem_limit_bytes=VMEM_LIMIT),
    )(emb, wi, wr, ctx, keep)


def backward_kernel(sg, carry0, keep, z, r, n, m, p, wr, low_o, cand_o, sum_o):
    R, H = carry0.shape
    steps = sg.shape[0] // R

    def step(i, carry):
        rows = pl.ds(pl.multiple_of((steps - 1 - i) * R, R), R)
        g = sg[rows, :] + carry
        zz = z[rows, :]
        cand = n[rows, :]
        rr = r[rows, :]
        pc = g * (1.0 - zz) * (1.0 - cand * cand)
        pz = g * (p[rows, :] - cand) * zz * (1.0 - zz)
        pr = pc * m[rows, :] * rr * (1.0 - rr)
        rec = jnp.concatenate([pz, pr, pc * rr], axis=1)
        low = rec.astype(bf16)
        low_o[rows, :] = low
        cand_o[rows, :] = pc.astype(bf16)
        sum_o[...] += rec
        return (g * zz + nt(low, wr[...])) * keep[rows, :]

    sum_o[...] = jnp.zeros_like(sum_o)
    lax.fori_loop(0, steps, step, carry0[...])


def gru_backward(sg, carry0, keep, record, wr):
    z, r, n, m, p = record
    tokens, H = sg.shape
    shape = jax.ShapeDtypeStruct
    return pl.pallas_call(
        backward_kernel,
        out_shape=[
            shape((tokens, 3 * H), bf16),
            shape((tokens, H), bf16),
            shape((carry0.shape[0], 3 * H), f32),
        ],
        in_specs=[VMEM] * 9,
        out_specs=[VMEM] * 3,
        compiler_params=pltpu.CompilerParams(vmem_limit_bytes=VMEM_LIMIT),
    )(sg, carry0, keep, z, r, n, m, p, wr)


def request_slots(ids, n, per, slots):
    count = ids.shape[0]
    index = jnp.arange(count, dtype=jnp.int32)
    same = ids[:, None] == ids[None, :]
    first = jnp.min(jnp.where(same, index[None, :], count), axis=1)
    leads = first == index
    owner = ids // per
    ahead = (owner[:, None] == owner[None, :]) & leads[None, :] & (index[None, :] < first[:, None])
    rank = jnp.sum(ahead.astype(jnp.int32), axis=1)
    return leads, owner, rank, ids - owner * per


def round_maps(plan, turn, n, slots):
    leads, owner, rank, local = plan
    place = rank - turn * slots
    inside = (place >= 0) & (place < slots)
    place = jnp.where(inside, owner * slots + place, -1)
    hit = place[:, None] == jnp.arange(n * slots, dtype=jnp.int32)[None, :]
    asked = jnp.max(jnp.where(hit & leads[:, None], local[:, None], -1), axis=0)
    return asked, hit.astype(bf16)


def swap(x, n):
    shape = x.shape
    return lax.all_to_all(x.reshape((n, -1) + shape[1:]), "dp", 0, 0, tiled=False).reshape(shape)


def owner_map(asked, n, per):
    asked_here = swap(asked, n)
    return (asked_here[:, None] == jnp.arange(per, dtype=jnp.int32)[None, :]).astype(bf16)


def per_device(
    token_ids,
    resets,
    targets,
    embedding,
    input_gates,
    recur_gates,
    square,
    context_gates,
    deep_embed,
    deep_context,
    softmax_weight,
):
    n = lax.axis_size("dp")
    s = lax.axis_index("section")
    d = lax.axis_index("dp")
    is_decoder = s == 1
    micro, rows, steps = token_ids.shape[1:]
    R = micro * rows
    tokens = R * steps
    H = square.shape[2]
    E = embedding.shape[2]
    M = softmax_weight.shape[1]
    per = embedding.shape[1]
    slots = max(512 // n, 8)
    scale = 1.0 / (R * n)

    def time_major(x):
        return jnp.transpose(x.reshape(R, steps), (1, 0)).reshape(-1)

    ids = time_major(token_ids[0])
    keep = time_major(1 - resets[0]).astype(f32)[:, None]
    labels = time_major(targets)

    plan = request_slots(ids, n, per, slots)
    rounds = lax.pmax(jnp.max(plan[2]) // slots + 1, ("section", "dp"))
    table = embedding[0]

    def fetch(turn):
        asked, hit = round_maps(plan, turn, n, slots)
        owners = owner_map(asked, n, per)
        came = swap(nn(owners, table).astype(bf16), n)
        return owners, hit, nn(hit, came).astype(bf16)

    owners, hit, emb = fetch(0)

    def more(carry):
        turn, emb = carry
        return turn + 1, emb + fetch(turn)[2]

    _, emb = lax.while_loop(lambda c: c[0] < rounds, more, (jnp.int32(1), emb))

    wr, wi, sq, sm, cg, de, dc = gather(
        n,
        [
            recur_gates[0],
            input_gates[0],
            square[0],
            softmax_weight,
            context_gates,
            deep_embed,
            deep_context,
        ],
        (False, False, False, False, True, True, True),
    )
    wr, wi, sq, sm = wr.reshape(H, 3 * H), wi.reshape(3 * H, E), sq.reshape(H, H), sm.reshape(-1, M)
    cg, de, dc = cg.reshape(H, 3 * H), de.reshape(2 * M, E), dc.reshape(H, 2 * M)

    enc = gru_forward(emb, wi, wr, jnp.zeros((R, 3 * H), f32), keep)
    last_low = enc[5][-R:]
    ctx_tanh = jnp.tanh(nn(last_low, sq))
    context = lax.ppermute(ctx_tanh.astype(bf16), "section", [(0, 1)])

    dec = gru_forward(emb, wi, wr, nn(context, cg), keep)
    states_low = dec[5]
    deep_pre = nn(states_low, sq) + nt(emb, de)
    deep_pre = (deep_pre.reshape(steps, R, -1) + nn(context, dc)[None]).reshape(tokens, -1)
    smooth = jnp.logaddexp(deep_pre[:, :M], deep_pre[:, M:])
    smooth_low = smooth.astype(bf16)

    came = lax.ppermute(smooth_low, "section", [(1, 0)])
    head_in = jnp.where(is_decoder, smooth_low, came)
    words = sm.shape[0]
    logits = nt(head_in, sm)
    top = jnp.max(logits, axis=1)
    total = jnp.sum(jnp.exp(logits - top[:, None]), axis=1)
    hits = lax.broadcasted_iota(jnp.int32, logits.shape, 1) == (labels - s * words)[:, None]
    picked = jnp.sum(jnp.where(hits, logits, 0.0), axis=1)
    stats = jnp.stack([top, total, picked])
    other = lax.ppermute(stats, "section", [(0, 1), (1, 0)])
    all_top = jnp.maximum(top, other[0])
    log_norm = all_top + jnp.log(
        total * jnp.exp(top - all_top) + other[1] * jnp.exp(other[0] - all_top)
    )
    loss = jnp.where(is_decoder, jnp.sum(log_norm - picked - other[2]) * scale, 0.0)
    logit_low = ((jnp.exp(logits - log_norm[:, None]) - hits.astype(f32)) * scale).astype(bf16)
    smooth_part = nn(logit_low, sm)
    smooth_grad = smooth_part + lax.ppermute(smooth_part, "section", [(0, 1)])
    softmax_term = tn(logit_low, head_in).astype(bf16)

    deep_grad = jnp.concatenate(
        [
            smooth_grad * jnp.exp(deep_pre[:, :M] - smooth),
            smooth_grad * jnp.exp(deep_pre[:, M:] - smooth),
        ],
        axis=1,
    )
    deep_low = deep_grad.astype(bf16)
    outer_low = jnp.sum(deep_grad.reshape(steps, R, -1), axis=0).astype(bf16)
    state_grad = nt(deep_low, sq)
    dec_low, dec_cand, drive_sum = gru_backward(
        state_grad, jnp.zeros((R, H), f32), keep, dec[:5], wr
    )
    drive_sum_low = drive_sum.astype(bf16)
    context_grad = (nt(outer_low, dc) + nt(drive_sum_low, cg)).astype(bf16)
    packed = lax.all_gather(jnp.concatenate([context, outer_low, drive_sum_low], axis=1), "dp", tiled=True)
    packed_came = lax.ppermute(packed, "section", [(1, 0)])
    packed = jnp.where(is_decoder, packed, packed_came)

    context_back = lax.ppermute(context_grad, "section", [(1, 0)])
    pre_low = (context_back.astype(f32) * (1.0 - ctx_tanh * ctx_tanh)).astype(bf16)
    enc_low, enc_cand, _ = gru_backward(
        jnp.zeros((tokens, H), f32), nt(pre_low, sq), keep, enc[:5], wr
    )

    def pick(of_encoder, of_decoder):
        return jnp.where(is_decoder, of_decoder, of_encoder)

    recur_low = pick(enc_low, dec_low)
    cand_low = pick(enc_cand, dec_cand)
    before_low = pick(enc[4], dec[4]).astype(bf16)
    drive_low = jnp.concatenate([recur_low[:, : 2 * H], cand_low], axis=1)
    recur_term = tn(before_low, recur_low).astype(bf16)
    input_term = tn(drive_low, emb).astype(bf16)
    deep_mask = jnp.where(is_decoder, deep_low, jnp.zeros_like(deep_low))
    input_grad = nn(drive_low, wi) + nn(deep_mask, de)
    rows_pad = jnp.zeros((tokens - R, H), bf16)
    square_term = tn(
        pick(jnp.concatenate([last_low, rows_pad]), states_low),
        pick(jnp.concatenate([pre_low, rows_pad]), deep_low),
    ).astype(bf16)
    deep_term = tn(deep_mask, emb).astype(bf16)

    input_grad_low = input_grad.astype(bf16)

    def give(owners, hit):
        return tn(owners, swap(tn(hit, input_grad_low).astype(bf16), n))

    def give_more(carry):
        turn, grad = carry
        asked, hit = round_maps(plan, turn, n, slots)
        return turn + 1, grad + give(owner_map(asked, n, per), hit)

    table_grad = give(owners, hit)
    _, table_grad = lax.while_loop(
        lambda c: c[0] < rounds, give_more, (jnp.int32(1), table_grad)
    )

    deep_blocks = jnp.stack(
        [x.reshape((n,) + deep_embed.shape) for x in jnp.split(deep_term, 2)], axis=1
    )
    deep_blocks = deep_blocks.reshape(n, 2 * deep_embed.shape[0], E)
    loss_blocks = jnp.broadcast_to(loss, (n, 8, 128))
    square_sum, recur_sum, input_sum, softmax_sum, deep_sum, loss_sum = scatter(
        n,
        [
            square_term.reshape((n,) + square.shape[1:]),
            recur_term.reshape((n,) + recur_gates.shape[1:]),
            input_term.reshape((n,) + input_gates.shape[1:]),
            softmax_term.reshape((n,) + softmax_weight.shape),
            deep_blocks,
            loss_blocks,
        ],
    )
    deep_halves = deep_sum.reshape((2,) + deep_embed.shape)
    both = lax.ppermute(
        jnp.concatenate([deep_halves[0].reshape(-1), loss_sum[:1].reshape(-1)]), "section", [(1, 0)]
    )
    deep_out = jnp.where(is_decoder, deep_halves[1], both[:-128].reshape(deep_embed.shape))
    loss_out = jnp.where(is_decoder, loss_sum[0, 0], both[-1])

    own = (s * n + d) * context_gates.shape[0]
    context_own = lax.dynamic_slice(packed, (0, own), (packed.shape[0], context_gates.shape[0]))
    gates_out = tn(context_own, packed[:, H + 2 * M :])
    context_out = tn(context_own, packed[:, H : H + 2 * M])

    return (
        loss_out,
        table_grad[None],
        input_sum[None],
        recur_sum[None],
        square_sum[None],
        gates_out,
        deep_out,
        context_out,
        softmax_sum,
    )


def solution(mesh):
    halves = P("section", "dp", None)
    whole = P(("section", "dp"), None)
    in_specs = (
        P("section", None, "dp", None),
        P("section", None, "dp", None),
        P(None, "dp", None),
        halves,
        halves,
        halves,
        halves,
        whole,
        whole,
        whole,
        whole,
    )
    out_specs = (P(), halves, halves, halves, halves, whole, whole, whole, whole)
    return jax.shard_map(
        per_device, mesh=mesh, in_specs=in_specs, out_specs=out_specs, check_vma=False
    )
```

```python
import functools

import jax
import jax.numpy as jnp
from jax import lax
from jax.experimental import pallas as pl
from jax.experimental.pallas import tpu as pltpu
from jax.sharding import PartitionSpec as P

MESH = pl.DeviceIdType.MESH
ANY = pl.BlockSpec(memory_space=pl.ANY)
VMEM = pl.BlockSpec(memory_space=pltpu.VMEM)
f32 = jnp.float32
bf16 = jnp.bfloat16
VMEM_LIMIT = 60 * 2**20


def nn(a, b):
    return jnp.dot(a, b, preferred_element_type=f32)


def nt(a, b):
    return lax.dot_general(a, b, (((1,), (1,)), ((), ())), preferred_element_type=f32)


def tn(a, b):
    return lax.dot_general(a, b, (((0,), (0,)), ((), ())), preferred_element_type=f32)


def factors(n):
    z = 4 if n % 8 == 0 else 1
    return z, n // (2 * z)


class Place:
    def __init__(self, n):
        self.Z, self.Y = factors(n)
        self.s = lax.axis_index("section")
        d = lax.axis_index("dp")
        self.d = d
        self.c = d % 2
        self.zy = d // 2
        self.y = self.zy % self.Y
        self.z = self.zy // self.Y

    def along_z(self, step):
        return lax.rem(self.z + step + self.Z, self.Z)

    def along_y(self, step):
        return lax.rem(self.y + step + self.Y, self.Y)

    def device(self, z, y, c):
        return (self.s, (z * self.Y + y) * 2 + c)

    def partners(self):
        found = [self.device(self.along_z(k), self.y, self.c) for k in range(1, self.Z)]
        found += [self.device(self.z, self.along_y(k), self.c) for k in range(1, self.Y)]
        return found + [self.device(self.z, self.y, 1 - self.c), (1 - self.s, self.d)]


def greet(devices):
    barrier = pltpu.get_barrier_semaphore()
    for device in devices:
        pl.semaphore_signal(barrier, inc=1, device_id=device, device_id_type=MESH)
    pl.semaphore_wait(barrier, len(devices))


def remote(src, dst, send, recv, device):
    return pltpu.make_async_remote_copy(
        src_ref=src, dst_ref=dst, send_sem=send, recv_sem=recv, device_id=device, device_id_type=MESH
    )


def arrival(ref, sem):
    return pltpu.make_async_copy(ref, ref, sem)


def gather_kernel(n, crossed, *refs):
    count = len(crossed)
    sources, outs = refs[:count], refs[count : 2 * count]
    z_sem, y_sem, c_sem, s_sem, l_sem, x_sem, xs_sem = refs[2 * count :]
    at = Place(n)
    Z, Y = at.Z, at.Y
    greet(at.partners())

    x_copies = []
    for item in range(count):
        if crossed[item]:
            copy = remote(
                sources[item],
                outs[item].at[at.s, at.zy, at.c],
                xs_sem.at[item],
                x_sem.at[item],
                (1 - at.s, at.d),
            )
            copy.start()
            x_copies.append(copy)

    units = []
    for item in range(count):
        if crossed[item]:
            units.append((item, outs[item].at[at.s], sources[item]))
        else:
            units.append((item, outs[item], sources[item]))
    own = len(units)
    for item in range(count):
        if crossed[item]:
            gathered = outs[item].at[1 - at.s]
            units.append((item, gathered, gathered.at[at.zy, at.c]))

    def spread(u, src, zy, z_slot, to_z, to_y):
        gathered = units[u][1]
        dst = gathered.at[zy, at.c]
        if to_z:
            for k in range(1, Z):
                remote(
                    src, dst, s_sem.at[u], z_sem.at[u, k - 1], at.device(at.along_z(k), at.y, at.c)
                ).start()
        if to_y:
            for k in range(1, Y):
                remote(
                    src,
                    dst,
                    s_sem.at[u],
                    y_sem.at[u, z_slot * (Y - 1) + k - 1],
                    at.device(at.z, at.along_y(k), at.c),
                ).start()
        remote(src, dst, s_sem.at[u], c_sem.at[u], at.device(at.z, at.y, 1 - at.c)).start()

    for u, (item, gathered, src) in enumerate(units):
        if u < own:
            pltpu.make_async_copy(src, gathered.at[at.zy, at.c], l_sem.at[u]).start()
        else:
            arrival(src, x_sem.at[item]).wait()
        spread(u, src, at.zy, 0, True, True)
    for u, (item, gathered, _) in enumerate(units):
        for k in range(1, Z):
            zy = at.along_z(-k) * Y + at.y
            block = gathered.at[zy, at.c]
            arrival(block, z_sem.at[u, k - 1]).wait()
            spread(u, block, zy, k, False, True)
        for slot in range(Z):
            for k in range(1, Y):
                zy = at.along_z(-slot) * Y + at.along_y(-k)
                block = gathered.at[zy, at.c]
                arrival(block, y_sem.at[u, slot * (Y - 1) + k - 1]).wait()
                spread(u, block, zy, 0, False, False)
    for u, (item, gathered, src) in enumerate(units):
        if u < own:
            pltpu.make_async_copy(src, gathered.at[at.zy, at.c], l_sem.at[u]).wait()
        theirs = gathered.at[:, 1 - at.c]
        arrival(theirs, c_sem.at[u]).wait()
        most = gathered.at[pl.ds(0, Z * Y - 1)]
        arrival(most, s_sem.at[u]).wait()
        arrival(gathered.at[0, 0], s_sem.at[u]).wait()
    for copy in x_copies:
        copy.wait_send()


def gather(n, arrays, crossed):
    Z, Y = factors(n)
    shapes = []
    for array, over_section in zip(arrays, crossed):
        lead = (2, Z * Y, 2) if over_section else (Z * Y, 2)
        shapes.append(jax.ShapeDtypeStruct(lead + array.shape, array.dtype))
    units = len(arrays) + sum(crossed)
    dma = pltpu.SemaphoreType.DMA
    return pl.pallas_call(
        functools.partial(gather_kernel, n, crossed),
        out_shape=shapes,
        in_specs=[ANY] * len(arrays),
        out_specs=[ANY] * len(arrays),
        scratch_shapes=[
            dma((units, max(Z - 1, 1))),
            dma((units, max(Z * (Y - 1), 1))),
            dma((units,)),
            dma((units,)),
            dma((units,)),
            dma((len(arrays),)),
            dma((len(arrays),)),
        ],
        compiler_params=pltpu.CompilerParams(collective_id=0, has_side_effects=True),
    )(*arrays)


def add_blocks(rows, terms, out, out_type):
    chunk = 16 if rows % 16 == 0 else rows

    def body(i, _):
        part = pl.ds(pl.multiple_of(i * chunk, chunk), chunk)
        total = terms[0][part, :].astype(f32)
        for term in terms[1:]:
            total = total + term[part, :].astype(f32)
        out[part, :] = total.astype(out_type)
        return _

    lax.fori_loop(0, rows // chunk, body, 0)


def scatter_kernel(n, count, *refs):
    sources, outs = refs[:count], refs[count : 2 * count]
    scratch = refs[2 * count :]
    mine, from_c, from_y, from_z = (scratch[k * count : (k + 1) * count] for k in range(4))
    l_sem, cs_sem, cr_sem, ys_sem, yr_sem, zs_sem, zr_sem = scratch[4 * count :]
    at = Place(n)
    Z, Y = at.Z, at.Y
    greet(at.partners()[:-1])

    c_copies, l_copies, y_copies, z_copies = [], [], [], []
    for i in range(count):
        copy = remote(
            sources[i].at[:, 1 - at.c],
            from_c[i],
            cs_sem.at[i],
            cr_sem.at[i],
            at.device(at.z, at.y, 1 - at.c),
        )
        copy.start()
        c_copies.append(copy)
        copy = pltpu.make_async_copy(sources[i].at[:, at.c], mine[i], l_sem.at[i])
        copy.start()
        l_copies.append(copy)

    def after_core(i):
        c_copies[i].wait_recv()
        l_copies[i].wait()
        rows = mine[i].shape[1]
        for k in list(range(1, Y)) + [0]:
            y = at.along_y(k)

            def per_z(z, _):
                zy = z * Y + y
                add_blocks(rows, [mine[i].at[zy], from_c[i].at[zy]], mine[i].at[zy], mine[i].dtype)
                return _

            lax.fori_loop(0, Z, per_z, 0)
            if k:
                for z in range(Z):
                    copy = remote(
                        mine[i].at[z * Y + y],
                        from_y[i].at[k - 1, z],
                        ys_sem.at[i, k - 1, z],
                        yr_sem.at[i, k - 1, z],
                        at.device(at.z, y, at.c),
                    )
                    copy.start()
                    y_copies.append(copy)

    def after_y(i):
        rows = mine[i].shape[1]
        for k in list(range(1, Z)) + [0]:
            z = at.along_z(k)
            block = mine[i].at[z * Y + at.y]
            for j in range(1, Y):
                arrival(from_y[i].at[j - 1, z], yr_sem.at[i, j - 1, z]).wait()
            terms = [block] + [from_y[i].at[j - 1, z] for j in range(1, Y)]
            add_blocks(rows, terms, block, mine[i].dtype)
            if k:
                copy = remote(
                    block,
                    from_z[i].at[k - 1],
                    zs_sem.at[i, k - 1],
                    zr_sem.at[i, k - 1],
                    at.device(z, at.y, at.c),
                )
                copy.start()
                z_copies.append(copy)

    def after_z(i):
        rows = mine[i].shape[1]
        for k in range(1, Z):
            arrival(from_z[i].at[k - 1], zr_sem.at[i, k - 1]).wait()
        terms = [mine[i].at[at.zy]] + [from_z[i].at[k - 1] for k in range(1, Z)]
        add_blocks(rows, terms, outs[i], outs[i].dtype)

    for turn in range(count + 2):
        if turn < count:
            after_core(turn)
        if 0 <= turn - 1 < count:
            after_y(turn - 1)
        if turn - 2 >= 0:
            after_z(turn - 2)
    for copy in c_copies + y_copies + z_copies:
        copy.wait_send()


def scatter(n, arrays, collective_id):
    Z, Y = factors(n)
    count = len(arrays)
    blocks = [a.shape[-2:] for a in arrays]
    arrays = [a.reshape((Z * Y, 2) + b) for a, b in zip(arrays, blocks)]
    dma = pltpu.SemaphoreType.DMA
    scratch = [pltpu.VMEM((Z * Y,) + b, a.dtype) for a, b in zip(arrays, blocks)]
    scratch += [pltpu.VMEM((Z * Y,) + b, a.dtype) for a, b in zip(arrays, blocks)]
    scratch += [pltpu.VMEM((max(Y - 1, 1), Z) + b, a.dtype) for a, b in zip(arrays, blocks)]
    scratch += [pltpu.VMEM((max(Z - 1, 1),) + b, a.dtype) for a, b in zip(arrays, blocks)]
    return pl.pallas_call(
        functools.partial(scatter_kernel, n, count),
        out_shape=[jax.ShapeDtypeStruct(b, f32) for b in blocks],
        in_specs=[ANY] * count,
        out_specs=[VMEM] * count,
        scratch_shapes=scratch
        + [
            dma((count,)),
            dma((count,)),
            dma((count,)),
            dma((count, max(Y - 1, 1), Z)),
            dma((count, max(Y - 1, 1), Z)),
            dma((count, max(Z - 1, 1))),
            dma((count, max(Z - 1, 1))),
        ],
        compiler_params=pltpu.CompilerParams(
            collective_id=collective_id, has_side_effects=True, vmem_limit_bytes=VMEM_LIMIT
        ),
    )(*arrays)


def scan_kernel(emb, wi, wr, ctx, keep, z_o, r_o, n_o, m_o, p_o, h_o, drive):
    R, H = ctx.shape[0], wr.shape[0]
    drive[...] = nt(emb[...], wi[...])

    def step(t, h):
        rows = pl.ds(pl.multiple_of(t * R, R), R)
        p = h * keep[rows, :]
        p_o[rows, :] = p
        rec = nn(p.astype(bf16), wr[...])
        d = drive[rows, :]
        z = jax.nn.sigmoid(d[:, :H] + rec[:, :H] + ctx[:, :H])
        r = jax.nn.sigmoid(d[:, H : 2 * H] + rec[:, H : 2 * H] + ctx[:, H : 2 * H])
        m = rec[:, 2 * H :] + ctx[:, 2 * H :]
        n = jnp.tanh(d[:, 2 * H :] + r * m)
        h = z * p + (1.0 - z) * n
        z_o[rows, :] = z
        r_o[rows, :] = r
        n_o[rows, :] = n
        m_o[rows, :] = m
        h_o[rows, :] = h.astype(bf16)
        return h

    lax.fori_loop(0, emb.shape[0] // R, step, jnp.zeros((R, H), f32))


def gru_forward(emb, wi, wr, ctx, keep):
    tokens, H = emb.shape[0], wr.shape[0]
    shape = jax.ShapeDtypeStruct
    return pl.pallas_call(
        scan_kernel,
        out_shape=[shape((tokens, H), f32)] * 5 + [shape((tokens, H), bf16)],
        in_specs=[VMEM] * 5,
        out_specs=[VMEM] * 6,
        scratch_shapes=[pltpu.VMEM((tokens, 3 * H), f32)],
        compiler_params=pltpu.CompilerParams(vmem_limit_bytes=VMEM_LIMIT),
    )(emb, wi, wr, ctx, keep)


def backward_kernel(sg, carry0, keep, z, r, n, m, p, wr, low_o, cand_o, sum_o):
    R, H = carry0.shape
    steps = sg.shape[0] // R

    def step(i, carry):
        rows = pl.ds(pl.multiple_of((steps - 1 - i) * R, R), R)
        g = sg[rows, :] + carry
        zz = z[rows, :]
        cand = n[rows, :]
        rr = r[rows, :]
        pc = g * (1.0 - zz) * (1.0 - cand * cand)
        pz = g * (p[rows, :] - cand) * zz * (1.0 - zz)
        pr = pc * m[rows, :] * rr * (1.0 - rr)
        rec = jnp.concatenate([pz, pr, pc * rr], axis=1)
        low = rec.astype(bf16)
        low_o[rows, :] = low
        cand_o[rows, :] = pc.astype(bf16)
        sum_o[...] += rec
        return (g * zz + nt(low, wr[...])) * keep[rows, :]

    sum_o[...] = jnp.zeros_like(sum_o)
    lax.fori_loop(0, steps, step, carry0[...])


def gru_backward(sg, carry0, keep, record, wr):
    z, r, n, m, p = record
    tokens, H = sg.shape
    shape = jax.ShapeDtypeStruct
    return pl.pallas_call(
        backward_kernel,
        out_shape=[
            shape((tokens, 3 * H), bf16),
            shape((tokens, H), bf16),
            shape((carry0.shape[0], 3 * H), f32),
        ],
        in_specs=[VMEM] * 9,
        out_specs=[VMEM] * 3,
        compiler_params=pltpu.CompilerParams(vmem_limit_bytes=VMEM_LIMIT),
    )(sg, carry0, keep, z, r, n, m, p, wr)


def request_slots(ids, n, per, slots):
    count = ids.shape[0]
    index = jnp.arange(count, dtype=jnp.int32)
    same = ids[:, None] == ids[None, :]
    first = jnp.min(jnp.where(same, index[None, :], count), axis=1)
    leads = first == index
    owner = ids // per
    ahead = (owner[:, None] == owner[None, :]) & leads[None, :] & (index[None, :] < first[:, None])
    rank = jnp.sum(ahead.astype(jnp.int32), axis=1)
    return leads, owner, rank, ids - owner * per


def round_maps(plan, turn, n, slots):
    leads, owner, rank, local = plan
    place = rank - turn * slots
    inside = (place >= 0) & (place < slots)
    place = jnp.where(inside, owner * slots + place, -1)
    hit = place[:, None] == jnp.arange(n * slots, dtype=jnp.int32)[None, :]
    asked = jnp.max(jnp.where(hit & leads[:, None], local[:, None], -1), axis=0)
    return asked, hit.astype(bf16)


def swap(x, n):
    shape = x.shape
    return lax.all_to_all(x.reshape((n, -1) + shape[1:]), "dp", 0, 0, tiled=False).reshape(shape)


def owner_map(asked, n, per):
    asked_here = swap(asked, n)
    return (asked_here[:, None] == jnp.arange(per, dtype=jnp.int32)[None, :]).astype(bf16)


def multiple(x, of):
    return pl.multiple_of(x, of)


class Unit:
    def __init__(self, index, src, dst, rows, base):
        self.index, self.src, self.dst, self.rows, self.base = index, src, dst, rows, base

    def block(self, zy, c):
        return self.dst.at[pl.ds(multiple(self.base + (zy * 2 + c) * self.rows, 16), self.rows)]

    def some(self, count):
        return self.dst.at[pl.ds(0, count * self.rows)]


class Gather:
    def __init__(self, at, z_sem, y_sem, c_sem, s_sem):
        self.at, self.z_sem, self.y_sem, self.c_sem, self.s_sem = at, z_sem, y_sem, c_sem, s_sem

    def to_y(self, u, src, dst, slot):
        at = self.at
        for k in range(1, at.Y):
            remote(
                src,
                dst,
                self.s_sem.at[u.index],
                self.y_sem.at[u.index, slot * (at.Y - 1) + k - 1],
                at.device(at.z, at.along_y(k), at.c),
            ).start()

    def to_core(self, u, src, dst):
        at = self.at
        remote(
            src, dst, self.s_sem.at[u.index], self.c_sem.at[u.index], at.device(at.z, at.y, 1 - at.c)
        ).start()

    def begin(self, u):
        at = self.at
        dst = u.block(at.zy, at.c)
        self.to_y(u, u.src, dst, 0)
        for k in range(1, at.Z):
            remote(
                u.src,
                dst,
                self.s_sem.at[u.index],
                self.z_sem.at[u.index, k - 1],
                at.device(at.along_z(k), at.y, at.c),
            ).start()
        self.to_core(u, u.src, dst)

    def pass_z(self, u):
        at = self.at
        for k in range(1, at.Z):
            block = u.block(at.along_z(-k) * at.Y + at.y, at.c)
            arrival(block, self.z_sem.at[u.index, k - 1]).wait()
            self.to_y(u, block, block, k)
            self.to_core(u, block, block)

    def pass_y(self, u):
        at = self.at
        for slot in range(at.Z):
            for k in range(1, at.Y):
                block = u.block(at.along_z(-slot) * at.Y + at.along_y(-k), at.c)
                arrival(block, self.y_sem.at[u.index, slot * (at.Y - 1) + k - 1]).wait()
                self.to_core(u, block, block)

    def end(self, u):
        blocks = self.at.Z * self.at.Y
        part = u.some(blocks)
        arrival(part, self.c_sem.at[u.index]).wait()
        part = u.some(2 * blocks - 1)
        arrival(part, self.s_sem.at[u.index]).wait()


def forward_kernel(n, sizes, *refs):
    R, H, E, M, slots, per, words = sizes
    (
        asked,
        hit,
        table,
        keep,
        labels,
        wr_s,
        wi_s,
        sq_s,
        sm_s,
        cg_s,
        de_s,
        dc_s,
    ) = refs[:12]
    (
        wr_o,
        wi_o,
        sq_o,
        cg_o,
        de_o,
        dc_o,
        term_o,
        rec_o,
        h_o,
        emb_o,
        pre_o,
        grad_o,
        tanh_o,
        ctx_o,
        loss_o,
        most_o,
        owners_o,
    ) = refs[12:29]
    (
        asked_in,
        rows_out,
        came,
        wr,
        wi,
        sq,
        sm,
        cg,
        de,
        dc,
        drive,
        rec,
        smooth_in,
        grad_out,
        m_part,
        s_part,
        p_part,
        fullest,
        z_sem,
        y_sem,
        c_sem,
        s_sem,
        l_sem,
        o_sem,
        x_recv,
        x_send,
        as_sem,
        ar_sem,
        rs_sem,
        rr_sem,
    ) = refs[29:]
    at = Place(n)
    tokens = hit.shape[0]
    steps = tokens // R
    is_decoder = at.s == 1
    beside = (1 - at.s, at.d)
    others = [lax.rem(at.d + k, n) for k in range(1, n)]
    greet([(at.s, d) for d in others] + [beside])

    def block_rows(ref, base, rows):
        return ref.at[pl.ds(multiple((base + at.d) * rows, 16), rows)]

    def to_beside(src, dst, k):
        return remote(src, dst, x_send.at[k], x_recv.at[k], beside)

    gather = Gather(at, z_sem, y_sem, c_sem, s_sem)
    u_wr = Unit(0, wr_s, wr, wr_s.shape[0], 0)
    u_wi = Unit(1, wi_s, wi, wi_s.shape[0], 0)
    u_sq = Unit(2, sq_s, sq, sq_s.shape[0], 0)
    own_sm = Unit(3, sm_s, sm, words, 0)
    far_sm = Unit(4, block_rows(sm, n, words), sm, words, n * words)
    crossed = []
    for k, (src, dst) in enumerate([(cg_s, cg), (de_s, de), (dc_s, dc)]):
        rows = src.shape[0]
        crossed.append(
            (
                Unit(3 + 2 * k, src, dst, rows, n * rows),
                Unit(4 + 2 * k, block_rows(dst, 0, rows), dst, rows, 0),
            )
        )

    asked_sends = []
    for k, d in enumerate(others):
        copy = remote(asked.at[d], asked_in.at[at.d], as_sem, ar_sem, (at.s, d))
        copy.start()
    gather.begin(u_wi)
    gather.begin(u_wr)

    @pl.when(is_decoder)
    def _():
        to_beside(sm_s, block_rows(sm, n, words), 0).start()

    @pl.when(jnp.logical_not(is_decoder))
    def _():
        for k, (src, dst) in enumerate([(cg_s, cg), (de_s, de), (dc_s, dc)]):
            to_beside(src, block_rows(dst, 0, src.shape[0]), 1 + k).start()

    locals_ = [
        pltpu.make_async_copy(src, block_rows(dst, 0, src.shape[0]), l_sem.at[k])
        for k, (src, dst) in enumerate([(wr_s, wr), (wi_s, wi), (sq_s, sq)])
    ]
    locals_.append(pltpu.make_async_copy(sm_s, block_rows(sm, 0, words), l_sem.at[3]))
    for k, (src, dst) in enumerate([(cg_s, cg), (de_s, de), (dc_s, dc)]):
        locals_.append(pltpu.make_async_copy(src, block_rows(dst, n, src.shape[0]), l_sem.at[4 + k]))
    for copy in locals_:
        copy.start()

    some_asked = asked_in.at[pl.ds(0, n - 1)]
    arrival(some_asked, ar_sem).wait()
    arrival(some_asked, as_sem).wait()
    asked_in[at.d] = asked[at.d]
    group = 128 // slots
    count = lax.broadcasted_iota(jnp.int32, (per, 128), 0)
    most = asked_in[0, 1:2, :]
    for g in range(n // group):
        wanted = asked_in[g * group, 0:1, :]
        for j in range(1, group):
            wanted = jnp.maximum(wanted, asked_in[g * group + j, 0:1, :])
        for j in range(group):
            most = jnp.maximum(most, asked_in[g * group + j, 1:2, :])
        match = (wanted == count).astype(f32).astype(bf16)
        owners_o[:, pl.ds(g * 128, 128)] = match
        rows_out[pl.ds(g * 128, 128), :] = tn(match, table[...]).astype(bf16)
    fullest[0] = jnp.broadcast_to(most, fullest.shape[1:])
    to_beside(fullest.at[0], fullest.at[1], 7).start()

    def slot_rows(ref, d):
        return ref.at[pl.ds(multiple(d * slots, 16), slots)]

    for d in others:
        remote(slot_rows(rows_out, d), slot_rows(came, at.d), rs_sem, rr_sem, (at.s, d)).start()
    gather.pass_z(u_wi)
    gather.pass_z(u_wr)

    @pl.when(is_decoder)
    def _():
        for own, _ in crossed[:1]:
            gather.begin(own)

    gather.begin(u_sq)

    @pl.when(is_decoder)
    def _():
        arrival(crossed[0][1].src, x_recv.at[1]).wait()
        gather.begin(crossed[0][1])
        for k, (own, far) in enumerate(crossed[1:]):
            gather.begin(own)
            arrival(far.src, x_recv.at[2 + k]).wait()
            gather.begin(far)

    @pl.when(jnp.logical_not(is_decoder))
    def _():
        gather.begin(own_sm)
        arrival(far_sm.src, x_recv.at[0]).wait()
        gather.begin(far_sm)

    gather.pass_y(u_wi)
    some_rows = came.at[pl.ds(0, (n - 1) * slots)]
    arrival(some_rows, rr_sem).wait()
    arrival(some_rows, rs_sem).wait()
    came[pl.ds(multiple(at.d * slots, 16), slots), :] = rows_out[
        pl.ds(multiple(at.d * slots, 16), slots), :
    ]
    emb_o[...] = nn(hit[...], came[...]).astype(bf16)
    to_beside(fullest.at[0], fullest.at[1], 7).wait()
    most_o[...] = jnp.maximum(fullest[0], fullest[1])
    for copy in locals_:
        copy.wait()
    gather.end(u_wi)

    def input_drive(i, _):
        cols = pl.ds(multiple(i * 512, 512), 512)
        drive[:, cols] = nt(emb_o[...], wi[cols, :])
        return _

    lax.fori_loop(0, 3 * H // 512, input_drive, 0)
    gather.pass_y(u_wr)
    gather.end(u_wr)

    def scan(ctx, service):
        def step(t, h):
            rows = pl.ds(multiple(t * R, R), R)
            p = h * keep[rows, :]
            rec[4, rows, :] = p
            mix = nn(p.astype(bf16), wr[...])
            d = drive[rows, :]
            z_in = d[:, :H] + mix[:, :H]
            r_in = d[:, H : 2 * H] + mix[:, H : 2 * H]
            m = mix[:, 2 * H :]
            if ctx is not None:
                z_in += ctx[:, :H]
                r_in += ctx[:, H : 2 * H]
                m += ctx[:, 2 * H :]
            z = jax.nn.sigmoid(z_in)
            r = jax.nn.sigmoid(r_in)
            cand = jnp.tanh(d[:, 2 * H :] + r * m)
            h = z * p + (1.0 - z) * cand
            rec[0, rows, :] = z
            rec[1, rows, :] = r
            rec[2, rows, :] = cand
            rec[3, rows, :] = m
            h_o[rows, :] = h.astype(bf16)
            for when, what in service:
                pl.when(t == when)(what)
            return h

        return lax.fori_loop(0, steps, step, jnp.zeros((R, H), f32))

    def keep_copies(pairs):
        copies = [pltpu.make_async_copy(a, b, o_sem.at[k]) for k, (a, b) in enumerate(pairs)]
        for copy in copies:
            copy.start()
        return copies

    last = pl.ds((steps - 1) * R, R)

    @pl.when(jnp.logical_not(is_decoder))
    def _():
        copies = keep_copies([(wr, wr_o), (wi, wi_o)])
        scan(None, [(2, lambda: gather.pass_z(u_sq)), (7, lambda: gather.pass_y(u_sq))])
        gather.end(u_sq)
        ctx_tanh = jnp.tanh(nn(h_o[last, :], sq[...]))
        tanh_o[...] = ctx_tanh
        ctx_o[...] = ctx_tanh.astype(bf16)
        send = to_beside(ctx_o, ctx_o, 4)
        send.start()
        copies += [
            pltpu.make_async_copy(rec, rec_o, o_sem.at[2]),
            pltpu.make_async_copy(sq, sq_o, o_sem.at[3]),
        ]
        for copy in copies[2:]:
            copy.start()
        for u in (own_sm, far_sm):
            gather.pass_z(u)
        for u in (own_sm, far_sm):
            gather.pass_y(u)
        for u in (own_sm, far_sm):
            gather.end(u)
        send.wait_send()
        for k, (src, dst) in enumerate([(cg_s, cg), (de_s, de), (dc_s, dc)]):
            to_beside(src, block_rows(dst, 0, src.shape[0]), 1 + k).wait_send()

        arrival(smooth_in, x_recv.at[5]).wait()
        tile = 512
        lanes = lax.broadcasted_iota(jnp.int32, (tokens, 128), 1)
        m_part[...] = jnp.full(m_part.shape, -jnp.inf, f32)
        s_part[...] = jnp.zeros_like(s_part)
        p_part[...] = jnp.zeros_like(p_part)

        def tops(i, _):
            rows = pl.ds(multiple(i * tile, tile), tile)
            logits = nt(smooth_in[...], sm[rows, :])
            parts = [logits[:, k * 128 : (k + 1) * 128] for k in range(tile // 128)]
            before = m_part[...]
            top = before
            for part in parts:
                top = jnp.maximum(top, part)
            total = s_part[...] * jnp.exp(before - top)
            picked = p_part[...]
            for k, part in enumerate(parts):
                total += jnp.exp(part - top)
                picked += jnp.where(lanes == labels[...] - (i * tile + k * 128), part, 0.0)
            m_part[...] = top
            s_part[...] = total
            p_part[...] = picked
            return _

        lax.fori_loop(0, 2 * n * words // tile, tops, 0)
        top = jnp.max(m_part[...], axis=1, keepdims=True)
        total = jnp.sum(s_part[...] * jnp.exp(m_part[...] - top), axis=1, keepdims=True)
        log_norm = top + jnp.log(total)
        picked = jnp.sum(p_part[...], axis=1, keepdims=True)
        scale = 1.0 / (R * n)
        loss = jnp.sum(log_norm - picked, axis=0, keepdims=True) * scale
        loss_o[...] = jnp.broadcast_to(loss, loss_o.shape)
        m_part[...] = jnp.broadcast_to(log_norm, m_part.shape)
        drive[:, pl.ds(0, M)] = jnp.zeros((tokens, M), f32)

        def grads(i, _):
            rows = pl.ds(multiple(i * tile, tile), tile)
            weight = sm[rows, :]
            logits = nt(smooth_in[...], weight)
            low = []
            for k in range(tile // 128):
                part = jnp.exp(logits[:, k * 128 : (k + 1) * 128] - m_part[...])
                hits = lanes == labels[...] - (i * tile + k * 128)
                low.append(((part - jnp.where(hits, 1.0, 0.0)) * scale).astype(bf16))
            low = jnp.concatenate(low, axis=1)
            drive[:, pl.ds(0, M)] += nn(low, weight)
            sm[rows, :] = tn(low, smooth_in[...]).astype(bf16)
            return _

        lax.fori_loop(0, 2 * n * words // tile, grads, 0)
        grad_out[...] = drive[:, pl.ds(0, M)].astype(bf16)
        send = to_beside(grad_out, grad_o, 6)
        send.start()
        copy = pltpu.make_async_copy(sm, term_o, o_sem.at[4])
        copy.start()
        copies.append(copy)
        send.wait_send()
        for copy in copies:
            copy.wait()

    @pl.when(is_decoder)
    def _():
        copies = keep_copies([(wr, wr_o), (wi, wi_o)])
        cg_own, cg_far = crossed[0]
        gather.pass_z(cg_own)
        gather.pass_z(cg_far)
        gather.pass_y(cg_own)
        gather.pass_y(cg_far)
        gather.pass_z(u_sq)
        gather.end(cg_own)
        gather.end(cg_far)
        copies.append(pltpu.make_async_copy(cg, cg_o, o_sem.at[2]))
        copies[-1].start()
        arrival(ctx_o, x_recv.at[4]).wait()
        rest = [u for pair in crossed[1:] for u in pair]
        service = [(2 + k, functools.partial(gather.pass_z, u)) for k, u in enumerate(rest)]
        service += [
            (5 + k, functools.partial(gather.pass_y, u)) for k, u in enumerate([u_sq] + rest)
        ]
        ctx = nn(ctx_o[...], cg[...])
        scan(ctx, service)
        for u in [u_sq] + rest:
            gather.end(u)
        later = [(rec, rec_o), (sq, sq_o), (de, de_o), (dc, dc_o)]
        later = [
            pltpu.make_async_copy(a, b, o_sem.at[3 + k]) for k, (a, b) in enumerate(later)
        ]
        for copy in later:
            copy.start()
        copies += later
        pre = nn(h_o[...], sq[...]) + nt(emb_o[...], de[...])
        outer = nn(ctx_o[...], dc[...])
        pre = (pre.reshape(steps, R, 2 * M) + outer[None]).reshape(tokens, 2 * M)
        pre_o[...] = pre
        a, b = pre[:, :M], pre[:, M:]
        high = jnp.maximum(a, b)
        smooth = high + jnp.log(jnp.exp(a - high) + jnp.exp(b - high))
        grad_out[...] = smooth.astype(bf16)
        send = to_beside(grad_out, smooth_in, 5)
        send.start()
        send.wait_send()
        to_beside(sm_s, block_rows(sm, n, words), 0).wait_send()
        arrival(grad_o, x_recv.at[6]).wait()
        for copy in copies:
            copy.wait()


def forward(n, sizes, asked, hit, table, keep, labels, shards):
    R, H, E, M, slots, per, words = sizes
    Z, Y = factors(n)
    tokens = hit.shape[0]
    shape = jax.ShapeDtypeStruct
    dma = pltpu.SemaphoreType.DMA
    units = 9
    cg_rows, de_rows, dc_rows = H, 2 * M, H
    return pl.pallas_call(
        functools.partial(forward_kernel, n, sizes),
        out_shape=[
            shape((H, 3 * H), bf16),
            shape((3 * H, E), bf16),
            shape((H, H), bf16),
            shape((cg_rows, 3 * H), bf16),
            shape((de_rows, E), bf16),
            shape((dc_rows, 2 * M), bf16),
            shape((2 * n * words, M), bf16),
            shape((5, tokens, H), f32),
            shape((tokens, H), bf16),
            shape((tokens, E), bf16),
            shape((tokens, 2 * M), f32),
            shape((tokens, M), bf16),
            shape((R, H), f32),
            shape((R, H), bf16),
            shape((8, 128), f32),
            shape((8, 128), jnp.int32),
            shape((per, n * slots), bf16),
        ],
        in_specs=[VMEM] * 5 + [ANY] * 7,
        out_specs=[ANY] * 8 + [VMEM] * 9,
        scratch_shapes=[
            pltpu.VMEM((n, 8, 128), jnp.int32),
            pltpu.VMEM((n * slots, E), bf16),
            pltpu.VMEM((n * slots, E), bf16),
            pltpu.VMEM((H, 3 * H), bf16),
            pltpu.VMEM((3 * H, E), bf16),
            pltpu.VMEM((H, H), bf16),
            pltpu.VMEM((2 * n * words, M), bf16),
            pltpu.VMEM((cg_rows, 3 * H), bf16),
            pltpu.VMEM((de_rows, E), bf16),
            pltpu.VMEM((dc_rows, 2 * M), bf16),
            pltpu.VMEM((tokens, 3 * H), f32),
            pltpu.VMEM((5, tokens, H), f32),
            pltpu.VMEM((tokens, M), bf16),
            pltpu.VMEM((tokens, M), bf16),
            pltpu.VMEM((tokens, 128), f32),
            pltpu.VMEM((tokens, 128), f32),
            pltpu.VMEM((tokens, 128), f32),
            pltpu.VMEM((2, 8, 128), jnp.int32),
            dma((units, max(Z - 1, 1))),
            dma((units, max(Z * (Y - 1), 1))),
            dma((units,)),
            dma((units,)),
            dma((7,)),
            dma((7,)),
            dma((8,)),
            dma((8,)),
            dma,
            dma,
            dma,
            dma,
        ],
        compiler_params=pltpu.CompilerParams(
            collective_id=2, has_side_effects=True, vmem_limit_bytes=VMEM_LIMIT
        ),
    )(asked, hit, table, keep, labels, *shards)


def in_rounds(
    token_ids,
    resets,
    targets,
    embedding,
    input_gates,
    recur_gates,
    square,
    context_gates,
    deep_embed,
    deep_context,
    softmax_weight,
):
    n = lax.axis_size("dp")
    s = lax.axis_index("section")
    d = lax.axis_index("dp")
    is_decoder = s == 1
    micro, rows, steps = token_ids.shape[1:]
    R = micro * rows
    tokens = R * steps
    H = square.shape[2]
    E = embedding.shape[2]
    M = softmax_weight.shape[1]
    per = embedding.shape[1]
    slots = max(512 // n, 8)
    scale = 1.0 / (R * n)

    def time_major(x):
        return jnp.transpose(x.reshape(R, steps), (1, 0)).reshape(-1)

    ids = time_major(token_ids[0])
    keep = time_major(1 - resets[0]).astype(f32)[:, None]
    labels = time_major(targets)

    plan = request_slots(ids, n, per, slots)
    rounds = lax.pmax(jnp.max(plan[2]) // slots + 1, ("section", "dp"))
    table = embedding[0]

    def fetch(turn):
        asked, hit = round_maps(plan, turn, n, slots)
        owners = owner_map(asked, n, per)
        came = swap(nn(owners, table).astype(bf16), n)
        return owners, hit, nn(hit, came).astype(bf16)

    owners, hit, emb = fetch(0)

    def more(carry):
        turn, emb = carry
        return turn + 1, emb + fetch(turn)[2]

    _, emb = lax.while_loop(lambda c: c[0] < rounds, more, (jnp.int32(1), emb))

    wr, wi, sq, sm, cg, de, dc = gather(
        n,
        [
            recur_gates[0],
            input_gates[0],
            square[0],
            softmax_weight,
            context_gates,
            deep_embed,
            deep_context,
        ],
        (False, False, False, False, True, True, True),
    )
    wr, wi, sq, sm = wr.reshape(H, 3 * H), wi.reshape(3 * H, E), sq.reshape(H, H), sm.reshape(-1, M)
    cg, de, dc = cg.reshape(H, 3 * H), de.reshape(2 * M, E), dc.reshape(H, 2 * M)

    enc = gru_forward(emb, wi, wr, jnp.zeros((R, 3 * H), f32), keep)
    last_low = enc[5][-R:]
    ctx_tanh = jnp.tanh(nn(last_low, sq))
    context = lax.ppermute(ctx_tanh.astype(bf16), "section", [(0, 1)])

    dec = gru_forward(emb, wi, wr, nn(context, cg), keep)
    states_low = dec[5]
    deep_pre = nn(states_low, sq) + nt(emb, de)
    deep_pre = (deep_pre.reshape(steps, R, -1) + nn(context, dc)[None]).reshape(tokens, -1)
    smooth = jnp.logaddexp(deep_pre[:, :M], deep_pre[:, M:])
    smooth_low = smooth.astype(bf16)

    came = lax.ppermute(smooth_low, "section", [(1, 0)])
    head_in = jnp.where(is_decoder, smooth_low, came)
    words = sm.shape[0]
    logits = nt(head_in, sm)
    top = jnp.max(logits, axis=1)
    total = jnp.sum(jnp.exp(logits - top[:, None]), axis=1)
    hits = lax.broadcasted_iota(jnp.int32, logits.shape, 1) == (labels - s * words)[:, None]
    picked = jnp.sum(jnp.where(hits, logits, 0.0), axis=1)
    stats = jnp.stack([top, total, picked])
    other = lax.ppermute(stats, "section", [(0, 1), (1, 0)])
    all_top = jnp.maximum(top, other[0])
    log_norm = all_top + jnp.log(
        total * jnp.exp(top - all_top) + other[1] * jnp.exp(other[0] - all_top)
    )
    loss = jnp.where(is_decoder, jnp.sum(log_norm - picked - other[2]) * scale, 0.0)
    logit_low = ((jnp.exp(logits - log_norm[:, None]) - hits.astype(f32)) * scale).astype(bf16)
    smooth_part = nn(logit_low, sm)
    smooth_grad = smooth_part + lax.ppermute(smooth_part, "section", [(0, 1)])
    softmax_term = tn(logit_low, head_in).astype(bf16)

    deep_grad = jnp.concatenate(
        [
            smooth_grad * jnp.exp(deep_pre[:, :M] - smooth),
            smooth_grad * jnp.exp(deep_pre[:, M:] - smooth),
        ],
        axis=1,
    )
    deep_low = deep_grad.astype(bf16)
    outer_low = jnp.sum(deep_grad.reshape(steps, R, -1), axis=0).astype(bf16)
    state_grad = nt(deep_low, sq)
    dec_low, dec_cand, drive_sum = gru_backward(
        state_grad, jnp.zeros((R, H), f32), keep, dec[:5], wr
    )
    drive_sum_low = drive_sum.astype(bf16)
    context_grad = (nt(outer_low, dc) + nt(drive_sum_low, cg)).astype(bf16)
    packed = lax.all_gather(jnp.concatenate([context, outer_low, drive_sum_low], axis=1), "dp", tiled=True)
    packed_came = lax.ppermute(packed, "section", [(1, 0)])
    packed = jnp.where(is_decoder, packed, packed_came)

    context_back = lax.ppermute(context_grad, "section", [(1, 0)])
    pre_low = (context_back.astype(f32) * (1.0 - ctx_tanh * ctx_tanh)).astype(bf16)
    enc_low, enc_cand, _ = gru_backward(
        jnp.zeros((tokens, H), f32), nt(pre_low, sq), keep, enc[:5], wr
    )

    def pick(of_encoder, of_decoder):
        return jnp.where(is_decoder, of_decoder, of_encoder)

    recur_low = pick(enc_low, dec_low)
    cand_low = pick(enc_cand, dec_cand)
    before_low = pick(enc[4], dec[4]).astype(bf16)
    drive_low = jnp.concatenate([recur_low[:, : 2 * H], cand_low], axis=1)
    recur_term = tn(before_low, recur_low).astype(bf16)
    input_term = tn(drive_low, emb).astype(bf16)
    deep_mask = jnp.where(is_decoder, deep_low, jnp.zeros_like(deep_low))
    input_grad = nn(drive_low, wi) + nn(deep_mask, de)
    rows_pad = jnp.zeros((tokens - R, H), bf16)
    square_term = tn(
        pick(jnp.concatenate([last_low, rows_pad]), states_low),
        pick(jnp.concatenate([pre_low, rows_pad]), deep_low),
    ).astype(bf16)
    deep_term = tn(deep_mask, emb).astype(bf16)

    input_grad_low = input_grad.astype(bf16)

    def give(owners, hit):
        return tn(owners, swap(tn(hit, input_grad_low).astype(bf16), n))

    def give_more(carry):
        turn, grad = carry
        asked, hit = round_maps(plan, turn, n, slots)
        return turn + 1, grad + give(owner_map(asked, n, per), hit)

    table_grad = give(owners, hit)
    _, table_grad = lax.while_loop(
        lambda c: c[0] < rounds, give_more, (jnp.int32(1), table_grad)
    )

    deep_blocks = jnp.stack(
        [x.reshape((n,) + deep_embed.shape) for x in jnp.split(deep_term, 2)], axis=1
    )
    deep_blocks = deep_blocks.reshape(n, 2 * deep_embed.shape[0], E)
    loss_blocks = jnp.broadcast_to(loss, (n, 8, 128))
    square_sum, recur_sum, input_sum, softmax_sum, deep_sum, loss_sum = scatter(
        n,
        [
            square_term.reshape((n,) + square.shape[1:]),
            recur_term.reshape((n,) + recur_gates.shape[1:]),
            input_term.reshape((n,) + input_gates.shape[1:]),
            softmax_term.reshape((n,) + softmax_weight.shape),
            deep_blocks,
            loss_blocks,
        ],
        1,
    )
    deep_halves = deep_sum.reshape((2,) + deep_embed.shape)
    both = lax.ppermute(
        jnp.concatenate([deep_halves[0].reshape(-1), loss_sum[:1].reshape(-1)]), "section", [(1, 0)]
    )
    deep_out = jnp.where(is_decoder, deep_halves[1], both[:-128].reshape(deep_embed.shape))
    loss_out = jnp.where(is_decoder, loss_sum[0, 0], both[-1])

    own = (s * n + d) * context_gates.shape[0]
    context_own = lax.dynamic_slice(packed, (0, own), (packed.shape[0], context_gates.shape[0]))
    gates_out = tn(context_own, packed[:, H + 2 * M :])
    context_out = tn(context_own, packed[:, H : H + 2 * M])

    return (
        loss_out,
        table_grad[None],
        input_sum[None],
        recur_sum[None],
        square_sum[None],
        gates_out,
        deep_out,
        context_out,
        softmax_sum,
    )


def in_one_round(
    token_ids,
    resets,
    targets,
    embedding,
    input_gates,
    recur_gates,
    square,
    context_gates,
    deep_embed,
    deep_context,
    softmax_weight,
):
    n = lax.axis_size("dp")
    s = lax.axis_index("section")
    d = lax.axis_index("dp")
    is_decoder = s == 1
    micro, rows, steps = token_ids.shape[1:]
    R = micro * rows
    tokens = R * steps
    H = square.shape[2]
    E = embedding.shape[2]
    M = softmax_weight.shape[1]
    per = embedding.shape[1]
    slots = 512 // n

    def time_major(x):
        return jnp.transpose(x.reshape(R, steps), (1, 0)).reshape(-1)

    ids = time_major(token_ids[0])
    keep = time_major(1 - resets[0]).astype(f32)[:, None]
    labels = time_major(targets)

    plan = request_slots(ids, n, per, slots)
    asked, hit = round_maps(plan, 0, n, slots)
    lane = jnp.arange(128, dtype=jnp.int32)
    asked = jnp.tile(asked.reshape(n, slots), (1, 128 // slots))
    asked = jnp.where(lane // slots == d % (128 // slots), asked, -1)
    fullest = jnp.broadcast_to(jnp.max(plan[2]), (n, 1, 128))
    asked = jnp.concatenate([asked[:, None], fullest, jnp.zeros((n, 6, 128), jnp.int32)], axis=1)

    shards = [
        recur_gates[0],
        input_gates[0],
        square[0],
        softmax_weight,
        context_gates,
        deep_embed,
        deep_context,
    ]
    sizes = (R, H, E, M, slots, per, softmax_weight.shape[0])
    results = forward(n, sizes, asked, hit, embedding[0], keep, labels[:, None], shards)

    def rest():
        (
            wr,
            wi,
            sq,
            cg,
            de,
            dc,
            softmax_term,
            rec,
            states_low,
            emb,
            deep_pre,
            smooth_grad,
            ctx_tanh,
            context,
            loss,
            _,
            owners,
        ) = results
        loss = jnp.where(is_decoder, 0.0, loss[0, 0])
        record = [rec[k] for k in range(5)]
        last_low = states_low[-R:]
        smooth = jnp.logaddexp(deep_pre[:, :M], deep_pre[:, M:])
        smooth_grad = smooth_grad.astype(f32)

        deep_grad = jnp.concatenate(
            [
                smooth_grad * jnp.exp(deep_pre[:, :M] - smooth),
                smooth_grad * jnp.exp(deep_pre[:, M:] - smooth),
            ],
            axis=1,
        )
        deep_low = deep_grad.astype(bf16)
        outer_low = jnp.sum(deep_grad.reshape(steps, R, -1), axis=0).astype(bf16)
        state_grad = nt(deep_low, sq)
        dec_low, dec_cand, drive_sum = gru_backward(
            state_grad, jnp.zeros((R, H), f32), keep, record, wr
        )
        drive_sum_low = drive_sum.astype(bf16)
        context_grad = (nt(outer_low, dc) + nt(drive_sum_low, cg)).astype(bf16)
        packed = lax.all_gather(jnp.concatenate([context, outer_low, drive_sum_low], axis=1), "dp", tiled=True)
        packed_came = lax.ppermute(packed, "section", [(1, 0)])
        packed = jnp.where(is_decoder, packed, packed_came)

        context_back = lax.ppermute(context_grad, "section", [(1, 0)])
        pre_low = (context_back.astype(f32) * (1.0 - ctx_tanh * ctx_tanh)).astype(bf16)
        enc_low, enc_cand, _ = gru_backward(
            jnp.zeros((tokens, H), f32), nt(pre_low, sq), keep, record, wr
        )

        def pick(of_encoder, of_decoder):
            return jnp.where(is_decoder, of_decoder, of_encoder)

        recur_low = pick(enc_low, dec_low)
        cand_low = pick(enc_cand, dec_cand)
        before_low = record[4].astype(bf16)
        drive_low = jnp.concatenate([recur_low[:, : 2 * H], cand_low], axis=1)
        recur_term = tn(before_low, recur_low).astype(bf16)
        input_term = tn(drive_low, emb).astype(bf16)
        deep_mask = jnp.where(is_decoder, deep_low, jnp.zeros_like(deep_low))
        input_grad = nn(drive_low, wi) + jnp.where(is_decoder, nn(deep_low, de), 0.0)
        rows_pad = jnp.zeros((tokens - R, H), bf16)
        square_term = tn(
            pick(jnp.concatenate([last_low, rows_pad]), states_low),
            pick(jnp.concatenate([pre_low, rows_pad]), deep_low),
        ).astype(bf16)
        deep_term = tn(deep_mask, emb).astype(bf16)

        input_grad_low = input_grad.astype(bf16)

        table_grad = nn(owners, swap(tn(hit, input_grad_low).astype(bf16), n))

        half = softmax_term.shape[0] // 2
        square_sum, recur_sum, input_sum, soft_0, soft_1, deep_0, deep_1, loss_sum = scatter(
            n,
            [
                square_term.reshape((n,) + square.shape[1:]),
                recur_term.reshape((n,) + recur_gates.shape[1:]),
                input_term.reshape((n,) + input_gates.shape[1:]),
                softmax_term[:half].reshape((n,) + softmax_weight.shape),
                softmax_term[half:].reshape((n,) + softmax_weight.shape),
                deep_term[:M].reshape((n,) + deep_embed.shape),
                deep_term[M:].reshape((n,) + deep_embed.shape),
                jnp.broadcast_to(loss, (n, 8, 128)),
            ],
            3,
        )
        deep_far = lax.ppermute(deep_0, "section", [(1, 0)])
        deep_out = jnp.where(is_decoder, deep_1, deep_far)
        soft_far, loss_far = lax.ppermute((soft_1, loss_sum), "section", [(0, 1)])
        softmax_sum = jnp.where(is_decoder, soft_far, soft_0)
        loss_out = jnp.where(is_decoder, loss_far, loss_sum)[0, 0]

        own = (s * n + d) * context_gates.shape[0]
        context_own = lax.dynamic_slice(packed, (0, own), (packed.shape[0], context_gates.shape[0]))
        gates_out = tn(context_own, packed[:, H + 2 * M :])
        context_out = tn(context_own, packed[:, H : H + 2 * M])

        return (
            loss_out,
            table_grad[None],
            input_sum[None],
            recur_sum[None],
            square_sum[None],
            gates_out,
            deep_out,
            context_out,
            softmax_sum,
        )

    def again():
        return in_rounds(
            token_ids,
            resets,
            targets,
            embedding,
            input_gates,
            recur_gates,
            square,
            context_gates,
            deep_embed,
            deep_context,
            softmax_weight,
        )

    return lax.cond(results[15][0, 0] < slots, rest, again)


def per_device(*args):
    n = lax.axis_size("dp")
    blocks = [args[k].shape[-2] for k in (4, 5, 6, 7, 8, 9, 10)]
    aligned = all(rows % 16 == 0 for rows in blocks)
    if aligned and n % 8 == 0 and n <= 32:
        return in_one_round(*args)
    return in_rounds(*args)


def solution(mesh):
    halves = P("section", "dp", None)
    whole = P(("section", "dp"), None)
    in_specs = (
        P("section", None, "dp", None),
        P("section", None, "dp", None),
        P(None, "dp", None),
        halves,
        halves,
        halves,
        halves,
        whole,
        whole,
        whole,
        whole,
    )
    out_specs = (P(), halves, halves, halves, halves, whole, whole, whole, whole)
    return jax.shard_map(
        per_device, mesh=mesh, in_specs=in_specs, out_specs=out_specs, check_vma=False
    )
```

```python
import functools

import jax
import jax.numpy as jnp
from jax import lax
from jax.experimental import pallas as pl
from jax.experimental.pallas import tpu as pltpu
from jax.sharding import PartitionSpec as P

MESH = pl.DeviceIdType.MESH
ANY = pl.BlockSpec(memory_space=pl.ANY)
VMEM = pl.BlockSpec(memory_space=pltpu.VMEM)
f32 = jnp.float32
bf16 = jnp.bfloat16
VMEM_LIMIT = 60 * 2**20


def nn(a, b):
    return jnp.dot(a, b, preferred_element_type=f32)


def nt(a, b):
    return lax.dot_general(a, b, (((1,), (1,)), ((), ())), preferred_element_type=f32)


def tn(a, b):
    return lax.dot_general(a, b, (((0,), (0,)), ((), ())), preferred_element_type=f32)


def factors(n):
    z = 4 if n % 8 == 0 else 1
    return z, n // (2 * z)


class Place:
    def __init__(self, n):
        self.Z, self.Y = factors(n)
        self.s = lax.axis_index("section")
        d = lax.axis_index("dp")
        self.d = d
        self.c = d % 2
        self.zy = d // 2
        self.y = self.zy % self.Y
        self.z = self.zy // self.Y

    def along_z(self, step):
        return lax.rem(self.z + step + self.Z, self.Z)

    def along_y(self, step):
        return lax.rem(self.y + step + self.Y, self.Y)

    def device(self, z, y, c):
        return (self.s, (z * self.Y + y) * 2 + c)

    def partners(self):
        found = [self.device(self.along_z(k), self.y, self.c) for k in range(1, self.Z)]
        found += [self.device(self.z, self.along_y(k), self.c) for k in range(1, self.Y)]
        return found + [self.device(self.z, self.y, 1 - self.c), (1 - self.s, self.d)]


def greet(devices):
    barrier = pltpu.get_barrier_semaphore()
    for device in devices:
        pl.semaphore_signal(barrier, inc=1, device_id=device, device_id_type=MESH)
    pl.semaphore_wait(barrier, len(devices))


def remote(src, dst, send, recv, device):
    return pltpu.make_async_remote_copy(
        src_ref=src, dst_ref=dst, send_sem=send, recv_sem=recv, device_id=device, device_id_type=MESH
    )


def arrival(ref, sem):
    return pltpu.make_async_copy(ref, ref, sem)


def gather_kernel(n, crossed, *refs):
    count = len(crossed)
    sources, outs = refs[:count], refs[count : 2 * count]
    z_sem, y_sem, c_sem, s_sem, l_sem, x_sem, xs_sem = refs[2 * count :]
    at = Place(n)
    Z, Y = at.Z, at.Y
    greet(at.partners())

    x_copies = []
    for item in range(count):
        if crossed[item]:
            copy = remote(
                sources[item],
                outs[item].at[at.s, at.zy, at.c],
                xs_sem.at[item],
                x_sem.at[item],
                (1 - at.s, at.d),
            )
            copy.start()
            x_copies.append(copy)

    units = []
    for item in range(count):
        if crossed[item]:
            units.append((item, outs[item].at[at.s], sources[item]))
        else:
            units.append((item, outs[item], sources[item]))
    own = len(units)
    for item in range(count):
        if crossed[item]:
            gathered = outs[item].at[1 - at.s]
            units.append((item, gathered, gathered.at[at.zy, at.c]))

    def spread(u, src, zy, z_slot, to_z, to_y):
        gathered = units[u][1]
        dst = gathered.at[zy, at.c]
        if to_z:
            for k in range(1, Z):
                remote(
                    src, dst, s_sem.at[u], z_sem.at[u, k - 1], at.device(at.along_z(k), at.y, at.c)
                ).start()
        if to_y:
            for k in range(1, Y):
                remote(
                    src,
                    dst,
                    s_sem.at[u],
                    y_sem.at[u, z_slot * (Y - 1) + k - 1],
                    at.device(at.z, at.along_y(k), at.c),
                ).start()
        remote(src, dst, s_sem.at[u], c_sem.at[u], at.device(at.z, at.y, 1 - at.c)).start()

    for u, (item, gathered, src) in enumerate(units):
        if u < own:
            pltpu.make_async_copy(src, gathered.at[at.zy, at.c], l_sem.at[u]).start()
        else:
            arrival(src, x_sem.at[item]).wait()
        spread(u, src, at.zy, 0, True, True)
    for u, (item, gathered, _) in enumerate(units):
        for k in range(1, Z):
            zy = at.along_z(-k) * Y + at.y
            block = gathered.at[zy, at.c]
            arrival(block, z_sem.at[u, k - 1]).wait()
            spread(u, block, zy, k, False, True)
        for slot in range(Z):
            for k in range(1, Y):
                zy = at.along_z(-slot) * Y + at.along_y(-k)
                block = gathered.at[zy, at.c]
                arrival(block, y_sem.at[u, slot * (Y - 1) + k - 1]).wait()
                spread(u, block, zy, 0, False, False)
    for u, (item, gathered, src) in enumerate(units):
        if u < own:
            pltpu.make_async_copy(src, gathered.at[at.zy, at.c], l_sem.at[u]).wait()
        theirs = gathered.at[:, 1 - at.c]
        arrival(theirs, c_sem.at[u]).wait()
        most = gathered.at[pl.ds(0, Z * Y - 1)]
        arrival(most, s_sem.at[u]).wait()
        arrival(gathered.at[0, 0], s_sem.at[u]).wait()
    for copy in x_copies:
        copy.wait_send()


def gather(n, arrays, crossed):
    Z, Y = factors(n)
    shapes = []
    for array, over_section in zip(arrays, crossed):
        lead = (2, Z * Y, 2) if over_section else (Z * Y, 2)
        shapes.append(jax.ShapeDtypeStruct(lead + array.shape, array.dtype))
    units = len(arrays) + sum(crossed)
    dma = pltpu.SemaphoreType.DMA
    return pl.pallas_call(
        functools.partial(gather_kernel, n, crossed),
        out_shape=shapes,
        in_specs=[ANY] * len(arrays),
        out_specs=[ANY] * len(arrays),
        scratch_shapes=[
            dma((units, max(Z - 1, 1))),
            dma((units, max(Z * (Y - 1), 1))),
            dma((units,)),
            dma((units,)),
            dma((units,)),
            dma((len(arrays),)),
            dma((len(arrays),)),
        ],
        compiler_params=pltpu.CompilerParams(collective_id=0, has_side_effects=True),
    )(*arrays)


def add_blocks(rows, terms, out, out_type):
    chunk = 16 if rows % 16 == 0 else rows

    def body(i, _):
        part = pl.ds(pl.multiple_of(i * chunk, chunk), chunk)
        total = terms[0][part, :].astype(f32)
        for term in terms[1:]:
            total = total + term[part, :].astype(f32)
        out[part, :] = total.astype(out_type)
        return _

    lax.fori_loop(0, rows // chunk, body, 0)


def scatter_kernel(n, count, *refs):
    sources, outs = refs[:count], refs[count : 2 * count]
    scratch = refs[2 * count :]
    mine, from_c, from_y, from_z = (scratch[k * count : (k + 1) * count] for k in range(4))
    l_sem, cs_sem, cr_sem, ys_sem, yr_sem, zs_sem, zr_sem = scratch[4 * count :]
    at = Place(n)
    Z, Y = at.Z, at.Y
    greet(at.partners()[:-1])

    c_copies, l_copies, y_copies, z_copies = [], [], [], []
    for i in range(count):
        copy = remote(
            sources[i].at[:, 1 - at.c],
            from_c[i],
            cs_sem.at[i],
            cr_sem.at[i],
            at.device(at.z, at.y, 1 - at.c),
        )
        copy.start()
        c_copies.append(copy)
        copy = pltpu.make_async_copy(sources[i].at[:, at.c], mine[i], l_sem.at[i])
        copy.start()
        l_copies.append(copy)

    def after_core(i):
        c_copies[i].wait_recv()
        l_copies[i].wait()
        rows = mine[i].shape[1]
        for k in list(range(1, Y)) + [0]:
            y = at.along_y(k)

            def per_z(z, _):
                zy = z * Y + y
                add_blocks(rows, [mine[i].at[zy], from_c[i].at[zy]], mine[i].at[zy], mine[i].dtype)
                return _

            lax.fori_loop(0, Z, per_z, 0)
            if k:
                for z in range(Z):
                    copy = remote(
                        mine[i].at[z * Y + y],
                        from_y[i].at[k - 1, z],
                        ys_sem.at[i, k - 1, z],
                        yr_sem.at[i, k - 1, z],
                        at.device(at.z, y, at.c),
                    )
                    copy.start()
                    y_copies.append(copy)

    def after_y(i):
        rows = mine[i].shape[1]
        for k in list(range(1, Z)) + [0]:
            z = at.along_z(k)
            block = mine[i].at[z * Y + at.y]
            for j in range(1, Y):
                arrival(from_y[i].at[j - 1, z], yr_sem.at[i, j - 1, z]).wait()
            terms = [block] + [from_y[i].at[j - 1, z] for j in range(1, Y)]
            add_blocks(rows, terms, block, mine[i].dtype)
            if k:
                copy = remote(
                    block,
                    from_z[i].at[k - 1],
                    zs_sem.at[i, k - 1],
                    zr_sem.at[i, k - 1],
                    at.device(z, at.y, at.c),
                )
                copy.start()
                z_copies.append(copy)

    def after_z(i):
        rows = mine[i].shape[1]
        for k in range(1, Z):
            arrival(from_z[i].at[k - 1], zr_sem.at[i, k - 1]).wait()
        terms = [mine[i].at[at.zy]] + [from_z[i].at[k - 1] for k in range(1, Z)]
        add_blocks(rows, terms, outs[i], outs[i].dtype)

    for turn in range(count + 2):
        if turn < count:
            after_core(turn)
        if 0 <= turn - 1 < count:
            after_y(turn - 1)
        if turn - 2 >= 0:
            after_z(turn - 2)
    for copy in c_copies + y_copies + z_copies:
        copy.wait_send()


def scatter(n, arrays, collective_id):
    Z, Y = factors(n)
    count = len(arrays)
    blocks = [a.shape[-2:] for a in arrays]
    arrays = [a.reshape((Z * Y, 2) + b) for a, b in zip(arrays, blocks)]
    dma = pltpu.SemaphoreType.DMA
    scratch = [pltpu.VMEM((Z * Y,) + b, a.dtype) for a, b in zip(arrays, blocks)]
    scratch += [pltpu.VMEM((Z * Y,) + b, a.dtype) for a, b in zip(arrays, blocks)]
    scratch += [pltpu.VMEM((max(Y - 1, 1), Z) + b, a.dtype) for a, b in zip(arrays, blocks)]
    scratch += [pltpu.VMEM((max(Z - 1, 1),) + b, a.dtype) for a, b in zip(arrays, blocks)]
    return pl.pallas_call(
        functools.partial(scatter_kernel, n, count),
        out_shape=[jax.ShapeDtypeStruct(b, f32) for b in blocks],
        in_specs=[ANY] * count,
        out_specs=[VMEM] * count,
        scratch_shapes=scratch
        + [
            dma((count,)),
            dma((count,)),
            dma((count,)),
            dma((count, max(Y - 1, 1), Z)),
            dma((count, max(Y - 1, 1), Z)),
            dma((count, max(Z - 1, 1))),
            dma((count, max(Z - 1, 1))),
        ],
        compiler_params=pltpu.CompilerParams(
            collective_id=collective_id, has_side_effects=True, vmem_limit_bytes=VMEM_LIMIT
        ),
    )(*arrays)


def scan_kernel(emb, wi, wr, ctx, keep, z_o, r_o, n_o, m_o, p_o, h_o, drive):
    R, H = ctx.shape[0], wr.shape[0]
    drive[...] = nt(emb[...], wi[...])

    def step(t, h):
        rows = pl.ds(pl.multiple_of(t * R, R), R)
        p = h * keep[rows, :]
        p_o[rows, :] = p
        rec = nn(p.astype(bf16), wr[...])
        d = drive[rows, :]
        z = jax.nn.sigmoid(d[:, :H] + rec[:, :H] + ctx[:, :H])
        r = jax.nn.sigmoid(d[:, H : 2 * H] + rec[:, H : 2 * H] + ctx[:, H : 2 * H])
        m = rec[:, 2 * H :] + ctx[:, 2 * H :]
        n = jnp.tanh(d[:, 2 * H :] + r * m)
        h = z * p + (1.0 - z) * n
        z_o[rows, :] = z
        r_o[rows, :] = r
        n_o[rows, :] = n
        m_o[rows, :] = m
        h_o[rows, :] = h.astype(bf16)
        return h

    lax.fori_loop(0, emb.shape[0] // R, step, jnp.zeros((R, H), f32))


def gru_forward(emb, wi, wr, ctx, keep):
    tokens, H = emb.shape[0], wr.shape[0]
    shape = jax.ShapeDtypeStruct
    return pl.pallas_call(
        scan_kernel,
        out_shape=[shape((tokens, H), f32)] * 5 + [shape((tokens, H), bf16)],
        in_specs=[VMEM] * 5,
        out_specs=[VMEM] * 6,
        scratch_shapes=[pltpu.VMEM((tokens, 3 * H), f32)],
        compiler_params=pltpu.CompilerParams(vmem_limit_bytes=VMEM_LIMIT),
    )(emb, wi, wr, ctx, keep)


def backward_kernel(sg, carry0, keep, z, r, n, m, p, wr, low_o, cand_o, sum_o):
    R, H = carry0.shape
    steps = sg.shape[0] // R

    def step(i, carry):
        rows = pl.ds(pl.multiple_of((steps - 1 - i) * R, R), R)
        g = sg[rows, :] + carry
        zz = z[rows, :]
        cand = n[rows, :]
        rr = r[rows, :]
        pc = g * (1.0 - zz) * (1.0 - cand * cand)
        pz = g * (p[rows, :] - cand) * zz * (1.0 - zz)
        pr = pc * m[rows, :] * rr * (1.0 - rr)
        rec = jnp.concatenate([pz, pr, pc * rr], axis=1)
        low = rec.astype(bf16)
        low_o[rows, :] = low
        cand_o[rows, :] = pc.astype(bf16)
        sum_o[...] += rec
        return (g * zz + nt(low, wr[...])) * keep[rows, :]

    sum_o[...] = jnp.zeros_like(sum_o)
    lax.fori_loop(0, steps, step, carry0[...])


def gru_backward(sg, carry0, keep, record, wr):
    z, r, n, m, p = record
    tokens, H = sg.shape
    shape = jax.ShapeDtypeStruct
    return pl.pallas_call(
        backward_kernel,
        out_shape=[
            shape((tokens, 3 * H), bf16),
            shape((tokens, H), bf16),
            shape((carry0.shape[0], 3 * H), f32),
        ],
        in_specs=[VMEM] * 9,
        out_specs=[VMEM] * 3,
        compiler_params=pltpu.CompilerParams(vmem_limit_bytes=VMEM_LIMIT),
    )(sg, carry0, keep, z, r, n, m, p, wr)


def request_slots(ids, n, per, slots):
    count = ids.shape[0]
    index = jnp.arange(count, dtype=jnp.int32)
    same = ids[:, None] == ids[None, :]
    first = jnp.min(jnp.where(same, index[None, :], count), axis=1)
    leads = first == index
    owner = ids // per
    ahead = (owner[:, None] == owner[None, :]) & leads[None, :] & (index[None, :] < first[:, None])
    rank = jnp.sum(ahead.astype(jnp.int32), axis=1)
    return leads, owner, rank, ids - owner * per


def round_maps(plan, turn, n, slots):
    leads, owner, rank, local = plan
    place = rank - turn * slots
    inside = (place >= 0) & (place < slots)
    place = jnp.where(inside, owner * slots + place, -1)
    hit = place[:, None] == jnp.arange(n * slots, dtype=jnp.int32)[None, :]
    asked = jnp.max(jnp.where(hit & leads[:, None], local[:, None], -1), axis=0)
    return asked, hit.astype(bf16)


def swap(x, n):
    shape = x.shape
    return lax.all_to_all(x.reshape((n, -1) + shape[1:]), "dp", 0, 0, tiled=False).reshape(shape)


def owner_map(asked, n, per):
    asked_here = swap(asked, n)
    return (asked_here[:, None] == jnp.arange(per, dtype=jnp.int32)[None, :]).astype(bf16)


def multiple(x, of):
    return pl.multiple_of(x, of)


class Unit:
    def __init__(self, index, src, dst, rows, base):
        self.index, self.src, self.dst, self.rows, self.base = index, src, dst, rows, base

    def block(self, zy, c):
        return self.dst.at[pl.ds(multiple(self.base + (zy * 2 + c) * self.rows, 16), self.rows)]

    def some(self, count):
        return self.dst.at[pl.ds(0, count * self.rows)]


class Gather:
    def __init__(self, at, z_sem, y_sem, c_sem, s_sem):
        self.at, self.z_sem, self.y_sem, self.c_sem, self.s_sem = at, z_sem, y_sem, c_sem, s_sem

    def to_y(self, u, src, dst, slot):
        at = self.at
        for k in range(1, at.Y):
            remote(
                src,
                dst,
                self.s_sem.at[u.index],
                self.y_sem.at[u.index, slot * (at.Y - 1) + k - 1],
                at.device(at.z, at.along_y(k), at.c),
            ).start()

    def to_core(self, u, src, dst):
        at = self.at
        remote(
            src, dst, self.s_sem.at[u.index], self.c_sem.at[u.index], at.device(at.z, at.y, 1 - at.c)
        ).start()

    def begin(self, u):
        at = self.at
        dst = u.block(at.zy, at.c)
        self.to_y(u, u.src, dst, 0)
        for k in range(1, at.Z):
            remote(
                u.src,
                dst,
                self.s_sem.at[u.index],
                self.z_sem.at[u.index, k - 1],
                at.device(at.along_z(k), at.y, at.c),
            ).start()
        self.to_core(u, u.src, dst)

    def pass_z(self, u):
        at = self.at
        for k in range(1, at.Z):
            block = u.block(at.along_z(-k) * at.Y + at.y, at.c)
            arrival(block, self.z_sem.at[u.index, k - 1]).wait()
            self.to_y(u, block, block, k)
            self.to_core(u, block, block)

    def pass_y(self, u):
        at = self.at
        for slot in range(at.Z):
            for k in range(1, at.Y):
                block = u.block(at.along_z(-slot) * at.Y + at.along_y(-k), at.c)
                arrival(block, self.y_sem.at[u.index, slot * (at.Y - 1) + k - 1]).wait()
                self.to_core(u, block, block)

    def end(self, u):
        blocks = self.at.Z * self.at.Y
        part = u.some(blocks)
        arrival(part, self.c_sem.at[u.index]).wait()
        part = u.some(2 * blocks - 1)
        arrival(part, self.s_sem.at[u.index]).wait()


def forward_kernel(n, sizes, *refs):
    R, H, E, M, slots, per, words = sizes
    (
        asked,
        hit,
        table,
        keep,
        labels,
        wr_s,
        wi_s,
        sq_s,
        sm_s,
        cg_s,
        de_s,
        dc_s,
    ) = refs[:12]
    (
        wr_o,
        wi_o,
        sq_o,
        cg_o,
        de_o,
        dc_o,
        term_o,
        rec_o,
        h_o,
        emb_o,
        pre_o,
        grad_o,
        tanh_o,
        ctx_o,
        loss_o,
        most_o,
        owners_o,
    ) = refs[12:29]
    (
        asked_in,
        rows_out,
        came,
        wr,
        wi,
        sq,
        sm,
        cg,
        de,
        dc,
        drive,
        rec,
        wrt,
        smooth_in,
        grad_out,
        m_part,
        s_part,
        p_part,
        fullest,
        z_sem,
        y_sem,
        c_sem,
        s_sem,
        l_sem,
        o_sem,
        x_recv,
        x_send,
        as_sem,
        ar_sem,
        rs_sem,
        rr_sem,
    ) = refs[29:]
    at = Place(n)
    tokens = hit.shape[0]
    steps = tokens // R
    is_decoder = at.s == 1
    beside = (1 - at.s, at.d)
    others = [lax.rem(at.d + k, n) for k in range(1, n)]
    greet([(at.s, d) for d in others] + [beside])

    def block_rows(ref, base, rows):
        return ref.at[pl.ds(multiple((base + at.d) * rows, 16), rows)]

    def to_beside(src, dst, k):
        return remote(src, dst, x_send.at[k], x_recv.at[k], beside)

    gather = Gather(at, z_sem, y_sem, c_sem, s_sem)
    u_wr = Unit(0, wr_s, wr, wr_s.shape[0], 0)
    u_wi = Unit(1, wi_s, wi, wi_s.shape[0], 0)
    u_sq = Unit(2, sq_s, sq, sq_s.shape[0], 0)
    own_sm = Unit(3, sm_s, sm, words, 0)
    far_sm = Unit(4, block_rows(sm, n, words), sm, words, n * words)
    crossed = []
    for k, (src, dst) in enumerate([(cg_s, cg), (de_s, de), (dc_s, dc)]):
        rows = src.shape[0]
        crossed.append(
            (
                Unit(3 + 2 * k, src, dst, rows, n * rows),
                Unit(4 + 2 * k, block_rows(dst, 0, rows), dst, rows, 0),
            )
        )

    asked_sends = []
    for k, d in enumerate(others):
        copy = remote(asked.at[d], asked_in.at[at.d], as_sem, ar_sem, (at.s, d))
        copy.start()
    gather.begin(u_wi)
    gather.begin(u_wr)

    @pl.when(is_decoder)
    def _():
        to_beside(sm_s, block_rows(sm, n, words), 0).start()

    @pl.when(jnp.logical_not(is_decoder))
    def _():
        for k, (src, dst) in enumerate([(cg_s, cg), (de_s, de), (dc_s, dc)]):
            to_beside(src, block_rows(dst, 0, src.shape[0]), 1 + k).start()

    locals_ = [
        pltpu.make_async_copy(src, block_rows(dst, 0, src.shape[0]), l_sem.at[k])
        for k, (src, dst) in enumerate([(wr_s, wr), (wi_s, wi), (sq_s, sq)])
    ]
    locals_.append(pltpu.make_async_copy(sm_s, block_rows(sm, 0, words), l_sem.at[3]))
    for k, (src, dst) in enumerate([(cg_s, cg), (de_s, de), (dc_s, dc)]):
        locals_.append(pltpu.make_async_copy(src, block_rows(dst, n, src.shape[0]), l_sem.at[4 + k]))
    for copy in locals_:
        copy.start()

    some_asked = asked_in.at[pl.ds(0, n - 1)]
    arrival(some_asked, ar_sem).wait()
    arrival(some_asked, as_sem).wait()
    asked_in[at.d] = asked[at.d]
    group = 128 // slots
    count = lax.broadcasted_iota(jnp.int32, (per, 128), 0)
    most = asked_in[0, 1:2, :]
    for g in range(n // group):
        wanted = asked_in[g * group, 0:1, :]
        for j in range(1, group):
            wanted = jnp.maximum(wanted, asked_in[g * group + j, 0:1, :])
        for j in range(group):
            most = jnp.maximum(most, asked_in[g * group + j, 1:2, :])
        match = (wanted == count).astype(f32).astype(bf16)
        owners_o[:, pl.ds(g * 128, 128)] = match
        rows_out[pl.ds(g * 128, 128), :] = tn(match, table[...]).astype(bf16)
    fullest[0] = jnp.broadcast_to(most, fullest.shape[1:])
    to_beside(fullest.at[0], fullest.at[1], 7).start()

    def slot_rows(ref, d):
        return ref.at[pl.ds(multiple(d * slots, 16), slots)]

    for d in others:
        remote(slot_rows(rows_out, d), slot_rows(came, at.d), rs_sem, rr_sem, (at.s, d)).start()
    gather.pass_z(u_wi)
    gather.pass_z(u_wr)

    @pl.when(is_decoder)
    def _():
        for own, _ in crossed[:1]:
            gather.begin(own)

    gather.begin(u_sq)

    @pl.when(is_decoder)
    def _():
        arrival(crossed[0][1].src, x_recv.at[1]).wait()
        gather.begin(crossed[0][1])
        for k, (own, far) in enumerate(crossed[1:]):
            gather.begin(own)
            arrival(far.src, x_recv.at[2 + k]).wait()
            gather.begin(far)

    @pl.when(jnp.logical_not(is_decoder))
    def _():
        gather.begin(own_sm)
        arrival(far_sm.src, x_recv.at[0]).wait()
        gather.begin(far_sm)

    gather.pass_y(u_wi)
    some_rows = came.at[pl.ds(0, (n - 1) * slots)]
    arrival(some_rows, rr_sem).wait()
    arrival(some_rows, rs_sem).wait()
    came[pl.ds(multiple(at.d * slots, 16), slots), :] = rows_out[
        pl.ds(multiple(at.d * slots, 16), slots), :
    ]
    emb_o[...] = nn(hit[...], came[...]).astype(bf16)
    to_beside(fullest.at[0], fullest.at[1], 7).wait()
    most_o[...] = jnp.maximum(fullest[0], fullest[1])
    for copy in locals_:
        copy.wait()
    gather.end(u_wi)

    def input_drive(i, _):
        cols = pl.ds(multiple(i * 512, 512), 512)
        drive[:, cols] = nt(emb_o[...], wi[cols, :])
        return _

    lax.fori_loop(0, 3 * H // 512, input_drive, 0)
    gather.pass_y(u_wr)
    gather.end(u_wr)

    def scan(ctx, service):
        def step(t, h):
            rows = pl.ds(multiple(t * R, R), R)
            p = h * keep[rows, :]
            rec[t, 4] = p
            mix = nn(p.astype(bf16), wr[...])
            d = drive[rows, :]
            z_in = d[:, :H] + mix[:, :H]
            r_in = d[:, H : 2 * H] + mix[:, H : 2 * H]
            m = mix[:, 2 * H :]
            if ctx is not None:
                z_in += ctx[:, :H]
                r_in += ctx[:, H : 2 * H]
                m += ctx[:, 2 * H :]
            z = jax.nn.sigmoid(z_in)
            r = jax.nn.sigmoid(r_in)
            cand = jnp.tanh(d[:, 2 * H :] + r * m)
            h = z * p + (1.0 - z) * cand
            rec[t, 0] = z
            rec[t, 1] = r
            rec[t, 2] = cand
            rec[t, 3] = m
            h_o[rows, :] = h.astype(bf16)
            for when, what in service:
                pl.when(t == when)(what)
            return h

        return lax.fori_loop(0, steps, step, jnp.zeros((R, H), f32))

    def keep_input_gates():
        copy = pltpu.make_async_copy(wi, wi_o, o_sem.at[0])
        copy.start()
        return copy

    def keep_transposed():
        def turn(i, _):
            part = pl.ds(multiple(i * 128, 128), 128)
            wrt[:, part] = wr[part, :].T
            return _

        lax.fori_loop(0, H // 128, turn, 0)
        copy = pltpu.make_async_copy(wrt, wr_o, o_sem.at[1])
        copy.start()
        return copy

    last = pl.ds((steps - 1) * R, R)

    @pl.when(jnp.logical_not(is_decoder))
    def _():
        copies = [keep_input_gates()]
        scan(None, [(2, lambda: gather.pass_z(u_sq)), (7, lambda: gather.pass_y(u_sq))])
        gather.end(u_sq)
        ctx_tanh = jnp.tanh(nn(h_o[last, :], sq[...]))
        tanh_o[...] = ctx_tanh
        ctx_o[...] = ctx_tanh.astype(bf16)
        send = to_beside(ctx_o, ctx_o, 4)
        send.start()
        copies += [
            pltpu.make_async_copy(rec, rec_o, o_sem.at[2]),
            pltpu.make_async_copy(sq, sq_o, o_sem.at[3]),
        ]
        for copy in copies[1:]:
            copy.start()
        for u in (own_sm, far_sm):
            gather.pass_z(u)
        for u in (own_sm, far_sm):
            gather.pass_y(u)
        for u in (own_sm, far_sm):
            gather.end(u)
        copies.append(keep_transposed())
        send.wait_send()
        for k, (src, dst) in enumerate([(cg_s, cg), (de_s, de), (dc_s, dc)]):
            to_beside(src, block_rows(dst, 0, src.shape[0]), 1 + k).wait_send()

        arrival(smooth_in, x_recv.at[5]).wait()
        tile = 512
        lanes = lax.broadcasted_iota(jnp.int32, (tokens, 128), 1)
        m_part[...] = jnp.full(m_part.shape, -jnp.inf, f32)
        s_part[...] = jnp.zeros_like(s_part)
        p_part[...] = jnp.zeros_like(p_part)

        def tops(i, _):
            rows = pl.ds(multiple(i * tile, tile), tile)
            logits = nt(smooth_in[...], sm[rows, :])
            parts = [logits[:, k * 128 : (k + 1) * 128] for k in range(tile // 128)]
            before = m_part[...]
            top = before
            for part in parts:
                top = jnp.maximum(top, part)
            total = s_part[...] * jnp.exp(before - top)
            picked = p_part[...]
            for k, part in enumerate(parts):
                total += jnp.exp(part - top)
                picked += jnp.where(lanes == labels[...] - (i * tile + k * 128), part, 0.0)
            m_part[...] = top
            s_part[...] = total
            p_part[...] = picked
            return _

        lax.fori_loop(0, 2 * n * words // tile, tops, 0)
        top = jnp.max(m_part[...], axis=1, keepdims=True)
        total = jnp.sum(s_part[...] * jnp.exp(m_part[...] - top), axis=1, keepdims=True)
        log_norm = top + jnp.log(total)
        picked = jnp.sum(p_part[...], axis=1, keepdims=True)
        scale = 1.0 / (R * n)
        loss = jnp.sum(log_norm - picked, axis=0, keepdims=True) * scale
        loss_o[...] = jnp.broadcast_to(loss, loss_o.shape)
        m_part[...] = jnp.broadcast_to(log_norm, m_part.shape)
        drive[:, pl.ds(0, M)] = jnp.zeros((tokens, M), f32)

        def grads(i, _):
            rows = pl.ds(multiple(i * tile, tile), tile)
            weight = sm[rows, :]
            logits = nt(smooth_in[...], weight)
            low = []
            for k in range(tile // 128):
                part = jnp.exp(logits[:, k * 128 : (k + 1) * 128] - m_part[...])
                hits = lanes == labels[...] - (i * tile + k * 128)
                low.append(((part - jnp.where(hits, 1.0, 0.0)) * scale).astype(bf16))
            low = jnp.concatenate(low, axis=1)
            drive[:, pl.ds(0, M)] += nn(low, weight)
            sm[rows, :] = tn(low, smooth_in[...]).astype(bf16)
            return _

        lax.fori_loop(0, 2 * n * words // tile, grads, 0)
        grad_out[...] = drive[:, pl.ds(0, M)].astype(bf16)
        send = to_beside(grad_out, grad_o, 6)
        send.start()
        copy = pltpu.make_async_copy(sm, term_o, o_sem.at[4])
        copy.start()
        copies.append(copy)
        send.wait_send()
        for copy in copies:
            copy.wait()

    @pl.when(is_decoder)
    def _():
        copies = [keep_input_gates()]
        cg_own, cg_far = crossed[0]
        gather.pass_z(cg_own)
        gather.pass_z(cg_far)
        gather.pass_y(cg_own)
        gather.pass_y(cg_far)
        gather.pass_z(u_sq)
        gather.end(cg_own)
        gather.end(cg_far)
        copies.append(pltpu.make_async_copy(cg, cg_o, o_sem.at[2]))
        copies[-1].start()
        arrival(ctx_o, x_recv.at[4]).wait()
        rest = [u for pair in crossed[1:] for u in pair]
        service = [(2 + k, functools.partial(gather.pass_z, u)) for k, u in enumerate(rest)]
        service += [
            (5 + k, functools.partial(gather.pass_y, u)) for k, u in enumerate([u_sq] + rest)
        ]
        ctx = nn(ctx_o[...], cg[...])
        scan(ctx, service)
        for u in [u_sq] + rest:
            gather.end(u)
        later = [(rec, rec_o), (sq, sq_o), (de, de_o), (dc, dc_o)]
        later = [
            pltpu.make_async_copy(a, b, o_sem.at[3 + k]) for k, (a, b) in enumerate(later)
        ]
        for copy in later:
            copy.start()
        copies += later
        pre = nn(h_o[...], sq[...]) + nt(emb_o[...], de[...])
        outer = nn(ctx_o[...], dc[...])
        pre = (pre.reshape(steps, R, 2 * M) + outer[None]).reshape(tokens, 2 * M)
        pre_o[...] = pre
        a, b = pre[:, :M], pre[:, M:]
        high = jnp.maximum(a, b)
        smooth = high + jnp.log(jnp.exp(a - high) + jnp.exp(b - high))
        grad_out[...] = smooth.astype(bf16)
        send = to_beside(grad_out, smooth_in, 5)
        send.start()
        copies.append(keep_transposed())
        send.wait_send()
        to_beside(sm_s, block_rows(sm, n, words), 0).wait_send()
        arrival(grad_o, x_recv.at[6]).wait()
        for copy in copies:
            copy.wait()


def forward(n, sizes, asked, hit, table, keep, labels, shards):
    R, H, E, M, slots, per, words = sizes
    Z, Y = factors(n)
    tokens = hit.shape[0]
    shape = jax.ShapeDtypeStruct
    dma = pltpu.SemaphoreType.DMA
    units = 9
    cg_rows, de_rows, dc_rows = H, 2 * M, H
    return pl.pallas_call(
        functools.partial(forward_kernel, n, sizes),
        out_shape=[
            shape((3 * H, H), bf16),
            shape((3 * H, E), bf16),
            shape((H, H), bf16),
            shape((cg_rows, 3 * H), bf16),
            shape((de_rows, E), bf16),
            shape((dc_rows, 2 * M), bf16),
            shape((2 * n * words, M), bf16),
            shape((tokens // R, 5, R, H), f32),
            shape((tokens, H), bf16),
            shape((tokens, E), bf16),
            shape((tokens, 2 * M), f32),
            shape((tokens, M), bf16),
            shape((R, H), f32),
            shape((R, H), bf16),
            shape((8, 128), f32),
            shape((8, 128), jnp.int32),
            shape((per, n * slots), bf16),
        ],
        in_specs=[VMEM] * 5 + [ANY] * 7,
        out_specs=[ANY] * 8 + [VMEM] * 9,
        scratch_shapes=[
            pltpu.VMEM((n, 8, 128), jnp.int32),
            pltpu.VMEM((n * slots, E), bf16),
            pltpu.VMEM((n * slots, E), bf16),
            pltpu.VMEM((H, 3 * H), bf16),
            pltpu.VMEM((3 * H, E), bf16),
            pltpu.VMEM((H, H), bf16),
            pltpu.VMEM((2 * n * words, M), bf16),
            pltpu.VMEM((cg_rows, 3 * H), bf16),
            pltpu.VMEM((de_rows, E), bf16),
            pltpu.VMEM((dc_rows, 2 * M), bf16),
            pltpu.VMEM((tokens, 3 * H), f32),
            pltpu.VMEM((tokens // R, 5, R, H), f32),
            pltpu.VMEM((3 * H, H), bf16),
            pltpu.VMEM((tokens, M), bf16),
            pltpu.VMEM((tokens, M), bf16),
            pltpu.VMEM((tokens, 128), f32),
            pltpu.VMEM((tokens, 128), f32),
            pltpu.VMEM((tokens, 128), f32),
            pltpu.VMEM((2, 8, 128), jnp.int32),
            dma((units, max(Z - 1, 1))),
            dma((units, max(Z * (Y - 1), 1))),
            dma((units,)),
            dma((units,)),
            dma((7,)),
            dma((7,)),
            dma((8,)),
            dma((8,)),
            dma,
            dma,
            dma,
            dma,
        ],
        compiler_params=pltpu.CompilerParams(
            collective_id=2, has_side_effects=True, vmem_limit_bytes=VMEM_LIMIT
        ),
    )(asked, hit, table, keep, labels, *shards)


class Sum:
    def __init__(self, at, sems, index, mine, theirs, from_c, from_y, from_z, wholes, rows, out):
        self.at, self.sems, self.index = at, sems, index
        self.mine, self.theirs = mine, theirs
        self.from_c, self.from_y, self.from_z = from_c, from_y, from_z
        self.wholes, self.rows, self.out = wholes, rows, out

    def begin(self):
        at, i = self.at, self.index
        cs, cr = self.sems[:2]
        for zy in range(at.Z * at.Y):
            remote(
                self.theirs(zy), self.from_c(zy), cs.at[i], cr.at[i], at.device(at.z, at.y, 1 - at.c)
            ).start()

    def after_core(self):
        at, i = self.at, self.index
        cs, cr, ys, yr = self.sems[:4]
        arrival(self.wholes[0], cr.at[i]).wait()
        for k in list(range(1, at.Y)) + [0]:
            y = at.along_y(k)

            def per_z(z, _):
                zy = z * at.Y + y
                block = self.mine(zy)
                add_blocks(self.rows, [block, self.from_c(zy)], block, block.dtype)
                return _

            lax.fori_loop(0, at.Z, per_z, 0)
            if k:
                for z in range(at.Z):
                    remote(
                        self.mine(z * at.Y + y),
                        self.from_y(k, z),
                        ys.at[i],
                        yr.at[i, k - 1, z],
                        at.device(at.z, y, at.c),
                    ).start()

    def after_y(self):
        at, i = self.at, self.index
        yr, zs, zr = self.sems[3:6]
        for k in list(range(1, at.Z)) + [0]:
            z = at.along_z(k)
            block = self.mine(z * at.Y + at.y)
            came = [self.from_y(j, z) for j in range(1, at.Y)]
            for j, part in enumerate(came):
                arrival(part, yr.at[i, j, z]).wait()
            add_blocks(self.rows, [block] + came, block, block.dtype)
            if k:
                remote(
                    block, self.from_z(k), zs.at[i], zr.at[i, k - 1], at.device(z, at.y, at.c)
                ).start()

    def after_z(self):
        at, i = self.at, self.index
        cs, _, ys, _, zs, zr = self.sems
        came = [self.from_z(k) for k in range(1, at.Z)]
        for k, part in enumerate(came):
            arrival(part, zr.at[i, k]).wait()
        add_blocks(self.rows, [self.mine(at.zy)] + came, self.out, self.out.dtype)
        for whole, sem in zip(self.wholes, (cs, ys, zs)):
            arrival(whole, sem.at[i]).wait()


def backward_kernel_all(n, sizes, *refs):
    R, H, E, M, slots, per, words = sizes
    (
        pre,
        grad,
        h,
        emb,
        keep,
        hit,
        owners,
        tanh,
        context,
        loss,
        wr_h,
        wi_h,
        sq_h,
        cg_h,
        de_h,
        dc_h,
        term_h,
        rec_h,
    ) = refs[:18]
    (
        table_o,
        input_o,
        recur_o,
        square_o,
        gates_o,
        deep_o,
        context_o,
        soft_o,
        loss_o,
        packed_h,
    ) = refs[18:28]
    (
        wrt,
        wi,
        sq,
        de,
        big,
        rec,
        low,
        cand,
        before,
        state_grad,
        total,
        deep_low,
        outer_low,
        packed,
        c_grad,
        c_came,
        pre_low,
        g_out,
        g_in,
        wide_c,
        wide_y,
        wide_z,
        thin_c,
        thin_y,
        thin_z,
        deep_c,
        deep_y,
        deep_z,
        soft_far,
        deep_far,
        far_rows,
        block_rows,
        chunks,
        ctx_cols,
        losses,
        loss_sum,
        cs_sem,
        cr_sem,
        ys_sem,
        yr_sem,
        zs_sem,
        zr_sem,
        pz_sem,
        py_sem,
        pc_sem,
        ps_sem,
        load_sem,
        rec_sem,
        big_sem,
        chunk_sem,
        x_send,
        x_recv,
        ls_sem,
        lr_sem,
        gs_sem,
        gr_sem,
    ) = refs[28:]
    at = Place(n)
    Z, Y = at.Z, at.Y
    ZY = Z * Y
    tokens = emb.shape[0]
    steps = tokens // R
    is_decoder = at.s == 1
    beside = (1 - at.s, at.d)
    others = [lax.rem(at.d + k, n) for k in range(1, n)]
    sems = (cs_sem, cr_sem, ys_sem, yr_sem, zs_sem, zr_sem)

    loads = [
        pltpu.make_async_copy(a, b, load_sem.at[k])
        for k, (a, b) in enumerate([(sq_h, sq), (wr_h, wrt), (wi_h, wi)])
    ]
    for copy in loads:
        copy.start()
    load_de = pltpu.make_async_copy(de_h, de, load_sem.at[3])

    def load_record(i):
        return pltpu.make_async_copy(
            rec_h.at[steps - 1 - i], rec.at[lax.rem(i, 2)], rec_sem.at[lax.rem(i, 2)]
        )

    load_record(0).start()
    greet([(at.s, d) for d in others] + [beside])

    def to_beside(src, dst, k):
        return remote(src, dst, x_send.at[k], x_recv.at[k], beside)

    def block_sum(index, term, rows, stride, off, bufs, slot, out):
        c_buf, y_buf, z_buf = bufs

        def block(zy, c):
            return term.at[pl.ds(multiple(off + (zy * 2 + c) * stride, 16), rows)]

        return Sum(
            at,
            sems,
            index,
            lambda zy: block(zy, at.c),
            lambda zy: block(zy, 1 - at.c),
            lambda zy: c_buf.at[slot, zy],
            lambda k, z: y_buf.at[slot, k - 1, z],
            lambda k: z_buf.at[slot, k - 1],
            (c_buf.at[slot], y_buf.at[slot], z_buf.at[slot]),
            rows,
            out,
        )

    wide, thin, deep = (wide_c, wide_y, wide_z), (thin_c, thin_y, thin_z), (deep_c, deep_y, deep_z)
    tall = recur_o.shape[0]
    recur_sums = [
        block_sum(g, wrt, tall, tall, g * H, wide, g, recur_o.at[:, pl.ds(g * H, H)])
        for g in range(3)
    ]
    square_sum = block_sum(3, sq, tall, tall, 0, wide, 3, square_o)
    high = input_o.shape[0]
    part = thin_c.shape[2]
    input_sums = [
        block_sum(4 + j, wi, part, high, j * part, thin, j, input_o.at[pl.ds(j * part, part)])
        for j in range(high // part)
    ]
    after = 4 + high // part
    deep_rows = deep_far.shape[0]
    deep_sums = [
        block_sum(
            after + j, de, deep_rows, deep_rows, j * n * deep_rows, deep, j, (deep_far, deep_o)[j]
        )
        for j in range(2)
    ]

    def big_rows(first, count):
        return big.at[pl.ds(multiple(first * words, 16), count * words)]

    def soft_sum(j):
        base_c, base_y, base_z = 2 * ZY, 4 * ZY, 4 * ZY + 2 * (Y - 1) * Z

        def mine(zy):
            return big_rows(j * ZY + zy, 1)

        def theirs(zy):
            first = (j * n + zy * 2 + 1 - at.c) * words
            return term_h.at[pl.ds(multiple(first, 16), words)]

        return Sum(
            at,
            sems,
            after + 2 + j,
            mine,
            theirs,
            lambda zy: big_rows(base_c + j * ZY + zy, 1),
            lambda k, z: big_rows(base_y + (j * (Y - 1) + k - 1) * Z + z, 1),
            lambda k: big_rows(base_z + j * (Z - 1) + k - 1, 1),
            (
                big_rows(base_c + j * ZY, ZY),
                big_rows(base_y + j * (Y - 1) * Z, (Y - 1) * Z),
                big_rows(base_z + j * (Z - 1), Z - 1),
            ),
            words,
            (soft_o, soft_far)[j],
        )

    soft_sums = [soft_sum(0), soft_sum(1)]

    def scan(first, with_state, service):
        def step(i, carry):
            t = steps - 1 - i
            rows = pl.ds(multiple(t * R, R), R)
            slot = lax.rem(i, 2)

            @pl.when(i + 1 < steps)
            def _():
                load_record(i + 1).start()

            load_record(i).wait()
            g = carry + state_grad[rows, :] if with_state else carry
            z, r, c, m, p = (rec[slot, k] for k in range(5))
            pc = g * (1.0 - z) * (1.0 - c * c)
            pz = g * (p - c) * z * (1.0 - z)
            pr = pc * m * r * (1.0 - r)
            pn = pc * r
            parts = [pz, pr, pn]
            back = g * z
            for k, x in enumerate(parts):
                x_low = x.astype(bf16)
                low[rows, pl.ds(k * H, H)] = x_low
                back += nn(x_low, wrt[pl.ds(k * H, H), :])
                if with_state:
                    total[:, pl.ds(k * H, H)] += x
            cand[rows, :] = pc.astype(bf16)
            before[rows, :] = p.astype(bf16)
            for when, what in service:
                pl.when(i == when)(what)
            return back * keep[rows, :]

        lax.fori_loop(0, steps, step, first)

    def recur_term(g):
        cols = pl.ds(g * H, H)

        def body(i, _):
            some = pl.ds(multiple(i * 256, 256), 256)
            rows = pl.ds(multiple(g * H + i * 256, 256), 256)
            wrt[rows, :] = tn(before[:, some], low[:, cols]).astype(bf16)
            return _

        lax.fori_loop(0, H // 256, body, 0)

    def input_term():
        def body(i, _):
            some = pl.ds(multiple(i * 256, 256), 256)
            wi[some, :] = tn(low[:, some], emb[...]).astype(bf16)
            return _

        lax.fori_loop(0, 2 * H // 256, body, 0)

        def last(i, _):
            some = pl.ds(multiple(i * 256, 256), 256)
            rows = pl.ds(multiple(2 * H + i * 256, 256), 256)
            wi[rows, :] = tn(cand[:, some], emb[...]).astype(bf16)
            return _

        lax.fori_loop(0, H // 256, last, 0)

    def slot_rows(ref, d):
        return ref.at[pl.ds(multiple(d * slots, 16), slots)]

    def give(extra):
        grads = nn(low[:, pl.ds(0, 2 * H)], wi[pl.ds(0, 2 * H), :])
        grads += nn(cand[...], wi[pl.ds(2 * H, H), :])
        if extra:
            grads += nn(deep_low[...], de[...])
        g_out[...] = tn(hit[...], grads.astype(bf16)).astype(bf16)
        for d in others:
            remote(slot_rows(g_out, d), slot_rows(g_in, at.d), gs_sem, gr_sem, (at.s, d)).start()

    def take():
        own = pl.ds(multiple(at.d * slots, 16), slots)
        some = g_in.at[pl.ds(0, (n - 1) * slots)]
        arrival(some, gr_sem).wait()
        arrival(some, gs_sem).wait()
        g_in[own, :] = g_out[own, :]
        table_o[...] = nn(owners[...], g_in[...])

    @pl.when(jnp.logical_not(is_decoder))
    def _():
        mine = []
        for j, item in enumerate(soft_sums):
            item.begin()
            for zy in range(ZY):
                src = term_h.at[pl.ds(multiple((j * n + zy * 2 + at.c) * words, 16), words)]
                mine.append(pltpu.make_async_copy(src, item.mine(zy), big_sem.at[j]))
                mine[-1].start()
        losses[at.d] = loss[...]
        for d in others:
            remote(loss, losses.at[at.d], ls_sem, lr_sem, (at.s, d)).start()
        for j, item in enumerate(soft_sums):
            whole = big_rows(j * ZY, ZY)
            arrival(whole, big_sem.at[j]).wait()
            item.after_core()
        for copy in loads:
            copy.wait()
        arrival(c_came, x_recv.at[0]).wait()
        c = tanh[...]
        pre_low[...] = (c_came[...].astype(f32) * (1.0 - c * c)).astype(bf16)
        first = nt(pre_low[...], sq[...])

        def square_term():
            sq[...] = tn(h[pl.ds((steps - 1) * R, R), :], pre_low[...]).astype(bf16)
            square_sum.begin()

        scan(
            first,
            False,
            [
                (1, soft_sums[0].after_y),
                (2, square_term),
                (5, square_sum.after_core),
                (9, soft_sums[1].after_y),
                (11, square_sum.after_y),
            ],
        )
        for g in range(3):
            recur_term(g)
            recur_sums[g].begin()
            if g:
                recur_sums[g - 1].after_core()
        give(False)
        recur_sums[2].after_core()
        input_term()
        for item in input_sums:
            item.begin()
        recur_sums[0].after_y()
        for item in input_sums:
            item.after_core()
        recur_sums[1].after_y()
        for item in soft_sums:
            item.after_z()
        send = to_beside(soft_far, soft_o, 1)
        send.start()
        recur_sums[2].after_y()
        square_sum.after_z()
        for item in recur_sums:
            item.after_z()
        some = losses.at[pl.ds(0, n - 1)]
        arrival(some, lr_sem).wait()
        arrival(some, ls_sem).wait()
        all_loss = losses[0]
        for d in range(1, n):
            all_loss += losses[d]
        loss_sum[...] = all_loss
        loss_o[...] = all_loss
        loss_send = to_beside(loss_sum, loss_o, 2)
        loss_send.start()
        take()
        for item in input_sums:
            item.after_y()
        for item in input_sums:
            item.after_z()
        send.wait_send()
        loss_send.wait_send()
        arrival(deep_o, x_recv.at[3]).wait()
        arrival(gates_o, x_recv.at[4]).wait()
        arrival(context_o, x_recv.at[5]).wait()

    @pl.when(is_decoder)
    def _():
        load_de.start()
        chunk = big.shape[1]
        for k in range(3 * H // chunk):
            pltpu.make_async_copy(
                cg_h.at[:, pl.ds(k * chunk, chunk)], big.at[pl.ds(k * H, H)], big_sem.at[0]
            ).start()
        for k in range(2 * M // chunk):
            pltpu.make_async_copy(
                dc_h.at[:, pl.ds(k * chunk, chunk)],
                big.at[pl.ds(3 * H * H // chunk + k * H, H)],
                big_sem.at[1],
            ).start()
        a, b = pre[:, pl.ds(0, M)], pre[:, pl.ds(M, M)]
        high = jnp.maximum(a, b)
        smooth = high + jnp.log(jnp.exp(a - high) + jnp.exp(b - high))
        sg = grad[...].astype(f32)
        for k, x in enumerate((a, b)):
            cols = pl.ds(k * M, M)
            deep_grad = sg * jnp.exp(x - smooth)
            deep_low[:, cols] = deep_grad.astype(bf16)
            outer_low[:, cols] = jnp.sum(deep_grad.reshape(steps, R, M), axis=0).astype(bf16)
        for copy in loads:
            copy.wait()
        load_de.wait()
        state_grad[...] = nt(deep_low[...], sq[...])
        total[...] = jnp.zeros_like(total)
        scan(jnp.zeros((R, H), f32), True, [])
        packed[:, pl.ds(0, H)] = context[...]
        packed[:, pl.ds(H, 2 * M)] = outer_low[...]
        packed[:, pl.ds(H + 2 * M, 3 * H)] = total[...].astype(bf16)
        gates_rows = big.at[pl.ds(0, 3 * H * H // chunk)]
        arrival(gates_rows, big_sem.at[0]).wait()
        deep_part = big.at[pl.ds(3 * H * H // chunk, 2 * M * H // chunk)]
        arrival(deep_part, big_sem.at[1]).wait()
        back = nt(outer_low[:, pl.ds(0, chunk)], deep_part[pl.ds(0, H), :])
        for k in range(1, 2 * M // chunk):
            back += nt(outer_low[:, pl.ds(k * chunk, chunk)], deep_part[pl.ds(k * H, H), :])
        for k in range(3 * H // chunk):
            cols = pl.ds(H + 2 * M + k * chunk, chunk)
            back += nt(packed[:, cols], big[pl.ds(k * H, H), :])
        c_grad[...] = back.astype(bf16)
        send = to_beside(c_grad, c_came, 0)
        send.start()

        gather = Gather(at, pz_sem, py_sem, pc_sem, ps_sem)
        unit = Unit(0, packed, packed_h, R, 0)
        own_copy = pltpu.make_async_copy(packed, unit.block(at.zy, at.c), big_sem.at[2])
        own_copy.start()
        gather.begin(unit)
        for g in range(3):
            recur_term(g)
            recur_sums[g].begin()
            if g:
                recur_sums[g - 1].after_core()
        give(True)
        recur_sums[2].after_core()
        gather.pass_z(unit)
        sq[...] = tn(h[...], deep_low[...]).astype(bf16)
        square_sum.begin()
        de[...] = tn(deep_low[...], emb[...]).astype(bf16)
        for item in deep_sums:
            item.begin()
        input_term()
        for item in input_sums:
            item.begin()
        recur_sums[0].after_y()
        square_sum.after_core()
        for item in deep_sums:
            item.after_core()
        gather.pass_y(unit)
        recur_sums[1].after_y()
        for item in input_sums:
            item.after_core()
        recur_sums[2].after_y()
        gather.end(unit)
        own_copy.wait()

        rows = gates_o.shape[0]
        firsts = [(sec * n + at.d) * rows for sec in (0, 1)]
        for k, first in enumerate(firsts):
            lanes = multiple(first // 128 * 128, 128)
            copy = pltpu.make_async_copy(
                packed_h.at[:, pl.ds(lanes, 128)], ctx_cols.at[k], big_sem.at[3]
            )
            copy.start()
            copy.wait()
        pieces = (2 * M + 3 * H) // chunk

        def load_chunk(k):
            return pltpu.make_async_copy(
                packed_h.at[:, pl.ds(H + k * chunk, chunk)], chunks.at[k % 2], chunk_sem.at[k % 2]
            )

        load_chunk(0).start()
        for k in range(pieces):
            if k + 1 < pieces:
                load_chunk(k + 1).start()
            load_chunk(k).wait()
            for j, first in enumerate(firsts):
                block_rows[...] = tn(ctx_cols[j], chunks[k % 2])
                product = block_rows[pl.ds(multiple(lax.rem(first, 128), 8), rows), :]
                if k < 2 * M // chunk:
                    dst, cols = context_o, pl.ds(k * chunk, chunk)
                else:
                    dst, cols = gates_o, pl.ds(k * chunk - 2 * M, chunk)
                if j == 0:
                    far_rows[:, pl.ds(k * chunk, chunk)] = product
                else:
                    dst[:, cols] = product
        sends = [
            to_beside(far_rows.at[:, pl.ds(2 * M, 3 * H)], gates_o, 4),
            to_beside(far_rows.at[:, pl.ds(0, 2 * M)], context_o, 5),
        ]
        for copy in sends:
            copy.start()
        take()
        square_sum.after_y()
        for item in deep_sums:
            item.after_y()
        for item in recur_sums:
            item.after_z()
        square_sum.after_z()
        for item in deep_sums:
            item.after_z()
        sends.append(to_beside(deep_far, deep_o, 3))
        sends[-1].start()
        for item in input_sums:
            item.after_y()
        for item in input_sums:
            item.after_z()
        for copy in sends + [send]:
            copy.wait_send()
        arrival(soft_o, x_recv.at[1]).wait()
        arrival(loss_o, x_recv.at[2]).wait()


def backward(n, sizes, blocks, arrays):
    R, H, E, M, slots, per, words = sizes
    Z, Y = factors(n)
    ZY = Z * Y
    tokens = arrays[3].shape[0]
    shape = jax.ShapeDtypeStruct
    vmem = pltpu.VMEM
    dma = pltpu.SemaphoreType.DMA
    input_b, recur_b, square_b, gates_b, deep_b, context_b = blocks
    tall = recur_b[0]
    part = next(k for k in (64, 48, 32, 16) if input_b[0] % k == 0)
    thin = input_b[0] // part
    units = 4 + thin + 4
    chunk = M
    big_rows = words * (4 * ZY + 2 * (Y - 1) * Z + 2 * (Z - 1))
    big_rows = max(big_rows, (3 * H + 2 * M) * H // chunk)
    y1, z1 = max(Y - 1, 1), max(Z - 1, 1)
    return pl.pallas_call(
        functools.partial(backward_kernel_all, n, sizes),
        out_shape=[
            shape((per, E), f32),
            shape(input_b, f32),
            shape(recur_b, f32),
            shape(square_b, f32),
            shape(gates_b, f32),
            shape(deep_b, f32),
            shape(context_b, f32),
            shape((words, M), f32),
            shape((8, 128), f32),
            shape((n * R, H + 2 * M + 3 * H), bf16),
        ],
        in_specs=[VMEM] * 10 + [ANY] * 8,
        out_specs=[VMEM] * 9 + [ANY],
        scratch_shapes=[
            vmem((3 * H, H), bf16),
            vmem((3 * H, E), bf16),
            vmem((H, H), bf16),
            vmem((2 * M, E), bf16),
            vmem((big_rows, chunk), bf16),
            vmem((2, 5, R, H), f32),
            vmem((tokens, 3 * H), bf16),
            vmem((tokens, H), bf16),
            vmem((tokens, H), bf16),
            vmem((tokens, H), f32),
            vmem((R, 3 * H), f32),
            vmem((tokens, 2 * M), bf16),
            vmem((R, 2 * M), bf16),
            vmem((R, H + 2 * M + 3 * H), bf16),
            vmem((R, H), bf16),
            vmem((R, H), bf16),
            vmem((R, H), bf16),
            vmem((n * slots, E), bf16),
            vmem((n * slots, E), bf16),
            vmem((4, ZY, tall, H), bf16),
            vmem((4, y1, Z, tall, H), bf16),
            vmem((4, z1, tall, H), bf16),
            vmem((thin, ZY, part, E), bf16),
            vmem((thin, y1, Z, part, E), bf16),
            vmem((thin, z1, part, E), bf16),
            vmem((2, ZY) + deep_b, bf16),
            vmem((2, y1, Z) + deep_b, bf16),
            vmem((2, z1) + deep_b, bf16),
            vmem((words, M), f32),
            vmem(deep_b, f32),
            vmem((gates_b[0], 2 * M + 3 * H), f32),
            vmem((128, chunk), f32),
            vmem((2, n * R, chunk), bf16),
            vmem((2, n * R, 128), bf16),
            vmem((n, 8, 128), f32),
            vmem((8, 128), f32),
            dma((units,)),
            dma((units,)),
            dma((units,)),
            dma((units, y1, Z)),
            dma((units,)),
            dma((units, z1)),
            dma((1, z1)),
            dma((1, Z * y1)),
            dma((1,)),
            dma((1,)),
            dma((4,)),
            dma((2,)),
            dma((4,)),
            dma((2,)),
            dma((6,)),
            dma((6,)),
            dma,
            dma,
            dma,
            dma,
        ],
        compiler_params=pltpu.CompilerParams(
            collective_id=3, has_side_effects=True, vmem_limit_bytes=VMEM_LIMIT
        ),
    )(*arrays)


def in_rounds(
    token_ids,
    resets,
    targets,
    embedding,
    input_gates,
    recur_gates,
    square,
    context_gates,
    deep_embed,
    deep_context,
    softmax_weight,
):
    n = lax.axis_size("dp")
    s = lax.axis_index("section")
    d = lax.axis_index("dp")
    is_decoder = s == 1
    micro, rows, steps = token_ids.shape[1:]
    R = micro * rows
    tokens = R * steps
    H = square.shape[2]
    E = embedding.shape[2]
    M = softmax_weight.shape[1]
    per = embedding.shape[1]
    slots = max(512 // n, 8)
    scale = 1.0 / (R * n)

    def time_major(x):
        return jnp.transpose(x.reshape(R, steps), (1, 0)).reshape(-1)

    ids = time_major(token_ids[0])
    keep = time_major(1 - resets[0]).astype(f32)[:, None]
    labels = time_major(targets)

    plan = request_slots(ids, n, per, slots)
    rounds = lax.pmax(jnp.max(plan[2]) // slots + 1, ("section", "dp"))
    table = embedding[0]

    def fetch(turn):
        asked, hit = round_maps(plan, turn, n, slots)
        owners = owner_map(asked, n, per)
        came = swap(nn(owners, table).astype(bf16), n)
        return owners, hit, nn(hit, came).astype(bf16)

    owners, hit, emb = fetch(0)

    def more(carry):
        turn, emb = carry
        return turn + 1, emb + fetch(turn)[2]

    _, emb = lax.while_loop(lambda c: c[0] < rounds, more, (jnp.int32(1), emb))

    wr, wi, sq, sm, cg, de, dc = gather(
        n,
        [
            recur_gates[0],
            input_gates[0],
            square[0],
            softmax_weight,
            context_gates,
            deep_embed,
            deep_context,
        ],
        (False, False, False, False, True, True, True),
    )
    wr, wi, sq, sm = wr.reshape(H, 3 * H), wi.reshape(3 * H, E), sq.reshape(H, H), sm.reshape(-1, M)
    cg, de, dc = cg.reshape(H, 3 * H), de.reshape(2 * M, E), dc.reshape(H, 2 * M)

    enc = gru_forward(emb, wi, wr, jnp.zeros((R, 3 * H), f32), keep)
    last_low = enc[5][-R:]
    ctx_tanh = jnp.tanh(nn(last_low, sq))
    context = lax.ppermute(ctx_tanh.astype(bf16), "section", [(0, 1)])

    dec = gru_forward(emb, wi, wr, nn(context, cg), keep)
    states_low = dec[5]
    deep_pre = nn(states_low, sq) + nt(emb, de)
    deep_pre = (deep_pre.reshape(steps, R, -1) + nn(context, dc)[None]).reshape(tokens, -1)
    smooth = jnp.logaddexp(deep_pre[:, :M], deep_pre[:, M:])
    smooth_low = smooth.astype(bf16)

    came = lax.ppermute(smooth_low, "section", [(1, 0)])
    head_in = jnp.where(is_decoder, smooth_low, came)
    words = sm.shape[0]
    logits = nt(head_in, sm)
    top = jnp.max(logits, axis=1)
    total = jnp.sum(jnp.exp(logits - top[:, None]), axis=1)
    hits = lax.broadcasted_iota(jnp.int32, logits.shape, 1) == (labels - s * words)[:, None]
    picked = jnp.sum(jnp.where(hits, logits, 0.0), axis=1)
    stats = jnp.stack([top, total, picked])
    other = lax.ppermute(stats, "section", [(0, 1), (1, 0)])
    all_top = jnp.maximum(top, other[0])
    log_norm = all_top + jnp.log(
        total * jnp.exp(top - all_top) + other[1] * jnp.exp(other[0] - all_top)
    )
    loss = jnp.where(is_decoder, jnp.sum(log_norm - picked - other[2]) * scale, 0.0)
    logit_low = ((jnp.exp(logits - log_norm[:, None]) - hits.astype(f32)) * scale).astype(bf16)
    smooth_part = nn(logit_low, sm)
    smooth_grad = smooth_part + lax.ppermute(smooth_part, "section", [(0, 1)])
    softmax_term = tn(logit_low, head_in).astype(bf16)

    deep_grad = jnp.concatenate(
        [
            smooth_grad * jnp.exp(deep_pre[:, :M] - smooth),
            smooth_grad * jnp.exp(deep_pre[:, M:] - smooth),
        ],
        axis=1,
    )
    deep_low = deep_grad.astype(bf16)
    outer_low = jnp.sum(deep_grad.reshape(steps, R, -1), axis=0).astype(bf16)
    state_grad = nt(deep_low, sq)
    dec_low, dec_cand, drive_sum = gru_backward(
        state_grad, jnp.zeros((R, H), f32), keep, dec[:5], wr
    )
    drive_sum_low = drive_sum.astype(bf16)
    context_grad = (nt(outer_low, dc) + nt(drive_sum_low, cg)).astype(bf16)
    packed = lax.all_gather(jnp.concatenate([context, outer_low, drive_sum_low], axis=1), "dp", tiled=True)
    packed_came = lax.ppermute(packed, "section", [(1, 0)])
    packed = jnp.where(is_decoder, packed, packed_came)

    context_back = lax.ppermute(context_grad, "section", [(1, 0)])
    pre_low = (context_back.astype(f32) * (1.0 - ctx_tanh * ctx_tanh)).astype(bf16)
    enc_low, enc_cand, _ = gru_backward(
        jnp.zeros((tokens, H), f32), nt(pre_low, sq), keep, enc[:5], wr
    )

    def pick(of_encoder, of_decoder):
        return jnp.where(is_decoder, of_decoder, of_encoder)

    recur_low = pick(enc_low, dec_low)
    cand_low = pick(enc_cand, dec_cand)
    before_low = pick(enc[4], dec[4]).astype(bf16)
    drive_low = jnp.concatenate([recur_low[:, : 2 * H], cand_low], axis=1)
    recur_term = tn(before_low, recur_low).astype(bf16)
    input_term = tn(drive_low, emb).astype(bf16)
    deep_mask = jnp.where(is_decoder, deep_low, jnp.zeros_like(deep_low))
    input_grad = nn(drive_low, wi) + nn(deep_mask, de)
    rows_pad = jnp.zeros((tokens - R, H), bf16)
    square_term = tn(
        pick(jnp.concatenate([last_low, rows_pad]), states_low),
        pick(jnp.concatenate([pre_low, rows_pad]), deep_low),
    ).astype(bf16)
    deep_term = tn(deep_mask, emb).astype(bf16)

    input_grad_low = input_grad.astype(bf16)

    def give(owners, hit):
        return tn(owners, swap(tn(hit, input_grad_low).astype(bf16), n))

    def give_more(carry):
        turn, grad = carry
        asked, hit = round_maps(plan, turn, n, slots)
        return turn + 1, grad + give(owner_map(asked, n, per), hit)

    table_grad = give(owners, hit)
    _, table_grad = lax.while_loop(
        lambda c: c[0] < rounds, give_more, (jnp.int32(1), table_grad)
    )

    deep_blocks = jnp.stack(
        [x.reshape((n,) + deep_embed.shape) for x in jnp.split(deep_term, 2)], axis=1
    )
    deep_blocks = deep_blocks.reshape(n, 2 * deep_embed.shape[0], E)
    loss_blocks = jnp.broadcast_to(loss, (n, 8, 128))
    square_sum, recur_sum, input_sum, softmax_sum, deep_sum, loss_sum = scatter(
        n,
        [
            square_term.reshape((n,) + square.shape[1:]),
            recur_term.reshape((n,) + recur_gates.shape[1:]),
            input_term.reshape((n,) + input_gates.shape[1:]),
            softmax_term.reshape((n,) + softmax_weight.shape),
            deep_blocks,
            loss_blocks,
        ],
        1,
    )
    deep_halves = deep_sum.reshape((2,) + deep_embed.shape)
    both = lax.ppermute(
        jnp.concatenate([deep_halves[0].reshape(-1), loss_sum[:1].reshape(-1)]), "section", [(1, 0)]
    )
    deep_out = jnp.where(is_decoder, deep_halves[1], both[:-128].reshape(deep_embed.shape))
    loss_out = jnp.where(is_decoder, loss_sum[0, 0], both[-1])

    own = (s * n + d) * context_gates.shape[0]
    context_own = lax.dynamic_slice(packed, (0, own), (packed.shape[0], context_gates.shape[0]))
    gates_out = tn(context_own, packed[:, H + 2 * M :])
    context_out = tn(context_own, packed[:, H : H + 2 * M])

    return (
        loss_out,
        table_grad[None],
        input_sum[None],
        recur_sum[None],
        square_sum[None],
        gates_out,
        deep_out,
        context_out,
        softmax_sum,
    )


def in_one_round(
    token_ids,
    resets,
    targets,
    embedding,
    input_gates,
    recur_gates,
    square,
    context_gates,
    deep_embed,
    deep_context,
    softmax_weight,
):
    n = lax.axis_size("dp")
    s = lax.axis_index("section")
    d = lax.axis_index("dp")
    is_decoder = s == 1
    micro, rows, steps = token_ids.shape[1:]
    R = micro * rows
    tokens = R * steps
    H = square.shape[2]
    E = embedding.shape[2]
    M = softmax_weight.shape[1]
    per = embedding.shape[1]
    slots = 512 // n

    def time_major(x):
        return jnp.transpose(x.reshape(R, steps), (1, 0)).reshape(-1)

    ids = time_major(token_ids[0])
    keep = time_major(1 - resets[0]).astype(f32)[:, None]
    labels = time_major(targets)

    plan = request_slots(ids, n, per, slots)
    asked, hit = round_maps(plan, 0, n, slots)
    lane = jnp.arange(128, dtype=jnp.int32)
    asked = jnp.tile(asked.reshape(n, slots), (1, 128 // slots))
    asked = jnp.where(lane // slots == d % (128 // slots), asked, -1)
    fullest = jnp.broadcast_to(jnp.max(plan[2]), (n, 1, 128))
    asked = jnp.concatenate([asked[:, None], fullest, jnp.zeros((n, 6, 128), jnp.int32)], axis=1)

    shards = [
        recur_gates[0],
        input_gates[0],
        square[0],
        softmax_weight,
        context_gates,
        deep_embed,
        deep_context,
    ]
    sizes = (R, H, E, M, slots, per, softmax_weight.shape[0])
    results = forward(n, sizes, asked, hit, embedding[0], keep, labels[:, None], shards)

    def rest():
        (
            wr,
            wi,
            sq,
            cg,
            de,
            dc,
            softmax_term,
            rec,
            states_low,
            emb,
            deep_pre,
            smooth_grad,
            ctx_tanh,
            context,
            loss,
            _,
            owners,
        ) = results
        blocks = [
            x.shape[-2:]
            for x in (input_gates, recur_gates, square, context_gates, deep_embed, deep_context)
        ]
        table, inputs, recur, squares, gates, deep, contexts, soft, loss, _ = backward(
            n,
            sizes,
            blocks,
            [
                deep_pre,
                smooth_grad,
                states_low,
                emb,
                keep,
                hit,
                owners,
                ctx_tanh,
                context,
                loss,
                wr,
                wi,
                sq,
                cg,
                de,
                dc,
                softmax_term,
                rec,
            ],
        )
        return (
            loss[0, 0],
            table[None],
            inputs[None],
            recur[None],
            squares[None],
            gates,
            deep,
            contexts,
            soft,
        )

    def again():
        return in_rounds(
            token_ids,
            resets,
            targets,
            embedding,
            input_gates,
            recur_gates,
            square,
            context_gates,
            deep_embed,
            deep_context,
            softmax_weight,
        )

    return lax.cond(results[15][0, 0] < slots, rest, again)


def per_device(*args):
    n = lax.axis_size("dp")
    blocks = [args[k].shape[-2] for k in (4, 5, 6, 7, 8, 9, 10)]
    aligned = all(rows % 16 == 0 for rows in blocks)
    if aligned and n % 8 == 0 and n <= 32:
        return in_one_round(*args)
    return in_rounds(*args)


def solution(mesh):
    halves = P("section", "dp", None)
    whole = P(("section", "dp"), None)
    in_specs = (
        P("section", None, "dp", None),
        P("section", None, "dp", None),
        P(None, "dp", None),
        halves,
        halves,
        halves,
        halves,
        whole,
        whole,
        whole,
        whole,
    )
    out_specs = (P(), halves, halves, halves, halves, whole, whole, whole, whole)
    return jax.shard_map(
        per_device, mesh=mesh, in_specs=in_specs, out_specs=out_specs, check_vma=False
    )
```

```python
import functools

import jax
import jax.numpy as jnp
from jax import lax
from jax.experimental import pallas as pl
from jax.experimental.pallas import tpu as pltpu
from jax.sharding import PartitionSpec as P

MESH = pl.DeviceIdType.MESH
ANY = pl.BlockSpec(memory_space=pl.ANY)
VMEM = pl.BlockSpec(memory_space=pltpu.VMEM)
f32 = jnp.float32
bf16 = jnp.bfloat16
VMEM_LIMIT = 62 * 2**20


def nn(a, b):
    return jnp.dot(a, b, preferred_element_type=f32)


def nt(a, b):
    return lax.dot_general(a, b, (((1,), (1,)), ((), ())), preferred_element_type=f32)


def tn(a, b):
    return lax.dot_general(a, b, (((0,), (0,)), ((), ())), preferred_element_type=f32)


def factors(n):
    z = 4 if n % 8 == 0 else 1
    return z, n // (2 * z)


class Place:
    def __init__(self, n):
        self.Z, self.Y = factors(n)
        self.s = lax.axis_index("section")
        d = lax.axis_index("dp")
        self.d = d
        self.c = d % 2
        self.zy = d // 2
        self.y = self.zy % self.Y
        self.z = self.zy // self.Y

    def along_z(self, step):
        return lax.rem(self.z + step + self.Z, self.Z)

    def along_y(self, step):
        return lax.rem(self.y + step + self.Y, self.Y)

    def device(self, z, y, c):
        return (self.s, (z * self.Y + y) * 2 + c)

    def z_near(self):
        return self.z + 1 - 2 * (self.z % 2)

    def z_far(self):
        return lax.rem(self.z + 2, 4)

    def partners(self):
        found = [self.device(self.along_z(k), self.y, self.c) for k in range(1, self.Z)]
        found += [self.device(self.z, self.along_y(k), self.c) for k in range(1, self.Y)]
        return found + [self.device(self.z, self.y, 1 - self.c), (1 - self.s, self.d)]


def greet(devices):
    barrier = pltpu.get_barrier_semaphore()
    for device in devices:
        pl.semaphore_signal(barrier, inc=1, device_id=device, device_id_type=MESH)
    pl.semaphore_wait(barrier, len(devices))


def remote(src, dst, send, recv, device):
    return pltpu.make_async_remote_copy(
        src_ref=src, dst_ref=dst, send_sem=send, recv_sem=recv, device_id=device, device_id_type=MESH
    )


def arrival(ref, sem):
    return pltpu.make_async_copy(ref, ref, sem)


def gather_kernel(n, crossed, *refs):
    count = len(crossed)
    sources, outs = refs[:count], refs[count : 2 * count]
    z_sem, y_sem, c_sem, s_sem, l_sem, x_sem, xs_sem = refs[2 * count :]
    at = Place(n)
    Z, Y = at.Z, at.Y
    greet(at.partners())

    x_copies = []
    for item in range(count):
        if crossed[item]:
            copy = remote(
                sources[item],
                outs[item].at[at.s, at.zy, at.c],
                xs_sem.at[item],
                x_sem.at[item],
                (1 - at.s, at.d),
            )
            copy.start()
            x_copies.append(copy)

    units = []
    for item in range(count):
        if crossed[item]:
            units.append((item, outs[item].at[at.s], sources[item]))
        else:
            units.append((item, outs[item], sources[item]))
    own = len(units)
    for item in range(count):
        if crossed[item]:
            gathered = outs[item].at[1 - at.s]
            units.append((item, gathered, gathered.at[at.zy, at.c]))

    def spread(u, src, zy, z_slot, to_z, to_y):
        gathered = units[u][1]
        dst = gathered.at[zy, at.c]
        if to_z:
            for k in range(1, Z):
                remote(
                    src, dst, s_sem.at[u], z_sem.at[u, k - 1], at.device(at.along_z(k), at.y, at.c)
                ).start()
        if to_y:
            for k in range(1, Y):
                remote(
                    src,
                    dst,
                    s_sem.at[u],
                    y_sem.at[u, z_slot * (Y - 1) + k - 1],
                    at.device(at.z, at.along_y(k), at.c),
                ).start()
        remote(src, dst, s_sem.at[u], c_sem.at[u], at.device(at.z, at.y, 1 - at.c)).start()

    for u, (item, gathered, src) in enumerate(units):
        if u < own:
            pltpu.make_async_copy(src, gathered.at[at.zy, at.c], l_sem.at[u]).start()
        else:
            arrival(src, x_sem.at[item]).wait()
        spread(u, src, at.zy, 0, True, True)
    for u, (item, gathered, _) in enumerate(units):
        for k in range(1, Z):
            zy = at.along_z(-k) * Y + at.y
            block = gathered.at[zy, at.c]
            arrival(block, z_sem.at[u, k - 1]).wait()
            spread(u, block, zy, k, False, True)
        for slot in range(Z):
            for k in range(1, Y):
                zy = at.along_z(-slot) * Y + at.along_y(-k)
                block = gathered.at[zy, at.c]
                arrival(block, y_sem.at[u, slot * (Y - 1) + k - 1]).wait()
                spread(u, block, zy, 0, False, False)
    for u, (item, gathered, src) in enumerate(units):
        if u < own:
            pltpu.make_async_copy(src, gathered.at[at.zy, at.c], l_sem.at[u]).wait()
        theirs = gathered.at[:, 1 - at.c]
        arrival(theirs, c_sem.at[u]).wait()
        most = gathered.at[pl.ds(0, Z * Y - 1)]
        arrival(most, s_sem.at[u]).wait()
        arrival(gathered.at[0, 0], s_sem.at[u]).wait()
    for copy in x_copies:
        copy.wait_send()


def gather(n, arrays, crossed):
    Z, Y = factors(n)
    shapes = []
    for array, over_section in zip(arrays, crossed):
        lead = (2, Z * Y, 2) if over_section else (Z * Y, 2)
        shapes.append(jax.ShapeDtypeStruct(lead + array.shape, array.dtype))
    units = len(arrays) + sum(crossed)
    dma = pltpu.SemaphoreType.DMA
    return pl.pallas_call(
        functools.partial(gather_kernel, n, crossed),
        out_shape=shapes,
        in_specs=[ANY] * len(arrays),
        out_specs=[ANY] * len(arrays),
        scratch_shapes=[
            dma((units, max(Z - 1, 1))),
            dma((units, max(Z * (Y - 1), 1))),
            dma((units,)),
            dma((units,)),
            dma((units,)),
            dma((len(arrays),)),
            dma((len(arrays),)),
        ],
        compiler_params=pltpu.CompilerParams(collective_id=0, has_side_effects=True),
    )(*arrays)


def add_blocks(rows, terms, out, out_type):
    chunk = 16 if rows % 16 == 0 else rows

    def body(i, _):
        part = pl.ds(pl.multiple_of(i * chunk, chunk), chunk)
        total = terms[0][part, :].astype(f32)
        for term in terms[1:]:
            total = total + term[part, :].astype(f32)
        out[part, :] = total.astype(out_type)
        return _

    lax.fori_loop(0, rows // chunk, body, 0)


def scatter_kernel(n, count, *refs):
    sources, outs = refs[:count], refs[count : 2 * count]
    scratch = refs[2 * count :]
    mine, from_c, from_y, from_z = (scratch[k * count : (k + 1) * count] for k in range(4))
    l_sem, cs_sem, cr_sem, ys_sem, yr_sem, zs_sem, zr_sem = scratch[4 * count :]
    at = Place(n)
    Z, Y = at.Z, at.Y
    greet(at.partners()[:-1])

    c_copies, l_copies, y_copies, z_copies = [], [], [], []
    for i in range(count):
        copy = remote(
            sources[i].at[:, 1 - at.c],
            from_c[i],
            cs_sem.at[i],
            cr_sem.at[i],
            at.device(at.z, at.y, 1 - at.c),
        )
        copy.start()
        c_copies.append(copy)
        copy = pltpu.make_async_copy(sources[i].at[:, at.c], mine[i], l_sem.at[i])
        copy.start()
        l_copies.append(copy)

    def after_core(i):
        c_copies[i].wait_recv()
        l_copies[i].wait()
        rows = mine[i].shape[1]
        for k in list(range(1, Y)) + [0]:
            y = at.along_y(k)

            def per_z(z, _):
                zy = z * Y + y
                add_blocks(rows, [mine[i].at[zy], from_c[i].at[zy]], mine[i].at[zy], mine[i].dtype)
                return _

            lax.fori_loop(0, Z, per_z, 0)
            if k:
                for z in range(Z):
                    copy = remote(
                        mine[i].at[z * Y + y],
                        from_y[i].at[k - 1, z],
                        ys_sem.at[i, k - 1, z],
                        yr_sem.at[i, k - 1, z],
                        at.device(at.z, y, at.c),
                    )
                    copy.start()
                    y_copies.append(copy)

    def after_y(i):
        rows = mine[i].shape[1]
        for k in list(range(1, Z)) + [0]:
            z = at.along_z(k)
            block = mine[i].at[z * Y + at.y]
            for j in range(1, Y):
                arrival(from_y[i].at[j - 1, z], yr_sem.at[i, j - 1, z]).wait()
            terms = [block] + [from_y[i].at[j - 1, z] for j in range(1, Y)]
            add_blocks(rows, terms, block, mine[i].dtype)
            if k:
                copy = remote(
                    block,
                    from_z[i].at[k - 1],
                    zs_sem.at[i, k - 1],
                    zr_sem.at[i, k - 1],
                    at.device(z, at.y, at.c),
                )
                copy.start()
                z_copies.append(copy)

    def after_z(i):
        rows = mine[i].shape[1]
        for k in range(1, Z):
            arrival(from_z[i].at[k - 1], zr_sem.at[i, k - 1]).wait()
        terms = [mine[i].at[at.zy]] + [from_z[i].at[k - 1] for k in range(1, Z)]
        add_blocks(rows, terms, outs[i], outs[i].dtype)

    for turn in range(count + 2):
        if turn < count:
            after_core(turn)
        if 0 <= turn - 1 < count:
            after_y(turn - 1)
        if turn - 2 >= 0:
            after_z(turn - 2)
    for copy in c_copies + y_copies + z_copies:
        copy.wait_send()


def scatter(n, arrays, collective_id):
    Z, Y = factors(n)
    count = len(arrays)
    blocks = [a.shape[-2:] for a in arrays]
    arrays = [a.reshape((Z * Y, 2) + b) for a, b in zip(arrays, blocks)]
    dma = pltpu.SemaphoreType.DMA
    scratch = [pltpu.VMEM((Z * Y,) + b, a.dtype) for a, b in zip(arrays, blocks)]
    scratch += [pltpu.VMEM((Z * Y,) + b, a.dtype) for a, b in zip(arrays, blocks)]
    scratch += [pltpu.VMEM((max(Y - 1, 1), Z) + b, a.dtype) for a, b in zip(arrays, blocks)]
    scratch += [pltpu.VMEM((max(Z - 1, 1),) + b, a.dtype) for a, b in zip(arrays, blocks)]
    return pl.pallas_call(
        functools.partial(scatter_kernel, n, count),
        out_shape=[jax.ShapeDtypeStruct(b, f32) for b in blocks],
        in_specs=[ANY] * count,
        out_specs=[VMEM] * count,
        scratch_shapes=scratch
        + [
            dma((count,)),
            dma((count,)),
            dma((count,)),
            dma((count, max(Y - 1, 1), Z)),
            dma((count, max(Y - 1, 1), Z)),
            dma((count, max(Z - 1, 1))),
            dma((count, max(Z - 1, 1))),
        ],
        compiler_params=pltpu.CompilerParams(
            collective_id=collective_id, has_side_effects=True, vmem_limit_bytes=VMEM_LIMIT
        ),
    )(*arrays)


def scan_kernel(emb, wi, wr, ctx, keep, z_o, r_o, n_o, m_o, p_o, h_o, drive):
    R, H = ctx.shape[0], wr.shape[0]
    drive[...] = nt(emb[...], wi[...])

    def step(t, h):
        rows = pl.ds(pl.multiple_of(t * R, R), R)
        p = h * keep[rows, :]
        p_o[rows, :] = p
        rec = nn(p.astype(bf16), wr[...])
        d = drive[rows, :]
        z = jax.nn.sigmoid(d[:, :H] + rec[:, :H] + ctx[:, :H])
        r = jax.nn.sigmoid(d[:, H : 2 * H] + rec[:, H : 2 * H] + ctx[:, H : 2 * H])
        m = rec[:, 2 * H :] + ctx[:, 2 * H :]
        n = jnp.tanh(d[:, 2 * H :] + r * m)
        h = z * p + (1.0 - z) * n
        z_o[rows, :] = z
        r_o[rows, :] = r
        n_o[rows, :] = n
        m_o[rows, :] = m
        h_o[rows, :] = h.astype(bf16)
        return h

    lax.fori_loop(0, emb.shape[0] // R, step, jnp.zeros((R, H), f32))


def gru_forward(emb, wi, wr, ctx, keep):
    tokens, H = emb.shape[0], wr.shape[0]
    shape = jax.ShapeDtypeStruct
    return pl.pallas_call(
        scan_kernel,
        out_shape=[shape((tokens, H), f32)] * 5 + [shape((tokens, H), bf16)],
        in_specs=[VMEM] * 5,
        out_specs=[VMEM] * 6,
        scratch_shapes=[pltpu.VMEM((tokens, 3 * H), f32)],
        compiler_params=pltpu.CompilerParams(vmem_limit_bytes=VMEM_LIMIT),
    )(emb, wi, wr, ctx, keep)


def backward_kernel(sg, carry0, keep, z, r, n, m, p, wr, low_o, cand_o, sum_o):
    R, H = carry0.shape
    steps = sg.shape[0] // R

    def step(i, carry):
        rows = pl.ds(pl.multiple_of((steps - 1 - i) * R, R), R)
        g = sg[rows, :] + carry
        zz = z[rows, :]
        cand = n[rows, :]
        rr = r[rows, :]
        pc = g * (1.0 - zz) * (1.0 - cand * cand)
        pz = g * (p[rows, :] - cand) * zz * (1.0 - zz)
        pr = pc * m[rows, :] * rr * (1.0 - rr)
        rec = jnp.concatenate([pz, pr, pc * rr], axis=1)
        low = rec.astype(bf16)
        low_o[rows, :] = low
        cand_o[rows, :] = pc.astype(bf16)
        sum_o[...] += rec
        return (g * zz + nt(low, wr[...])) * keep[rows, :]

    sum_o[...] = jnp.zeros_like(sum_o)
    lax.fori_loop(0, steps, step, carry0[...])


def gru_backward(sg, carry0, keep, record, wr):
    z, r, n, m, p = record
    tokens, H = sg.shape
    shape = jax.ShapeDtypeStruct
    return pl.pallas_call(
        backward_kernel,
        out_shape=[
            shape((tokens, 3 * H), bf16),
            shape((tokens, H), bf16),
            shape((carry0.shape[0], 3 * H), f32),
        ],
        in_specs=[VMEM] * 9,
        out_specs=[VMEM] * 3,
        compiler_params=pltpu.CompilerParams(vmem_limit_bytes=VMEM_LIMIT),
    )(sg, carry0, keep, z, r, n, m, p, wr)


def request_slots(ids, n, per, slots):
    count = ids.shape[0]
    index = jnp.arange(count, dtype=jnp.int32)
    same = ids[:, None] == ids[None, :]
    first = jnp.min(jnp.where(same, index[None, :], count), axis=1)
    leads = first == index
    owner = ids // per
    ahead = (owner[:, None] == owner[None, :]) & leads[None, :] & (index[None, :] < first[:, None])
    rank = jnp.sum(ahead.astype(jnp.int32), axis=1)
    return leads, owner, rank, ids - owner * per


def round_maps(plan, turn, n, slots):
    leads, owner, rank, local = plan
    place = rank - turn * slots
    inside = (place >= 0) & (place < slots)
    place = jnp.where(inside, owner * slots + place, -1)
    hit = place[:, None] == jnp.arange(n * slots, dtype=jnp.int32)[None, :]
    asked = jnp.max(jnp.where(hit & leads[:, None], local[:, None], -1), axis=0)
    return asked, hit.astype(bf16)


def swap(x, n):
    shape = x.shape
    return lax.all_to_all(x.reshape((n, -1) + shape[1:]), "dp", 0, 0, tiled=False).reshape(shape)


def owner_map(asked, n, per):
    asked_here = swap(asked, n)
    return (asked_here[:, None] == jnp.arange(per, dtype=jnp.int32)[None, :]).astype(bf16)


def multiple(x, of):
    return pl.multiple_of(x, of)


class Unit:
    def __init__(self, index, src, dst, rows, base, y_first=False):
        self.index, self.src, self.dst, self.rows, self.base = index, src, dst, rows, base
        self.y_first = y_first

    def block(self, zy, c):
        return self.dst.at[pl.ds(multiple(self.base + (zy * 2 + c) * self.rows, 16), self.rows)]

    def some(self, count):
        return self.dst.at[pl.ds(0, count * self.rows)]


class Gather:
    def __init__(self, at, z_sem, y_sem, c_sem, s_sem):
        self.at, self.z_sem, self.y_sem, self.c_sem, self.s_sem = at, z_sem, y_sem, c_sem, s_sem

    def to_z(self, u, src, dst, z, slot):
        at = self.at
        remote(
            src,
            dst,
            self.s_sem.at[u.index],
            self.z_sem.at[u.index, slot],
            at.device(z, at.y, at.c),
        ).start()

    def to_y(self, u, src, dst, z):
        at = self.at
        remote(
            src,
            dst,
            self.s_sem.at[u.index],
            self.y_sem.at[u.index, z],
            at.device(at.z, at.along_y(1), at.c),
        ).start()

    def to_core(self, u, src, dst):
        at = self.at
        remote(
            src, dst, self.s_sem.at[u.index], self.c_sem.at[u.index], at.device(at.z, at.y, 1 - at.c)
        ).start()

    def begin(self, u):
        at = self.at
        dst = u.block(at.zy, at.c)
        if not u.y_first:
            self.to_z(u, u.src, dst, at.z_far(), 0)
        self.to_y(u, u.src, dst, at.z)
        self.to_core(u, u.src, dst)

    def by_z(self, u, z, y, slot):
        at = self.at
        block = u.block(z * at.Y + y, at.c)
        arrival(block, self.z_sem.at[u.index, slot]).wait()
        return block

    def by_y(self, u, z):
        at = self.at
        block = u.block(z * at.Y + at.along_y(1), at.c)
        arrival(block, self.y_sem.at[u.index, z]).wait()
        return block

    def step1(self, u):
        at = self.at
        far, near = at.z_far(), at.z_near()
        if u.y_first:
            self.to_z(u, u.src, u.block(at.zy, at.c), far, 0)
            block = self.by_y(u, at.z)
            self.to_z(u, block, block, far, 1)
            self.to_core(u, block, block)
            return
        self.to_z(u, u.src, u.block(at.zy, at.c), near, 1)
        block = self.by_z(u, far, at.y, 0)
        self.to_z(u, block, block, near, 2)
        self.to_y(u, block, block, far)
        self.to_core(u, block, block)

    def step2(self, u):
        at = self.at
        far, near = at.z_far(), at.z_near()
        other = at.along_y(1)
        if u.y_first:
            self.to_z(u, u.src, u.block(at.zy, at.c), near, 2)
            block = u.block(at.z * at.Y + other, at.c)
            self.to_z(u, block, block, near, 3)
            for slot, y in ((0, at.y), (1, other)):
                block = self.by_z(u, far, y, slot)
                self.to_z(u, block, block, near, 4 + slot)
                self.to_core(u, block, block)
            return
        for slot, z in ((1, near), (2, lax.rem(near + 2, 4))):
            block = self.by_z(u, z, at.y, slot)
            self.to_y(u, block, block, z)
            self.to_core(u, block, block)

    def step3(self, u):
        at = self.at
        far, near = at.z_far(), at.z_near()
        next_far = lax.rem(near + 2, 4)
        if u.y_first:
            other = at.along_y(1)
            for slot, z, y in (
                (2, near, at.y),
                (3, near, other),
                (4, next_far, at.y),
                (5, next_far, other),
            ):
                block = self.by_z(u, z, y, slot)
                self.to_core(u, block, block)
            return
        for z in (at.z, far, near, next_far):
            block = self.by_y(u, z)
            self.to_core(u, block, block)

    def end(self, u):
        blocks = self.at.Z * self.at.Y
        part = u.some(blocks)
        arrival(part, self.c_sem.at[u.index]).wait()
        part = u.some(2 * blocks - 1)
        arrival(part, self.s_sem.at[u.index]).wait()


class Chain(Gather):
    def on(self, u, src, dst, up, hops):
        at = self.at
        slot = hops - 1 if up else at.Z - 1 + hops - 1

        @pl.when(at.z < at.Z - 1 if up else at.z > 0)
        def _():
            remote(
                src,
                dst,
                self.on_sem.at[u.index],
                self.z_sem.at[u.index, slot],
                at.device(at.z + (1 if up else -1), at.y, at.c),
            ).start()

    def begin(self, u):
        at = self.at
        dst = u.block(at.zy, at.c)
        self.on(u, u.src, dst, True, 1)
        self.on(u, u.src, dst, False, 1)
        self.to_y(u, u.src, dst, at.z)
        self.to_core(u, u.src, dst)

    def pass_z(self, u, k):
        at = self.at
        for up in (True, False):
            z = at.z - k if up else at.z + k

            @pl.when(z >= 0 if up else z < at.Z)
            def _():
                slot = k - 1 if up else at.Z - 1 + k - 1
                block = self.by_z(u, z, at.y, slot)
                if k + 1 < at.Z:
                    self.on(u, block, block, up, k + 1)
                self.to_y(u, block, block, z)
                self.to_core(u, block, block)

    def end(self, u):
        at = self.at
        blocks = at.Z * at.Y
        part = u.some(blocks)
        arrival(part, self.c_sem.at[u.index]).wait()
        part = u.some(2 * blocks - at.Z)
        arrival(part, self.s_sem.at[u.index]).wait()
        for z in range(at.Z):
            sent = (z + 1 if z < at.Z - 1 else 0) + (at.Z - z if z > 0 else 0)

            @pl.when(at.z == z)
            def _():
                part = u.some(sent)
                arrival(part, self.on_sem.at[u.index]).wait()


def forward_kernel(n, sizes, *refs):
    R, H, E, M, slots, per, words = sizes
    (
        asked,
        hit,
        table,
        keep,
        labels,
        wr_s,
        wi_s,
        sq_s,
        sm_s,
        cg_s,
        de_s,
        dc_s,
    ) = refs[:12]
    (
        wr_o,
        wi_o,
        sq_o,
        cg_o,
        de_o,
        dc_o,
        term_o,
        rec_o,
        h_h,
        emb_h,
        pre_h,
        tanh_h,
        ctx_h,
        owners_h,
        grad_o,
        loss_o,
        most_o,
    ) = refs[12:29]
    (
        asked_in,
        rows_out,
        came,
        wr,
        wi,
        sq,
        sm,
        cg,
        de,
        dc,
        drive,
        rec,
        wrt,
        smooth_in,
        grad_out,
        m_part,
        s_part,
        p_part,
        fullest,
        outer,
        h_o,
        emb_o,
        pre_o,
        tanh_o,
        ctx_o,
        owners_o,
        z_sem,
        y_sem,
        c_sem,
        s_sem,
        l_sem,
        o_sem,
        x_recv,
        x_send,
        as_sem,
        ar_sem,
        rs_sem,
        rr_sem,
        t_send,
        t_recv,
        k_sem,
        on_sem,
    ) = refs[29:]
    at = Place(n)
    tokens = hit.shape[0]
    steps = tokens // R
    is_decoder = at.s == 1
    beside = (1 - at.s, at.d)
    others = [lax.rem(at.d + k, n) for k in range(1, n)]
    greet([(at.s, d) for d in others] + [beside])

    def block_rows(ref, base, rows):
        return ref.at[pl.ds(multiple((base + at.d) * rows, 16), rows)]

    def to_beside(src, dst, k):
        return remote(src, dst, x_send.at[k], x_recv.at[k], beside)

    gather = Gather(at, z_sem, y_sem, c_sem, s_sem)
    chain = Chain(at, z_sem, y_sem, c_sem, s_sem)
    chain.on_sem = on_sem
    u_wi = Unit(1, wi_s, wi, wi_s.shape[0], 0)
    u_wr = Unit(0, wr_s, wr, wr_s.shape[0], 0)
    u_sq = Unit(2, sq_s, sq, sq_s.shape[0], 0)
    own_sm = Unit(3, sm_s, sm, words, 0)
    far_sm = Unit(4, block_rows(sm, n, words), sm, words, n * words)
    crossed = []
    for k, (src, dst) in enumerate([(cg_s, cg), (de_s, de)]):
        rows = src.shape[0]
        crossed.append(
            (
                Unit(3 + 2 * k, src, dst, rows, n * rows),
                Unit(4 + 2 * k, block_rows(dst, 0, rows), dst, rows, 0, k == 0),
            )
        )
    rows = dc_s.shape[0]
    own_dc = Unit(5, dc_s, dc, rows, 0)
    far_dc = Unit(6, block_rows(dc, n, rows), dc, rows, n * rows)

    for d in others:
        remote(asked.at[d], asked_in.at[at.d], as_sem, ar_sem, (at.s, d)).start()
    some_asked = asked_in.at[pl.ds(0, n - 1)]
    arrival(some_asked, ar_sem).wait()
    chain.begin(u_wi)
    chain.begin(u_wr)

    @pl.when(is_decoder)
    def _():
        to_beside(dc_s, block_rows(dc, n, dc_s.shape[0]), 3).start()
        to_beside(sm_s, block_rows(sm, n, words), 0).start()

    @pl.when(jnp.logical_not(is_decoder))
    def _():
        for k, (src, dst) in enumerate([(cg_s, cg), (de_s, de)]):
            to_beside(src, block_rows(dst, 0, src.shape[0]), 1 + k).start()

    locals_ = [
        pltpu.make_async_copy(src, block_rows(dst, 0, src.shape[0]), l_sem.at[k])
        for k, (src, dst) in enumerate([(wr_s, wr), (wi_s, wi), (sq_s, sq)])
    ]
    locals_.append(pltpu.make_async_copy(sm_s, block_rows(sm, 0, words), l_sem.at[3]))
    for k, (src, dst) in enumerate([(cg_s, cg), (de_s, de)]):
        locals_.append(pltpu.make_async_copy(src, block_rows(dst, n, src.shape[0]), l_sem.at[4 + k]))
    locals_.append(pltpu.make_async_copy(dc_s, block_rows(dc, 0, dc_s.shape[0]), l_sem.at[6]))
    for copy in locals_:
        copy.start()

    asked_in[at.d] = asked[at.d]
    group = 128 // slots
    count = lax.broadcasted_iota(jnp.int32, (per, 128), 0)
    most = asked_in[0, 1:2, :]
    for g in range(n // group):
        wanted = asked_in[g * group, 0:1, :]
        for j in range(1, group):
            wanted = jnp.maximum(wanted, asked_in[g * group + j, 0:1, :])
        for j in range(group):
            most = jnp.maximum(most, asked_in[g * group + j, 1:2, :])
        match = (wanted == count).astype(f32).astype(bf16)
        owners_o[:, pl.ds(g * 128, 128)] = match
        rows_out[pl.ds(g * 128, 128), :] = tn(match, table[...]).astype(bf16)
    fullest[0] = jnp.broadcast_to(most, fullest.shape[1:])
    to_beside(fullest.at[0], fullest.at[1], 7).start()

    def slot_rows(ref, d):
        return ref.at[pl.ds(multiple(d * slots, 16), slots)]

    for d in others:
        remote(slot_rows(rows_out, d), slot_rows(came, at.d), rs_sem, rr_sem, (at.s, d)).start()
    for k in (1, 2, 3):
        if k == 2:

            @pl.when(is_decoder)
            def _():
                arrival(crossed[0][1].src, x_recv.at[1]).wait()
                gather.begin(crossed[0][1])

        chain.pass_z(u_wi, k)
        chain.pass_z(u_wr, k)

    @pl.when(is_decoder)
    def _():
        gather.begin(crossed[0][0])
        gather.step1(crossed[0][1])

    @pl.when(jnp.logical_not(is_decoder))
    def _():
        gather.begin(u_sq)

    gather.step3(u_wi)
    some_rows = came.at[pl.ds(0, (n - 1) * slots)]
    arrival(some_rows, rr_sem).wait()
    came[pl.ds(multiple(at.d * slots, 16), slots), :] = rows_out[
        pl.ds(multiple(at.d * slots, 16), slots), :
    ]
    emb_o[...] = nn(hit[...], came[...]).astype(bf16)
    to_beside(fullest.at[0], fullest.at[1], 7).wait()
    most_o[...] = jnp.maximum(fullest[0], fullest[1])
    for copy in locals_:
        copy.wait()
    chain.end(u_wi)

    def input_drive(i, _):
        cols = pl.ds(multiple(i * 512, 512), 512)
        drive[:, cols] = nt(emb_o[...], wi[cols, :])
        return _

    lax.fori_loop(0, 3 * H // 512, input_drive, 0)
    gather.step3(u_wr)
    chain.end(u_wr)

    def scan(ctx, service):
        def step(t, h):
            rows = pl.ds(multiple(t * R, R), R)
            p = h * keep[rows, :]
            rec[t, 4] = p
            mix = nn(p.astype(bf16), wr[...])
            d = drive[rows, :]
            z_in = d[:, :H] + mix[:, :H]
            r_in = d[:, H : 2 * H] + mix[:, H : 2 * H]
            m = mix[:, 2 * H :]
            if ctx is not None:
                z_in += ctx[:, :H]
                r_in += ctx[:, H : 2 * H]
                m += ctx[:, 2 * H :]
            z = jax.nn.sigmoid(z_in)
            r = jax.nn.sigmoid(r_in)
            cand = jnp.tanh(d[:, 2 * H :] + r * m)
            h = z * p + (1.0 - z) * cand
            rec[t, 0] = z
            rec[t, 1] = r
            rec[t, 2] = cand
            rec[t, 3] = m
            h_o[rows, :] = h.astype(bf16)
            for when, what in service:
                pl.when(t == when)(what)
            return h

        return lax.fori_loop(0, steps, step, jnp.zeros((R, H), f32))

    def keep_input_gates():
        copy = pltpu.make_async_copy(wi, wi_o, o_sem.at[0])
        copy.start()
        return copy

    def keep_transposed():
        def turn(i, _):
            part = pl.ds(multiple(i * 128, 128), 128)
            wrt[:, part] = wr[part, :].T
            return _

        lax.fori_loop(0, H // 128, turn, 0)
        copy = pltpu.make_async_copy(wrt, wr_o, o_sem.at[1])
        copy.start()
        return copy

    def keep_small(pairs):
        copies = [pltpu.make_async_copy(a, b, k_sem.at[k]) for k, a, b in pairs]
        for copy in copies:
            copy.start()
        return copies

    def end_requests():
        arrival(some_asked, as_sem).wait()
        arrival(some_rows, rs_sem).wait()

    last = pl.ds((steps - 1) * R, R)

    @pl.when(jnp.logical_not(is_decoder))
    def _():
        copies = [keep_input_gates()] + keep_small([(0, emb_o, emb_h), (1, owners_o, owners_h)])
        wide = (own_dc, far_dc, own_sm, far_sm)

        def begin_wide():
            gather.step2(u_sq)
            gather.begin(own_dc)
            arrival(far_dc.src, x_recv.at[3]).wait()
            gather.begin(far_dc)
            gather.begin(own_sm)

        scan(
            None,
            [(4, lambda: gather.step1(u_sq)), (8, begin_wide)],
        )
        gather.step3(u_sq)
        gather.end(u_sq)
        ctx_tanh = jnp.tanh(nn(h_o[last, :], sq[...]))
        tanh_o[...] = ctx_tanh
        ctx_o[...] = ctx_tanh.astype(bf16)
        sends = [to_beside(ctx_o, ctx_o, 4)]
        sends[0].start()
        copies += [
            pltpu.make_async_copy(rec, rec_o, o_sem.at[2]),
            pltpu.make_async_copy(sq, sq_o, o_sem.at[3]),
        ]
        for copy in copies[-2:]:
            copy.start()
        copies += keep_small([(2, h_o, h_h), (3, tanh_o, tanh_h), (4, ctx_o, ctx_h)])
        for u in wide[:2]:
            gather.step1(u)
        arrival(far_sm.src, x_recv.at[0]).wait()
        gather.begin(far_sm)
        for u in wide[:2]:
            gather.step2(u)
        gather.step1(own_sm)
        for u in wide[:2]:
            gather.step3(u)
        for u in wide[:2]:
            gather.end(u)
        outer[...] = nn(ctx_o[...], dc[...])
        sends.append(to_beside(outer, outer, 8))
        sends[1].start()
        copies.append(pltpu.make_async_copy(dc, dc_o, o_sem.at[5]))
        copies[-1].start()
        gather.step2(own_sm)
        gather.step1(far_sm)
        copies.append(keep_transposed())
        gather.step2(far_sm)
        for u in wide[2:]:
            gather.step3(u)
        for u in wide[2:]:
            gather.end(u)
        for send in sends:
            send.wait_send()
        for k, (src, dst) in enumerate([(cg_s, cg), (de_s, de)]):
            to_beside(src, block_rows(dst, 0, src.shape[0]), 1 + k).wait_send()
        end_requests()

        half = n * words
        ZY = at.Z * at.Y
        across = cg.shape[1] // M
        landed = cg.at[pl.ds(0, half // 4), pl.ds(0, 2 * M)]

        def term_block(j, zy, c):
            return sm.at[pl.ds(multiple((j * n + zy * 2 + c) * words, 16), words)]

        def landing(j, zy):
            place = j * ZY + zy
            rows = pl.ds(multiple(place // across * words, 16), words)
            return cg.at[rows, pl.ds(multiple(place % across * M, 128), M)]

        def core_send(j):
            for zy in range(ZY):
                remote(
                    term_block(j, zy, 1 - at.c),
                    landing(j, zy),
                    t_send.at[j],
                    t_recv.at[j],
                    at.device(at.z, at.y, 1 - at.c),
                ).start()

        arrival(smooth_in, x_recv.at[5]).wait()
        tile = half // 5 if half % 640 == 0 else 512
        lanes = lax.broadcasted_iota(jnp.int32, (tokens, 128), 1)
        m_part[...] = jnp.full(m_part.shape, -jnp.inf, f32)
        s_part[...] = jnp.zeros_like(s_part)
        p_part[...] = jnp.zeros_like(p_part)

        def tops(i, _):
            rows = pl.ds(multiple(i * tile, tile), tile)
            logits = nt(smooth_in[...], sm[rows, :])
            parts = [logits[:, k * 128 : (k + 1) * 128] for k in range(tile // 128)]
            before = m_part[...]
            top = before
            for part in parts:
                top = jnp.maximum(top, part)
            total = s_part[...] * jnp.exp(before - top)
            picked = p_part[...]
            for k, part in enumerate(parts):
                total += jnp.exp(part - top)
                picked += jnp.where(lanes == labels[...] - (i * tile + k * 128), part, 0.0)
            m_part[...] = top
            s_part[...] = total
            p_part[...] = picked
            return _

        lax.fori_loop(0, 2 * n * words // tile, tops, 0)
        top = jnp.max(m_part[...], axis=1, keepdims=True)
        total = jnp.sum(s_part[...] * jnp.exp(m_part[...] - top), axis=1, keepdims=True)
        log_norm = top + jnp.log(total)
        picked = jnp.sum(p_part[...], axis=1, keepdims=True)
        scale = 1.0 / (R * n)
        loss = jnp.sum(log_norm - picked, axis=0, keepdims=True) * scale
        loss_o[...] = jnp.broadcast_to(loss, loss_o.shape)
        m_part[...] = jnp.broadcast_to(log_norm, m_part.shape)
        drive[:, pl.ds(0, M)] = jnp.zeros((tokens, M), f32)

        def grads(i, _):
            rows = pl.ds(multiple(i * tile, tile), tile)
            weight = sm[rows, :]
            logits = nt(smooth_in[...], weight)
            low = []
            for k in range(tile // 128):
                part = jnp.exp(logits[:, k * 128 : (k + 1) * 128] - m_part[...])
                hits = lanes == labels[...] - (i * tile + k * 128)
                low.append(((part - jnp.where(hits, 1.0, 0.0)) * scale).astype(bf16))
            low = jnp.concatenate(low, axis=1)
            drive[:, pl.ds(0, M)] += nn(low, weight)
            sm[rows, :] = tn(low, smooth_in[...]).astype(bf16)
            pl.when(i == half // tile)(lambda: core_send(0))
            return _

        lax.fori_loop(0, 2 * n * words // tile, grads, 0)
        grad_out[...] = drive[:, pl.ds(0, M)].astype(bf16)
        send = to_beside(grad_out, grad_o, 6)
        send.start()
        core_send(1)
        for j in (0, 1):
            arrival(landed, t_recv.at[j]).wait()

            def add(zy, _):
                block = term_block(j, zy, at.c)
                add_blocks(words, [block, landing(j, zy)], block, bf16)
                pltpu.make_async_copy(block, term_o.at[j, zy], o_sem.at[4]).start()
                return _

            lax.fori_loop(0, ZY, add, 0)
        for j in (0, 1):
            arrival(landed, t_send.at[j]).wait()
        arrival(term_o, o_sem.at[4]).wait()
        send.wait_send()
        for copy in copies:
            copy.wait()

    @pl.when(is_decoder)
    def _():
        copies = [keep_input_gates()] + keep_small([(0, emb_o, emb_h), (1, owners_o, owners_h)])
        cg_own, cg_far = crossed[0]
        de_own, de_far = crossed[1]
        gather.step1(cg_own)
        gather.step2(cg_far)
        gather.step2(cg_own)
        gather.begin(u_sq)
        gather.begin(de_own)
        arrival(de_far.src, x_recv.at[2]).wait()
        gather.begin(de_far)
        gather.step3(cg_own)
        gather.step3(cg_far)
        gather.end(cg_own)
        gather.end(cg_far)
        copies.append(pltpu.make_async_copy(cg, cg_o, o_sem.at[2]))
        copies[-1].start()
        arrival(ctx_o, x_recv.at[4]).wait()
        rest = [de_own, de_far]
        service = [
            (3, functools.partial(gather.step1, u_sq)),
            (5, functools.partial(gather.step1, de_own)),
            (6, functools.partial(gather.step1, de_far)),
            (8, functools.partial(gather.step2, u_sq)),
            (10, functools.partial(gather.step2, de_own)),
            (11, functools.partial(gather.step2, de_far)),
        ]
        ctx = nn(ctx_o[...], cg[...])
        scan(ctx, service)
        for u in [u_sq] + rest:
            gather.step3(u)
        for u in [u_sq] + rest:
            gather.end(u)
        later = [(rec, rec_o), (sq, sq_o), (de, de_o)]
        later = [
            pltpu.make_async_copy(a, b, o_sem.at[3 + k]) for k, (a, b) in enumerate(later)
        ]
        for copy in later:
            copy.start()
        copies += later
        copies += keep_small([(2, h_o, h_h), (4, ctx_o, ctx_h)])
        pre = nn(h_o[...], sq[...]) + nt(emb_o[...], de[...])
        arrival(outer, x_recv.at[8]).wait()
        pre = (pre.reshape(steps, R, 2 * M) + outer[...][None]).reshape(tokens, 2 * M)
        pre_o[...] = pre
        copies += keep_small([(5, pre_o, pre_h)])
        a, b = pre[:, :M], pre[:, M:]
        high = jnp.maximum(a, b)
        smooth = high + jnp.log(jnp.exp(a - high) + jnp.exp(b - high))
        grad_out[...] = smooth.astype(bf16)
        send = to_beside(grad_out, smooth_in, 5)
        send.start()
        copies.append(keep_transposed())
        send.wait_send()
        to_beside(sm_s, block_rows(sm, n, words), 0).wait_send()
        to_beside(dc_s, block_rows(dc, n, dc_s.shape[0]), 3).wait_send()
        end_requests()
        arrival(grad_o, x_recv.at[6]).wait()
        for copy in copies:
            copy.wait()


def forward(n, sizes, asked, hit, table, keep, labels, shards):
    R, H, E, M, slots, per, words = sizes
    Z, Y = factors(n)
    tokens = hit.shape[0]
    shape = jax.ShapeDtypeStruct
    dma = pltpu.SemaphoreType.DMA
    units = 9
    cg_rows, de_rows, dc_rows = H, 2 * M, H
    return pl.pallas_call(
        functools.partial(forward_kernel, n, sizes),
        out_shape=[
            shape((3 * H, H), bf16),
            shape((3 * H, E), bf16),
            shape((H, H), bf16),
            shape((cg_rows, 3 * H), bf16),
            shape((de_rows, E), bf16),
            shape((dc_rows, 2 * M), bf16),
            shape((2, Z * Y, words, M), bf16),
            shape((tokens // R, 5, R, H), f32),
            shape((tokens, H), bf16),
            shape((tokens, E), bf16),
            shape((tokens, 2 * M), f32),
            shape((R, H), f32),
            shape((R, H), bf16),
            shape((per, n * slots), bf16),
            shape((tokens, M), bf16),
            shape((8, 128), f32),
            shape((8, 128), jnp.int32),
        ],
        in_specs=[VMEM] * 5 + [ANY] * 7,
        out_specs=[ANY] * 14 + [VMEM] * 3,
        scratch_shapes=[
            pltpu.VMEM((n, 8, 128), jnp.int32),
            pltpu.VMEM((n * slots, E), bf16),
            pltpu.VMEM((n * slots, E), bf16),
            pltpu.VMEM((H, 3 * H), bf16),
            pltpu.VMEM((3 * H, E), bf16),
            pltpu.VMEM((H, H), bf16),
            pltpu.VMEM((2 * n * words, M), bf16),
            pltpu.VMEM((cg_rows, 3 * H), bf16),
            pltpu.VMEM((de_rows, E), bf16),
            pltpu.VMEM((dc_rows, 2 * M), bf16),
            pltpu.VMEM((tokens, 3 * H), f32),
            pltpu.VMEM((tokens // R, 5, R, H), f32),
            pltpu.VMEM((3 * H, H), bf16),
            pltpu.VMEM((tokens, M), bf16),
            pltpu.VMEM((tokens, M), bf16),
            pltpu.VMEM((tokens, 128), f32),
            pltpu.VMEM((tokens, 128), f32),
            pltpu.VMEM((tokens, 128), f32),
            pltpu.VMEM((2, 8, 128), jnp.int32),
            pltpu.VMEM((R, 2 * M), f32),
            pltpu.VMEM((tokens, H), bf16),
            pltpu.VMEM((tokens, E), bf16),
            pltpu.VMEM((tokens, 2 * M), f32),
            pltpu.VMEM((R, H), f32),
            pltpu.VMEM((R, H), bf16),
            pltpu.VMEM((per, n * slots), bf16),
            dma((units, 6)),
            dma((units, Z)),
            dma((units,)),
            dma((units,)),
            dma((7,)),
            dma((7,)),
            dma((10,)),
            dma((10,)),
            dma,
            dma,
            dma,
            dma,
            dma((2,)),
            dma((2,)),
            dma((6,)),
            dma((2,)),
        ],
        compiler_params=pltpu.CompilerParams(
            collective_id=2, has_side_effects=True, vmem_limit_bytes=VMEM_LIMIT
        ),
    )(asked, hit, table, keep, labels, *shards)


class Sum:
    def __init__(self, at, sems, index, mine, theirs, from_c, from_y, from_z, wholes, rows, out):
        self.at, self.sems, self.index = at, sems, index
        self.mine, self.theirs = mine, theirs
        self.from_c, self.from_y, self.from_z = from_c, from_y, from_z
        self.wholes, self.rows, self.out = wholes, rows, out

    def begin(self):
        at, i = self.at, self.index
        cs, cr = self.sems[:2]
        for zy in range(at.Z * at.Y):
            remote(
                self.theirs(zy), self.from_c(zy), cs.at[i], cr.at[i], at.device(at.z, at.y, 1 - at.c)
            ).start()

    def to_y(self, k, source):
        at, i = self.at, self.index
        ys, yr = self.sems[2:4]
        y = at.along_y(k)
        for z in range(at.Z):
            remote(
                source(z * at.Y + y),
                self.from_y(k, z),
                ys.at[i],
                yr.at[i, k - 1, z],
                at.device(at.z, y, at.c),
            ).start()

    def after_core(self):
        at, i = self.at, self.index
        arrival(self.wholes[0], self.sems[1].at[i]).wait()
        for k in list(range(1, at.Y)) + [0]:
            y = at.along_y(k)

            def per_z(z, _):
                zy = z * at.Y + y
                block = self.mine(zy)
                add_blocks(self.rows, [block, self.from_c(zy)], block, block.dtype)
                return _

            lax.fori_loop(0, at.Z, per_z, 0)
            if k:
                self.to_y(k, self.mine)

    def to_z(self, target, z, slot):
        at, i = self.at, self.index
        zs, zr = self.sems[4:6]
        remote(
            self.mine(target * at.Y + at.y),
            self.from_z(slot),
            zs.at[i],
            zr.at[i, slot],
            at.device(z, at.y, at.c),
        ).start()

    def after_y(self):
        at, i = self.at, self.index
        yr = self.sems[3]

        def per_z(z, _):
            block = self.mine(z * at.Y + at.y)
            came = [self.from_y(j, z) for j in range(1, at.Y)]
            for j, part in enumerate(came):
                arrival(part, yr.at[i, j, z]).wait()
            add_blocks(self.rows, [block] + came, block, block.dtype)
            return _

        lax.fori_loop(0, at.Z, per_z, 0)

        near = at.z_near()
        self.to_z(lax.rem(near + 2, 4), near, 0)
        self.to_z(near, near, 1)

    def add_z(self, target, slot):
        at, i = self.at, self.index
        part = self.from_z(slot)
        arrival(part, self.sems[5].at[i, slot]).wait()
        block = self.mine(target * at.Y + at.y)
        add_blocks(self.rows, [block, part], block, block.dtype)

    def mid_z(self):
        far = self.at.z_far()
        self.add_z(far, 0)
        self.to_z(far, far, 2)

    def after_z(self):
        at, i = self.at, self.index
        cs, _, ys, _, zs, zr = self.sems
        came = [self.from_z(slot) for slot in (1, 2)]
        for slot, part in zip((1, 2), came):
            arrival(part, zr.at[i, slot]).wait()
        add_blocks(self.rows, [self.mine(at.zy)] + came, self.out, self.out.dtype)
        for whole, sem in zip(self.wholes, (cs, ys, zs)):
            if whole is not None:
                arrival(whole, sem.at[i]).wait()


class SumZFirst(Sum):
    def after_core(self):
        at, i = self.at, self.index
        arrival(self.wholes[0], self.sems[1].at[i]).wait()

        def per_zy(zy, _):
            block = self.mine(zy)
            add_blocks(self.rows, [block, self.from_c(zy)], block, block.dtype)
            return _

        lax.fori_loop(0, at.Z * at.Y, per_zy, 0)
        near = at.z_near()
        ys, yr = self.sems[2:4]
        for k, target in enumerate((lax.rem(near + 2, 4), near)):
            for y in range(at.Y):
                remote(
                    self.mine(target * at.Y + y),
                    self.from_y(1, 2 * k + y),
                    ys.at[i],
                    yr.at[i, 0, 2 * k + y],
                    at.device(near, at.y, at.c),
                ).start()

    def add(self, zy, part, sem):
        arrival(part, sem).wait()
        block = self.mine(zy)
        add_blocks(self.rows, [block, part], block, block.dtype)

    def after_near(self):
        at, i = self.at, self.index
        yr, zs, zr = self.sems[3:6]
        far = at.z_far()
        for k, target in enumerate((far, at.z)):
            for y in range(at.Y):
                self.add(target * at.Y + y, self.from_y(1, 2 * k + y), yr.at[i, 0, 2 * k + y])
                if k == 0:
                    remote(
                        self.mine(far * at.Y + y),
                        self.from_z(y),
                        zs.at[i],
                        zr.at[i, y],
                        at.device(far, at.y, at.c),
                    ).start()

    def after_far(self):
        at, i = self.at, self.index
        zs, zr = self.sems[4:6]
        for y in range(at.Y):
            self.add(at.z * at.Y + y, self.from_z(y), zr.at[i, y])
        other = at.along_y(1)
        remote(
            self.mine(at.z * at.Y + other),
            self.from_z(2),
            zs.at[i],
            zr.at[i, 2],
            at.device(at.z, other, at.c),
        ).start()

    def finish(self):
        at, i = self.at, self.index
        cs, _, ys, _, zs, zr = self.sems
        part = self.from_z(2)
        arrival(part, zr.at[i, 2]).wait()
        add_blocks(self.rows, [self.mine(at.zy), part], self.out, self.out.dtype)
        for whole, sem in zip(self.wholes, (cs, ys, zs)):
            arrival(whole, sem.at[i]).wait()


def backward_kernel_all(n, sizes, *refs):
    R, H, E, M, slots, per, words = sizes
    (
        pre,
        grad,
        keep,
        tanh,
        context,
        loss,
        h_h,
        emb_h,
        hit_h,
        owners_h,
        wr_h,
        wi_h,
        sq_h,
        cg_h,
        de_h,
        dc_h,
        term_h,
        rec_h,
    ) = refs[:18]
    (
        table_o,
        input_o,
        recur_o,
        square_o,
        gates_o,
        deep_o,
        context_o,
        soft_o,
        loss_o,
        early_h,
        late_h,
    ) = refs[18:29]
    (
        wrt,
        wi,
        sq,
        de,
        dc,
        big,
        rec,
        low,
        cand,
        before,
        state_grad,
        total,
        deep_low,
        outer_low,
        early_pack,
        late_pack,
        c_grad,
        c_came,
        pre_low,
        g_out,
        g_in,
        wide_c,
        wide_y,
        wide_z,
        thin_c,
        thin_y,
        thin_z,
        deep_c,
        deep_y,
        deep_z,
        soft_far,
        deep_far,
        far_rows,
        block_rows,
        chunks,
        ctx_cols,
        losses,
        loss_sum,
        cs_sem,
        cr_sem,
        ys_sem,
        yr_sem,
        zs_sem,
        zr_sem,
        pz_sem,
        py_sem,
        pc_sem,
        ps_sem,
        load_sem,
        rec_sem,
        big_sem,
        chunk_sem,
        x_send,
        x_recv,
        ls_sem,
        lr_sem,
        gs_sem,
        gr_sem,
        h,
        emb,
        hit,
        owners,
        small_sem,
    ) = refs[29:]
    at = Place(n)
    Z, Y = at.Z, at.Y
    ZY = Z * Y
    tokens = emb.shape[0]
    steps = tokens // R
    is_decoder = at.s == 1
    beside = (1 - at.s, at.d)
    others = [lax.rem(at.d + k, n) for k in range(1, n)]
    sems = (cs_sem, cr_sem, ys_sem, yr_sem, zs_sem, zr_sem)

    loads = [
        pltpu.make_async_copy(a, b, load_sem.at[k])
        for k, (a, b) in enumerate([(sq_h, sq), (wr_h, wrt), (wi_h, wi)])
    ]
    for copy in loads:
        copy.start()
    small = [
        pltpu.make_async_copy(a, b, small_sem.at[k])
        for k, (a, b) in enumerate([(h_h, h), (emb_h, emb), (hit_h, hit), (owners_h, owners)])
    ]
    for copy in small:
        copy.start()
    load_de = pltpu.make_async_copy(de_h, de, load_sem.at[3])
    load_dc = pltpu.make_async_copy(dc_h, dc, load_sem.at[4])

    def load_record(i):
        return pltpu.make_async_copy(
            rec_h.at[steps - 1 - i], rec.at[lax.rem(i, 2)], rec_sem.at[lax.rem(i, 2)]
        )

    load_record(0).start()
    greet([(at.s, d) for d in others] + [beside])

    def to_beside(src, dst, k):
        return remote(src, dst, x_send.at[k], x_recv.at[k], beside)

    def block_sum(index, term, rows, stride, off, bufs, slot, out, kind=Sum):
        c_buf, y_buf, z_buf = bufs

        def block(zy, c):
            return term.at[pl.ds(multiple(off + (zy * 2 + c) * stride, 16), rows)]

        return kind(
            at,
            sems,
            index,
            lambda zy: block(zy, at.c),
            lambda zy: block(zy, 1 - at.c),
            lambda zy: c_buf.at[slot, zy],
            lambda k, z: y_buf.at[slot, k - 1, z],
            lambda k: z_buf.at[slot, k],
            (c_buf.at[slot], y_buf.at[slot], z_buf.at[slot]),
            rows,
            out,
        )

    wide, thin, deep = (wide_c, wide_y, wide_z), (thin_c, thin_y, thin_z), (deep_c, deep_y, deep_z)
    tall = recur_o.shape[0]
    recur_sums = [
        block_sum(g, wrt, tall, tall, g * H, wide, g, recur_o.at[:, pl.ds(g * H, H)])
        for g in range(3)
    ]
    square_sum = block_sum(3, sq, tall, tall, 0, wide, 3, square_o, SumZFirst)
    high = input_o.shape[0]
    part = thin_c.shape[2]
    input_sums = [
        block_sum(4 + j, wi, part, high, j * part, thin, j, input_o.at[pl.ds(j * part, part)])
        for j in range(high // part)
    ]
    after = 4 + high // part
    deep_rows = deep_far.shape[0]
    deep_sums = [
        block_sum(
            after + j, de, deep_rows, deep_rows, j * n * deep_rows, deep, j, (deep_far, deep_o)[j]
        )
        for j in range(2)
    ]

    def big_rows(first, count):
        return big.at[pl.ds(multiple(first * words, 16), count * words)]

    def soft_sum(j):
        base_y, base_z = 2 * Z, 2 * Z + 2 * (Y - 1) * Z

        def mine(zy):
            return big_rows(j * Z + zy // Y, 1)

        return Sum(
            at,
            sems,
            after + 2 + j,
            mine,
            None,
            None,
            lambda k, z: big_rows(base_y + (j * (Y - 1) + k - 1) * Z + z, 1),
            lambda k: big_rows(base_z + j * 3 + k, 1),
            (
                None,
                big_rows(base_y + j * (Y - 1) * Z, (Y - 1) * Z),
                big_rows(base_z + j * 3, 3),
            ),
            words,
            (soft_o, soft_far)[j],
        )

    soft_sums = [soft_sum(0), soft_sum(1)]

    def scan(first, with_state, service):
        def step(i, carry):
            t = steps - 1 - i
            rows = pl.ds(multiple(t * R, R), R)
            slot = lax.rem(i, 2)

            @pl.when(i + 1 < steps)
            def _():
                load_record(i + 1).start()

            load_record(i).wait()
            g = carry + state_grad[rows, :] if with_state else carry
            z, r, c, m, p = (rec[slot, k] for k in range(5))
            pc = g * (1.0 - z) * (1.0 - c * c)
            pz = g * (p - c) * z * (1.0 - z)
            pr = pc * m * r * (1.0 - r)
            pn = pc * r
            parts = [pz, pr, pn]
            back = g * z
            for k, x in enumerate(parts):
                x_low = x.astype(bf16)
                low[rows, pl.ds(k * H, H)] = x_low
                back += nn(x_low, wrt[pl.ds(k * H, H), :])
                if with_state:
                    total[:, pl.ds(k * H, H)] += x
            cand[rows, :] = pc.astype(bf16)
            before[rows, :] = p.astype(bf16)
            for when, what in service:
                pl.when(i == when)(what)
            return back * keep[rows, :]

        lax.fori_loop(0, steps, step, first)

    def recur_term(g):
        cols = pl.ds(g * H, H)

        def body(i, _):
            some = pl.ds(multiple(i * 256, 256), 256)
            rows = pl.ds(multiple(g * H + i * 256, 256), 256)
            wrt[rows, :] = tn(before[:, some], low[:, cols]).astype(bf16)
            return _

        lax.fori_loop(0, H // 256, body, 0)

    def input_term():
        def body(i, _):
            some = pl.ds(multiple(i * 256, 256), 256)
            wi[some, :] = tn(low[:, some], emb[...]).astype(bf16)
            return _

        lax.fori_loop(0, 2 * H // 256, body, 0)

        def last(i, _):
            some = pl.ds(multiple(i * 256, 256), 256)
            rows = pl.ds(multiple(2 * H + i * 256, 256), 256)
            wi[rows, :] = tn(cand[:, some], emb[...]).astype(bf16)
            return _

        lax.fori_loop(0, H // 256, last, 0)

    def slot_rows(ref, d):
        return ref.at[pl.ds(multiple(d * slots, 16), slots)]

    def give(extra):
        grads = nn(low[:, pl.ds(0, 2 * H)], wi[pl.ds(0, 2 * H), :])
        grads += nn(cand[...], wi[pl.ds(2 * H, H), :])
        if extra:
            grads += nn(deep_low[...], de[...])
        g_out[...] = tn(hit[...], grads.astype(bf16)).astype(bf16)
        for d in others:
            remote(slot_rows(g_out, d), slot_rows(g_in, at.d), gs_sem, gr_sem, (at.s, d)).start()

    def take():
        own = pl.ds(multiple(at.d * slots, 16), slots)
        some = g_in.at[pl.ds(0, (n - 1) * slots)]
        arrival(some, gr_sem).wait()
        arrival(some, gs_sem).wait()
        g_in[own, :] = g_out[own, :]
        table_o[...] = nn(owners[...], g_in[...])

    def end_sums(before):
        items = list(before) + list(input_sums)
        at_y, at_mid, at_end = len(before), max(len(before) - 1, 0), 0
        while at_end < len(items):
            if at_y < len(items):
                items[at_y].after_y()
                at_y += 1
            if at_mid < min(at_y - 1, len(items)) or at_y == len(items) > at_mid:
                items[at_mid].mid_z()
                at_mid += 1
            if at_end < at_mid - 1 or at_mid == len(items):
                items[at_end].after_z()
                at_end += 1

    @pl.when(jnp.logical_not(is_decoder))
    def _():
        load_dc.start()
        def soft_to_y(j):
            for k in range(1, Y):
                soft_sums[j].to_y(k, lambda zy: term_h.at[j, zy])

        for j, item in enumerate(soft_sums):
            soft_to_y(j)
            for z in range(Z):
                zy = z * Y + at.y
                pltpu.make_async_copy(term_h.at[j, zy], item.mine(zy), big_sem.at[j]).start()
        losses[at.d] = loss[...]
        for d in others:
            remote(loss, losses.at[at.d], ls_sem, lr_sem, (at.s, d)).start()
        for j, item in enumerate(soft_sums):
            whole = big_rows(j * Z, Z)
            arrival(whole, big_sem.at[j]).wait()
        for copy in loads:
            copy.wait()
        load_dc.wait()
        arrival(outer_low, x_recv.at[6]).wait()
        back = nt(outer_low[...], dc[...])
        arrival(c_came, x_recv.at[0]).wait()
        c = tanh[...]
        c_low = (back + c_came[...].astype(f32)).astype(bf16).astype(f32)
        pre_low[...] = (c_low * (1.0 - c * c)).astype(bf16)
        first = nt(pre_low[...], sq[...])

        def square_term():
            sq[...] = tn(h[pl.ds((steps - 1) * R, R), :], pre_low[...]).astype(bf16)
            square_sum.begin()

        small[0].wait()
        scan(
            first,
            False,
            [
                (1, soft_sums[0].after_y),
                (2, square_term),
                (5, square_sum.after_core),
                (9, soft_sums[0].mid_z),
            ],
        )
        for copy in small[1:]:
            copy.wait()
        for g in range(3):
            recur_term(g)
            recur_sums[g].begin()
            if g:
                recur_sums[g - 1].after_core()
        soft_sums[1].after_y()
        give(False)
        recur_sums[2].after_core()
        input_term()
        for item in input_sums:
            item.begin()
        soft_sums[0].after_z()
        for item in input_sums:
            item.after_core()
        square_sum.after_near()
        soft_sums[1].mid_z()
        recur_sums[0].after_y()
        square_sum.after_far()
        recur_sums[1].after_y()
        recur_sums[0].mid_z()
        soft_sums[1].after_z()
        send = to_beside(soft_far, soft_o, 1)
        send.start()
        some = losses.at[pl.ds(0, n - 1)]
        arrival(some, lr_sem).wait()
        arrival(some, ls_sem).wait()
        all_loss = losses[0]
        for d in range(1, n):
            all_loss += losses[d]
        loss_sum[...] = all_loss
        loss_o[...] = all_loss
        loss_send = to_beside(loss_sum, loss_o, 2)
        loss_send.start()
        recur_sums[2].after_y()
        recur_sums[1].mid_z()
        recur_sums[0].after_z()
        take()
        end_sums([recur_sums[1], recur_sums[2]])
        square_sum.finish()
        send.wait_send()
        loss_send.wait_send()
        arrival(deep_o, x_recv.at[3]).wait()
        arrival(gates_o, x_recv.at[4]).wait()
        arrival(context_o, x_recv.at[5]).wait()

    @pl.when(is_decoder)
    def _():
        load_de.start()
        chunk = big.shape[1]
        for k in range(3 * H // chunk):
            pltpu.make_async_copy(
                cg_h.at[:, pl.ds(k * chunk, chunk)], big.at[pl.ds(k * H, H)], big_sem.at[0]
            ).start()
        a, b = pre[:, pl.ds(0, M)], pre[:, pl.ds(M, M)]
        high = jnp.maximum(a, b)
        smooth = high + jnp.log(jnp.exp(a - high) + jnp.exp(b - high))
        sg = grad[...].astype(f32)
        for k, x in enumerate((a, b)):
            cols = pl.ds(k * M, M)
            deep_grad = sg * jnp.exp(x - smooth)
            deep_low[:, cols] = deep_grad.astype(bf16)
            outer_low[:, cols] = jnp.sum(deep_grad.reshape(steps, R, M), axis=0).astype(bf16)
        outer_send = to_beside(outer_low, outer_low, 6)
        outer_send.start()
        for copy in loads:
            copy.wait()
        state_grad[...] = nt(deep_low[...], sq[...])
        total[...] = jnp.zeros_like(total)
        gather = Gather(at, pz_sem, py_sem, pc_sem, ps_sem)
        early = Unit(0, early_pack, early_h, R, 0)
        late = Unit(1, late_pack, late_h, R, 0)
        early_pack[:, pl.ds(0, H)] = context[...]
        early_pack[:, pl.ds(H, 2 * M)] = outer_low[...]
        own_copies = [
            pltpu.make_async_copy(early_pack, early.block(at.zy, at.c), big_sem.at[1]),
            pltpu.make_async_copy(late_pack, late.block(at.zy, at.c), big_sem.at[2]),
        ]
        own_copies[0].start()
        gather.begin(early)
        scan(
            jnp.zeros((R, H), f32),
            True,
            [
                (7, lambda: gather.step1(early)),
                (11, lambda: gather.step2(early)),
            ],
        )
        late_pack[...] = total[...].astype(bf16)
        gates_rows = big.at[pl.ds(0, 3 * H * H // chunk)]
        arrival(gates_rows, big_sem.at[0]).wait()
        for k in range(3 * H // chunk):
            cols = pl.ds(k * chunk, chunk)
            term = nt(late_pack[:, cols], big[pl.ds(k * H, H), :])
            back = term if k == 0 else back + term
        c_grad[...] = back.astype(bf16)
        send = to_beside(c_grad, c_came, 0)
        send.start()

        own_copies[1].start()
        gather.begin(late)
        for copy in small:
            copy.wait()
        for g in range(3):
            recur_term(g)
            recur_sums[g].begin()
            if g:
                recur_sums[g - 1].after_core()
        gather.step1(late)
        load_de.wait()
        give(True)
        recur_sums[2].after_core()
        sq[...] = tn(h[...], deep_low[...]).astype(bf16)
        square_sum.begin()
        gather.step2(late)
        de[...] = tn(deep_low[...], emb[...]).astype(bf16)
        for item in deep_sums:
            item.begin()
        input_term()
        for item in input_sums:
            item.begin()
        square_sum.after_core()
        for item in deep_sums:
            item.after_core()
        for item in input_sums:
            item.after_core()
        gather.step3(early)
        recur_sums[0].after_y()
        square_sum.after_near()
        recur_sums[1].after_y()
        recur_sums[0].mid_z()
        gather.step3(late)
        recur_sums[2].after_y()
        recur_sums[1].mid_z()
        square_sum.after_far()
        for u in (early, late):
            gather.end(u)
        for copy in own_copies:
            copy.wait()
        recur_sums[0].after_z()

        rows = gates_o.shape[0]
        firsts = [(sec * n + at.d) * rows for sec in (0, 1)]
        for k, first in enumerate(firsts):
            lanes = multiple(first // 128 * 128, 128)
            copy = pltpu.make_async_copy(
                early_h.at[:, pl.ds(lanes, 128)], ctx_cols.at[k], big_sem.at[3]
            )
            copy.start()
            copy.wait()
        pieces = (2 * M + 3 * H) // chunk

        def load_chunk(k):
            if k < 2 * M // chunk:
                src = early_h.at[:, pl.ds(H + k * chunk, chunk)]
            else:
                src = late_h.at[:, pl.ds(k * chunk - 2 * M, chunk)]
            return pltpu.make_async_copy(src, chunks.at[k % 2], chunk_sem.at[k % 2])

        load_chunk(0).start()
        for k in range(pieces):
            if k + 1 < pieces:
                load_chunk(k + 1).start()
            load_chunk(k).wait()
            for j, first in enumerate(firsts):
                block_rows[...] = tn(ctx_cols[j], chunks[k % 2])
                product = block_rows[pl.ds(multiple(lax.rem(first, 128), 8), rows), :]
                if k < 2 * M // chunk:
                    dst, cols = context_o, pl.ds(k * chunk, chunk)
                else:
                    dst, cols = gates_o, pl.ds(k * chunk - 2 * M, chunk)
                if j == 0:
                    far_rows[:, pl.ds(k * chunk, chunk)] = product
                else:
                    dst[:, cols] = product
        sends = [
            to_beside(far_rows.at[:, pl.ds(2 * M, 3 * H)], gates_o, 4),
            to_beside(far_rows.at[:, pl.ds(0, 2 * M)], context_o, 5),
        ]
        for copy in sends:
            copy.start()
        take()
        recur_sums[2].mid_z()
        for item in deep_sums:
            item.after_y()
        recur_sums[1].after_z()
        for item in deep_sums:
            item.mid_z()
        recur_sums[2].after_z()
        end_sums([])
        square_sum.finish()
        for item in deep_sums:
            item.after_z()
        sends.append(to_beside(deep_far, deep_o, 3))
        sends[-1].start()
        for copy in sends + [send, outer_send]:
            copy.wait_send()
        arrival(soft_o, x_recv.at[1]).wait()
        arrival(loss_o, x_recv.at[2]).wait()


def backward(n, sizes, blocks, arrays):
    R, H, E, M, slots, per, words = sizes
    Z, Y = factors(n)
    ZY = Z * Y
    tokens = arrays[0].shape[0]
    shape = jax.ShapeDtypeStruct
    vmem = pltpu.VMEM
    dma = pltpu.SemaphoreType.DMA
    input_b, recur_b, square_b, gates_b, deep_b, context_b = blocks
    tall = recur_b[0]
    part = next(k for k in (64, 48, 32, 16) if input_b[0] % k == 0)
    thin = input_b[0] // part
    units = 4 + thin + 4
    chunk = M
    big_rows = words * (2 * Z + 2 * (Y - 1) * Z + 6)
    big_rows = max(big_rows, 3 * H * H // chunk)
    y1 = max(Y - 1, 1)
    return pl.pallas_call(
        functools.partial(backward_kernel_all, n, sizes),
        out_shape=[
            shape((per, E), f32),
            shape(input_b, f32),
            shape(recur_b, f32),
            shape(square_b, f32),
            shape(gates_b, f32),
            shape(deep_b, f32),
            shape(context_b, f32),
            shape((words, M), f32),
            shape((8, 128), f32),
            shape((n * R, H + 2 * M), bf16),
            shape((n * R, 3 * H), bf16),
        ],
        in_specs=[VMEM] * 6 + [ANY] * 12,
        out_specs=[VMEM] * 9 + [ANY] * 2,
        scratch_shapes=[
            vmem((3 * H, H), bf16),
            vmem((3 * H, E), bf16),
            vmem((H, H), bf16),
            vmem((2 * M, E), bf16),
            vmem((H, 2 * M), bf16),
            vmem((big_rows, chunk), bf16),
            vmem((2, 5, R, H), f32),
            vmem((tokens, 3 * H), bf16),
            vmem((tokens, H), bf16),
            vmem((tokens, H), bf16),
            vmem((tokens, H), f32),
            vmem((R, 3 * H), f32),
            vmem((tokens, 2 * M), bf16),
            vmem((R, 2 * M), bf16),
            vmem((R, H + 2 * M), bf16),
            vmem((R, 3 * H), bf16),
            vmem((R, H), bf16),
            vmem((R, H), bf16),
            vmem((R, H), bf16),
            vmem((n * slots, E), bf16),
            vmem((n * slots, E), bf16),
            vmem((4, ZY, tall, H), bf16),
            vmem((4, y1, Z, tall, H), bf16),
            vmem((4, 3, tall, H), bf16),
            vmem((thin, ZY, part, E), bf16),
            vmem((thin, y1, Z, part, E), bf16),
            vmem((thin, 3, part, E), bf16),
            vmem((2, ZY) + deep_b, bf16),
            vmem((2, y1, Z) + deep_b, bf16),
            vmem((2, 3) + deep_b, bf16),
            vmem((words, M), f32),
            vmem(deep_b, f32),
            vmem((gates_b[0], 2 * M + 3 * H), f32),
            vmem((128, chunk), f32),
            vmem((2, n * R, chunk), bf16),
            vmem((2, n * R, 128), bf16),
            vmem((n, 8, 128), f32),
            vmem((8, 128), f32),
            dma((units,)),
            dma((units,)),
            dma((units,)),
            dma((units, y1, Z)),
            dma((units,)),
            dma((units, 3)),
            dma((2, 6)),
            dma((2, Z)),
            dma((2,)),
            dma((2,)),
            dma((5,)),
            dma((2,)),
            dma((4,)),
            dma((2,)),
            dma((7,)),
            dma((7,)),
            dma,
            dma,
            dma,
            dma,
            vmem((tokens, H), bf16),
            vmem((tokens, E), bf16),
            vmem((tokens, n * slots), bf16),
            vmem((per, n * slots), bf16),
            dma((4,)),
        ],
        compiler_params=pltpu.CompilerParams(
            collective_id=3, has_side_effects=True, vmem_limit_bytes=VMEM_LIMIT
        ),
    )(*arrays)


def in_rounds(
    token_ids,
    resets,
    targets,
    embedding,
    input_gates,
    recur_gates,
    square,
    context_gates,
    deep_embed,
    deep_context,
    softmax_weight,
):
    n = lax.axis_size("dp")
    s = lax.axis_index("section")
    d = lax.axis_index("dp")
    is_decoder = s == 1
    micro, rows, steps = token_ids.shape[1:]
    R = micro * rows
    tokens = R * steps
    H = square.shape[2]
    E = embedding.shape[2]
    M = softmax_weight.shape[1]
    per = embedding.shape[1]
    slots = max(512 // n, 8)
    scale = 1.0 / (R * n)

    def time_major(x):
        return jnp.transpose(x.reshape(R, steps), (1, 0)).reshape(-1)

    ids = time_major(token_ids[0])
    keep = time_major(1 - resets[0]).astype(f32)[:, None]
    labels = time_major(targets)

    plan = request_slots(ids, n, per, slots)
    rounds = lax.pmax(jnp.max(plan[2]) // slots + 1, ("section", "dp"))
    table = embedding[0]

    def fetch(turn):
        asked, hit = round_maps(plan, turn, n, slots)
        owners = owner_map(asked, n, per)
        came = swap(nn(owners, table).astype(bf16), n)
        return owners, hit, nn(hit, came).astype(bf16)

    owners, hit, emb = fetch(0)

    def more(carry):
        turn, emb = carry
        return turn + 1, emb + fetch(turn)[2]

    _, emb = lax.while_loop(lambda c: c[0] < rounds, more, (jnp.int32(1), emb))

    wr, wi, sq, sm, cg, de, dc = gather(
        n,
        [
            recur_gates[0],
            input_gates[0],
            square[0],
            softmax_weight,
            context_gates,
            deep_embed,
            deep_context,
        ],
        (False, False, False, False, True, True, True),
    )
    wr, wi, sq, sm = wr.reshape(H, 3 * H), wi.reshape(3 * H, E), sq.reshape(H, H), sm.reshape(-1, M)
    cg, de, dc = cg.reshape(H, 3 * H), de.reshape(2 * M, E), dc.reshape(H, 2 * M)

    enc = gru_forward(emb, wi, wr, jnp.zeros((R, 3 * H), f32), keep)
    last_low = enc[5][-R:]
    ctx_tanh = jnp.tanh(nn(last_low, sq))
    context = lax.ppermute(ctx_tanh.astype(bf16), "section", [(0, 1)])

    dec = gru_forward(emb, wi, wr, nn(context, cg), keep)
    states_low = dec[5]
    deep_pre = nn(states_low, sq) + nt(emb, de)
    deep_pre = (deep_pre.reshape(steps, R, -1) + nn(context, dc)[None]).reshape(tokens, -1)
    smooth = jnp.logaddexp(deep_pre[:, :M], deep_pre[:, M:])
    smooth_low = smooth.astype(bf16)

    came = lax.ppermute(smooth_low, "section", [(1, 0)])
    head_in = jnp.where(is_decoder, smooth_low, came)
    words = sm.shape[0]
    logits = nt(head_in, sm)
    top = jnp.max(logits, axis=1)
    total = jnp.sum(jnp.exp(logits - top[:, None]), axis=1)
    hits = lax.broadcasted_iota(jnp.int32, logits.shape, 1) == (labels - s * words)[:, None]
    picked = jnp.sum(jnp.where(hits, logits, 0.0), axis=1)
    stats = jnp.stack([top, total, picked])
    other = lax.ppermute(stats, "section", [(0, 1), (1, 0)])
    all_top = jnp.maximum(top, other[0])
    log_norm = all_top + jnp.log(
        total * jnp.exp(top - all_top) + other[1] * jnp.exp(other[0] - all_top)
    )
    loss = jnp.where(is_decoder, jnp.sum(log_norm - picked - other[2]) * scale, 0.0)
    logit_low = ((jnp.exp(logits - log_norm[:, None]) - hits.astype(f32)) * scale).astype(bf16)
    smooth_part = nn(logit_low, sm)
    smooth_grad = smooth_part + lax.ppermute(smooth_part, "section", [(0, 1)])
    softmax_term = tn(logit_low, head_in).astype(bf16)

    deep_grad = jnp.concatenate(
        [
            smooth_grad * jnp.exp(deep_pre[:, :M] - smooth),
            smooth_grad * jnp.exp(deep_pre[:, M:] - smooth),
        ],
        axis=1,
    )
    deep_low = deep_grad.astype(bf16)
    outer_low = jnp.sum(deep_grad.reshape(steps, R, -1), axis=0).astype(bf16)
    state_grad = nt(deep_low, sq)
    dec_low, dec_cand, drive_sum = gru_backward(
        state_grad, jnp.zeros((R, H), f32), keep, dec[:5], wr
    )
    drive_sum_low = drive_sum.astype(bf16)
    context_grad = (nt(outer_low, dc) + nt(drive_sum_low, cg)).astype(bf16)
    packed = lax.all_gather(jnp.concatenate([context, outer_low, drive_sum_low], axis=1), "dp", tiled=True)
    packed_came = lax.ppermute(packed, "section", [(1, 0)])
    packed = jnp.where(is_decoder, packed, packed_came)

    context_back = lax.ppermute(context_grad, "section", [(1, 0)])
    pre_low = (context_back.astype(f32) * (1.0 - ctx_tanh * ctx_tanh)).astype(bf16)
    enc_low, enc_cand, _ = gru_backward(
        jnp.zeros((tokens, H), f32), nt(pre_low, sq), keep, enc[:5], wr
    )

    def pick(of_encoder, of_decoder):
        return jnp.where(is_decoder, of_decoder, of_encoder)

    recur_low = pick(enc_low, dec_low)
    cand_low = pick(enc_cand, dec_cand)
    before_low = pick(enc[4], dec[4]).astype(bf16)
    drive_low = jnp.concatenate([recur_low[:, : 2 * H], cand_low], axis=1)
    recur_term = tn(before_low, recur_low).astype(bf16)
    input_term = tn(drive_low, emb).astype(bf16)
    deep_mask = jnp.where(is_decoder, deep_low, jnp.zeros_like(deep_low))
    input_grad = nn(drive_low, wi) + nn(deep_mask, de)
    rows_pad = jnp.zeros((tokens - R, H), bf16)
    square_term = tn(
        pick(jnp.concatenate([last_low, rows_pad]), states_low),
        pick(jnp.concatenate([pre_low, rows_pad]), deep_low),
    ).astype(bf16)
    deep_term = tn(deep_mask, emb).astype(bf16)

    input_grad_low = input_grad.astype(bf16)

    def give(owners, hit):
        return tn(owners, swap(tn(hit, input_grad_low).astype(bf16), n))

    def give_more(carry):
        turn, grad = carry
        asked, hit = round_maps(plan, turn, n, slots)
        return turn + 1, grad + give(owner_map(asked, n, per), hit)

    table_grad = give(owners, hit)
    _, table_grad = lax.while_loop(
        lambda c: c[0] < rounds, give_more, (jnp.int32(1), table_grad)
    )

    deep_blocks = jnp.stack(
        [x.reshape((n,) + deep_embed.shape) for x in jnp.split(deep_term, 2)], axis=1
    )
    deep_blocks = deep_blocks.reshape(n, 2 * deep_embed.shape[0], E)
    loss_blocks = jnp.broadcast_to(loss, (n, 8, 128))
    square_sum, recur_sum, input_sum, softmax_sum, deep_sum, loss_sum = scatter(
        n,
        [
            square_term.reshape((n,) + square.shape[1:]),
            recur_term.reshape((n,) + recur_gates.shape[1:]),
            input_term.reshape((n,) + input_gates.shape[1:]),
            softmax_term.reshape((n,) + softmax_weight.shape),
            deep_blocks,
            loss_blocks,
        ],
        1,
    )
    deep_halves = deep_sum.reshape((2,) + deep_embed.shape)
    both = lax.ppermute(
        jnp.concatenate([deep_halves[0].reshape(-1), loss_sum[:1].reshape(-1)]), "section", [(1, 0)]
    )
    deep_out = jnp.where(is_decoder, deep_halves[1], both[:-128].reshape(deep_embed.shape))
    loss_out = jnp.where(is_decoder, loss_sum[0, 0], both[-1])

    own = (s * n + d) * context_gates.shape[0]
    context_own = lax.dynamic_slice(packed, (0, own), (packed.shape[0], context_gates.shape[0]))
    gates_out = tn(context_own, packed[:, H + 2 * M :])
    context_out = tn(context_own, packed[:, H : H + 2 * M])

    return (
        loss_out,
        table_grad[None],
        input_sum[None],
        recur_sum[None],
        square_sum[None],
        gates_out,
        deep_out,
        context_out,
        softmax_sum,
    )


def in_one_round(
    token_ids,
    resets,
    targets,
    embedding,
    input_gates,
    recur_gates,
    square,
    context_gates,
    deep_embed,
    deep_context,
    softmax_weight,
):
    n = lax.axis_size("dp")
    s = lax.axis_index("section")
    d = lax.axis_index("dp")
    is_decoder = s == 1
    micro, rows, steps = token_ids.shape[1:]
    R = micro * rows
    tokens = R * steps
    H = square.shape[2]
    E = embedding.shape[2]
    M = softmax_weight.shape[1]
    per = embedding.shape[1]
    slots = 512 // n

    def time_major(x):
        return jnp.transpose(x.reshape(R, steps), (1, 0)).reshape(-1)

    ids = time_major(token_ids[0])
    keep = time_major(1 - resets[0]).astype(f32)[:, None]
    labels = time_major(targets)

    plan = request_slots(ids, n, per, slots)
    asked, hit = round_maps(plan, 0, n, slots)
    lane = jnp.arange(128, dtype=jnp.int32)
    asked = jnp.tile(asked.reshape(n, slots), (1, 128 // slots))
    asked = jnp.where(lane // slots == d % (128 // slots), asked, -1)
    fullest = jnp.broadcast_to(jnp.max(plan[2]), (n, 1, 128))
    asked = jnp.concatenate([asked[:, None], fullest, jnp.zeros((n, 6, 128), jnp.int32)], axis=1)

    shards = [
        recur_gates[0],
        input_gates[0],
        square[0],
        softmax_weight,
        context_gates,
        deep_embed,
        deep_context,
    ]
    sizes = (R, H, E, M, slots, per, softmax_weight.shape[0])
    results = forward(n, sizes, asked, hit, embedding[0], keep, labels[:, None], shards)

    (
        wr,
        wi,
        sq,
        cg,
        de,
        dc,
        softmax_term,
        rec,
        states_low,
        emb,
        deep_pre,
        ctx_tanh,
        context,
        owners,
        smooth_grad,
        loss,
        most,
    ) = results
    blocks = [
        x.shape[-2:]
        for x in (input_gates, recur_gates, square, context_gates, deep_embed, deep_context)
    ]
    table, inputs, recur, squares, gates, deep, contexts, soft, loss, _, _ = backward(
        n,
        sizes,
        blocks,
        [
            deep_pre,
            smooth_grad,
            keep,
            ctx_tanh,
            context,
            loss,
            states_low,
            emb,
            hit,
            owners,
            wr,
            wi,
            sq,
            cg,
            de,
            dc,
            softmax_term,
            rec,
        ],
    )
    fast = (
        loss[0, 0],
        table[None],
        inputs[None],
        recur[None],
        squares[None],
        gates,
        deep,
        contexts,
        soft,
    )

    def again(carry):
        return False, in_rounds(
            token_ids,
            resets,
            targets,
            embedding,
            input_gates,
            recur_gates,
            square,
            context_gates,
            deep_embed,
            deep_context,
            softmax_weight,
        )

    too_full = most[0, 0] >= slots
    return lax.while_loop(lambda carry: carry[0], again, (too_full, fast))[1]


def per_device(*args):
    n = lax.axis_size("dp")
    blocks = [args[k].shape[-2] for k in (4, 5, 6, 7, 8, 9, 10)]
    aligned = all(rows % 16 == 0 for rows in blocks)
    if aligned and n == 16:
        return in_one_round(*args)
    return in_rounds(*args)


def solution(mesh):
    halves = P("section", "dp", None)
    whole = P(("section", "dp"), None)
    in_specs = (
        P("section", None, "dp", None),
        P("section", None, "dp", None),
        P(None, "dp", None),
        halves,
        halves,
        halves,
        halves,
        whole,
        whole,
        whole,
        whole,
    )
    out_specs = (P(), halves, halves, halves, halves, whole, whole, whole, whole)
    return jax.shard_map(
        per_device, mesh=mesh, in_specs=in_specs, out_specs=out_specs, check_vma=False
    )
```

```python
import functools

import jax
import jax.numpy as jnp
from jax import lax
from jax.experimental import pallas as pl
from jax.experimental.pallas import tpu as pltpu
from jax.sharding import PartitionSpec as P

MESH = pl.DeviceIdType.MESH
ANY = pl.BlockSpec(memory_space=pl.ANY)
VMEM = pl.BlockSpec(memory_space=pltpu.VMEM)
f32 = jnp.float32
bf16 = jnp.bfloat16
VMEM_LIMIT = 62 * 2**20


def nn(a, b):
    return jnp.dot(a, b, preferred_element_type=f32)


def nt(a, b):
    return lax.dot_general(a, b, (((1,), (1,)), ((), ())), preferred_element_type=f32)


def tn(a, b):
    return lax.dot_general(a, b, (((0,), (0,)), ((), ())), preferred_element_type=f32)


def factors(n):
    z = 4 if n % 8 == 0 else 1
    return z, n // (2 * z)


class Place:
    def __init__(self, n):
        self.Z, self.Y = factors(n)
        self.s = lax.axis_index("section")
        d = lax.axis_index("dp")
        self.d = d
        self.c = d % 2
        self.zy = d // 2
        self.y = self.zy % self.Y
        self.z = self.zy // self.Y

    def along_z(self, step):
        return lax.rem(self.z + step + self.Z, self.Z)

    def along_y(self, step):
        return lax.rem(self.y + step + self.Y, self.Y)

    def device(self, z, y, c):
        return (self.s, (z * self.Y + y) * 2 + c)

    def z_near(self):
        return self.z + 1 - 2 * (self.z % 2)

    def z_far(self):
        return lax.rem(self.z + 2, 4)

    def partners(self):
        found = [self.device(self.along_z(k), self.y, self.c) for k in range(1, self.Z)]
        found += [self.device(self.z, self.along_y(k), self.c) for k in range(1, self.Y)]
        return found + [self.device(self.z, self.y, 1 - self.c), (1 - self.s, self.d)]


def greet(devices):
    barrier = pltpu.get_barrier_semaphore()
    for device in devices:
        pl.semaphore_signal(barrier, inc=1, device_id=device, device_id_type=MESH)
    pl.semaphore_wait(barrier, len(devices))


def remote(src, dst, send, recv, device):
    return pltpu.make_async_remote_copy(
        src_ref=src, dst_ref=dst, send_sem=send, recv_sem=recv, device_id=device, device_id_type=MESH
    )


def arrival(ref, sem):
    return pltpu.make_async_copy(ref, ref, sem)


def gather_kernel(n, crossed, *refs):
    count = len(crossed)
    sources, outs = refs[:count], refs[count : 2 * count]
    z_sem, y_sem, c_sem, s_sem, l_sem, x_sem, xs_sem = refs[2 * count :]
    at = Place(n)
    Z, Y = at.Z, at.Y
    greet(at.partners())

    x_copies = []
    for item in range(count):
        if crossed[item]:
            copy = remote(
                sources[item],
                outs[item].at[at.s, at.zy, at.c],
                xs_sem.at[item],
                x_sem.at[item],
                (1 - at.s, at.d),
            )
            copy.start()
            x_copies.append(copy)

    units = []
    for item in range(count):
        if crossed[item]:
            units.append((item, outs[item].at[at.s], sources[item]))
        else:
            units.append((item, outs[item], sources[item]))
    own = len(units)
    for item in range(count):
        if crossed[item]:
            gathered = outs[item].at[1 - at.s]
            units.append((item, gathered, gathered.at[at.zy, at.c]))

    def spread(u, src, zy, z_slot, to_z, to_y):
        gathered = units[u][1]
        dst = gathered.at[zy, at.c]
        if to_z:
            for k in range(1, Z):
                remote(
                    src, dst, s_sem.at[u], z_sem.at[u, k - 1], at.device(at.along_z(k), at.y, at.c)
                ).start()
        if to_y:
            for k in range(1, Y):
                remote(
                    src,
                    dst,
                    s_sem.at[u],
                    y_sem.at[u, z_slot * (Y - 1) + k - 1],
                    at.device(at.z, at.along_y(k), at.c),
                ).start()
        remote(src, dst, s_sem.at[u], c_sem.at[u], at.device(at.z, at.y, 1 - at.c)).start()

    for u, (item, gathered, src) in enumerate(units):
        if u < own:
            pltpu.make_async_copy(src, gathered.at[at.zy, at.c], l_sem.at[u]).start()
        else:
            arrival(src, x_sem.at[item]).wait()
        spread(u, src, at.zy, 0, True, True)
    for u, (item, gathered, _) in enumerate(units):
        for k in range(1, Z):
            zy = at.along_z(-k) * Y + at.y
            block = gathered.at[zy, at.c]
            arrival(block, z_sem.at[u, k - 1]).wait()
            spread(u, block, zy, k, False, True)
        for slot in range(Z):
            for k in range(1, Y):
                zy = at.along_z(-slot) * Y + at.along_y(-k)
                block = gathered.at[zy, at.c]
                arrival(block, y_sem.at[u, slot * (Y - 1) + k - 1]).wait()
                spread(u, block, zy, 0, False, False)
    for u, (item, gathered, src) in enumerate(units):
        if u < own:
            pltpu.make_async_copy(src, gathered.at[at.zy, at.c], l_sem.at[u]).wait()
        theirs = gathered.at[:, 1 - at.c]
        arrival(theirs, c_sem.at[u]).wait()
        most = gathered.at[pl.ds(0, Z * Y - 1)]
        arrival(most, s_sem.at[u]).wait()
        arrival(gathered.at[0, 0], s_sem.at[u]).wait()
    for copy in x_copies:
        copy.wait_send()


def gather(n, arrays, crossed):
    Z, Y = factors(n)
    shapes = []
    for array, over_section in zip(arrays, crossed):
        lead = (2, Z * Y, 2) if over_section else (Z * Y, 2)
        shapes.append(jax.ShapeDtypeStruct(lead + array.shape, array.dtype))
    units = len(arrays) + sum(crossed)
    dma = pltpu.SemaphoreType.DMA
    return pl.pallas_call(
        functools.partial(gather_kernel, n, crossed),
        out_shape=shapes,
        in_specs=[ANY] * len(arrays),
        out_specs=[ANY] * len(arrays),
        scratch_shapes=[
            dma((units, max(Z - 1, 1))),
            dma((units, max(Z * (Y - 1), 1))),
            dma((units,)),
            dma((units,)),
            dma((units,)),
            dma((len(arrays),)),
            dma((len(arrays),)),
        ],
        compiler_params=pltpu.CompilerParams(collective_id=0, has_side_effects=True),
    )(*arrays)


def add_blocks(rows, terms, out, out_type):
    chunk = 16 if rows % 16 == 0 else rows

    def body(i, _):
        part = pl.ds(pl.multiple_of(i * chunk, chunk), chunk)
        total = terms[0][part, :].astype(f32)
        for term in terms[1:]:
            total = total + term[part, :].astype(f32)
        out[part, :] = total.astype(out_type)
        return _

    lax.fori_loop(0, rows // chunk, body, 0)


def scatter_kernel(n, count, *refs):
    sources, outs = refs[:count], refs[count : 2 * count]
    scratch = refs[2 * count :]
    mine, from_c, from_y, from_z = (scratch[k * count : (k + 1) * count] for k in range(4))
    l_sem, cs_sem, cr_sem, ys_sem, yr_sem, zs_sem, zr_sem = scratch[4 * count :]
    at = Place(n)
    Z, Y = at.Z, at.Y
    greet(at.partners()[:-1])

    c_copies, l_copies, y_copies, z_copies = [], [], [], []
    for i in range(count):
        copy = remote(
            sources[i].at[:, 1 - at.c],
            from_c[i],
            cs_sem.at[i],
            cr_sem.at[i],
            at.device(at.z, at.y, 1 - at.c),
        )
        copy.start()
        c_copies.append(copy)
        copy = pltpu.make_async_copy(sources[i].at[:, at.c], mine[i], l_sem.at[i])
        copy.start()
        l_copies.append(copy)

    def after_core(i):
        c_copies[i].wait_recv()
        l_copies[i].wait()
        rows = mine[i].shape[1]
        for k in list(range(1, Y)) + [0]:
            y = at.along_y(k)

            def per_z(z, _):
                zy = z * Y + y
                add_blocks(rows, [mine[i].at[zy], from_c[i].at[zy]], mine[i].at[zy], mine[i].dtype)
                return _

            lax.fori_loop(0, Z, per_z, 0)
            if k:
                for z in range(Z):
                    copy = remote(
                        mine[i].at[z * Y + y],
                        from_y[i].at[k - 1, z],
                        ys_sem.at[i, k - 1, z],
                        yr_sem.at[i, k - 1, z],
                        at.device(at.z, y, at.c),
                    )
                    copy.start()
                    y_copies.append(copy)

    def after_y(i):
        rows = mine[i].shape[1]
        for k in list(range(1, Z)) + [0]:
            z = at.along_z(k)
            block = mine[i].at[z * Y + at.y]
            for j in range(1, Y):
                arrival(from_y[i].at[j - 1, z], yr_sem.at[i, j - 1, z]).wait()
            terms = [block] + [from_y[i].at[j - 1, z] for j in range(1, Y)]
            add_blocks(rows, terms, block, mine[i].dtype)
            if k:
                copy = remote(
                    block,
                    from_z[i].at[k - 1],
                    zs_sem.at[i, k - 1],
                    zr_sem.at[i, k - 1],
                    at.device(z, at.y, at.c),
                )
                copy.start()
                z_copies.append(copy)

    def after_z(i):
        rows = mine[i].shape[1]
        for k in range(1, Z):
            arrival(from_z[i].at[k - 1], zr_sem.at[i, k - 1]).wait()
        terms = [mine[i].at[at.zy]] + [from_z[i].at[k - 1] for k in range(1, Z)]
        add_blocks(rows, terms, outs[i], outs[i].dtype)

    for turn in range(count + 2):
        if turn < count:
            after_core(turn)
        if 0 <= turn - 1 < count:
            after_y(turn - 1)
        if turn - 2 >= 0:
            after_z(turn - 2)
    for copy in c_copies + y_copies + z_copies:
        copy.wait_send()


def scatter(n, arrays, collective_id):
    Z, Y = factors(n)
    count = len(arrays)
    blocks = [a.shape[-2:] for a in arrays]
    arrays = [a.reshape((Z * Y, 2) + b) for a, b in zip(arrays, blocks)]
    dma = pltpu.SemaphoreType.DMA
    scratch = [pltpu.VMEM((Z * Y,) + b, a.dtype) for a, b in zip(arrays, blocks)]
    scratch += [pltpu.VMEM((Z * Y,) + b, a.dtype) for a, b in zip(arrays, blocks)]
    scratch += [pltpu.VMEM((max(Y - 1, 1), Z) + b, a.dtype) for a, b in zip(arrays, blocks)]
    scratch += [pltpu.VMEM((max(Z - 1, 1),) + b, a.dtype) for a, b in zip(arrays, blocks)]
    return pl.pallas_call(
        functools.partial(scatter_kernel, n, count),
        out_shape=[jax.ShapeDtypeStruct(b, f32) for b in blocks],
        in_specs=[ANY] * count,
        out_specs=[VMEM] * count,
        scratch_shapes=scratch
        + [
            dma((count,)),
            dma((count,)),
            dma((count,)),
            dma((count, max(Y - 1, 1), Z)),
            dma((count, max(Y - 1, 1), Z)),
            dma((count, max(Z - 1, 1))),
            dma((count, max(Z - 1, 1))),
        ],
        compiler_params=pltpu.CompilerParams(
            collective_id=collective_id, has_side_effects=True, vmem_limit_bytes=VMEM_LIMIT
        ),
    )(*arrays)


def scan_kernel(emb, wi, wr, ctx, keep, z_o, r_o, n_o, m_o, p_o, h_o, drive):
    R, H = ctx.shape[0], wr.shape[0]
    drive[...] = nt(emb[...], wi[...])

    def step(t, h):
        rows = pl.ds(pl.multiple_of(t * R, R), R)
        p = h * keep[rows, :]
        p_o[rows, :] = p
        rec = nn(p.astype(bf16), wr[...])
        d = drive[rows, :]
        z = jax.nn.sigmoid(d[:, :H] + rec[:, :H] + ctx[:, :H])
        r = jax.nn.sigmoid(d[:, H : 2 * H] + rec[:, H : 2 * H] + ctx[:, H : 2 * H])
        m = rec[:, 2 * H :] + ctx[:, 2 * H :]
        n = jnp.tanh(d[:, 2 * H :] + r * m)
        h = z * p + (1.0 - z) * n
        z_o[rows, :] = z
        r_o[rows, :] = r
        n_o[rows, :] = n
        m_o[rows, :] = m
        h_o[rows, :] = h.astype(bf16)
        return h

    lax.fori_loop(0, emb.shape[0] // R, step, jnp.zeros((R, H), f32))


def gru_forward(emb, wi, wr, ctx, keep):
    tokens, H = emb.shape[0], wr.shape[0]
    shape = jax.ShapeDtypeStruct
    return pl.pallas_call(
        scan_kernel,
        out_shape=[shape((tokens, H), f32)] * 5 + [shape((tokens, H), bf16)],
        in_specs=[VMEM] * 5,
        out_specs=[VMEM] * 6,
        scratch_shapes=[pltpu.VMEM((tokens, 3 * H), f32)],
        compiler_params=pltpu.CompilerParams(vmem_limit_bytes=VMEM_LIMIT),
    )(emb, wi, wr, ctx, keep)


def backward_kernel(sg, carry0, keep, z, r, n, m, p, wr, low_o, cand_o, sum_o):
    R, H = carry0.shape
    steps = sg.shape[0] // R

    def step(i, carry):
        rows = pl.ds(pl.multiple_of((steps - 1 - i) * R, R), R)
        g = sg[rows, :] + carry
        zz = z[rows, :]
        cand = n[rows, :]
        rr = r[rows, :]
        pc = g * (1.0 - zz) * (1.0 - cand * cand)
        pz = g * (p[rows, :] - cand) * zz * (1.0 - zz)
        pr = pc * m[rows, :] * rr * (1.0 - rr)
        rec = jnp.concatenate([pz, pr, pc * rr], axis=1)
        low = rec.astype(bf16)
        low_o[rows, :] = low
        cand_o[rows, :] = pc.astype(bf16)
        sum_o[...] += rec
        return (g * zz + nt(low, wr[...])) * keep[rows, :]

    sum_o[...] = jnp.zeros_like(sum_o)
    lax.fori_loop(0, steps, step, carry0[...])


def gru_backward(sg, carry0, keep, record, wr):
    z, r, n, m, p = record
    tokens, H = sg.shape
    shape = jax.ShapeDtypeStruct
    return pl.pallas_call(
        backward_kernel,
        out_shape=[
            shape((tokens, 3 * H), bf16),
            shape((tokens, H), bf16),
            shape((carry0.shape[0], 3 * H), f32),
        ],
        in_specs=[VMEM] * 9,
        out_specs=[VMEM] * 3,
        compiler_params=pltpu.CompilerParams(vmem_limit_bytes=VMEM_LIMIT),
    )(sg, carry0, keep, z, r, n, m, p, wr)


def finish_kernel(count, *refs):
    loss_in, loss_out = refs[0], refs[count]
    sources, outs, held = refs[1:count], refs[count + 1 : 2 * count], refs[2 * count : 3 * count - 1]
    in_sem, out_sem = refs[-2:]
    ins = [pltpu.make_async_copy(a, b, in_sem.at[k]) for k, (a, b) in enumerate(zip(sources, held))]
    puts = [pltpu.make_async_copy(a, b, out_sem.at[k]) for k, (a, b) in enumerate(zip(held, outs))]
    for copy in ins:
        copy.start()
    loss_out[0, 0] = jnp.max(loss_in[...])
    for copy, put in zip(ins, puts):
        copy.wait()
        put.start()
    for put in puts:
        put.wait()


def finish(loss, *arrays):
    shape = jax.ShapeDtypeStruct
    count = len(arrays)
    return pl.pallas_call(
        functools.partial(finish_kernel, count + 1),
        out_shape=[shape((1, 1), f32)] + [shape(a.shape, a.dtype) for a in arrays],
        in_specs=[VMEM] + [ANY] * count,
        out_specs=[pl.BlockSpec(memory_space=pltpu.SMEM)] + [ANY] * count,
        scratch_shapes=[pltpu.VMEM(a.shape, a.dtype) for a in arrays]
        + [pltpu.SemaphoreType.DMA((count,))] * 2,
        compiler_params=pltpu.CompilerParams(vmem_limit_bytes=16 * 2**20),
    )(loss, *arrays)


def request_slots(ids, n, per, slots):
    count = ids.shape[0]
    index = jnp.arange(count, dtype=jnp.int32)
    same = ids[:, None] == ids[None, :]
    first = jnp.min(jnp.where(same, index[None, :], count), axis=1)
    leads = first == index
    owner = ids // per
    ahead = (owner[:, None] == owner[None, :]) & leads[None, :] & (index[None, :] < first[:, None])
    rank = jnp.sum(ahead.astype(jnp.int32), axis=1)
    return leads, owner, rank, ids - owner * per


def round_maps(plan, turn, n, slots):
    leads, owner, rank, local = plan
    place = rank - turn * slots
    inside = (place >= 0) & (place < slots)
    place = jnp.where(inside, owner * slots + place, -1)
    hit = place[:, None] == jnp.arange(n * slots, dtype=jnp.int32)[None, :]
    asked = jnp.max(jnp.where(hit & leads[:, None], local[:, None], -1), axis=0)
    return asked, hit.astype(bf16)


def swap(x, n):
    shape = x.shape
    return lax.all_to_all(x.reshape((n, -1) + shape[1:]), "dp", 0, 0, tiled=False).reshape(shape)


def owner_map(asked, n, per):
    asked_here = swap(asked, n)
    return (asked_here[:, None] == jnp.arange(per, dtype=jnp.int32)[None, :]).astype(bf16)


def multiple(x, of):
    return pl.multiple_of(x, of)


class Unit:
    def __init__(self, index, src, dst, rows, base, y_first=False, stride=None):
        self.index, self.src, self.dst, self.rows, self.base = index, src, dst, rows, base
        self.y_first, self.stride = y_first, stride or rows

    def block(self, zy, c):
        return self.dst.at[pl.ds(multiple(self.base + (zy * 2 + c) * self.stride, 16), self.rows)]

    def some(self, count):
        return self.dst.at[pl.ds(0, count * self.rows)]


class Gather:
    def __init__(self, at, z_sem, y_sem, c_sem, s_sem):
        self.at, self.z_sem, self.y_sem, self.c_sem, self.s_sem = at, z_sem, y_sem, c_sem, s_sem

    def to_z(self, u, src, dst, z, slot):
        at = self.at
        remote(
            src,
            dst,
            self.s_sem.at[u.index],
            self.z_sem.at[u.index, slot],
            at.device(z, at.y, at.c),
        ).start()

    def to_y(self, u, src, dst, z):
        at = self.at
        remote(
            src,
            dst,
            self.s_sem.at[u.index],
            self.y_sem.at[u.index, z],
            at.device(at.z, at.along_y(1), at.c),
        ).start()

    def to_core(self, u, src, dst):
        at = self.at
        remote(
            src, dst, self.s_sem.at[u.index], self.c_sem.at[u.index], at.device(at.z, at.y, 1 - at.c)
        ).start()

    def begin(self, u):
        at = self.at
        dst = u.block(at.zy, at.c)
        if not u.y_first:
            self.to_z(u, u.src, dst, at.z_far(), 0)
        self.to_y(u, u.src, dst, at.z)
        self.to_core(u, u.src, dst)

    def by_z(self, u, z, y, slot):
        at = self.at
        block = u.block(z * at.Y + y, at.c)
        arrival(block, self.z_sem.at[u.index, slot]).wait()
        return block

    def by_y(self, u, z):
        at = self.at
        block = u.block(z * at.Y + at.along_y(1), at.c)
        arrival(block, self.y_sem.at[u.index, z]).wait()
        return block

    def step1(self, u):
        at = self.at
        far, near = at.z_far(), at.z_near()
        if u.y_first:
            self.to_z(u, u.src, u.block(at.zy, at.c), far, 0)
            block = self.by_y(u, at.z)
            self.to_z(u, block, block, far, 1)
            self.to_core(u, block, block)
            return
        self.to_z(u, u.src, u.block(at.zy, at.c), near, 1)
        block = self.by_z(u, far, at.y, 0)
        self.to_z(u, block, block, near, 2)
        self.to_y(u, block, block, far)
        self.to_core(u, block, block)

    def step2(self, u):
        at = self.at
        far, near = at.z_far(), at.z_near()
        other = at.along_y(1)
        if u.y_first:
            self.to_z(u, u.src, u.block(at.zy, at.c), near, 2)
            block = u.block(at.z * at.Y + other, at.c)
            self.to_z(u, block, block, near, 3)
            for slot, y in ((0, at.y), (1, other)):
                block = self.by_z(u, far, y, slot)
                self.to_z(u, block, block, near, 4 + slot)
                self.to_core(u, block, block)
            return
        for slot, z in ((1, near), (2, lax.rem(near + 2, 4))):
            block = self.by_z(u, z, at.y, slot)
            self.to_y(u, block, block, z)
            self.to_core(u, block, block)

    def step3(self, u):
        at = self.at
        far, near = at.z_far(), at.z_near()
        next_far = lax.rem(near + 2, 4)
        if u.y_first:
            other = at.along_y(1)
            for slot, z, y in (
                (2, near, at.y),
                (3, near, other),
                (4, next_far, at.y),
                (5, next_far, other),
            ):
                block = self.by_z(u, z, y, slot)
                self.to_core(u, block, block)
            return
        for z in (at.z, far, near, next_far):
            block = self.by_y(u, z)
            self.to_core(u, block, block)

    def ready(self, u):
        part = u.some(self.at.Z * self.at.Y)
        arrival(part, self.c_sem.at[u.index]).wait()

    def drain(self, u):
        part = u.some(2 * self.at.Z * self.at.Y - 1)
        arrival(part, self.s_sem.at[u.index]).wait()


class Chain(Gather):
    def on(self, u, src, dst, up, hops):
        at = self.at
        slot = hops - 1 if up else at.Z - 1 + hops - 1

        @pl.when(at.z < at.Z - 1 if up else at.z > 0)
        def _():
            remote(
                src,
                dst,
                self.on_sem.at[u.index],
                self.z_sem.at[u.index, slot],
                at.device(at.z + (1 if up else -1), at.y, at.c),
            ).start()

    def begin(self, u):
        at = self.at
        dst = u.block(at.zy, at.c)
        self.on(u, u.src, dst, True, 1)
        self.on(u, u.src, dst, False, 1)
        self.to_y(u, u.src, dst, at.z)
        self.to_core(u, u.src, dst)

    def pass_z(self, u, k):
        at = self.at
        for up in (True, False):
            z = at.z - k if up else at.z + k

            @pl.when(z >= 0 if up else z < at.Z)
            def _():
                slot = k - 1 if up else at.Z - 1 + k - 1
                block = self.by_z(u, z, at.y, slot)
                if k + 1 < at.Z:
                    self.on(u, block, block, up, k + 1)
                self.to_y(u, block, block, z)
                self.to_core(u, block, block)

    def drain(self, u):
        at = self.at
        part = u.some(2 * at.Z * at.Y - at.Z)
        arrival(part, self.s_sem.at[u.index]).wait()
        for z in range(at.Z):
            sent = (z + 1 if z < at.Z - 1 else 0) + (at.Z - z if z > 0 else 0)

            @pl.when(at.z == z)
            def _():
                part = u.some(sent)
                arrival(part, self.on_sem.at[u.index]).wait()


def forward_kernel(n, sizes, *refs):
    R, H, E, M, slots, per, words = sizes
    (
        asked,
        hit,
        table,
        keep,
        labels,
        wr_s,
        wi_s,
        sq_s,
        sm_s,
        cg_s,
        de_s,
        dc_s,
    ) = refs[:12]
    (
        wr_o,
        wi_o,
        sq_o,
        cg_o,
        de_o,
        dc_o,
        term_o,
        rec_o,
        h_h,
        emb_h,
        pre_h,
        tanh_h,
        ctx_h,
        owners_h,
        grad_o,
        loss_o,
        most_o,
    ) = refs[12:29]
    (
        asked_in,
        rows_out,
        came,
        wr,
        wi,
        sq,
        sm,
        cg,
        de,
        dc,
        drive,
        rec,
        wrt,
        smooth_in,
        grad_out,
        m_part,
        s_part,
        p_part,
        fullest,
        outer,
        h_o,
        emb_o,
        pre_o,
        tanh_o,
        ctx_o,
        owners_o,
        z_sem,
        y_sem,
        c_sem,
        s_sem,
        l_sem,
        o_sem,
        x_recv,
        x_send,
        as_sem,
        ar_sem,
        rs_sem,
        rr_sem,
        t_send,
        t_recv,
        k_sem,
        on_sem,
    ) = refs[29:]
    at = Place(n)
    tokens = hit.shape[0]
    steps = tokens // R
    is_decoder = at.s == 1
    beside = (1 - at.s, at.d)
    others = [lax.rem(at.d + k, n) for k in range(1, n)]
    greet([(at.s, d) for d in others] + [beside])

    def block_rows(ref, base, rows):
        return ref.at[pl.ds(multiple((base + at.d) * rows, 16), rows)]

    def to_beside(src, dst, k):
        return remote(src, dst, x_send.at[k], x_recv.at[k], beside)

    gather = Gather(at, z_sem, y_sem, c_sem, s_sem)
    chain = Chain(at, z_sem, y_sem, c_sem, s_sem)
    chain.on_sem = on_sem
    u_wi = Unit(1, wi_s, wi, wi_s.shape[0], 0)
    u_wr = Unit(0, wr_s, wr, wr_s.shape[0], 0)
    u_sq = Unit(2, sq_s, sq, sq_s.shape[0], 0)
    own_sm = Unit(3, sm_s, sm, words, 0)
    far_sm = Unit(4, block_rows(sm, n, words), sm, words, n * words)
    crossed = []
    for k, (src, dst) in enumerate([(cg_s, cg), (de_s, de)]):
        rows = src.shape[0]
        crossed.append(
            (
                Unit(3 + 2 * k, src, dst, rows, n * rows),
                Unit(4 + 2 * k, block_rows(dst, 0, rows), dst, rows, 0, k == 0),
            )
        )
    rows = cg_s.shape[0]
    far_block = block_rows(cg, 0, rows)
    cg_halves = [
        Unit(index, far_block.at[pl.ds(k * 16, 16)], cg, 16, k * 16, k == 0, rows)
        for k, index in enumerate((4, 7))
    ]
    rows = dc_s.shape[0]
    own_dc = Unit(5, dc_s, dc, rows, 0)
    far_dc = Unit(6, block_rows(dc, n, rows), dc, rows, n * rows)

    for d in others:
        remote(asked.at[d], asked_in.at[at.d], as_sem, ar_sem, (at.s, d)).start()
    some_asked = asked_in.at[pl.ds(0, n - 1)]
    arrival(some_asked, ar_sem).wait()
    chain.begin(u_wi)
    chain.begin(u_wr)

    @pl.when(is_decoder)
    def _():
        to_beside(dc_s, block_rows(dc, n, dc_s.shape[0]), 3).start()
        to_beside(sm_s, block_rows(sm, n, words), 0).start()

    @pl.when(jnp.logical_not(is_decoder))
    def _():
        for k, (src, dst) in enumerate([(cg_s, cg), (de_s, de)]):
            to_beside(src, block_rows(dst, 0, src.shape[0]), 1 + k).start()

    locals_ = [
        pltpu.make_async_copy(src, block_rows(dst, 0, src.shape[0]), l_sem.at[k])
        for k, (src, dst) in enumerate([(wr_s, wr), (wi_s, wi), (sq_s, sq)])
    ]
    locals_.append(pltpu.make_async_copy(sm_s, block_rows(sm, 0, words), l_sem.at[3]))
    for k, (src, dst) in enumerate([(cg_s, cg), (de_s, de)]):
        locals_.append(pltpu.make_async_copy(src, block_rows(dst, n, src.shape[0]), l_sem.at[4 + k]))
    locals_.append(pltpu.make_async_copy(dc_s, block_rows(dc, 0, dc_s.shape[0]), l_sem.at[6]))
    for copy in locals_:
        copy.start()

    asked_in[at.d] = asked[at.d]
    group = 128 // slots
    count = lax.broadcasted_iota(jnp.int32, (per, 128), 0)
    most = asked_in[0, 1:2, :]
    for g in range(n // group):
        wanted = asked_in[g * group, 0:1, :]
        for j in range(1, group):
            wanted = jnp.maximum(wanted, asked_in[g * group + j, 0:1, :])
        for j in range(group):
            most = jnp.maximum(most, asked_in[g * group + j, 1:2, :])
        match = (wanted == count).astype(f32).astype(bf16)
        owners_o[:, pl.ds(g * 128, 128)] = match
        rows_out[pl.ds(g * 128, 128), :] = tn(match, table[...]).astype(bf16)
    fullest[0] = jnp.broadcast_to(most, fullest.shape[1:])
    to_beside(fullest.at[0], fullest.at[1], 7).start()

    def slot_rows(ref, d):
        return ref.at[pl.ds(multiple(d * slots, 16), slots)]

    for d in others:
        remote(slot_rows(rows_out, d), slot_rows(came, at.d), rs_sem, rr_sem, (at.s, d)).start()
    cg_own = crossed[0][0]
    far_a, far_b = cg_halves
    de_own, de_far = crossed[1]
    for k in (1, 2, 3):
        if k == 2:

            @pl.when(is_decoder)
            def _():
                arrival(far_block, x_recv.at[1]).wait()
                gather.begin(far_a)

        chain.pass_z(u_wi, k)
        chain.pass_z(u_wr, k)

    @pl.when(is_decoder)
    def _():
        gather.begin(cg_own)
        gather.step1(far_a)
        gather.begin(far_b)

    @pl.when(jnp.logical_not(is_decoder))
    def _():
        gather.begin(u_sq)

    gather.step3(u_wi)
    some_rows = came.at[pl.ds(0, (n - 1) * slots)]
    arrival(some_rows, rr_sem).wait()
    came[pl.ds(multiple(at.d * slots, 16), slots), :] = rows_out[
        pl.ds(multiple(at.d * slots, 16), slots), :
    ]
    emb_o[...] = nn(hit[...], came[...]).astype(bf16)
    to_beside(fullest.at[0], fullest.at[1], 7).wait()
    rank = jnp.max(jnp.maximum(fullest[0], fullest[1]))
    most_o[0, 0] = jnp.where(rank >= slots, 1, 0)
    for copy in locals_:
        copy.wait()
    chain.ready(u_wi)

    @pl.when(is_decoder)
    def _():
        gather.step1(cg_own)
        gather.step2(far_a)
        gather.step1(far_b)

    def input_drive(i, _):
        cols = pl.ds(multiple(i * 512, 512), 512)
        drive[:, cols] = nt(emb_o[...], wi[cols, :])
        return _

    lax.fori_loop(0, 3 * H // 512, input_drive, 0)
    gather.step3(u_wr)
    chain.ready(u_wr)

    def scan(ctx, service):
        def step(t, h):
            rows = pl.ds(multiple(t * R, R), R)
            p = h * keep[rows, :]
            rec[t, 4] = p
            mix = nn(p.astype(bf16), wr[...])
            d = drive[rows, :]
            z_in = d[:, :H] + mix[:, :H]
            r_in = d[:, H : 2 * H] + mix[:, H : 2 * H]
            m = mix[:, 2 * H :]
            if ctx is not None:
                z_in += ctx[:, :H]
                r_in += ctx[:, H : 2 * H]
                m += ctx[:, 2 * H :]
            z = jax.nn.sigmoid(z_in)
            r = jax.nn.sigmoid(r_in)
            cand = jnp.tanh(d[:, 2 * H :] + r * m)
            h = z * p + (1.0 - z) * cand
            rec[t, 0] = z
            rec[t, 1] = r
            rec[t, 2] = cand
            rec[t, 3] = m
            h_o[rows, :] = h.astype(bf16)
            for when, what in service:
                pl.when(t == when)(what)
            return h

        return lax.fori_loop(0, steps, step, jnp.zeros((R, H), f32))

    def keep_input_gates():
        copy = pltpu.make_async_copy(wi, wi_o, o_sem.at[0])
        copy.start()
        return copy

    def keep_transposed():
        def turn(i, _):
            part = pl.ds(multiple(i * 128, 128), 128)
            wrt[:, part] = wr[part, :].T
            return _

        lax.fori_loop(0, H // 128, turn, 0)
        copy = pltpu.make_async_copy(wrt, wr_o, o_sem.at[1])
        copy.start()
        return copy

    def keep_small(pairs):
        copies = [pltpu.make_async_copy(a, b, k_sem.at[k]) for k, a, b in pairs]
        for copy in copies:
            copy.start()
        return copies

    def end_requests(units):
        arrival(some_asked, as_sem).wait()
        arrival(some_rows, rs_sem).wait()
        for u in (u_wi, u_wr):
            chain.drain(u)
        for u in units:
            gather.drain(u)

    last = pl.ds((steps - 1) * R, R)

    @pl.when(jnp.logical_not(is_decoder))
    def _():
        copies = [keep_input_gates()] + keep_small([(0, emb_o, emb_h), (1, owners_o, owners_h)])
        wide = (own_dc, far_dc, own_sm, far_sm)

        def begin_dc():
            gather.begin(own_dc)
            arrival(far_dc.src, x_recv.at[3]).wait()
            gather.begin(far_dc)

        def begin_far_sm():
            gather.step1(own_sm)
            arrival(far_sm.src, x_recv.at[0]).wait()
            gather.begin(far_sm)

        scan(
            None,
            [
                (1, lambda: gather.begin(own_sm)),
                (4, lambda: gather.step1(u_sq)),
                (6, lambda: gather.step2(u_sq)),
                (8, begin_dc),
                (10, begin_far_sm),
            ],
        )
        gather.step3(u_sq)
        gather.ready(u_sq)
        ctx_tanh = jnp.tanh(nn(h_o[last, :], sq[...]))
        tanh_o[...] = ctx_tanh
        ctx_o[...] = ctx_tanh.astype(bf16)
        sends = [to_beside(ctx_o, ctx_o, 4)]
        sends[0].start()
        copies += [
            pltpu.make_async_copy(rec, rec_o, o_sem.at[2]),
            pltpu.make_async_copy(sq, sq_o, o_sem.at[3]),
        ]
        for copy in copies[-2:]:
            copy.start()
        copies += keep_small([(2, h_o, h_h), (3, tanh_o, tanh_h), (4, ctx_o, ctx_h)])
        for u in wide[:2]:
            gather.step1(u)
        gather.step2(own_sm)
        gather.step1(far_sm)
        for u in wide[:2]:
            gather.step2(u)
        gather.step2(far_sm)
        for u in wide[:2]:
            gather.step3(u)
        for u in wide[:2]:
            gather.ready(u)
        outer[...] = nn(ctx_o[...], dc[...])
        sends.append(to_beside(outer, outer, 8))
        sends[1].start()
        copies.append(pltpu.make_async_copy(dc, dc_o, o_sem.at[5]))
        copies[-1].start()
        copies.append(keep_transposed())
        for u in wide[2:]:
            gather.step3(u)
        for u in wide[2:]:
            gather.ready(u)
        for send in sends:
            send.wait_send()
        for k, (src, dst) in enumerate([(cg_s, cg), (de_s, de)]):
            to_beside(src, block_rows(dst, 0, src.shape[0]), 1 + k).wait_send()
        end_requests((u_sq,) + wide)

        half = n * words
        ZY = at.Z * at.Y
        across = cg.shape[1] // M
        landed = cg.at[pl.ds(0, half // 4), pl.ds(0, 2 * M)]

        def term_block(j, zy, c):
            return sm.at[pl.ds(multiple((j * n + zy * 2 + c) * words, 16), words)]

        def landing(j, zy):
            place = j * ZY + zy
            rows = pl.ds(multiple(place // across * words, 16), words)
            return cg.at[rows, pl.ds(multiple(place % across * M, 128), M)]

        def core_send(j):
            for zy in range(ZY):
                remote(
                    term_block(j, zy, 1 - at.c),
                    landing(j, zy),
                    t_send.at[j],
                    t_recv.at[j],
                    at.device(at.z, at.y, 1 - at.c),
                ).start()

        arrival(smooth_in, x_recv.at[5]).wait()
        tile = half // 5 if half % 640 == 0 else 512
        lanes = lax.broadcasted_iota(jnp.int32, (tokens, 128), 1)
        m_part[...] = jnp.full(m_part.shape, -jnp.inf, f32)
        s_part[...] = jnp.zeros_like(s_part)
        p_part[...] = jnp.zeros_like(p_part)

        def tops(i, _):
            rows = pl.ds(multiple(i * tile, tile), tile)
            logits = nt(smooth_in[...], sm[rows, :])
            parts = [logits[:, k * 128 : (k + 1) * 128] for k in range(tile // 128)]
            before = m_part[...]
            top = before
            for part in parts:
                top = jnp.maximum(top, part)
            total = s_part[...] * jnp.exp(before - top)
            picked = p_part[...]
            for k, part in enumerate(parts):
                total += jnp.exp(part - top)
                picked += jnp.where(lanes == labels[...] - (i * tile + k * 128), part, 0.0)
            m_part[...] = top
            s_part[...] = total
            p_part[...] = picked
            return _

        lax.fori_loop(0, 2 * n * words // tile, tops, 0)
        top = jnp.max(m_part[...], axis=1, keepdims=True)
        total = jnp.sum(s_part[...] * jnp.exp(m_part[...] - top), axis=1, keepdims=True)
        log_norm = top + jnp.log(total)
        picked = jnp.sum(p_part[...], axis=1, keepdims=True)
        scale = 1.0 / (R * n)
        loss = jnp.sum(log_norm - picked, axis=0, keepdims=True) * scale
        loss_o[...] = jnp.broadcast_to(loss, loss_o.shape)
        m_part[...] = jnp.broadcast_to(log_norm, m_part.shape)
        drive[:, pl.ds(0, M)] = jnp.zeros((tokens, M), f32)

        def grads(i, _):
            rows = pl.ds(multiple(i * tile, tile), tile)
            weight = sm[rows, :]
            logits = nt(smooth_in[...], weight)
            low = []
            for k in range(tile // 128):
                part = jnp.exp(logits[:, k * 128 : (k + 1) * 128] - m_part[...])
                hits = lanes == labels[...] - (i * tile + k * 128)
                low.append(((part - jnp.where(hits, 1.0, 0.0)) * scale).astype(bf16))
            low = jnp.concatenate(low, axis=1)
            drive[:, pl.ds(0, M)] += nn(low, weight)
            sm[rows, :] = tn(low, smooth_in[...]).astype(bf16)
            pl.when(i == half // tile)(lambda: core_send(0))
            return _

        lax.fori_loop(0, 2 * n * words // tile, grads, 0)
        grad_out[...] = drive[:, pl.ds(0, M)].astype(bf16)
        send = to_beside(grad_out, grad_o, 6)
        send.start()
        core_send(1)
        for j in (0, 1):
            arrival(landed, t_recv.at[j]).wait()

            def add(zy, _):
                block = term_block(j, zy, at.c)
                add_blocks(words, [block, landing(j, zy)], block, bf16)
                pltpu.make_async_copy(block, term_o.at[j, zy], o_sem.at[4]).start()
                return _

            lax.fori_loop(0, ZY, add, 0)
        for j in (0, 1):
            arrival(landed, t_send.at[j]).wait()
        arrival(term_o, o_sem.at[4]).wait()
        send.wait_send()
        for copy in copies:
            copy.wait()

    @pl.when(is_decoder)
    def _():
        copies = [keep_input_gates()] + keep_small([(0, emb_o, emb_h), (1, owners_o, owners_h)])
        gather.step2(cg_own)
        gather.step2(far_b)
        gather.begin(u_sq)
        gather.begin(de_own)
        arrival(de_far.src, x_recv.at[2]).wait()
        gather.begin(de_far)
        gather.step3(cg_own)
        gather.step3(far_a)
        gather.step3(far_b)
        for u in (cg_own, far_a, far_b):
            gather.ready(u)
        copies.append(pltpu.make_async_copy(cg, cg_o, o_sem.at[2]))
        copies[-1].start()
        arrival(ctx_o, x_recv.at[4]).wait()
        rest = [de_own, de_far]
        service = [
            (3, functools.partial(gather.step1, u_sq)),
            (5, functools.partial(gather.step1, de_own)),
            (6, functools.partial(gather.step1, de_far)),
            (8, functools.partial(gather.step2, u_sq)),
            (10, functools.partial(gather.step2, de_own)),
            (11, functools.partial(gather.step2, de_far)),
        ]
        ctx = nn(ctx_o[...], cg[...])
        scan(ctx, service)
        for u in [u_sq] + rest:
            gather.step3(u)
        for u in [u_sq] + rest:
            gather.ready(u)
        later = [(rec, rec_o), (sq, sq_o), (de, de_o)]
        later = [
            pltpu.make_async_copy(a, b, o_sem.at[3 + k]) for k, (a, b) in enumerate(later)
        ]
        for copy in later:
            copy.start()
        copies += later
        copies += keep_small([(2, h_o, h_h), (4, ctx_o, ctx_h)])
        pre = nn(h_o[...], sq[...]) + nt(emb_o[...], de[...])
        arrival(outer, x_recv.at[8]).wait()
        pre = (pre.reshape(steps, R, 2 * M) + outer[...][None]).reshape(tokens, 2 * M)
        pre_o[...] = pre
        copies += keep_small([(5, pre_o, pre_h)])
        a, b = pre[:, :M], pre[:, M:]
        high = jnp.maximum(a, b)
        smooth = high + jnp.log(jnp.exp(a - high) + jnp.exp(b - high))
        grad_out[...] = smooth.astype(bf16)
        send = to_beside(grad_out, smooth_in, 5)
        send.start()
        copies.append(keep_transposed())
        send.wait_send()
        to_beside(sm_s, block_rows(sm, n, words), 0).wait_send()
        to_beside(dc_s, block_rows(dc, n, dc_s.shape[0]), 3).wait_send()
        end_requests((u_sq, cg_own, far_a, far_b, de_own, de_far))
        arrival(grad_o, x_recv.at[6]).wait()
        for copy in copies:
            copy.wait()


def forward(n, sizes, asked, hit, table, keep, labels, shards):
    R, H, E, M, slots, per, words = sizes
    Z, Y = factors(n)
    tokens = hit.shape[0]
    shape = jax.ShapeDtypeStruct
    dma = pltpu.SemaphoreType.DMA
    units = 9
    cg_rows, de_rows, dc_rows = H, 2 * M, H
    return pl.pallas_call(
        functools.partial(forward_kernel, n, sizes),
        out_shape=[
            shape((3 * H, H), bf16),
            shape((3 * H, E), bf16),
            shape((H, H), bf16),
            shape((cg_rows, 3 * H), bf16),
            shape((de_rows, E), bf16),
            shape((dc_rows, 2 * M), bf16),
            shape((2, Z * Y, words, M), bf16),
            shape((tokens // R, 5, R, H), f32),
            shape((tokens, H), bf16),
            shape((tokens, E), bf16),
            shape((tokens, 2 * M), f32),
            shape((R, H), f32),
            shape((R, H), bf16),
            shape((per, n * slots), bf16),
            shape((tokens, M), bf16),
            shape((8, 128), f32),
            shape((1, 1), jnp.int32),
        ],
        in_specs=[VMEM] * 5 + [ANY] * 7,
        out_specs=[ANY] * 14 + [VMEM] * 2 + [pl.BlockSpec(memory_space=pltpu.SMEM)],
        scratch_shapes=[
            pltpu.VMEM((n, 8, 128), jnp.int32),
            pltpu.VMEM((n * slots, E), bf16),
            pltpu.VMEM((n * slots, E), bf16),
            pltpu.VMEM((H, 3 * H), bf16),
            pltpu.VMEM((3 * H, E), bf16),
            pltpu.VMEM((H, H), bf16),
            pltpu.VMEM((2 * n * words, M), bf16),
            pltpu.VMEM((cg_rows, 3 * H), bf16),
            pltpu.VMEM((de_rows, E), bf16),
            pltpu.VMEM((dc_rows, 2 * M), bf16),
            pltpu.VMEM((tokens, 3 * H), f32),
            pltpu.VMEM((tokens // R, 5, R, H), f32),
            pltpu.VMEM((3 * H, H), bf16),
            pltpu.VMEM((tokens, M), bf16),
            pltpu.VMEM((tokens, M), bf16),
            pltpu.VMEM((tokens, 128), f32),
            pltpu.VMEM((tokens, 128), f32),
            pltpu.VMEM((tokens, 128), f32),
            pltpu.VMEM((2, 8, 128), jnp.int32),
            pltpu.VMEM((R, 2 * M), f32),
            pltpu.VMEM((tokens, H), bf16),
            pltpu.VMEM((tokens, E), bf16),
            pltpu.VMEM((tokens, 2 * M), f32),
            pltpu.VMEM((R, H), f32),
            pltpu.VMEM((R, H), bf16),
            pltpu.VMEM((per, n * slots), bf16),
            dma((units, 6)),
            dma((units, Z)),
            dma((units,)),
            dma((units,)),
            dma((7,)),
            dma((7,)),
            dma((10,)),
            dma((10,)),
            dma,
            dma,
            dma,
            dma,
            dma((2,)),
            dma((2,)),
            dma((6,)),
            dma((2,)),
        ],
        compiler_params=pltpu.CompilerParams(
            collective_id=2, has_side_effects=True, vmem_limit_bytes=VMEM_LIMIT
        ),
    )(asked, hit, table, keep, labels, *shards)


class Sum:
    def __init__(self, at, sems, index, mine, theirs, from_c, from_y, from_z, wholes, rows, out):
        self.at, self.sems, self.index = at, sems, index
        self.mine, self.theirs = mine, theirs
        self.from_c, self.from_y, self.from_z = from_c, from_y, from_z
        self.wholes, self.rows, self.out = wholes, rows, out

    def begin(self):
        at, i = self.at, self.index
        cs, cr = self.sems[:2]
        for zy in range(at.Z * at.Y):
            remote(
                self.theirs(zy), self.from_c(zy), cs.at[i], cr.at[i], at.device(at.z, at.y, 1 - at.c)
            ).start()

    def to_y(self, k, source):
        at, i = self.at, self.index
        ys, yr = self.sems[2:4]
        y = at.along_y(k)
        for z in range(at.Z):
            remote(
                source(z * at.Y + y),
                self.from_y(k, z),
                ys.at[i],
                yr.at[i, k - 1, z],
                at.device(at.z, y, at.c),
            ).start()

    def after_core(self):
        at, i = self.at, self.index
        arrival(self.wholes[0], self.sems[1].at[i]).wait()
        for k in list(range(1, at.Y)) + [0]:
            y = at.along_y(k)

            def per_z(z, _):
                zy = z * at.Y + y
                block = self.mine(zy)
                add_blocks(self.rows, [block, self.from_c(zy)], block, block.dtype)
                return _

            lax.fori_loop(0, at.Z, per_z, 0)
            if k:
                self.to_y(k, self.mine)

    def to_z(self, target, z, slot):
        at, i = self.at, self.index
        zs, zr = self.sems[4:6]
        remote(
            self.mine(target * at.Y + at.y),
            self.from_z(slot),
            zs.at[i],
            zr.at[i, slot],
            at.device(z, at.y, at.c),
        ).start()

    def after_y(self):
        at, i = self.at, self.index
        yr = self.sems[3]

        def per_z(z, _):
            block = self.mine(z * at.Y + at.y)
            came = [self.from_y(j, z) for j in range(1, at.Y)]
            for j, part in enumerate(came):
                arrival(part, yr.at[i, j, z]).wait()
            add_blocks(self.rows, [block] + came, block, block.dtype)
            return _

        lax.fori_loop(0, at.Z, per_z, 0)

        near = at.z_near()
        self.to_z(lax.rem(near + 2, 4), near, 0)
        self.to_z(near, near, 1)

    def add_z(self, target, slot):
        at, i = self.at, self.index
        part = self.from_z(slot)
        arrival(part, self.sems[5].at[i, slot]).wait()
        block = self.mine(target * at.Y + at.y)
        add_blocks(self.rows, [block, part], block, block.dtype)

    def mid_z(self):
        far = self.at.z_far()
        self.add_z(far, 0)
        self.to_z(far, far, 2)

    def after_z(self):
        at, i = self.at, self.index
        cs, _, ys, _, zs, zr = self.sems
        came = [self.from_z(slot) for slot in (1, 2)]
        for slot, part in zip((1, 2), came):
            arrival(part, zr.at[i, slot]).wait()
        add_blocks(self.rows, [self.mine(at.zy)] + came, self.out, self.out.dtype)
        for whole, sem in zip(self.wholes, (cs, ys, zs)):
            if whole is not None:
                arrival(whole, sem.at[i]).wait()


class SumZFirst(Sum):
    def after_core(self):
        at, i = self.at, self.index
        arrival(self.wholes[0], self.sems[1].at[i]).wait()

        def per_zy(zy, _):
            block = self.mine(zy)
            add_blocks(self.rows, [block, self.from_c(zy)], block, block.dtype)
            return _

        lax.fori_loop(0, at.Z * at.Y, per_zy, 0)
        self.to_near(self.mine)

    def to_near(self, source):
        at, i = self.at, self.index
        near = at.z_near()
        ys, yr = self.sems[2:4]
        for k, target in enumerate((lax.rem(near + 2, 4), near)):
            for y in range(at.Y):
                remote(
                    source(target * at.Y + y),
                    self.from_y(1, 2 * k + y),
                    ys.at[i],
                    yr.at[i, 0, 2 * k + y],
                    at.device(near, at.y, at.c),
                ).start()

    def add(self, zy, part, sem):
        arrival(part, sem).wait()
        block = self.mine(zy)
        add_blocks(self.rows, [block, part], block, block.dtype)

    def after_near(self):
        at, i = self.at, self.index
        yr, zs, zr = self.sems[3:6]
        far = at.z_far()
        for k, target in enumerate((far, at.z)):
            for y in range(at.Y):
                self.add(target * at.Y + y, self.from_y(1, 2 * k + y), yr.at[i, 0, 2 * k + y])
                if k == 0:
                    remote(
                        self.mine(far * at.Y + y),
                        self.from_z(y),
                        zs.at[i],
                        zr.at[i, y],
                        at.device(far, at.y, at.c),
                    ).start()

    def after_far(self):
        at, i = self.at, self.index
        zs, zr = self.sems[4:6]
        for y in range(at.Y):
            self.add(at.z * at.Y + y, self.from_z(y), zr.at[i, y])
        other = at.along_y(1)
        remote(
            self.mine(at.z * at.Y + other),
            self.from_z(2),
            zs.at[i],
            zr.at[i, 2],
            at.device(at.z, other, at.c),
        ).start()

    def finish(self):
        at, i = self.at, self.index
        cs, _, ys, _, zs, zr = self.sems
        part = self.from_z(2)
        arrival(part, zr.at[i, 2]).wait()
        add_blocks(self.rows, [self.mine(at.zy), part], self.out, self.out.dtype)
        for whole, sem in zip(self.wholes, (cs, ys, zs)):
            if whole is not None:
                arrival(whole, sem.at[i]).wait()


def backward_kernel_all(n, sizes, *refs):
    R, H, E, M, slots, per, words = sizes
    (
        pre,
        grad,
        keep,
        tanh,
        context,
        loss,
        h_h,
        emb_h,
        hit_h,
        owners_h,
        wr_h,
        wi_h,
        sq_h,
        cg_h,
        de_h,
        dc_h,
        term_h,
        rec_h,
    ) = refs[:18]
    (
        table_h,
        input_h,
        recur_h,
        square_h,
        gates_h,
        deep_h,
        context_h,
        soft_h,
        loss_h,
        early_h,
        late_h,
    ) = refs[18:29]
    (
        wrt,
        wi,
        sq,
        de,
        dc,
        big,
        rec,
        low,
        cand,
        before,
        state_grad,
        total,
        deep_low,
        outer_low,
        early_pack,
        late_pack,
        c_grad,
        c_came,
        pre_low,
        g_out,
        g_in,
        wide_c,
        wide_y,
        wide_z,
        thin_c,
        thin_y,
        thin_z,
        deep_c,
        deep_y,
        deep_z,
        soft_far,
        deep_far,
        far_rows,
        block_rows,
        chunks,
        ctx_cols,
        losses,
        loss_sum,
        cs_sem,
        cr_sem,
        ys_sem,
        yr_sem,
        zs_sem,
        zr_sem,
        pz_sem,
        py_sem,
        pc_sem,
        ps_sem,
        load_sem,
        rec_sem,
        big_sem,
        chunk_sem,
        x_send,
        x_recv,
        ls_sem,
        lr_sem,
        gs_sem,
        gr_sem,
        h,
        emb,
        hit,
        owners,
        small_sem,
        table_o,
        input_o,
        recur_o,
        square_o,
        gates_o,
        deep_o,
        context_o,
        soft_o,
        loss_o,
        put_sem,
    ) = refs[29:]
    at = Place(n)
    Z, Y = at.Z, at.Y
    ZY = Z * Y
    tokens = emb.shape[0]
    steps = tokens // R
    is_decoder = at.s == 1
    beside = (1 - at.s, at.d)
    others = [lax.rem(at.d + k, n) for k in range(1, n)]
    sems = (cs_sem, cr_sem, ys_sem, yr_sem, zs_sem, zr_sem)

    loads = [
        pltpu.make_async_copy(a, b, load_sem.at[k])
        for k, (a, b) in enumerate([(sq_h, sq), (wr_h, wrt), (wi_h, wi)])
    ]
    for copy in loads:
        copy.start()
    small = [
        pltpu.make_async_copy(a, b, small_sem.at[k])
        for k, (a, b) in enumerate([(h_h, h), (emb_h, emb), (hit_h, hit), (owners_h, owners)])
    ]
    for copy in small:
        copy.start()
    load_de = pltpu.make_async_copy(de_h, de, load_sem.at[3])
    load_dc = pltpu.make_async_copy(dc_h, dc, load_sem.at[4])

    def load_record(i):
        return pltpu.make_async_copy(
            rec_h.at[steps - 1 - i], rec.at[lax.rem(i, 2)], rec_sem.at[lax.rem(i, 2)]
        )

    load_record(0).start()
    greet([(at.s, d) for d in others] + [beside])

    def to_beside(src, dst, k):
        return remote(src, dst, x_send.at[k], x_recv.at[k], beside)

    def block_sum(index, term, rows, stride, off, bufs, slot, out, kind=Sum):
        c_buf, y_buf, z_buf = bufs

        def block(zy, c):
            return term.at[pl.ds(multiple(off + (zy * 2 + c) * stride, 16), rows)]

        return kind(
            at,
            sems,
            index,
            lambda zy: block(zy, at.c),
            lambda zy: block(zy, 1 - at.c),
            lambda zy: c_buf.at[slot, zy],
            lambda k, z: y_buf.at[slot, k - 1, z],
            lambda k: z_buf.at[slot, k],
            (c_buf.at[slot], y_buf.at[slot], z_buf.at[slot]),
            rows,
            out,
        )

    wide, thin, deep = (wide_c, wide_y, wide_z), (thin_c, thin_y, thin_z), (deep_c, deep_y, deep_z)
    tall = recur_o.shape[0]
    recur_sums = [
        block_sum(g, wrt, tall, tall, g * H, wide, g, recur_o.at[:, pl.ds(g * H, H)])
        for g in range(3)
    ]
    square_by_y, square_by_z = (
        block_sum(3, sq, tall, tall, 0, wide, 3, square_o, kind) for kind in (Sum, SumZFirst)
    )
    high = input_o.shape[0]
    part = thin_c.shape[2]
    input_sums = [
        block_sum(4 + j, wi, part, high, j * part, thin, j, input_o.at[pl.ds(j * part, part)])
        for j in range(high // part)
    ]
    after = 4 + high // part
    deep_rows = deep_far.shape[0]
    deep_sums = [
        block_sum(
            after + j, de, deep_rows, deep_rows, j * n * deep_rows, deep, j, (deep_far, deep_o)[j]
        )
        for j in range(2)
    ]

    def big_rows(first, count):
        return big.at[pl.ds(multiple(first * words, 16), count * words)]

    def soft_sum(j):
        base_y, base_z = 2 * Z, 2 * Z + 2 * (Y - 1) * Z

        def mine(zy):
            if j == 0:
                apart = zy // Y - at.z
                return big_rows((1 - apart * apart // 4) * Y + zy % Y, 1)
            return big_rows(Z + zy // Y, 1)

        return (SumZFirst, Sum)[j](
            at,
            sems,
            after + 2 + j,
            mine,
            None,
            None,
            lambda k, z: big_rows(base_y + (j * (Y - 1) + k - 1) * Z + z, 1),
            lambda k: big_rows(base_z + j * 3 + k, 1),
            (
                None,
                big_rows(base_y + j * (Y - 1) * Z, (Y - 1) * Z),
                big_rows(base_z + j * 3, 3),
            ),
            words,
            (soft_o, soft_far)[j],
        )

    soft_sums = [soft_sum(0), soft_sum(1)]

    def scan(first, with_state, service):
        def step(i, carry):
            t = steps - 1 - i
            rows = pl.ds(multiple(t * R, R), R)
            slot = lax.rem(i, 2)

            @pl.when(i + 1 < steps)
            def _():
                load_record(i + 1).start()

            load_record(i).wait()
            g = carry + state_grad[rows, :] if with_state else carry
            z, r, c, m, p = (rec[slot, k] for k in range(5))
            pc = g * (1.0 - z) * (1.0 - c * c)
            pz = g * (p - c) * z * (1.0 - z)
            pr = pc * m * r * (1.0 - r)
            pn = pc * r
            parts = [pz, pr, pn]
            back = g * z
            for k, x in enumerate(parts):
                x_low = x.astype(bf16)
                low[rows, pl.ds(k * H, H)] = x_low
                back += nn(x_low, wrt[pl.ds(k * H, H), :])
                if with_state:
                    total[:, pl.ds(k * H, H)] += x
            cand[rows, :] = pc.astype(bf16)
            before[rows, :] = p.astype(bf16)
            for when, what in service:
                pl.when(i == when)(what)
            return back * keep[rows, :]

        lax.fori_loop(0, steps, step, first)

    def recur_term(g):
        cols = pl.ds(g * H, H)

        def body(i, _):
            some = pl.ds(multiple(i * 256, 256), 256)
            rows = pl.ds(multiple(g * H + i * 256, 256), 256)
            wrt[rows, :] = tn(before[:, some], low[:, cols]).astype(bf16)
            return _

        lax.fori_loop(0, H // 256, body, 0)

    def input_term():
        def body(i, _):
            some = pl.ds(multiple(i * 256, 256), 256)
            wi[some, :] = tn(low[:, some], emb[...]).astype(bf16)
            return _

        lax.fori_loop(0, 2 * H // 256, body, 0)

        def last(i, _):
            some = pl.ds(multiple(i * 256, 256), 256)
            rows = pl.ds(multiple(2 * H + i * 256, 256), 256)
            wi[rows, :] = tn(cand[:, some], emb[...]).astype(bf16)
            return _

        lax.fori_loop(0, H // 256, last, 0)

    def slot_rows(ref, d):
        return ref.at[pl.ds(multiple(d * slots, 16), slots)]

    def give(extra):
        grads = nn(low[:, pl.ds(0, 2 * H)], wi[pl.ds(0, 2 * H), :])
        grads += nn(cand[...], wi[pl.ds(2 * H, H), :])
        if extra:
            grads += nn(deep_low[...], de[...])
        g_out[...] = tn(hit[...], grads.astype(bf16)).astype(bf16)
        for d in others:
            remote(slot_rows(g_out, d), slot_rows(g_in, at.d), gs_sem, gr_sem, (at.s, d)).start()

    def take():
        own = pl.ds(multiple(at.d * slots, 16), slots)
        some = g_in.at[pl.ds(0, (n - 1) * slots)]
        arrival(some, gr_sem).wait()
        arrival(some, gs_sem).wait()
        g_in[own, :] = g_out[own, :]
        table_o[...] = nn(owners[...], g_in[...])

    puts = []

    def put(src, dst):
        copy = pltpu.make_async_copy(src, dst, put_sem.at[len(puts)])
        copy.start()
        puts.append(copy)

    def thirds(ref, g):
        return ref.at[:, pl.ds(g * H, H)]

    places = {id(recur_sums[g]): (thirds(recur_o, g), thirds(recur_h, g)) for g in range(3)}
    for j, item in enumerate(input_sums):
        rows = pl.ds(j * part, part)
        places[id(item)] = (input_o.at[rows], input_h.at[rows])

    def end_sums(before, between=None):
        items = list(before) + list(input_sums)
        at_y, at_mid, at_end = len(before), max(len(before) - 1, 0), 0
        while at_end < len(items):
            if at_y < len(items):
                items[at_y].after_y()
                at_y += 1
                if at_y == len(items) and between:
                    between()
            if at_mid < min(at_y - 1, len(items)) or at_y == len(items) > at_mid:
                items[at_mid].mid_z()
                at_mid += 1
            if at_end < at_mid - 1 or at_mid == len(items):
                items[at_end].after_z()
                put(*places[id(items[at_end])])
                at_end += 1

    @pl.when(jnp.logical_not(is_decoder))
    def _():
        puts.clear()
        load_dc.start()
        by_z, by_y = soft_sums
        by_z.to_near(lambda zy: term_h.at[0, zy])
        by_y.to_y(1, lambda zy: term_h.at[1, zy])
        for y in range(Y):
            for z in (at.z_far(), at.z):
                zy = z * Y + y
                pltpu.make_async_copy(term_h.at[0, zy], by_z.mine(zy), big_sem.at[0]).start()
        for z in range(Z):
            zy = z * Y + at.y
            pltpu.make_async_copy(term_h.at[1, zy], by_y.mine(zy), big_sem.at[1]).start()
        losses[at.d] = loss[...]
        for d in others:
            remote(loss, losses.at[at.d], ls_sem, lr_sem, (at.s, d)).start()
        for j, item in enumerate(soft_sums):
            whole = big_rows(j * Z, Z)
            arrival(whole, big_sem.at[j]).wait()
        for copy in loads:
            copy.wait()
        load_dc.wait()
        arrival(outer_low, x_recv.at[6]).wait()
        back = nt(outer_low[...], dc[...])
        arrival(c_came, x_recv.at[0]).wait()
        c = tanh[...]
        c_low = (back + c_came[...].astype(f32)).astype(bf16).astype(f32)
        pre_low[...] = (c_low * (1.0 - c * c)).astype(bf16)
        first = nt(pre_low[...], sq[...])

        def square_term():
            sq[...] = tn(h[pl.ds((steps - 1) * R, R), :], pre_low[...]).astype(bf16)
            square_by_y.begin()

        small[0].wait()
        scan(
            first,
            False,
            [
                (1, square_term),
                (3, by_z.after_near),
                (5, square_by_y.after_core),
                (7, by_y.after_y),
            ],
        )
        for copy in small[1:]:
            copy.wait()
        for g in range(3):
            recur_term(g)
            recur_sums[g].begin()
            if g:
                recur_sums[g - 1].after_core()
        by_z.after_far()
        give(False)
        recur_sums[2].after_core()
        input_term()
        for item in input_sums:
            item.begin()
        square_by_y.after_y()
        for item in input_sums:
            item.after_core()
        by_y.mid_z()
        recur_sums[0].after_y()
        square_by_y.mid_z()
        recur_sums[1].after_y()
        recur_sums[0].mid_z()
        by_y.after_z()
        send = to_beside(soft_far, soft_o, 1)
        send.start()
        some = losses.at[pl.ds(0, n - 1)]
        arrival(some, lr_sem).wait()
        arrival(some, ls_sem).wait()
        all_loss = losses[0]
        for d in range(1, n):
            all_loss += losses[d]
        loss_sum[...] = all_loss
        loss_o[...] = all_loss
        put(loss_o, loss_h)
        loss_send = to_beside(loss_sum, loss_o, 2)
        loss_send.start()
        recur_sums[2].after_y()
        recur_sums[1].mid_z()
        recur_sums[0].after_z()
        put(*places[id(recur_sums[0])])
        take()
        put(table_o, table_h)
        square_by_y.after_z()
        put(square_o, square_h)

        def finish_soft():
            by_z.finish()
            put(soft_o, soft_h)

        end_sums([recur_sums[1], recur_sums[2]], finish_soft)
        send.wait_send()
        loss_send.wait_send()
        arrival(gates_o, x_recv.at[4]).wait()
        put(gates_o, gates_h)
        arrival(context_o, x_recv.at[5]).wait()
        put(context_o, context_h)
        arrival(deep_o, x_recv.at[3]).wait()
        put(deep_o, deep_h)
        for copy in puts:
            copy.wait()

    @pl.when(is_decoder)
    def _():
        puts.clear()
        load_de.start()
        chunk = big.shape[1]
        for k in range(3 * H // chunk):
            pltpu.make_async_copy(
                cg_h.at[:, pl.ds(k * chunk, chunk)], big.at[pl.ds(k * H, H)], big_sem.at[0]
            ).start()
        a, b = pre[:, pl.ds(0, M)], pre[:, pl.ds(M, M)]
        high = jnp.maximum(a, b)
        smooth = high + jnp.log(jnp.exp(a - high) + jnp.exp(b - high))
        sg = grad[...].astype(f32)
        for k, x in enumerate((a, b)):
            cols = pl.ds(k * M, M)
            deep_grad = sg * jnp.exp(x - smooth)
            deep_low[:, cols] = deep_grad.astype(bf16)
            outer_low[:, cols] = jnp.sum(deep_grad.reshape(steps, R, M), axis=0).astype(bf16)
        outer_send = to_beside(outer_low, outer_low, 6)
        outer_send.start()
        for copy in loads:
            copy.wait()
        state_grad[...] = nt(deep_low[...], sq[...])
        total[...] = jnp.zeros_like(total)
        gather = Gather(at, pz_sem, py_sem, pc_sem, ps_sem)
        early = Unit(0, early_pack, early_h, R, 0)
        late = Unit(1, late_pack, late_h, R, 0)
        early_pack[:, pl.ds(0, H)] = context[...]
        early_pack[:, pl.ds(H, 2 * M)] = outer_low[...]
        own_copies = [
            pltpu.make_async_copy(early_pack, early.block(at.zy, at.c), big_sem.at[1]),
            pltpu.make_async_copy(late_pack, late.block(at.zy, at.c), big_sem.at[2]),
        ]
        own_copies[0].start()
        gather.begin(early)
        scan(
            jnp.zeros((R, H), f32),
            True,
            [
                (10, lambda: gather.step1(early)),
            ],
        )
        late_pack[...] = total[...].astype(bf16)
        gates_rows = big.at[pl.ds(0, 3 * H * H // chunk)]
        arrival(gates_rows, big_sem.at[0]).wait()
        for k in range(3 * H // chunk):
            cols = pl.ds(k * chunk, chunk)
            term = nt(late_pack[:, cols], big[pl.ds(k * H, H), :])
            back = term if k == 0 else back + term
        c_grad[...] = back.astype(bf16)
        send = to_beside(c_grad, c_came, 0)
        send.start()
        gather.step2(early)
        own_copies[1].start()
        gather.begin(late)
        for copy in small:
            copy.wait()
        for g in range(3):
            recur_term(g)
            recur_sums[g].begin()
            if g:
                recur_sums[g - 1].after_core()
        gather.step1(late)
        load_de.wait()
        give(True)
        recur_sums[2].after_core()
        sq[...] = tn(h[...], deep_low[...]).astype(bf16)
        square_by_z.begin()
        gather.step2(late)
        de[...] = tn(deep_low[...], emb[...]).astype(bf16)
        for item in deep_sums:
            item.begin()
        input_term()
        for item in input_sums:
            item.begin()
        square_by_z.after_core()
        for item in deep_sums:
            item.after_core()
        for item in input_sums:
            item.after_core()
        gather.step3(early)
        recur_sums[0].after_y()
        square_by_z.after_near()
        recur_sums[1].after_y()
        recur_sums[0].mid_z()
        gather.step3(late)
        recur_sums[2].after_y()
        recur_sums[1].mid_z()
        square_by_z.after_far()
        for u in (early, late):
            gather.ready(u)
        for copy in own_copies:
            copy.wait()
        recur_sums[0].after_z()
        put(*places[id(recur_sums[0])])

        rows = gates_o.shape[0]
        firsts = [(sec * n + at.d) * rows for sec in (0, 1)]
        for k, first in enumerate(firsts):
            lanes = multiple(first // 128 * 128, 128)
            copy = pltpu.make_async_copy(
                early_h.at[:, pl.ds(lanes, 128)], ctx_cols.at[k], big_sem.at[3]
            )
            copy.start()
            copy.wait()
        pieces = (2 * M + 3 * H) // chunk

        def load_chunk(k):
            if k < 2 * M // chunk:
                src = early_h.at[:, pl.ds(H + k * chunk, chunk)]
            else:
                src = late_h.at[:, pl.ds(k * chunk - 2 * M, chunk)]
            return pltpu.make_async_copy(src, chunks.at[k % 2], chunk_sem.at[k % 2])

        load_chunk(0).start()
        for k in range(pieces):
            if k + 1 < pieces:
                load_chunk(k + 1).start()
            load_chunk(k).wait()
            for j, first in enumerate(firsts):
                block_rows[...] = tn(ctx_cols[j], chunks[k % 2])
                product = block_rows[pl.ds(multiple(lax.rem(first, 128), 8), rows), :]
                if k < 2 * M // chunk:
                    dst, cols = context_o, pl.ds(k * chunk, chunk)
                else:
                    dst, cols = gates_o, pl.ds(k * chunk - 2 * M, chunk)
                if j == 0:
                    far_rows[:, pl.ds(k * chunk, chunk)] = product
                else:
                    dst[:, cols] = product
        sends = [
            to_beside(far_rows.at[:, pl.ds(2 * M, 3 * H)], gates_o, 4),
            to_beside(far_rows.at[:, pl.ds(0, 2 * M)], context_o, 5),
        ]
        for copy in sends:
            copy.start()
        put(gates_o, gates_h)
        put(context_o, context_h)
        take()
        put(table_o, table_h)
        recur_sums[2].mid_z()
        for item in deep_sums:
            item.after_y()
        recur_sums[1].after_z()
        put(*places[id(recur_sums[1])])
        for item in deep_sums:
            item.mid_z()
        recur_sums[2].after_z()
        put(*places[id(recur_sums[2])])

        def finish_deep():
            for item in deep_sums:
                item.after_z()
            put(deep_o, deep_h)
            sends.append(to_beside(deep_far, deep_o, 3))
            sends[-1].start()

        end_sums([], finish_deep)
        square_by_z.finish()
        put(square_o, square_h)
        for copy in sends + [send, outer_send]:
            copy.wait_send()
        for u in (early, late):
            gather.drain(u)
        arrival(soft_o, x_recv.at[1]).wait()
        put(soft_o, soft_h)
        arrival(loss_o, x_recv.at[2]).wait()
        put(loss_o, loss_h)
        for copy in puts:
            copy.wait()


def backward(n, sizes, blocks, arrays):
    R, H, E, M, slots, per, words = sizes
    Z, Y = factors(n)
    ZY = Z * Y
    tokens = arrays[0].shape[0]
    shape = jax.ShapeDtypeStruct
    vmem = pltpu.VMEM
    dma = pltpu.SemaphoreType.DMA
    input_b, recur_b, square_b, gates_b, deep_b, context_b = blocks
    tall = recur_b[0]
    part = next(k for k in (64, 48, 32, 16) if input_b[0] % k == 0)
    thin = input_b[0] // part
    units = 4 + thin + 4
    chunk = M
    big_rows = words * (2 * Z + 2 * (Y - 1) * Z + 6)
    big_rows = max(big_rows, 3 * H * H // chunk)
    y1 = max(Y - 1, 1)
    return pl.pallas_call(
        functools.partial(backward_kernel_all, n, sizes),
        out_shape=[
            shape((per, E), f32),
            shape(input_b, f32),
            shape(recur_b, f32),
            shape(square_b, f32),
            shape(gates_b, f32),
            shape(deep_b, f32),
            shape(context_b, f32),
            shape((words, M), f32),
            shape((8, 128), f32),
            shape((n * R, H + 2 * M), bf16),
            shape((n * R, 3 * H), bf16),
        ],
        in_specs=[VMEM] * 6 + [ANY] * 12,
        out_specs=[ANY] * 11,
        scratch_shapes=[
            vmem((3 * H, H), bf16),
            vmem((3 * H, E), bf16),
            vmem((H, H), bf16),
            vmem((2 * M, E), bf16),
            vmem((H, 2 * M), bf16),
            vmem((big_rows, chunk), bf16),
            vmem((2, 5, R, H), f32),
            vmem((tokens, 3 * H), bf16),
            vmem((tokens, H), bf16),
            vmem((tokens, H), bf16),
            vmem((tokens, H), f32),
            vmem((R, 3 * H), f32),
            vmem((tokens, 2 * M), bf16),
            vmem((R, 2 * M), bf16),
            vmem((R, H + 2 * M), bf16),
            vmem((R, 3 * H), bf16),
            vmem((R, H), bf16),
            vmem((R, H), bf16),
            vmem((R, H), bf16),
            vmem((n * slots, E), bf16),
            vmem((n * slots, E), bf16),
            vmem((4, ZY, tall, H), bf16),
            vmem((4, y1, Z, tall, H), bf16),
            vmem((4, 3, tall, H), bf16),
            vmem((thin, ZY, part, E), bf16),
            vmem((thin, y1, Z, part, E), bf16),
            vmem((thin, 3, part, E), bf16),
            vmem((2, ZY) + deep_b, bf16),
            vmem((2, y1, Z) + deep_b, bf16),
            vmem((2, 3) + deep_b, bf16),
            vmem((words, M), f32),
            vmem(deep_b, f32),
            vmem((gates_b[0], 2 * M + 3 * H), f32),
            vmem((128, chunk), f32),
            vmem((2, n * R, chunk), bf16),
            vmem((2, n * R, 128), bf16),
            vmem((n, 8, 128), f32),
            vmem((8, 128), f32),
            dma((units,)),
            dma((units,)),
            dma((units,)),
            dma((units, y1, Z)),
            dma((units,)),
            dma((units, 3)),
            dma((2, 6)),
            dma((2, Z)),
            dma((2,)),
            dma((2,)),
            dma((5,)),
            dma((2,)),
            dma((4,)),
            dma((2,)),
            dma((7,)),
            dma((7,)),
            dma,
            dma,
            dma,
            dma,
            vmem((tokens, H), bf16),
            vmem((tokens, E), bf16),
            vmem((tokens, n * slots), bf16),
            vmem((per, n * slots), bf16),
            dma((4,)),
            vmem((per, E), f32),
            vmem(input_b, f32),
            vmem(recur_b, f32),
            vmem(square_b, f32),
            vmem(gates_b, f32),
            vmem(deep_b, f32),
            vmem(context_b, f32),
            vmem((words, M), f32),
            vmem((8, 128), f32),
            dma((16,)),
        ],
        compiler_params=pltpu.CompilerParams(
            collective_id=3, has_side_effects=True, vmem_limit_bytes=VMEM_LIMIT
        ),
    )(*arrays)


def in_rounds(
    token_ids,
    resets,
    targets,
    embedding,
    input_gates,
    recur_gates,
    square,
    context_gates,
    deep_embed,
    deep_context,
    softmax_weight,
):
    n = lax.axis_size("dp")
    s = lax.axis_index("section")
    d = lax.axis_index("dp")
    is_decoder = s == 1
    micro, rows, steps = token_ids.shape[1:]
    R = micro * rows
    tokens = R * steps
    H = square.shape[2]
    E = embedding.shape[2]
    M = softmax_weight.shape[1]
    per = embedding.shape[1]
    slots = max(512 // n, 8)
    scale = 1.0 / (R * n)

    def time_major(x):
        return jnp.transpose(x.reshape(R, steps), (1, 0)).reshape(-1)

    ids = time_major(token_ids[0])
    keep = time_major(1 - resets[0]).astype(f32)[:, None]
    labels = time_major(targets)

    plan = request_slots(ids, n, per, slots)
    rounds = lax.pmax(jnp.max(plan[2]) // slots + 1, ("section", "dp"))
    table = embedding[0]

    def fetch(turn):
        asked, hit = round_maps(plan, turn, n, slots)
        owners = owner_map(asked, n, per)
        came = swap(nn(owners, table).astype(bf16), n)
        return owners, hit, nn(hit, came).astype(bf16)

    owners, hit, emb = fetch(0)

    def more(carry):
        turn, emb = carry
        return turn + 1, emb + fetch(turn)[2]

    _, emb = lax.while_loop(lambda c: c[0] < rounds, more, (jnp.int32(1), emb))

    wr, wi, sq, sm, cg, de, dc = gather(
        n,
        [
            recur_gates[0],
            input_gates[0],
            square[0],
            softmax_weight,
            context_gates,
            deep_embed,
            deep_context,
        ],
        (False, False, False, False, True, True, True),
    )
    wr, wi, sq, sm = wr.reshape(H, 3 * H), wi.reshape(3 * H, E), sq.reshape(H, H), sm.reshape(-1, M)
    cg, de, dc = cg.reshape(H, 3 * H), de.reshape(2 * M, E), dc.reshape(H, 2 * M)

    enc = gru_forward(emb, wi, wr, jnp.zeros((R, 3 * H), f32), keep)
    last_low = enc[5][-R:]
    ctx_tanh = jnp.tanh(nn(last_low, sq))
    context = lax.ppermute(ctx_tanh.astype(bf16), "section", [(0, 1)])

    dec = gru_forward(emb, wi, wr, nn(context, cg), keep)
    states_low = dec[5]
    deep_pre = nn(states_low, sq) + nt(emb, de)
    deep_pre = (deep_pre.reshape(steps, R, -1) + nn(context, dc)[None]).reshape(tokens, -1)
    smooth = jnp.logaddexp(deep_pre[:, :M], deep_pre[:, M:])
    smooth_low = smooth.astype(bf16)

    came = lax.ppermute(smooth_low, "section", [(1, 0)])
    head_in = jnp.where(is_decoder, smooth_low, came)
    words = sm.shape[0]
    logits = nt(head_in, sm)
    top = jnp.max(logits, axis=1)
    total = jnp.sum(jnp.exp(logits - top[:, None]), axis=1)
    hits = lax.broadcasted_iota(jnp.int32, logits.shape, 1) == (labels - s * words)[:, None]
    picked = jnp.sum(jnp.where(hits, logits, 0.0), axis=1)
    stats = jnp.stack([top, total, picked])
    other = lax.ppermute(stats, "section", [(0, 1), (1, 0)])
    all_top = jnp.maximum(top, other[0])
    log_norm = all_top + jnp.log(
        total * jnp.exp(top - all_top) + other[1] * jnp.exp(other[0] - all_top)
    )
    loss = jnp.where(is_decoder, jnp.sum(log_norm - picked - other[2]) * scale, 0.0)
    logit_low = ((jnp.exp(logits - log_norm[:, None]) - hits.astype(f32)) * scale).astype(bf16)
    smooth_part = nn(logit_low, sm)
    smooth_grad = smooth_part + lax.ppermute(smooth_part, "section", [(0, 1)])
    softmax_term = tn(logit_low, head_in).astype(bf16)

    deep_grad = jnp.concatenate(
        [
            smooth_grad * jnp.exp(deep_pre[:, :M] - smooth),
            smooth_grad * jnp.exp(deep_pre[:, M:] - smooth),
        ],
        axis=1,
    )
    deep_low = deep_grad.astype(bf16)
    outer_low = jnp.sum(deep_grad.reshape(steps, R, -1), axis=0).astype(bf16)
    state_grad = nt(deep_low, sq)
    dec_low, dec_cand, drive_sum = gru_backward(
        state_grad, jnp.zeros((R, H), f32), keep, dec[:5], wr
    )
    drive_sum_low = drive_sum.astype(bf16)
    context_grad = (nt(outer_low, dc) + nt(drive_sum_low, cg)).astype(bf16)
    packed = lax.all_gather(jnp.concatenate([context, outer_low, drive_sum_low], axis=1), "dp", tiled=True)
    packed_came = lax.ppermute(packed, "section", [(1, 0)])
    packed = jnp.where(is_decoder, packed, packed_came)

    context_back = lax.ppermute(context_grad, "section", [(1, 0)])
    pre_low = (context_back.astype(f32) * (1.0 - ctx_tanh * ctx_tanh)).astype(bf16)
    enc_low, enc_cand, _ = gru_backward(
        jnp.zeros((tokens, H), f32), nt(pre_low, sq), keep, enc[:5], wr
    )

    def pick(of_encoder, of_decoder):
        return jnp.where(is_decoder, of_decoder, of_encoder)

    recur_low = pick(enc_low, dec_low)
    cand_low = pick(enc_cand, dec_cand)
    before_low = pick(enc[4], dec[4]).astype(bf16)
    drive_low = jnp.concatenate([recur_low[:, : 2 * H], cand_low], axis=1)
    recur_term = tn(before_low, recur_low).astype(bf16)
    input_term = tn(drive_low, emb).astype(bf16)
    deep_mask = jnp.where(is_decoder, deep_low, jnp.zeros_like(deep_low))
    input_grad = nn(drive_low, wi) + nn(deep_mask, de)
    rows_pad = jnp.zeros((tokens - R, H), bf16)
    square_term = tn(
        pick(jnp.concatenate([last_low, rows_pad]), states_low),
        pick(jnp.concatenate([pre_low, rows_pad]), deep_low),
    ).astype(bf16)
    deep_term = tn(deep_mask, emb).astype(bf16)

    input_grad_low = input_grad.astype(bf16)

    def give(owners, hit):
        return tn(owners, swap(tn(hit, input_grad_low).astype(bf16), n))

    def give_more(carry):
        turn, grad = carry
        asked, hit = round_maps(plan, turn, n, slots)
        return turn + 1, grad + give(owner_map(asked, n, per), hit)

    table_grad = give(owners, hit)
    _, table_grad = lax.while_loop(
        lambda c: c[0] < rounds, give_more, (jnp.int32(1), table_grad)
    )

    deep_blocks = jnp.stack(
        [x.reshape((n,) + deep_embed.shape) for x in jnp.split(deep_term, 2)], axis=1
    )
    deep_blocks = deep_blocks.reshape(n, 2 * deep_embed.shape[0], E)
    loss_blocks = jnp.broadcast_to(loss, (n, 8, 128))
    square_sum, recur_sum, input_sum, softmax_sum, deep_sum, loss_sum = scatter(
        n,
        [
            square_term.reshape((n,) + square.shape[1:]),
            recur_term.reshape((n,) + recur_gates.shape[1:]),
            input_term.reshape((n,) + input_gates.shape[1:]),
            softmax_term.reshape((n,) + softmax_weight.shape),
            deep_blocks,
            loss_blocks,
        ],
        1,
    )
    deep_halves = deep_sum.reshape((2,) + deep_embed.shape)
    both = lax.ppermute(
        jnp.concatenate([deep_halves[0].reshape(-1), loss_sum[:1].reshape(-1)]), "section", [(1, 0)]
    )
    deep_out = jnp.where(is_decoder, deep_halves[1], both[:-128].reshape(deep_embed.shape))
    loss_out = jnp.where(is_decoder, loss_sum[0, 0], both[-1])

    own = (s * n + d) * context_gates.shape[0]
    context_own = lax.dynamic_slice(packed, (0, own), (packed.shape[0], context_gates.shape[0]))
    gates_out = tn(context_own, packed[:, H + 2 * M :])
    context_out = tn(context_own, packed[:, H : H + 2 * M])

    return (
        loss_out,
        table_grad[None],
        input_sum[None],
        recur_sum[None],
        square_sum[None],
        gates_out,
        deep_out,
        context_out,
        softmax_sum,
    )


def in_one_round(
    token_ids,
    resets,
    targets,
    embedding,
    input_gates,
    recur_gates,
    square,
    context_gates,
    deep_embed,
    deep_context,
    softmax_weight,
):
    n = lax.axis_size("dp")
    s = lax.axis_index("section")
    d = lax.axis_index("dp")
    is_decoder = s == 1
    micro, rows, steps = token_ids.shape[1:]
    R = micro * rows
    tokens = R * steps
    H = square.shape[2]
    E = embedding.shape[2]
    M = softmax_weight.shape[1]
    per = embedding.shape[1]
    slots = 512 // n

    def time_major(x):
        return jnp.transpose(x.reshape(R, steps), (1, 0)).reshape(-1)

    ids = time_major(token_ids[0])
    keep = time_major(1 - resets[0]).astype(f32)[:, None]
    labels = time_major(targets)

    plan = request_slots(ids, n, per, slots)
    asked, hit = round_maps(plan, 0, n, slots)
    lane = jnp.arange(128, dtype=jnp.int32)
    asked = jnp.tile(asked.reshape(n, slots), (1, 128 // slots))
    asked = jnp.where(lane // slots == d % (128 // slots), asked, -1)
    fullest = jnp.broadcast_to(jnp.max(plan[2]), (n, 1, 128))
    asked = jnp.concatenate([asked[:, None], fullest, jnp.zeros((n, 6, 128), jnp.int32)], axis=1)

    shards = [
        recur_gates[0],
        input_gates[0],
        square[0],
        softmax_weight,
        context_gates,
        deep_embed,
        deep_context,
    ]
    sizes = (R, H, E, M, slots, per, softmax_weight.shape[0])
    results = forward(n, sizes, asked, hit, embedding[0], keep, labels[:, None], shards)

    (
        wr,
        wi,
        sq,
        cg,
        de,
        dc,
        softmax_term,
        rec,
        states_low,
        emb,
        deep_pre,
        ctx_tanh,
        context,
        owners,
        smooth_grad,
        loss,
        most,
    ) = results
    blocks = [
        x.shape[-2:]
        for x in (input_gates, recur_gates, square, context_gates, deep_embed, deep_context)
    ]
    table, inputs, recur, squares, gates, deep, contexts, soft, loss, _, _ = backward(
        n,
        sizes,
        blocks,
        [
            deep_pre,
            smooth_grad,
            keep,
            ctx_tanh,
            context,
            loss,
            states_low,
            emb,
            hit,
            owners,
            wr,
            wi,
            sq,
            cg,
            de,
            dc,
            softmax_term,
            rec,
        ],
    )
    def again(carry):
        slow = in_rounds(
            token_ids,
            resets,
            targets,
            embedding,
            input_gates,
            recur_gates,
            square,
            context_gates,
            deep_embed,
            deep_context,
            softmax_weight,
        )
        flat = [x.reshape(x.shape[-2:]) for x in slow[1:]]
        return jnp.int32(0), (jnp.broadcast_to(slow[0], (8, 128)), *flat)

    fast = (loss, table, inputs, recur, squares, gates, deep, contexts, soft)
    done = lax.while_loop(lambda carry: carry[0] > 0, again, (most.reshape(()), fast))[1]
    loss, table, inputs, recur, squares, gates, deep, contexts, soft = finish(*done)
    return (
        loss.reshape(()),
        table[None],
        inputs[None],
        recur[None],
        squares[None],
        gates,
        deep,
        contexts,
        soft,
    )


def per_device(*args):
    n = lax.axis_size("dp")
    blocks = [args[k].shape[-2] for k in (4, 5, 6, 7, 8, 9, 10)]
    aligned = all(rows % 16 == 0 for rows in blocks)
    if aligned and n == 16:
        return in_one_round(*args)
    return in_rounds(*args)


def solution(mesh):
    halves = P("section", "dp", None)
    whole = P(("section", "dp"), None)
    in_specs = (
        P("section", None, "dp", None),
        P("section", None, "dp", None),
        P(None, "dp", None),
        halves,
        halves,
        halves,
        halves,
        whole,
        whole,
        whole,
        whole,
    )
    out_specs = (P(), halves, halves, halves, halves, whole, whole, whole, whole)
    return jax.shard_map(
        per_device, mesh=mesh, in_specs=in_specs, out_specs=out_specs, check_vma=False
    )
```

```python
import functools

import jax
import jax.numpy as jnp
from jax import lax
from jax.experimental import pallas as pl
from jax.experimental.pallas import tpu as pltpu
from jax.sharding import PartitionSpec as P

MESH = pl.DeviceIdType.MESH
ANY = pl.BlockSpec(memory_space=pl.ANY)
VMEM = pl.BlockSpec(memory_space=pltpu.VMEM)
f32 = jnp.float32
bf16 = jnp.bfloat16
VMEM_LIMIT = 62 * 2**20


def nn(a, b):
    return jnp.dot(a, b, preferred_element_type=f32)


def nt(a, b):
    return lax.dot_general(a, b, (((1,), (1,)), ((), ())), preferred_element_type=f32)


def tn(a, b):
    return lax.dot_general(a, b, (((0,), (0,)), ((), ())), preferred_element_type=f32)


def factors(n):
    z = 4 if n % 8 == 0 else 1
    return z, n // (2 * z)


class Place:
    def __init__(self, n):
        self.Z, self.Y = factors(n)
        self.s = lax.axis_index("section")
        d = lax.axis_index("dp")
        self.d = d
        self.c = d % 2
        self.zy = d // 2
        self.y = self.zy % self.Y
        self.z = self.zy // self.Y

    def along_z(self, step):
        return lax.rem(self.z + step + self.Z, self.Z)

    def along_y(self, step):
        return lax.rem(self.y + step + self.Y, self.Y)

    def device(self, z, y, c):
        return (self.s, (z * self.Y + y) * 2 + c)

    def z_near(self):
        return self.z + 1 - 2 * (self.z % 2)

    def z_far(self):
        return lax.rem(self.z + 2, 4)

    def partners(self):
        found = [self.device(self.along_z(k), self.y, self.c) for k in range(1, self.Z)]
        found += [self.device(self.z, self.along_y(k), self.c) for k in range(1, self.Y)]
        return found + [self.device(self.z, self.y, 1 - self.c), (1 - self.s, self.d)]


def greet(devices):
    barrier = pltpu.get_barrier_semaphore()
    for device in devices:
        pl.semaphore_signal(barrier, inc=1, device_id=device, device_id_type=MESH)
    pl.semaphore_wait(barrier, len(devices))


def remote(src, dst, send, recv, device):
    return pltpu.make_async_remote_copy(
        src_ref=src, dst_ref=dst, send_sem=send, recv_sem=recv, device_id=device, device_id_type=MESH
    )


def arrival(ref, sem):
    return pltpu.make_async_copy(ref, ref, sem)


def gather_kernel(n, crossed, *refs):
    count = len(crossed)
    sources, outs = refs[:count], refs[count : 2 * count]
    z_sem, y_sem, c_sem, s_sem, l_sem, x_sem, xs_sem = refs[2 * count :]
    at = Place(n)
    Z, Y = at.Z, at.Y
    greet(at.partners())

    x_copies = []
    for item in range(count):
        if crossed[item]:
            copy = remote(
                sources[item],
                outs[item].at[at.s, at.zy, at.c],
                xs_sem.at[item],
                x_sem.at[item],
                (1 - at.s, at.d),
            )
            copy.start()
            x_copies.append(copy)

    units = []
    for item in range(count):
        if crossed[item]:
            units.append((item, outs[item].at[at.s], sources[item]))
        else:
            units.append((item, outs[item], sources[item]))
    own = len(units)
    for item in range(count):
        if crossed[item]:
            gathered = outs[item].at[1 - at.s]
            units.append((item, gathered, gathered.at[at.zy, at.c]))

    def spread(u, src, zy, z_slot, to_z, to_y):
        gathered = units[u][1]
        dst = gathered.at[zy, at.c]
        if to_z:
            for k in range(1, Z):
                remote(
                    src, dst, s_sem.at[u], z_sem.at[u, k - 1], at.device(at.along_z(k), at.y, at.c)
                ).start()
        if to_y:
            for k in range(1, Y):
                remote(
                    src,
                    dst,
                    s_sem.at[u],
                    y_sem.at[u, z_slot * (Y - 1) + k - 1],
                    at.device(at.z, at.along_y(k), at.c),
                ).start()
        remote(src, dst, s_sem.at[u], c_sem.at[u], at.device(at.z, at.y, 1 - at.c)).start()

    for u, (item, gathered, src) in enumerate(units):
        if u < own:
            pltpu.make_async_copy(src, gathered.at[at.zy, at.c], l_sem.at[u]).start()
        else:
            arrival(src, x_sem.at[item]).wait()
        spread(u, src, at.zy, 0, True, True)
    for u, (item, gathered, _) in enumerate(units):
        for k in range(1, Z):
            zy = at.along_z(-k) * Y + at.y
            block = gathered.at[zy, at.c]
            arrival(block, z_sem.at[u, k - 1]).wait()
            spread(u, block, zy, k, False, True)
        for slot in range(Z):
            for k in range(1, Y):
                zy = at.along_z(-slot) * Y + at.along_y(-k)
                block = gathered.at[zy, at.c]
                arrival(block, y_sem.at[u, slot * (Y - 1) + k - 1]).wait()
                spread(u, block, zy, 0, False, False)
    for u, (item, gathered, src) in enumerate(units):
        if u < own:
            pltpu.make_async_copy(src, gathered.at[at.zy, at.c], l_sem.at[u]).wait()
        theirs = gathered.at[:, 1 - at.c]
        arrival(theirs, c_sem.at[u]).wait()
        most = gathered.at[pl.ds(0, Z * Y - 1)]
        arrival(most, s_sem.at[u]).wait()
        arrival(gathered.at[0, 0], s_sem.at[u]).wait()
    for copy in x_copies:
        copy.wait_send()


def gather(n, arrays, crossed):
    Z, Y = factors(n)
    shapes = []
    for array, over_section in zip(arrays, crossed):
        lead = (2, Z * Y, 2) if over_section else (Z * Y, 2)
        shapes.append(jax.ShapeDtypeStruct(lead + array.shape, array.dtype))
    units = len(arrays) + sum(crossed)
    dma = pltpu.SemaphoreType.DMA
    return pl.pallas_call(
        functools.partial(gather_kernel, n, crossed),
        out_shape=shapes,
        in_specs=[ANY] * len(arrays),
        out_specs=[ANY] * len(arrays),
        scratch_shapes=[
            dma((units, max(Z - 1, 1))),
            dma((units, max(Z * (Y - 1), 1))),
            dma((units,)),
            dma((units,)),
            dma((units,)),
            dma((len(arrays),)),
            dma((len(arrays),)),
        ],
        compiler_params=pltpu.CompilerParams(collective_id=0, has_side_effects=True),
    )(*arrays)


def add_blocks(rows, terms, out, out_type):
    chunk = 16 if rows % 16 == 0 else rows

    def body(i, _):
        part = pl.ds(pl.multiple_of(i * chunk, chunk), chunk)
        total = terms[0][part, :].astype(f32)
        for term in terms[1:]:
            total = total + term[part, :].astype(f32)
        out[part, :] = total.astype(out_type)
        return _

    lax.fori_loop(0, rows // chunk, body, 0)


def scatter_kernel(n, count, *refs):
    sources, outs = refs[:count], refs[count : 2 * count]
    scratch = refs[2 * count :]
    mine, from_c, from_y, from_z = (scratch[k * count : (k + 1) * count] for k in range(4))
    l_sem, cs_sem, cr_sem, ys_sem, yr_sem, zs_sem, zr_sem = scratch[4 * count :]
    at = Place(n)
    Z, Y = at.Z, at.Y
    greet(at.partners()[:-1])

    c_copies, l_copies, y_copies, z_copies = [], [], [], []
    for i in range(count):
        copy = remote(
            sources[i].at[:, 1 - at.c],
            from_c[i],
            cs_sem.at[i],
            cr_sem.at[i],
            at.device(at.z, at.y, 1 - at.c),
        )
        copy.start()
        c_copies.append(copy)
        copy = pltpu.make_async_copy(sources[i].at[:, at.c], mine[i], l_sem.at[i])
        copy.start()
        l_copies.append(copy)

    def after_core(i):
        c_copies[i].wait_recv()
        l_copies[i].wait()
        rows = mine[i].shape[1]
        for k in list(range(1, Y)) + [0]:
            y = at.along_y(k)

            def per_z(z, _):
                zy = z * Y + y
                add_blocks(rows, [mine[i].at[zy], from_c[i].at[zy]], mine[i].at[zy], mine[i].dtype)
                return _

            lax.fori_loop(0, Z, per_z, 0)
            if k:
                for z in range(Z):
                    copy = remote(
                        mine[i].at[z * Y + y],
                        from_y[i].at[k - 1, z],
                        ys_sem.at[i, k - 1, z],
                        yr_sem.at[i, k - 1, z],
                        at.device(at.z, y, at.c),
                    )
                    copy.start()
                    y_copies.append(copy)

    def after_y(i):
        rows = mine[i].shape[1]
        for k in list(range(1, Z)) + [0]:
            z = at.along_z(k)
            block = mine[i].at[z * Y + at.y]
            for j in range(1, Y):
                arrival(from_y[i].at[j - 1, z], yr_sem.at[i, j - 1, z]).wait()
            terms = [block] + [from_y[i].at[j - 1, z] for j in range(1, Y)]
            add_blocks(rows, terms, block, mine[i].dtype)
            if k:
                copy = remote(
                    block,
                    from_z[i].at[k - 1],
                    zs_sem.at[i, k - 1],
                    zr_sem.at[i, k - 1],
                    at.device(z, at.y, at.c),
                )
                copy.start()
                z_copies.append(copy)

    def after_z(i):
        rows = mine[i].shape[1]
        for k in range(1, Z):
            arrival(from_z[i].at[k - 1], zr_sem.at[i, k - 1]).wait()
        terms = [mine[i].at[at.zy]] + [from_z[i].at[k - 1] for k in range(1, Z)]
        add_blocks(rows, terms, outs[i], outs[i].dtype)

    for turn in range(count + 2):
        if turn < count:
            after_core(turn)
        if 0 <= turn - 1 < count:
            after_y(turn - 1)
        if turn - 2 >= 0:
            after_z(turn - 2)
    for copy in c_copies + y_copies + z_copies:
        copy.wait_send()


def scatter(n, arrays, collective_id):
    Z, Y = factors(n)
    count = len(arrays)
    blocks = [a.shape[-2:] for a in arrays]
    arrays = [a.reshape((Z * Y, 2) + b) for a, b in zip(arrays, blocks)]
    dma = pltpu.SemaphoreType.DMA
    scratch = [pltpu.VMEM((Z * Y,) + b, a.dtype) for a, b in zip(arrays, blocks)]
    scratch += [pltpu.VMEM((Z * Y,) + b, a.dtype) for a, b in zip(arrays, blocks)]
    scratch += [pltpu.VMEM((max(Y - 1, 1), Z) + b, a.dtype) for a, b in zip(arrays, blocks)]
    scratch += [pltpu.VMEM((max(Z - 1, 1),) + b, a.dtype) for a, b in zip(arrays, blocks)]
    return pl.pallas_call(
        functools.partial(scatter_kernel, n, count),
        out_shape=[jax.ShapeDtypeStruct(b, f32) for b in blocks],
        in_specs=[ANY] * count,
        out_specs=[VMEM] * count,
        scratch_shapes=scratch
        + [
            dma((count,)),
            dma((count,)),
            dma((count,)),
            dma((count, max(Y - 1, 1), Z)),
            dma((count, max(Y - 1, 1), Z)),
            dma((count, max(Z - 1, 1))),
            dma((count, max(Z - 1, 1))),
        ],
        compiler_params=pltpu.CompilerParams(
            collective_id=collective_id, has_side_effects=True, vmem_limit_bytes=VMEM_LIMIT
        ),
    )(*arrays)


def scan_kernel(emb, wi, wr, ctx, keep, z_o, r_o, n_o, m_o, p_o, h_o, drive):
    R, H = ctx.shape[0], wr.shape[0]
    drive[...] = nt(emb[...], wi[...])

    def step(t, h):
        rows = pl.ds(pl.multiple_of(t * R, R), R)
        p = h * keep[rows, :]
        p_o[rows, :] = p
        rec = nn(p.astype(bf16), wr[...])
        d = drive[rows, :]
        z = jax.nn.sigmoid(d[:, :H] + rec[:, :H] + ctx[:, :H])
        r = jax.nn.sigmoid(d[:, H : 2 * H] + rec[:, H : 2 * H] + ctx[:, H : 2 * H])
        m = rec[:, 2 * H :] + ctx[:, 2 * H :]
        n = jnp.tanh(d[:, 2 * H :] + r * m)
        h = z * p + (1.0 - z) * n
        z_o[rows, :] = z
        r_o[rows, :] = r
        n_o[rows, :] = n
        m_o[rows, :] = m
        h_o[rows, :] = h.astype(bf16)
        return h

    lax.fori_loop(0, emb.shape[0] // R, step, jnp.zeros((R, H), f32))


def gru_forward(emb, wi, wr, ctx, keep):
    tokens, H = emb.shape[0], wr.shape[0]
    shape = jax.ShapeDtypeStruct
    return pl.pallas_call(
        scan_kernel,
        out_shape=[shape((tokens, H), f32)] * 5 + [shape((tokens, H), bf16)],
        in_specs=[VMEM] * 5,
        out_specs=[VMEM] * 6,
        scratch_shapes=[pltpu.VMEM((tokens, 3 * H), f32)],
        compiler_params=pltpu.CompilerParams(vmem_limit_bytes=VMEM_LIMIT),
    )(emb, wi, wr, ctx, keep)


def backward_kernel(sg, carry0, keep, z, r, n, m, p, wr, low_o, cand_o, sum_o):
    R, H = carry0.shape
    steps = sg.shape[0] // R

    def step(i, carry):
        rows = pl.ds(pl.multiple_of((steps - 1 - i) * R, R), R)
        g = sg[rows, :] + carry
        zz = z[rows, :]
        cand = n[rows, :]
        rr = r[rows, :]
        pc = g * (1.0 - zz) * (1.0 - cand * cand)
        pz = g * (p[rows, :] - cand) * zz * (1.0 - zz)
        pr = pc * m[rows, :] * rr * (1.0 - rr)
        rec = jnp.concatenate([pz, pr, pc * rr], axis=1)
        low = rec.astype(bf16)
        low_o[rows, :] = low
        cand_o[rows, :] = pc.astype(bf16)
        sum_o[...] += rec
        return (g * zz + nt(low, wr[...])) * keep[rows, :]

    sum_o[...] = jnp.zeros_like(sum_o)
    lax.fori_loop(0, steps, step, carry0[...])


def gru_backward(sg, carry0, keep, record, wr):
    z, r, n, m, p = record
    tokens, H = sg.shape
    shape = jax.ShapeDtypeStruct
    return pl.pallas_call(
        backward_kernel,
        out_shape=[
            shape((tokens, 3 * H), bf16),
            shape((tokens, H), bf16),
            shape((carry0.shape[0], 3 * H), f32),
        ],
        in_specs=[VMEM] * 9,
        out_specs=[VMEM] * 3,
        compiler_params=pltpu.CompilerParams(vmem_limit_bytes=VMEM_LIMIT),
    )(sg, carry0, keep, z, r, n, m, p, wr)


def finish_kernel(count, *refs):
    loss_in, loss_out = refs[0], refs[count]
    sources, outs, held = refs[1:count], refs[count + 1 : 2 * count], refs[2 * count : 3 * count - 1]
    in_sem, out_sem = refs[-2:]
    ins = [pltpu.make_async_copy(a, b, in_sem.at[k]) for k, (a, b) in enumerate(zip(sources, held))]
    puts = [pltpu.make_async_copy(a, b, out_sem.at[k]) for k, (a, b) in enumerate(zip(held, outs))]
    for copy in ins:
        copy.start()
    loss_out[0, 0] = jnp.max(loss_in[...])
    for copy, put in zip(ins, puts):
        copy.wait()
        put.start()
    for put in puts:
        put.wait()


def finish(loss, *arrays):
    shape = jax.ShapeDtypeStruct
    count = len(arrays)
    return pl.pallas_call(
        functools.partial(finish_kernel, count + 1),
        out_shape=[shape((1, 1), f32)] + [shape(a.shape, a.dtype) for a in arrays],
        in_specs=[VMEM] + [ANY] * count,
        out_specs=[pl.BlockSpec(memory_space=pltpu.SMEM)] + [ANY] * count,
        scratch_shapes=[pltpu.VMEM(a.shape, a.dtype) for a in arrays]
        + [pltpu.SemaphoreType.DMA((count,))] * 2,
        compiler_params=pltpu.CompilerParams(vmem_limit_bytes=16 * 2**20),
    )(loss, *arrays)


def request_slots(ids, n, per, slots):
    count = ids.shape[0]
    index = jnp.arange(count, dtype=jnp.int32)
    same = ids[:, None] == ids[None, :]
    first = jnp.min(jnp.where(same, index[None, :], count), axis=1)
    leads = first == index
    owner = ids // per
    ahead = (owner[:, None] == owner[None, :]) & leads[None, :] & (index[None, :] < first[:, None])
    rank = jnp.sum(ahead.astype(jnp.int32), axis=1)
    return leads, owner, rank, ids - owner * per


def round_maps(plan, turn, n, slots):
    leads, owner, rank, local = plan
    place = rank - turn * slots
    inside = (place >= 0) & (place < slots)
    place = jnp.where(inside, owner * slots + place, -1)
    hit = place[:, None] == jnp.arange(n * slots, dtype=jnp.int32)[None, :]
    asked = jnp.max(jnp.where(hit & leads[:, None], local[:, None], -1), axis=0)
    return asked, hit.astype(bf16)


def swap(x, n):
    shape = x.shape
    return lax.all_to_all(x.reshape((n, -1) + shape[1:]), "dp", 0, 0, tiled=False).reshape(shape)


def owner_map(asked, n, per):
    asked_here = swap(asked, n)
    return (asked_here[:, None] == jnp.arange(per, dtype=jnp.int32)[None, :]).astype(bf16)


def multiple(x, of):
    return pl.multiple_of(x, of)


class Unit:
    def __init__(self, index, src, dst, rows, base, y_first=False, stride=None):
        self.index, self.src, self.dst, self.rows, self.base = index, src, dst, rows, base
        self.y_first, self.stride = y_first, stride or rows

    def block(self, zy, c):
        return self.dst.at[pl.ds(multiple(self.base + (zy * 2 + c) * self.stride, 16), self.rows)]

    def some(self, count):
        return self.dst.at[pl.ds(0, count * self.rows)]


class Gather:
    def __init__(self, at, z_sem, y_sem, c_sem, s_sem):
        self.at, self.z_sem, self.y_sem, self.c_sem, self.s_sem = at, z_sem, y_sem, c_sem, s_sem

    def to_z(self, u, src, dst, z, slot):
        at = self.at
        remote(
            src,
            dst,
            self.s_sem.at[u.index],
            self.z_sem.at[u.index, slot],
            at.device(z, at.y, at.c),
        ).start()

    def to_y(self, u, src, dst, z):
        at = self.at
        remote(
            src,
            dst,
            self.s_sem.at[u.index],
            self.y_sem.at[u.index, z],
            at.device(at.z, at.along_y(1), at.c),
        ).start()

    def to_core(self, u, src, dst):
        at = self.at
        remote(
            src, dst, self.s_sem.at[u.index], self.c_sem.at[u.index], at.device(at.z, at.y, 1 - at.c)
        ).start()

    def begin(self, u):
        at = self.at
        dst = u.block(at.zy, at.c)
        if not u.y_first:
            self.to_z(u, u.src, dst, at.z_far(), 0)
        self.to_y(u, u.src, dst, at.z)
        self.to_core(u, u.src, dst)

    def by_z(self, u, z, y, slot):
        at = self.at
        block = u.block(z * at.Y + y, at.c)
        arrival(block, self.z_sem.at[u.index, slot]).wait()
        return block

    def by_y(self, u, z):
        at = self.at
        block = u.block(z * at.Y + at.along_y(1), at.c)
        arrival(block, self.y_sem.at[u.index, z]).wait()
        return block

    def step1(self, u):
        at = self.at
        far, near = at.z_far(), at.z_near()
        if u.y_first:
            self.to_z(u, u.src, u.block(at.zy, at.c), far, 0)
            block = self.by_y(u, at.z)
            self.to_z(u, block, block, far, 1)
            self.to_core(u, block, block)
            return
        self.to_z(u, u.src, u.block(at.zy, at.c), near, 1)
        block = self.by_z(u, far, at.y, 0)
        self.to_z(u, block, block, near, 2)
        self.to_y(u, block, block, far)
        self.to_core(u, block, block)

    def step2(self, u):
        at = self.at
        far, near = at.z_far(), at.z_near()
        other = at.along_y(1)
        if u.y_first:
            self.to_z(u, u.src, u.block(at.zy, at.c), near, 2)
            block = u.block(at.z * at.Y + other, at.c)
            self.to_z(u, block, block, near, 3)
            for slot, y in ((0, at.y), (1, other)):
                block = self.by_z(u, far, y, slot)
                self.to_z(u, block, block, near, 4 + slot)
                self.to_core(u, block, block)
            return
        for slot, z in ((1, near), (2, lax.rem(near + 2, 4))):
            block = self.by_z(u, z, at.y, slot)
            self.to_y(u, block, block, z)
            self.to_core(u, block, block)

    def step3(self, u):
        at = self.at
        far, near = at.z_far(), at.z_near()
        next_far = lax.rem(near + 2, 4)
        if u.y_first:
            other = at.along_y(1)
            for slot, z, y in (
                (2, near, at.y),
                (3, near, other),
                (4, next_far, at.y),
                (5, next_far, other),
            ):
                block = self.by_z(u, z, y, slot)
                self.to_core(u, block, block)
            return
        for z in (at.z, far, near, next_far):
            block = self.by_y(u, z)
            self.to_core(u, block, block)

    def ready(self, u):
        part = u.some(self.at.Z * self.at.Y)
        arrival(part, self.c_sem.at[u.index]).wait()

    def drain(self, u):
        part = u.some(2 * self.at.Z * self.at.Y - 1)
        arrival(part, self.s_sem.at[u.index]).wait()


class Chain(Gather):
    def on(self, u, src, dst, up, hops):
        at = self.at
        slot = hops - 1 if up else at.Z - 1 + hops - 1

        @pl.when(at.z < at.Z - 1 if up else at.z > 0)
        def _():
            remote(
                src,
                dst,
                self.on_sem.at[u.index],
                self.z_sem.at[u.index, slot],
                at.device(at.z + (1 if up else -1), at.y, at.c),
            ).start()

    def begin(self, u):
        at = self.at
        dst = u.block(at.zy, at.c)
        self.on(u, u.src, dst, True, 1)
        self.on(u, u.src, dst, False, 1)
        self.to_y(u, u.src, dst, at.z)
        self.to_core(u, u.src, dst)

    def pass_z(self, u, k):
        at = self.at
        for up in (True, False):
            z = at.z - k if up else at.z + k

            @pl.when(z >= 0 if up else z < at.Z)
            def _():
                slot = k - 1 if up else at.Z - 1 + k - 1
                block = self.by_z(u, z, at.y, slot)
                if k + 1 < at.Z:
                    self.on(u, block, block, up, k + 1)
                self.to_y(u, block, block, z)
                self.to_core(u, block, block)

    def drain(self, u):
        at = self.at
        part = u.some(2 * at.Z * at.Y - at.Z)
        arrival(part, self.s_sem.at[u.index]).wait()
        for z in range(at.Z):
            sent = (z + 1 if z < at.Z - 1 else 0) + (at.Z - z if z > 0 else 0)

            @pl.when(at.z == z)
            def _():
                part = u.some(sent)
                arrival(part, self.on_sem.at[u.index]).wait()


def column(ref, t):
    rows = ref.shape[2]
    square = (rows, rows)
    diagonal = lax.broadcasted_iota(jnp.int32, square, 0) == lax.broadcasted_iota(jnp.int32, square, 1)
    parts = []
    for k in range(ref.shape[1]):
        line = jnp.broadcast_to(ref[t, k : k + 1, :], square)
        parts.append(jnp.sum(jnp.where(diagonal, line, 0), axis=1, keepdims=True))
    return jnp.concatenate(parts, axis=0)


def forward_kernel(n, sizes, *refs):
    R, H, E, M, slots, per, words = sizes
    (
        asked_rows,
        own_most,
        hit,
        table,
        resets,
        words_in,
        wr_s,
        wi_s,
        sq_s,
        sm_s,
        cg_s,
        de_s,
        dc_s,
    ) = refs[:13]
    (
        wr_o,
        wi_o,
        sq_o,
        cg_o,
        de_o,
        dc_o,
        term_o,
        rec_o,
        h_h,
        emb_h,
        pre_h,
        tanh_h,
        ctx_h,
        owners_h,
        grad_o,
        loss_o,
        most_o,
    ) = refs[13:30]
    (
        asked_in,
        rows_out,
        came,
        wr,
        wi,
        sq,
        sm,
        cg,
        de,
        dc,
        drive,
        rec,
        wrt,
        smooth_in,
        grad_out,
        m_part,
        s_part,
        p_part,
        fullest,
        outer,
        h_o,
        emb_o,
        pre_o,
        tanh_o,
        ctx_o,
        owners_o,
        z_sem,
        y_sem,
        c_sem,
        s_sem,
        l_sem,
        o_sem,
        x_recv,
        x_send,
        as_sem,
        ar_sem,
        rs_sem,
        rr_sem,
        t_send,
        t_recv,
        k_sem,
        on_sem,
        keep,
        labels,
        asked,
    ) = refs[30:]
    at = Place(n)
    tokens = hit.shape[0]
    steps = tokens // R
    is_decoder = at.s == 1
    beside = (1 - at.s, at.d)
    others = [lax.rem(at.d + k, n) for k in range(1, n)]
    for d in range(n):
        asked[d, 0:1, :] = asked_rows[d : d + 1, :]
        asked[d, 1:2, :] = jnp.full((1, 128), own_most[0, 0], jnp.int32)
    greet([(at.s, d) for d in others] + [beside])

    def block_rows(ref, base, rows):
        return ref.at[pl.ds(multiple((base + at.d) * rows, 16), rows)]

    def to_beside(src, dst, k):
        return remote(src, dst, x_send.at[k], x_recv.at[k], beside)

    gather = Gather(at, z_sem, y_sem, c_sem, s_sem)
    chain = Chain(at, z_sem, y_sem, c_sem, s_sem)
    chain.on_sem = on_sem
    u_wi = Unit(1, wi_s, wi, wi_s.shape[0], 0)
    u_wr = Unit(0, wr_s, wr, wr_s.shape[0], 0)
    u_sq = Unit(2, sq_s, sq, sq_s.shape[0], 0)
    own_sm = Unit(3, sm_s, sm, words, 0)
    far_sm = Unit(4, block_rows(sm, n, words), sm, words, n * words)
    crossed = []
    for k, (src, dst) in enumerate([(cg_s, cg), (de_s, de)]):
        rows = src.shape[0]
        crossed.append(
            (
                Unit(3 + 2 * k, src, dst, rows, n * rows),
                Unit(4 + 2 * k, block_rows(dst, 0, rows), dst, rows, 0, k == 0),
            )
        )
    rows = cg_s.shape[0]
    far_block = block_rows(cg, 0, rows)
    cg_halves = [
        Unit(index, far_block.at[pl.ds(k * 16, 16)], cg, 16, k * 16, k == 0, rows)
        for k, index in enumerate((4, 7))
    ]
    rows = dc_s.shape[0]
    own_dc = Unit(5, dc_s, dc, rows, 0)
    far_dc = Unit(6, block_rows(dc, n, rows), dc, rows, n * rows)

    for d in others:
        remote(asked.at[d], asked_in.at[at.d], as_sem, ar_sem, (at.s, d)).start()
    chain.begin(u_wi)
    chain.begin(u_wr)

    @pl.when(is_decoder)
    def _():
        to_beside(dc_s, block_rows(dc, n, dc_s.shape[0]), 3).start()
        to_beside(sm_s, block_rows(sm, n, words), 0).start()

    @pl.when(jnp.logical_not(is_decoder))
    def _():
        for k, (src, dst) in enumerate([(cg_s, cg), (de_s, de)]):
            to_beside(src, block_rows(dst, 0, src.shape[0]), 1 + k).start()

    locals_ = [
        pltpu.make_async_copy(src, block_rows(dst, 0, src.shape[0]), l_sem.at[k])
        for k, (src, dst) in enumerate([(wr_s, wr), (wi_s, wi), (sq_s, sq)])
    ]
    locals_.append(pltpu.make_async_copy(sm_s, block_rows(sm, 0, words), l_sem.at[3]))
    for k, (src, dst) in enumerate([(cg_s, cg), (de_s, de)]):
        locals_.append(pltpu.make_async_copy(src, block_rows(dst, n, src.shape[0]), l_sem.at[4 + k]))
    locals_.append(pltpu.make_async_copy(dc_s, block_rows(dc, 0, dc_s.shape[0]), l_sem.at[6]))
    for copy in locals_:
        copy.start()

    for t in range(steps):
        rows = pl.ds(t * R, R)
        keep[rows, :] = 1.0 - column(resets, t).astype(f32)
        labels[rows, :] = column(words_in, t)

    chain.pass_z(u_wi, 1)
    chain.pass_z(u_wr, 1)
    some_asked = asked_in.at[pl.ds(0, n - 1)]
    arrival(some_asked, ar_sem).wait()
    asked_in[at.d] = asked[at.d]
    group = 128 // slots
    count = lax.broadcasted_iota(jnp.int32, (per, 128), 0)
    most = asked_in[0, 1:2, :]
    for g in range(n // group):
        wanted = asked_in[g * group, 0:1, :]
        for j in range(1, group):
            wanted = jnp.maximum(wanted, asked_in[g * group + j, 0:1, :])
        for j in range(group):
            most = jnp.maximum(most, asked_in[g * group + j, 1:2, :])
        match = (wanted == count).astype(f32).astype(bf16)
        owners_o[:, pl.ds(g * 128, 128)] = match
        rows_out[pl.ds(g * 128, 128), :] = tn(match, table[...]).astype(bf16)
    fullest[0] = jnp.broadcast_to(most, fullest.shape[1:])
    to_beside(fullest.at[0], fullest.at[1], 7).start()

    def slot_rows(ref, d):
        return ref.at[pl.ds(multiple(d * slots, 16), slots)]

    for d in others:
        remote(slot_rows(rows_out, d), slot_rows(came, at.d), rs_sem, rr_sem, (at.s, d)).start()
    cg_own = crossed[0][0]
    far_a, far_b = cg_halves
    de_own, de_far = crossed[1]
    for k in (2, 3):
        if k == 2:

            @pl.when(is_decoder)
            def _():
                arrival(far_block, x_recv.at[1]).wait()
                gather.begin(far_a)

        chain.pass_z(u_wi, k)
        chain.pass_z(u_wr, k)

    gather.step3(u_wi)

    @pl.when(is_decoder)
    def _():
        chain.begin(cg_own)
        chain.begin(far_b)
        gather.step1(far_a)

    @pl.when(jnp.logical_not(is_decoder))
    def _():
        gather.begin(u_sq)

    some_rows = came.at[pl.ds(0, (n - 1) * slots)]
    arrival(some_rows, rr_sem).wait()
    came[pl.ds(multiple(at.d * slots, 16), slots), :] = rows_out[
        pl.ds(multiple(at.d * slots, 16), slots), :
    ]
    emb_o[...] = nn(hit[...], came[...]).astype(bf16)
    to_beside(fullest.at[0], fullest.at[1], 7).wait()
    rank = jnp.max(jnp.maximum(fullest[0], fullest[1]))
    most_o[0, 0] = jnp.where(rank >= slots, 1, 0)
    for copy in locals_:
        copy.wait()
    chain.ready(u_wi)

    def input_drive(i, _):
        cols = pl.ds(multiple(i * 512, 512), 512)
        drive[:, cols] = nt(emb_o[...], wi[cols, :])
        return _

    lax.fori_loop(0, 3 * H // 512, input_drive, 0)
    @pl.when(is_decoder)
    def _():
        chain.pass_z(cg_own, 1)
        chain.pass_z(far_b, 1)

    gather.step3(u_wr)
    chain.ready(u_wr)

    def scan(ctx, service):
        def step(t, h):
            rows = pl.ds(multiple(t * R, R), R)
            p = h * keep[rows, :]
            rec[t, 4] = p
            mix = nn(p.astype(bf16), wr[...])
            d = drive[rows, :]
            z_in = d[:, :H] + mix[:, :H]
            r_in = d[:, H : 2 * H] + mix[:, H : 2 * H]
            m = mix[:, 2 * H :]
            if ctx is not None:
                z_in += ctx[:, :H]
                r_in += ctx[:, H : 2 * H]
                m += ctx[:, 2 * H :]
            z = jax.nn.sigmoid(z_in)
            r = jax.nn.sigmoid(r_in)
            cand = jnp.tanh(d[:, 2 * H :] + r * m)
            h = z * p + (1.0 - z) * cand
            rec[t, 0] = z
            rec[t, 1] = r
            rec[t, 2] = cand
            rec[t, 3] = m
            h_o[rows, :] = h.astype(bf16)
            for when, what in service:
                pl.when(t == when)(what)
            return h

        return lax.fori_loop(0, steps, step, jnp.zeros((R, H), f32))

    def keep_input_gates():
        copy = pltpu.make_async_copy(wi, wi_o, o_sem.at[0])
        copy.start()
        return copy

    def keep_transposed():
        def turn(i, _):
            part = pl.ds(multiple(i * 128, 128), 128)
            wrt[:, part] = wr[part, :].T
            return _

        lax.fori_loop(0, H // 128, turn, 0)
        copy = pltpu.make_async_copy(wrt, wr_o, o_sem.at[1])
        copy.start()
        return copy

    def keep_small(pairs):
        copies = [pltpu.make_async_copy(a, b, k_sem.at[k]) for k, a, b in pairs]
        for copy in copies:
            copy.start()
        return copies

    def end_requests(units, chained=()):
        arrival(some_asked, as_sem).wait()
        arrival(some_rows, rs_sem).wait()
        for u in (u_wi, u_wr) + chained:
            chain.drain(u)
        for u in units:
            gather.drain(u)

    last = pl.ds((steps - 1) * R, R)

    @pl.when(jnp.logical_not(is_decoder))
    def _():
        copies = [keep_input_gates()] + keep_small([(0, emb_o, emb_h), (1, owners_o, owners_h)])
        wide = (own_dc, far_dc, own_sm, far_sm)

        def begin_dc():
            gather.begin(own_dc)
            arrival(far_dc.src, x_recv.at[3]).wait()
            gather.begin(far_dc)

        def begin_far_sm():
            gather.step1(own_sm)
            arrival(far_sm.src, x_recv.at[0]).wait()
            gather.begin(far_sm)

        def dc_step1():
            gather.step1(own_dc)
            gather.step1(far_dc)

        scan(
            None,
            [
                (1, lambda: gather.step1(u_sq)),
                (2, begin_dc),
                (5, lambda: gather.begin(own_sm)),
                (8, lambda: gather.step2(u_sq)),
                (10, dc_step1),
            ],
        )
        gather.step3(u_sq)
        gather.ready(u_sq)
        ctx_tanh = jnp.tanh(nn(h_o[last, :], sq[...]))
        tanh_o[...] = ctx_tanh
        ctx_o[...] = ctx_tanh.astype(bf16)
        sends = [to_beside(ctx_o, ctx_o, 4)]
        sends[0].start()
        copies += [
            pltpu.make_async_copy(rec, rec_o, o_sem.at[2]),
            pltpu.make_async_copy(sq, sq_o, o_sem.at[3]),
        ]
        for copy in copies[-2:]:
            copy.start()
        copies += keep_small([(2, h_o, h_h), (3, tanh_o, tanh_h), (4, ctx_o, ctx_h)])
        for u in wide[:2]:
            gather.step2(u)
        begin_far_sm()
        for u in wide[:2]:
            gather.step3(u)
        for u in wide[:2]:
            gather.ready(u)
        outer[...] = nn(ctx_o[...], dc[...])
        sends.append(to_beside(outer, outer, 8))
        sends[1].start()
        copies.append(pltpu.make_async_copy(dc, dc_o, o_sem.at[5]))
        copies[-1].start()
        gather.step2(own_sm)
        gather.step1(far_sm)
        copies.append(keep_transposed())
        gather.step2(far_sm)
        for u in wide[2:]:
            gather.step3(u)
        for u in wide[2:]:
            gather.ready(u)
        for send in sends:
            send.wait_send()
        for k, (src, dst) in enumerate([(cg_s, cg), (de_s, de)]):
            to_beside(src, block_rows(dst, 0, src.shape[0]), 1 + k).wait_send()
        end_requests((u_sq,) + wide)

        half = n * words
        ZY = at.Z * at.Y
        across = cg.shape[1] // M
        landed = cg.at[pl.ds(0, half // 4), pl.ds(0, 2 * M)]

        def term_block(j, zy, c):
            return sm.at[pl.ds(multiple((j * n + zy * 2 + c) * words, 16), words)]

        def landing(j, zy):
            place = j * ZY + zy
            rows = pl.ds(multiple(place // across * words, 16), words)
            return cg.at[rows, pl.ds(multiple(place % across * M, 128), M)]

        def core_send(j):
            for zy in range(ZY):
                remote(
                    term_block(j, zy, 1 - at.c),
                    landing(j, zy),
                    t_send.at[j],
                    t_recv.at[j],
                    at.device(at.z, at.y, 1 - at.c),
                ).start()

        arrival(smooth_in, x_recv.at[5]).wait()
        tile = half // 5 if half % 640 == 0 else 512
        lanes = lax.broadcasted_iota(jnp.int32, (tokens, 128), 1)
        m_part[...] = jnp.full(m_part.shape, -jnp.inf, f32)
        s_part[...] = jnp.zeros_like(s_part)
        p_part[...] = jnp.zeros_like(p_part)

        def tops(i, _):
            rows = pl.ds(multiple(i * tile, tile), tile)
            logits = nt(smooth_in[...], sm[rows, :])
            parts = [logits[:, k * 128 : (k + 1) * 128] for k in range(tile // 128)]
            before = m_part[...]
            top = before
            for part in parts:
                top = jnp.maximum(top, part)
            total = s_part[...] * jnp.exp(before - top)
            picked = p_part[...]
            for k, part in enumerate(parts):
                total += jnp.exp(part - top)
                picked += jnp.where(lanes == labels[...] - (i * tile + k * 128), part, 0.0)
            m_part[...] = top
            s_part[...] = total
            p_part[...] = picked
            return _

        lax.fori_loop(0, 2 * n * words // tile, tops, 0)
        top = jnp.max(m_part[...], axis=1, keepdims=True)
        total = jnp.sum(s_part[...] * jnp.exp(m_part[...] - top), axis=1, keepdims=True)
        log_norm = top + jnp.log(total)
        picked = jnp.sum(p_part[...], axis=1, keepdims=True)
        scale = 1.0 / (R * n)
        loss = jnp.sum(log_norm - picked, axis=0, keepdims=True) * scale
        loss_o[...] = jnp.broadcast_to(loss, loss_o.shape)
        m_part[...] = jnp.broadcast_to(log_norm, m_part.shape)
        drive[:, pl.ds(0, M)] = jnp.zeros((tokens, M), f32)

        def grads(i, _):
            rows = pl.ds(multiple(i * tile, tile), tile)
            weight = sm[rows, :]
            logits = nt(smooth_in[...], weight)
            low = []
            for k in range(tile // 128):
                part = jnp.exp(logits[:, k * 128 : (k + 1) * 128] - m_part[...])
                hits = lanes == labels[...] - (i * tile + k * 128)
                low.append(((part - jnp.where(hits, 1.0, 0.0)) * scale).astype(bf16))
            low = jnp.concatenate(low, axis=1)
            drive[:, pl.ds(0, M)] += nn(low, weight)
            sm[rows, :] = tn(low, smooth_in[...]).astype(bf16)
            pl.when(i == half // tile)(lambda: core_send(0))
            return _

        lax.fori_loop(0, 2 * n * words // tile, grads, 0)
        grad_out[...] = drive[:, pl.ds(0, M)].astype(bf16)
        send = to_beside(grad_out, grad_o, 6)
        send.start()
        core_send(1)
        for j in (0, 1):
            arrival(landed, t_recv.at[j]).wait()

            def add(zy, _):
                block = term_block(j, zy, at.c)
                add_blocks(words, [block, landing(j, zy)], block, bf16)
                pltpu.make_async_copy(block, term_o.at[j, zy], o_sem.at[4]).start()
                return _

            lax.fori_loop(0, ZY, add, 0)
        for j in (0, 1):
            arrival(landed, t_send.at[j]).wait()
        arrival(term_o, o_sem.at[4]).wait()
        send.wait_send()
        for copy in copies:
            copy.wait()

    @pl.when(is_decoder)
    def _():
        copies = [keep_input_gates()] + keep_small([(0, emb_o, emb_h), (1, owners_o, owners_h)])
        rest = [de_own, de_far]
        chain.pass_z(cg_own, 2)
        chain.pass_z(far_b, 2)
        gather.step2(far_a)
        chain.pass_z(cg_own, 3)
        chain.pass_z(far_b, 3)
        gather.begin(u_sq)
        gather.begin(de_own)
        arrival(de_far.src, x_recv.at[2]).wait()
        gather.begin(de_far)
        gather.step3(far_a)
        gather.step3(cg_own)
        gather.step3(far_b)
        for u in (cg_own, far_a, far_b):
            gather.ready(u)
        copies.append(pltpu.make_async_copy(cg, cg_o, o_sem.at[2]))
        copies[-1].start()
        arrival(ctx_o, x_recv.at[4]).wait()
        service = [
            (1, functools.partial(gather.step1, u_sq)),
            (2, functools.partial(gather.step1, de_own)),
            (3, functools.partial(gather.step1, de_far)),
            (6, functools.partial(gather.step2, u_sq)),
            (8, functools.partial(gather.step2, de_own)),
            (9, functools.partial(gather.step2, de_far)),
        ]
        ctx = nn(ctx_o[...], cg[...])
        scan(ctx, service)
        for u in [u_sq] + rest:
            gather.step3(u)
        for u in [u_sq] + rest:
            gather.ready(u)
        later = [(rec, rec_o), (sq, sq_o), (de, de_o)]
        later = [
            pltpu.make_async_copy(a, b, o_sem.at[3 + k]) for k, (a, b) in enumerate(later)
        ]
        for copy in later:
            copy.start()
        copies += later
        copies += keep_small([(2, h_o, h_h), (4, ctx_o, ctx_h)])
        pre = nn(h_o[...], sq[...]) + nt(emb_o[...], de[...])
        arrival(outer, x_recv.at[8]).wait()
        pre = (pre.reshape(steps, R, 2 * M) + outer[...][None]).reshape(tokens, 2 * M)
        pre_o[...] = pre
        copies += keep_small([(5, pre_o, pre_h)])
        a, b = pre[:, :M], pre[:, M:]
        high = jnp.maximum(a, b)
        smooth = high + jnp.log(jnp.exp(a - high) + jnp.exp(b - high))
        grad_out[...] = smooth.astype(bf16)
        send = to_beside(grad_out, smooth_in, 5)
        send.start()
        copies.append(keep_transposed())
        send.wait_send()
        to_beside(sm_s, block_rows(sm, n, words), 0).wait_send()
        to_beside(dc_s, block_rows(dc, n, dc_s.shape[0]), 3).wait_send()
        end_requests((u_sq, far_a, de_own, de_far), (cg_own, far_b))
        arrival(grad_o, x_recv.at[6]).wait()
        for copy in copies:
            copy.wait()


def forward(n, sizes, asked, fullest, hit, table, resets, targets, shards):
    R, H, E, M, slots, per, words = sizes
    Z, Y = factors(n)
    tokens = hit.shape[0]
    shape = jax.ShapeDtypeStruct
    dma = pltpu.SemaphoreType.DMA
    units = 9
    cg_rows, de_rows, dc_rows = H, 2 * M, H
    return pl.pallas_call(
        functools.partial(forward_kernel, n, sizes),
        out_shape=[
            shape((3 * H, H), bf16),
            shape((3 * H, E), bf16),
            shape((H, H), bf16),
            shape((cg_rows, 3 * H), bf16),
            shape((de_rows, E), bf16),
            shape((dc_rows, 2 * M), bf16),
            shape((2, Z * Y, words, M), bf16),
            shape((tokens // R, 5, R, H), f32),
            shape((tokens, H), bf16),
            shape((tokens, E), bf16),
            shape((tokens, 2 * M), f32),
            shape((R, H), f32),
            shape((R, H), bf16),
            shape((per, n * slots), bf16),
            shape((tokens, M), bf16),
            shape((8, 128), f32),
            shape((1, 1), jnp.int32),
        ],
        in_specs=[VMEM, pl.BlockSpec(memory_space=pltpu.SMEM)] + [VMEM] * 4 + [ANY] * 7,
        out_specs=[ANY] * 14 + [VMEM] * 2 + [pl.BlockSpec(memory_space=pltpu.SMEM)],
        scratch_shapes=[
            pltpu.VMEM((n, 8, 128), jnp.int32),
            pltpu.VMEM((n * slots, E), bf16),
            pltpu.VMEM((n * slots, E), bf16),
            pltpu.VMEM((H, 3 * H), bf16),
            pltpu.VMEM((3 * H, E), bf16),
            pltpu.VMEM((H, H), bf16),
            pltpu.VMEM((2 * n * words, M), bf16),
            pltpu.VMEM((cg_rows, 3 * H), bf16),
            pltpu.VMEM((de_rows, E), bf16),
            pltpu.VMEM((dc_rows, 2 * M), bf16),
            pltpu.VMEM((tokens, 3 * H), f32),
            pltpu.VMEM((tokens // R, 5, R, H), f32),
            pltpu.VMEM((3 * H, H), bf16),
            pltpu.VMEM((tokens, M), bf16),
            pltpu.VMEM((tokens, M), bf16),
            pltpu.VMEM((tokens, 128), f32),
            pltpu.VMEM((tokens, 128), f32),
            pltpu.VMEM((tokens, 128), f32),
            pltpu.VMEM((2, 8, 128), jnp.int32),
            pltpu.VMEM((R, 2 * M), f32),
            pltpu.VMEM((tokens, H), bf16),
            pltpu.VMEM((tokens, E), bf16),
            pltpu.VMEM((tokens, 2 * M), f32),
            pltpu.VMEM((R, H), f32),
            pltpu.VMEM((R, H), bf16),
            pltpu.VMEM((per, n * slots), bf16),
            dma((units, 6)),
            dma((units, Z)),
            dma((units,)),
            dma((units,)),
            dma((7,)),
            dma((7,)),
            dma((10,)),
            dma((10,)),
            dma,
            dma,
            dma,
            dma,
            dma((2,)),
            dma((2,)),
            dma((6,)),
            dma((units,)),
            pltpu.VMEM((tokens, 1), f32),
            pltpu.VMEM((tokens, 1), jnp.int32),
            pltpu.VMEM((n, 8, 128), jnp.int32),
        ],
        compiler_params=pltpu.CompilerParams(
            collective_id=2, has_side_effects=True, vmem_limit_bytes=VMEM_LIMIT
        ),
    )(asked, fullest, hit, table, resets, targets, *shards)


class Sum:
    def __init__(self, at, sems, index, mine, theirs, from_c, from_y, from_z, wholes, rows, out):
        self.at, self.sems, self.index = at, sems, index
        self.mine, self.theirs = mine, theirs
        self.from_c, self.from_y, self.from_z = from_c, from_y, from_z
        self.wholes, self.rows, self.out = wholes, rows, out

    def begin(self):
        at, i = self.at, self.index
        cs, cr = self.sems[:2]
        for zy in range(at.Z * at.Y):
            remote(
                self.theirs(zy), self.from_c(zy), cs.at[i], cr.at[i], at.device(at.z, at.y, 1 - at.c)
            ).start()

    def to_y(self, k, source):
        at, i = self.at, self.index
        ys, yr = self.sems[2:4]
        y = at.along_y(k)
        for z in range(at.Z):
            remote(
                source(z * at.Y + y),
                self.from_y(k, z),
                ys.at[i],
                yr.at[i, k - 1, z],
                at.device(at.z, y, at.c),
            ).start()

    def after_core(self):
        at, i = self.at, self.index
        arrival(self.wholes[0], self.sems[1].at[i]).wait()
        for k in list(range(1, at.Y)) + [0]:
            y = at.along_y(k)

            def per_z(z, _):
                zy = z * at.Y + y
                block = self.mine(zy)
                add_blocks(self.rows, [block, self.from_c(zy)], block, block.dtype)
                return _

            lax.fori_loop(0, at.Z, per_z, 0)
            if k:
                self.to_y(k, self.mine)

    def to_z(self, target, z, slot):
        at, i = self.at, self.index
        zs, zr = self.sems[4:6]
        remote(
            self.mine(target * at.Y + at.y),
            self.from_z(slot),
            zs.at[i],
            zr.at[i, slot],
            at.device(z, at.y, at.c),
        ).start()

    def after_y(self):
        at, i = self.at, self.index
        yr = self.sems[3]

        def per_z(z, _):
            block = self.mine(z * at.Y + at.y)
            came = [self.from_y(j, z) for j in range(1, at.Y)]
            for j, part in enumerate(came):
                arrival(part, yr.at[i, j, z]).wait()
            add_blocks(self.rows, [block] + came, block, block.dtype)
            return _

        lax.fori_loop(0, at.Z, per_z, 0)

        near = at.z_near()
        self.to_z(lax.rem(near + 2, 4), near, 0)
        self.to_z(near, near, 1)

    def add_z(self, target, slot):
        at, i = self.at, self.index
        part = self.from_z(slot)
        arrival(part, self.sems[5].at[i, slot]).wait()
        block = self.mine(target * at.Y + at.y)
        add_blocks(self.rows, [block, part], block, block.dtype)

    def mid_z(self):
        far = self.at.z_far()
        self.add_z(far, 0)
        self.to_z(far, far, 2)

    def after_z(self):
        at, i = self.at, self.index
        cs, _, ys, _, zs, zr = self.sems
        came = [self.from_z(slot) for slot in (1, 2)]
        for slot, part in zip((1, 2), came):
            arrival(part, zr.at[i, slot]).wait()
        add_blocks(self.rows, [self.mine(at.zy)] + came, self.out, self.out.dtype)
        for whole, sem in zip(self.wholes, (cs, ys, zs)):
            if whole is not None:
                arrival(whole, sem.at[i]).wait()


class SumZFirst(Sum):
    def after_core(self):
        at, i = self.at, self.index
        arrival(self.wholes[0], self.sems[1].at[i]).wait()

        def per_zy(zy, _):
            block = self.mine(zy)
            add_blocks(self.rows, [block, self.from_c(zy)], block, block.dtype)
            return _

        lax.fori_loop(0, at.Z * at.Y, per_zy, 0)
        self.to_near(self.mine)

    def to_near(self, source):
        at, i = self.at, self.index
        near = at.z_near()
        ys, yr = self.sems[2:4]
        for k, target in enumerate((lax.rem(near + 2, 4), near)):
            for y in range(at.Y):
                remote(
                    source(target * at.Y + y),
                    self.from_y(1, 2 * k + y),
                    ys.at[i],
                    yr.at[i, 0, 2 * k + y],
                    at.device(near, at.y, at.c),
                ).start()

    def add(self, zy, part, sem):
        arrival(part, sem).wait()
        block = self.mine(zy)
        add_blocks(self.rows, [block, part], block, block.dtype)

    def after_near(self):
        at, i = self.at, self.index
        yr, zs, zr = self.sems[3:6]
        far = at.z_far()
        for k, target in enumerate((far, at.z)):
            for y in range(at.Y):
                self.add(target * at.Y + y, self.from_y(1, 2 * k + y), yr.at[i, 0, 2 * k + y])
                if k == 0:
                    remote(
                        self.mine(far * at.Y + y),
                        self.from_z(y),
                        zs.at[i],
                        zr.at[i, y],
                        at.device(far, at.y, at.c),
                    ).start()

    def after_far(self):
        at, i = self.at, self.index
        zs, zr = self.sems[4:6]
        for y in range(at.Y):
            self.add(at.z * at.Y + y, self.from_z(y), zr.at[i, y])
        other = at.along_y(1)
        remote(
            self.mine(at.z * at.Y + other),
            self.from_z(2),
            zs.at[i],
            zr.at[i, 2],
            at.device(at.z, other, at.c),
        ).start()

    def finish(self):
        at, i = self.at, self.index
        cs, _, ys, _, zs, zr = self.sems
        part = self.from_z(2)
        arrival(part, zr.at[i, 2]).wait()
        add_blocks(self.rows, [self.mine(at.zy), part], self.out, self.out.dtype)
        for whole, sem in zip(self.wholes, (cs, ys, zs)):
            if whole is not None:
                arrival(whole, sem.at[i]).wait()


def backward_kernel_all(n, sizes, *refs):
    R, H, E, M, slots, per, words = sizes
    (
        pre,
        grad,
        resets,
        tanh,
        context,
        loss,
        h_h,
        emb_h,
        hit_h,
        owners_h,
        wr_h,
        wi_h,
        sq_h,
        cg_h,
        de_h,
        dc_h,
        term_h,
        rec_h,
    ) = refs[:18]
    (
        table_h,
        input_h,
        recur_h,
        square_h,
        gates_h,
        deep_h,
        context_h,
        soft_h,
        loss_h,
        early_h,
        late_h,
    ) = refs[18:29]
    (
        wrt,
        wi,
        sq,
        de,
        dc,
        big,
        rec,
        low,
        cand,
        before,
        state_grad,
        total,
        deep_low,
        outer_low,
        early_pack,
        late_pack,
        c_grad,
        c_came,
        pre_low,
        g_out,
        g_in,
        wide_c,
        wide_y,
        wide_z,
        thin_c,
        thin_y,
        thin_z,
        deep_c,
        deep_y,
        deep_z,
        soft_far,
        deep_far,
        far_rows,
        block_rows,
        chunks,
        ctx_cols,
        losses,
        loss_sum,
        cs_sem,
        cr_sem,
        ys_sem,
        yr_sem,
        zs_sem,
        zr_sem,
        pz_sem,
        py_sem,
        pc_sem,
        ps_sem,
        load_sem,
        rec_sem,
        big_sem,
        chunk_sem,
        x_send,
        x_recv,
        ls_sem,
        lr_sem,
        gs_sem,
        gr_sem,
        h,
        emb,
        hit,
        owners,
        small_sem,
        table_o,
        input_o,
        recur_o,
        square_o,
        gates_o,
        deep_o,
        context_o,
        soft_o,
        loss_o,
        put_sem,
        keep,
    ) = refs[29:]
    at = Place(n)
    Z, Y = at.Z, at.Y
    ZY = Z * Y
    tokens = emb.shape[0]
    steps = tokens // R
    is_decoder = at.s == 1
    beside = (1 - at.s, at.d)
    others = [lax.rem(at.d + k, n) for k in range(1, n)]
    sems = (cs_sem, cr_sem, ys_sem, yr_sem, zs_sem, zr_sem)

    loads = [
        pltpu.make_async_copy(a, b, load_sem.at[k])
        for k, (a, b) in enumerate([(sq_h, sq), (wr_h, wrt), (wi_h, wi)])
    ]
    for copy in loads:
        copy.start()
    small = [
        pltpu.make_async_copy(a, b, small_sem.at[k])
        for k, (a, b) in enumerate([(h_h, h), (emb_h, emb), (hit_h, hit), (owners_h, owners)])
    ]
    for copy in small:
        copy.start()
    load_de = pltpu.make_async_copy(de_h, de, load_sem.at[3])
    load_dc = pltpu.make_async_copy(dc_h, dc, load_sem.at[4])

    def load_record(i):
        return pltpu.make_async_copy(
            rec_h.at[steps - 1 - i], rec.at[lax.rem(i, 2)], rec_sem.at[lax.rem(i, 2)]
        )

    load_record(0).start()
    for t in range(steps):
        keep[pl.ds(t * R, R), :] = 1.0 - column(resets, t).astype(f32)
    greet([(at.s, d) for d in others] + [beside])

    def to_beside(src, dst, k):
        return remote(src, dst, x_send.at[k], x_recv.at[k], beside)

    def block_sum(index, term, rows, stride, off, bufs, slot, out, kind=Sum):
        c_buf, y_buf, z_buf = bufs

        def block(zy, c):
            return term.at[pl.ds(multiple(off + (zy * 2 + c) * stride, 16), rows)]

        return kind(
            at,
            sems,
            index,
            lambda zy: block(zy, at.c),
            lambda zy: block(zy, 1 - at.c),
            lambda zy: c_buf.at[slot, zy],
            lambda k, z: y_buf.at[slot, k - 1, z],
            lambda k: z_buf.at[slot, k],
            (c_buf.at[slot], y_buf.at[slot], z_buf.at[slot]),
            rows,
            out,
        )

    wide, thin, deep = (wide_c, wide_y, wide_z), (thin_c, thin_y, thin_z), (deep_c, deep_y, deep_z)
    tall = recur_o.shape[0]
    recur_sums = [
        block_sum(g, wrt, tall, tall, g * H, wide, g, recur_o.at[:, pl.ds(g * H, H)])
        for g in range(3)
    ]
    square_by_y, square_by_z = (
        block_sum(3, sq, tall, tall, 0, wide, 3, square_o, kind) for kind in (Sum, SumZFirst)
    )
    high = input_o.shape[0]
    part = thin_c.shape[2]
    input_sums = [
        block_sum(4 + j, wi, part, high, j * part, thin, j, input_o.at[pl.ds(j * part, part)])
        for j in range(high // part)
    ]
    after = 4 + high // part
    deep_rows = deep_far.shape[0]
    deep_sums = [
        block_sum(
            after + j, de, deep_rows, deep_rows, j * n * deep_rows, deep, j, (deep_far, deep_o)[j]
        )
        for j in range(2)
    ]

    def big_rows(first, count):
        return big.at[pl.ds(multiple(first * words, 16), count * words)]

    def soft_sum(j):
        base_y, base_z = 2 * Z, 2 * Z + 2 * (Y - 1) * Z

        def mine(zy):
            if j == 0:
                apart = zy // Y - at.z
                return big_rows((1 - apart * apart // 4) * Y + zy % Y, 1)
            return big_rows(Z + zy // Y, 1)

        return (SumZFirst, Sum)[j](
            at,
            sems,
            after + 2 + j,
            mine,
            None,
            None,
            lambda k, z: big_rows(base_y + (j * (Y - 1) + k - 1) * Z + z, 1),
            lambda k: big_rows(base_z + j * 3 + k, 1),
            (
                None,
                big_rows(base_y + j * (Y - 1) * Z, (Y - 1) * Z),
                big_rows(base_z + j * 3, 3),
            ),
            words,
            (soft_o, soft_far)[j],
        )

    soft_sums = [soft_sum(0), soft_sum(1)]

    def scan(first, with_state, service):
        def step(i, carry):
            t = steps - 1 - i
            rows = pl.ds(multiple(t * R, R), R)
            slot = lax.rem(i, 2)

            @pl.when(i + 1 < steps)
            def _():
                load_record(i + 1).start()

            load_record(i).wait()
            g = carry + state_grad[rows, :] if with_state else carry
            z, r, c, m, p = (rec[slot, k] for k in range(5))
            pc = g * (1.0 - z) * (1.0 - c * c)
            pz = g * (p - c) * z * (1.0 - z)
            pr = pc * m * r * (1.0 - r)
            pn = pc * r
            parts = [pz, pr, pn]
            back = g * z
            for k, x in enumerate(parts):
                x_low = x.astype(bf16)
                low[rows, pl.ds(k * H, H)] = x_low
                back += nn(x_low, wrt[pl.ds(k * H, H), :])
                if with_state:
                    total[:, pl.ds(k * H, H)] += x
            cand[rows, :] = pc.astype(bf16)
            before[rows, :] = p.astype(bf16)
            for when, what in service:
                pl.when(i == when)(what)
            return back * keep[rows, :]

        lax.fori_loop(0, steps, step, first)

    def recur_term(g):
        cols = pl.ds(g * H, H)

        def body(i, _):
            some = pl.ds(multiple(i * 256, 256), 256)
            rows = pl.ds(multiple(g * H + i * 256, 256), 256)
            wrt[rows, :] = tn(before[:, some], low[:, cols]).astype(bf16)
            return _

        lax.fori_loop(0, H // 256, body, 0)

    def input_term():
        def body(i, _):
            some = pl.ds(multiple(i * 256, 256), 256)
            wi[some, :] = tn(low[:, some], emb[...]).astype(bf16)
            return _

        lax.fori_loop(0, 2 * H // 256, body, 0)

        def last(i, _):
            some = pl.ds(multiple(i * 256, 256), 256)
            rows = pl.ds(multiple(2 * H + i * 256, 256), 256)
            wi[rows, :] = tn(cand[:, some], emb[...]).astype(bf16)
            return _

        lax.fori_loop(0, H // 256, last, 0)

    def slot_rows(ref, d):
        return ref.at[pl.ds(multiple(d * slots, 16), slots)]

    def give(extra):
        grads = nn(low[:, pl.ds(0, 2 * H)], wi[pl.ds(0, 2 * H), :])
        grads += nn(cand[...], wi[pl.ds(2 * H, H), :])
        if extra:
            grads += nn(deep_low[...], de[...])
        g_out[...] = tn(hit[...], grads.astype(bf16)).astype(bf16)
        for d in others:
            remote(slot_rows(g_out, d), slot_rows(g_in, at.d), gs_sem, gr_sem, (at.s, d)).start()

    def take():
        own = pl.ds(multiple(at.d * slots, 16), slots)
        some = g_in.at[pl.ds(0, (n - 1) * slots)]
        arrival(some, gr_sem).wait()
        arrival(some, gs_sem).wait()
        g_in[own, :] = g_out[own, :]
        table_o[...] = nn(owners[...], g_in[...])

    puts = []

    def put(src, dst):
        copy = pltpu.make_async_copy(src, dst, put_sem.at[len(puts)])
        copy.start()
        puts.append(copy)

    def thirds(ref, g):
        return ref.at[:, pl.ds(g * H, H)]

    places = {id(recur_sums[g]): (thirds(recur_o, g), thirds(recur_h, g)) for g in range(3)}
    for j, item in enumerate(input_sums):
        rows = pl.ds(j * part, part)
        places[id(item)] = (input_o.at[rows], input_h.at[rows])

    def end_sums(before, between=None):
        items = list(before) + list(input_sums)
        at_y, at_mid, at_end = len(before), max(len(before) - 1, 0), 0
        while at_end < len(items):
            if at_y < len(items):
                items[at_y].after_y()
                at_y += 1
                if at_y == len(items) and between:
                    between()
            if at_mid < min(at_y - 1, len(items)) or at_y == len(items) > at_mid:
                items[at_mid].mid_z()
                at_mid += 1
            if at_end < at_mid - 1 or at_mid == len(items):
                items[at_end].after_z()
                put(*places[id(items[at_end])])
                at_end += 1

    @pl.when(jnp.logical_not(is_decoder))
    def _():
        puts.clear()
        load_dc.start()
        by_z, by_y = soft_sums
        by_z.to_near(lambda zy: term_h.at[0, zy])
        by_y.to_y(1, lambda zy: term_h.at[1, zy])
        for y in range(Y):
            for z in (at.z_far(), at.z):
                zy = z * Y + y
                pltpu.make_async_copy(term_h.at[0, zy], by_z.mine(zy), big_sem.at[0]).start()
        for z in range(Z):
            zy = z * Y + at.y
            pltpu.make_async_copy(term_h.at[1, zy], by_y.mine(zy), big_sem.at[1]).start()
        losses[at.d] = loss[...]
        for d in others:
            remote(loss, losses.at[at.d], ls_sem, lr_sem, (at.s, d)).start()
        for j, item in enumerate(soft_sums):
            whole = big_rows(j * Z, Z)
            arrival(whole, big_sem.at[j]).wait()
        for copy in loads:
            copy.wait()
        load_dc.wait()
        arrival(outer_low, x_recv.at[6]).wait()
        back = nt(outer_low[...], dc[...])
        arrival(c_came, x_recv.at[0]).wait()
        c = tanh[...]
        c_low = (back + c_came[...].astype(f32)).astype(bf16).astype(f32)
        pre_low[...] = (c_low * (1.0 - c * c)).astype(bf16)
        first = nt(pre_low[...], sq[...])

        def square_term():
            sq[...] = tn(h[pl.ds((steps - 1) * R, R), :], pre_low[...]).astype(bf16)
            square_by_y.begin()

        small[0].wait()
        scan(
            first,
            False,
            [
                (1, square_term),
                (3, by_z.after_near),
                (5, square_by_y.after_core),
                (7, by_y.after_y),
            ],
        )
        for copy in small[1:]:
            copy.wait()
        for g in range(3):
            recur_term(g)
            recur_sums[g].begin()
            if g:
                recur_sums[g - 1].after_core()
        by_z.after_far()
        give(False)
        recur_sums[2].after_core()
        input_term()
        for item in input_sums:
            item.begin()
        square_by_y.after_y()
        for item in input_sums:
            item.after_core()
        by_y.mid_z()
        recur_sums[0].after_y()
        square_by_y.mid_z()
        recur_sums[1].after_y()
        recur_sums[0].mid_z()
        by_y.after_z()
        send = to_beside(soft_far, soft_o, 1)
        send.start()
        some = losses.at[pl.ds(0, n - 1)]
        arrival(some, lr_sem).wait()
        arrival(some, ls_sem).wait()
        all_loss = losses[0]
        for d in range(1, n):
            all_loss += losses[d]
        loss_sum[...] = all_loss
        loss_o[...] = all_loss
        put(loss_o, loss_h)
        loss_send = to_beside(loss_sum, loss_o, 2)
        loss_send.start()
        recur_sums[2].after_y()
        recur_sums[1].mid_z()
        recur_sums[0].after_z()
        put(*places[id(recur_sums[0])])
        take()
        put(table_o, table_h)
        square_by_y.after_z()
        put(square_o, square_h)

        def finish_soft():
            by_z.finish()
            put(soft_o, soft_h)

        end_sums([recur_sums[1], recur_sums[2]], finish_soft)
        send.wait_send()
        loss_send.wait_send()
        arrival(gates_o, x_recv.at[4]).wait()
        put(gates_o, gates_h)
        arrival(context_o, x_recv.at[5]).wait()
        put(context_o, context_h)
        arrival(deep_o, x_recv.at[3]).wait()
        put(deep_o, deep_h)
        for copy in puts:
            copy.wait()

    @pl.when(is_decoder)
    def _():
        puts.clear()
        load_de.start()
        chunk = big.shape[1]
        for k in range(3 * H // chunk):
            pltpu.make_async_copy(
                cg_h.at[:, pl.ds(k * chunk, chunk)], big.at[pl.ds(k * H, H)], big_sem.at[0]
            ).start()
        a, b = pre[:, pl.ds(0, M)], pre[:, pl.ds(M, M)]
        high = jnp.maximum(a, b)
        smooth = high + jnp.log(jnp.exp(a - high) + jnp.exp(b - high))
        sg = grad[...].astype(f32)
        for k, x in enumerate((a, b)):
            cols = pl.ds(k * M, M)
            deep_grad = sg * jnp.exp(x - smooth)
            deep_low[:, cols] = deep_grad.astype(bf16)
            outer_low[:, cols] = jnp.sum(deep_grad.reshape(steps, R, M), axis=0).astype(bf16)
        outer_send = to_beside(outer_low, outer_low, 6)
        outer_send.start()
        for copy in loads:
            copy.wait()
        state_grad[...] = nt(deep_low[...], sq[...])
        total[...] = jnp.zeros_like(total)
        gather = Gather(at, pz_sem, py_sem, pc_sem, ps_sem)
        early = Unit(0, early_pack, early_h, R, 0)
        late = Unit(1, late_pack, late_h, R, 0)
        early_pack[:, pl.ds(0, H)] = context[...]
        early_pack[:, pl.ds(H, 2 * M)] = outer_low[...]
        own_copies = [
            pltpu.make_async_copy(early_pack, early.block(at.zy, at.c), big_sem.at[1]),
            pltpu.make_async_copy(late_pack, late.block(at.zy, at.c), big_sem.at[2]),
        ]
        own_copies[0].start()
        gather.begin(early)
        scan(
            jnp.zeros((R, H), f32),
            True,
            [
                (10, lambda: gather.step1(early)),
            ],
        )
        late_pack[...] = total[...].astype(bf16)
        gates_rows = big.at[pl.ds(0, 3 * H * H // chunk)]
        arrival(gates_rows, big_sem.at[0]).wait()
        for k in range(3 * H // chunk):
            cols = pl.ds(k * chunk, chunk)
            term = nt(late_pack[:, cols], big[pl.ds(k * H, H), :])
            back = term if k == 0 else back + term
        c_grad[...] = back.astype(bf16)
        send = to_beside(c_grad, c_came, 0)
        send.start()
        gather.step2(early)
        own_copies[1].start()
        gather.begin(late)
        for copy in small:
            copy.wait()
        for g in range(3):
            recur_term(g)
            recur_sums[g].begin()
            if g:
                recur_sums[g - 1].after_core()
        gather.step1(late)
        load_de.wait()
        give(True)
        recur_sums[2].after_core()
        sq[...] = tn(h[...], deep_low[...]).astype(bf16)
        square_by_z.begin()
        gather.step2(late)
        de[...] = tn(deep_low[...], emb[...]).astype(bf16)
        for item in deep_sums:
            item.begin()
        input_term()
        for item in input_sums:
            item.begin()
        square_by_z.after_core()
        for item in deep_sums:
            item.after_core()
        for item in input_sums:
            item.after_core()
        gather.step3(early)
        recur_sums[0].after_y()
        square_by_z.after_near()
        recur_sums[1].after_y()
        recur_sums[0].mid_z()
        gather.step3(late)
        recur_sums[2].after_y()
        recur_sums[1].mid_z()
        square_by_z.after_far()
        for u in (early, late):
            gather.ready(u)
        for copy in own_copies:
            copy.wait()
        recur_sums[0].after_z()
        put(*places[id(recur_sums[0])])

        rows = gates_o.shape[0]
        firsts = [(sec * n + at.d) * rows for sec in (0, 1)]
        for k, first in enumerate(firsts):
            lanes = multiple(first // 128 * 128, 128)
            copy = pltpu.make_async_copy(
                early_h.at[:, pl.ds(lanes, 128)], ctx_cols.at[k], big_sem.at[3]
            )
            copy.start()
            copy.wait()
        pieces = (2 * M + 3 * H) // chunk

        def load_chunk(k):
            if k < 2 * M // chunk:
                src = early_h.at[:, pl.ds(H + k * chunk, chunk)]
            else:
                src = late_h.at[:, pl.ds(k * chunk - 2 * M, chunk)]
            return pltpu.make_async_copy(src, chunks.at[k % 2], chunk_sem.at[k % 2])

        load_chunk(0).start()
        for k in range(pieces):
            if k + 1 < pieces:
                load_chunk(k + 1).start()
            load_chunk(k).wait()
            for j, first in enumerate(firsts):
                block_rows[...] = tn(ctx_cols[j], chunks[k % 2])
                product = block_rows[pl.ds(multiple(lax.rem(first, 128), 8), rows), :]
                if k < 2 * M // chunk:
                    dst, cols = context_o, pl.ds(k * chunk, chunk)
                else:
                    dst, cols = gates_o, pl.ds(k * chunk - 2 * M, chunk)
                if j == 0:
                    far_rows[:, pl.ds(k * chunk, chunk)] = product
                else:
                    dst[:, cols] = product
        sends = [
            to_beside(far_rows.at[:, pl.ds(2 * M, 3 * H)], gates_o, 4),
            to_beside(far_rows.at[:, pl.ds(0, 2 * M)], context_o, 5),
        ]
        for copy in sends:
            copy.start()
        put(gates_o, gates_h)
        put(context_o, context_h)
        take()
        put(table_o, table_h)
        recur_sums[2].mid_z()
        for item in deep_sums:
            item.after_y()
        recur_sums[1].after_z()
        put(*places[id(recur_sums[1])])
        for item in deep_sums:
            item.mid_z()
        recur_sums[2].after_z()
        put(*places[id(recur_sums[2])])

        def finish_deep():
            for item in deep_sums:
                item.after_z()
            put(deep_o, deep_h)
            sends.append(to_beside(deep_far, deep_o, 3))
            sends[-1].start()

        end_sums([], finish_deep)
        square_by_z.finish()
        put(square_o, square_h)
        for copy in sends + [send, outer_send]:
            copy.wait_send()
        for u in (early, late):
            gather.drain(u)
        arrival(soft_o, x_recv.at[1]).wait()
        put(soft_o, soft_h)
        arrival(loss_o, x_recv.at[2]).wait()
        put(loss_o, loss_h)
        for copy in puts:
            copy.wait()


def backward(n, sizes, blocks, arrays):
    R, H, E, M, slots, per, words = sizes
    Z, Y = factors(n)
    ZY = Z * Y
    tokens = arrays[0].shape[0]
    shape = jax.ShapeDtypeStruct
    vmem = pltpu.VMEM
    dma = pltpu.SemaphoreType.DMA
    input_b, recur_b, square_b, gates_b, deep_b, context_b = blocks
    tall = recur_b[0]
    part = next(k for k in (64, 48, 32, 16) if input_b[0] % k == 0)
    thin = input_b[0] // part
    units = 4 + thin + 4
    chunk = M
    big_rows = words * (2 * Z + 2 * (Y - 1) * Z + 6)
    big_rows = max(big_rows, 3 * H * H // chunk)
    y1 = max(Y - 1, 1)
    return pl.pallas_call(
        functools.partial(backward_kernel_all, n, sizes),
        out_shape=[
            shape((per, E), f32),
            shape(input_b, f32),
            shape(recur_b, f32),
            shape(square_b, f32),
            shape(gates_b, f32),
            shape(deep_b, f32),
            shape(context_b, f32),
            shape((words, M), f32),
            shape((8, 128), f32),
            shape((n * R, H + 2 * M), bf16),
            shape((n * R, 3 * H), bf16),
        ],
        in_specs=[VMEM] * 6 + [ANY] * 12,
        out_specs=[ANY] * 11,
        scratch_shapes=[
            vmem((3 * H, H), bf16),
            vmem((3 * H, E), bf16),
            vmem((H, H), bf16),
            vmem((2 * M, E), bf16),
            vmem((H, 2 * M), bf16),
            vmem((big_rows, chunk), bf16),
            vmem((2, 5, R, H), f32),
            vmem((tokens, 3 * H), bf16),
            vmem((tokens, H), bf16),
            vmem((tokens, H), bf16),
            vmem((tokens, H), f32),
            vmem((R, 3 * H), f32),
            vmem((tokens, 2 * M), bf16),
            vmem((R, 2 * M), bf16),
            vmem((R, H + 2 * M), bf16),
            vmem((R, 3 * H), bf16),
            vmem((R, H), bf16),
            vmem((R, H), bf16),
            vmem((R, H), bf16),
            vmem((n * slots, E), bf16),
            vmem((n * slots, E), bf16),
            vmem((4, ZY, tall, H), bf16),
            vmem((4, y1, Z, tall, H), bf16),
            vmem((4, 3, tall, H), bf16),
            vmem((thin, ZY, part, E), bf16),
            vmem((thin, y1, Z, part, E), bf16),
            vmem((thin, 3, part, E), bf16),
            vmem((2, ZY) + deep_b, bf16),
            vmem((2, y1, Z) + deep_b, bf16),
            vmem((2, 3) + deep_b, bf16),
            vmem((words, M), f32),
            vmem(deep_b, f32),
            vmem((gates_b[0], 2 * M + 3 * H), f32),
            vmem((128, chunk), f32),
            vmem((2, n * R, chunk), bf16),
            vmem((2, n * R, 128), bf16),
            vmem((n, 8, 128), f32),
            vmem((8, 128), f32),
            dma((units,)),
            dma((units,)),
            dma((units,)),
            dma((units, y1, Z)),
            dma((units,)),
            dma((units, 3)),
            dma((2, 6)),
            dma((2, Z)),
            dma((2,)),
            dma((2,)),
            dma((5,)),
            dma((2,)),
            dma((4,)),
            dma((2,)),
            dma((7,)),
            dma((7,)),
            dma,
            dma,
            dma,
            dma,
            vmem((tokens, H), bf16),
            vmem((tokens, E), bf16),
            vmem((tokens, n * slots), bf16),
            vmem((per, n * slots), bf16),
            dma((4,)),
            vmem((per, E), f32),
            vmem(input_b, f32),
            vmem(recur_b, f32),
            vmem(square_b, f32),
            vmem(gates_b, f32),
            vmem(deep_b, f32),
            vmem(context_b, f32),
            vmem((words, M), f32),
            vmem((8, 128), f32),
            dma((16,)),
            vmem((tokens, 1), f32),
        ],
        compiler_params=pltpu.CompilerParams(
            collective_id=3, has_side_effects=True, vmem_limit_bytes=VMEM_LIMIT
        ),
    )(*arrays)


def in_rounds(
    token_ids,
    resets,
    targets,
    embedding,
    input_gates,
    recur_gates,
    square,
    context_gates,
    deep_embed,
    deep_context,
    softmax_weight,
):
    n = lax.axis_size("dp")
    s = lax.axis_index("section")
    d = lax.axis_index("dp")
    is_decoder = s == 1
    micro, rows, steps = token_ids.shape[1:]
    R = micro * rows
    tokens = R * steps
    H = square.shape[2]
    E = embedding.shape[2]
    M = softmax_weight.shape[1]
    per = embedding.shape[1]
    slots = max(512 // n, 8)
    scale = 1.0 / (R * n)

    def time_major(x):
        return jnp.transpose(x.reshape(R, steps), (1, 0)).reshape(-1)

    ids = time_major(token_ids[0])
    keep = time_major(1 - resets[0]).astype(f32)[:, None]
    labels = time_major(targets)

    plan = request_slots(ids, n, per, slots)
    rounds = lax.pmax(jnp.max(plan[2]) // slots + 1, ("section", "dp"))
    table = embedding[0]

    def fetch(turn):
        asked, hit = round_maps(plan, turn, n, slots)
        owners = owner_map(asked, n, per)
        came = swap(nn(owners, table).astype(bf16), n)
        return owners, hit, nn(hit, came).astype(bf16)

    owners, hit, emb = fetch(0)

    def more(carry):
        turn, emb = carry
        return turn + 1, emb + fetch(turn)[2]

    _, emb = lax.while_loop(lambda c: c[0] < rounds, more, (jnp.int32(1), emb))

    wr, wi, sq, sm, cg, de, dc = gather(
        n,
        [
            recur_gates[0],
            input_gates[0],
            square[0],
            softmax_weight,
            context_gates,
            deep_embed,
            deep_context,
        ],
        (False, False, False, False, True, True, True),
    )
    wr, wi, sq, sm = wr.reshape(H, 3 * H), wi.reshape(3 * H, E), sq.reshape(H, H), sm.reshape(-1, M)
    cg, de, dc = cg.reshape(H, 3 * H), de.reshape(2 * M, E), dc.reshape(H, 2 * M)

    enc = gru_forward(emb, wi, wr, jnp.zeros((R, 3 * H), f32), keep)
    last_low = enc[5][-R:]
    ctx_tanh = jnp.tanh(nn(last_low, sq))
    context = lax.ppermute(ctx_tanh.astype(bf16), "section", [(0, 1)])

    dec = gru_forward(emb, wi, wr, nn(context, cg), keep)
    states_low = dec[5]
    deep_pre = nn(states_low, sq) + nt(emb, de)
    deep_pre = (deep_pre.reshape(steps, R, -1) + nn(context, dc)[None]).reshape(tokens, -1)
    smooth = jnp.logaddexp(deep_pre[:, :M], deep_pre[:, M:])
    smooth_low = smooth.astype(bf16)

    came = lax.ppermute(smooth_low, "section", [(1, 0)])
    head_in = jnp.where(is_decoder, smooth_low, came)
    words = sm.shape[0]
    logits = nt(head_in, sm)
    top = jnp.max(logits, axis=1)
    total = jnp.sum(jnp.exp(logits - top[:, None]), axis=1)
    hits = lax.broadcasted_iota(jnp.int32, logits.shape, 1) == (labels - s * words)[:, None]
    picked = jnp.sum(jnp.where(hits, logits, 0.0), axis=1)
    stats = jnp.stack([top, total, picked])
    other = lax.ppermute(stats, "section", [(0, 1), (1, 0)])
    all_top = jnp.maximum(top, other[0])
    log_norm = all_top + jnp.log(
        total * jnp.exp(top - all_top) + other[1] * jnp.exp(other[0] - all_top)
    )
    loss = jnp.where(is_decoder, jnp.sum(log_norm - picked - other[2]) * scale, 0.0)
    logit_low = ((jnp.exp(logits - log_norm[:, None]) - hits.astype(f32)) * scale).astype(bf16)
    smooth_part = nn(logit_low, sm)
    smooth_grad = smooth_part + lax.ppermute(smooth_part, "section", [(0, 1)])
    softmax_term = tn(logit_low, head_in).astype(bf16)

    deep_grad = jnp.concatenate(
        [
            smooth_grad * jnp.exp(deep_pre[:, :M] - smooth),
            smooth_grad * jnp.exp(deep_pre[:, M:] - smooth),
        ],
        axis=1,
    )
    deep_low = deep_grad.astype(bf16)
    outer_low = jnp.sum(deep_grad.reshape(steps, R, -1), axis=0).astype(bf16)
    state_grad = nt(deep_low, sq)
    dec_low, dec_cand, drive_sum = gru_backward(
        state_grad, jnp.zeros((R, H), f32), keep, dec[:5], wr
    )
    drive_sum_low = drive_sum.astype(bf16)
    context_grad = (nt(outer_low, dc) + nt(drive_sum_low, cg)).astype(bf16)
    packed = lax.all_gather(jnp.concatenate([context, outer_low, drive_sum_low], axis=1), "dp", tiled=True)
    packed_came = lax.ppermute(packed, "section", [(1, 0)])
    packed = jnp.where(is_decoder, packed, packed_came)

    context_back = lax.ppermute(context_grad, "section", [(1, 0)])
    pre_low = (context_back.astype(f32) * (1.0 - ctx_tanh * ctx_tanh)).astype(bf16)
    enc_low, enc_cand, _ = gru_backward(
        jnp.zeros((tokens, H), f32), nt(pre_low, sq), keep, enc[:5], wr
    )

    def pick(of_encoder, of_decoder):
        return jnp.where(is_decoder, of_decoder, of_encoder)

    recur_low = pick(enc_low, dec_low)
    cand_low = pick(enc_cand, dec_cand)
    before_low = pick(enc[4], dec[4]).astype(bf16)
    drive_low = jnp.concatenate([recur_low[:, : 2 * H], cand_low], axis=1)
    recur_term = tn(before_low, recur_low).astype(bf16)
    input_term = tn(drive_low, emb).astype(bf16)
    deep_mask = jnp.where(is_decoder, deep_low, jnp.zeros_like(deep_low))
    input_grad = nn(drive_low, wi) + nn(deep_mask, de)
    rows_pad = jnp.zeros((tokens - R, H), bf16)
    square_term = tn(
        pick(jnp.concatenate([last_low, rows_pad]), states_low),
        pick(jnp.concatenate([pre_low, rows_pad]), deep_low),
    ).astype(bf16)
    deep_term = tn(deep_mask, emb).astype(bf16)

    input_grad_low = input_grad.astype(bf16)

    def give(owners, hit):
        return tn(owners, swap(tn(hit, input_grad_low).astype(bf16), n))

    def give_more(carry):
        turn, grad = carry
        asked, hit = round_maps(plan, turn, n, slots)
        return turn + 1, grad + give(owner_map(asked, n, per), hit)

    table_grad = give(owners, hit)
    _, table_grad = lax.while_loop(
        lambda c: c[0] < rounds, give_more, (jnp.int32(1), table_grad)
    )

    deep_blocks = jnp.stack(
        [x.reshape((n,) + deep_embed.shape) for x in jnp.split(deep_term, 2)], axis=1
    )
    deep_blocks = deep_blocks.reshape(n, 2 * deep_embed.shape[0], E)
    loss_blocks = jnp.broadcast_to(loss, (n, 8, 128))
    square_sum, recur_sum, input_sum, softmax_sum, deep_sum, loss_sum = scatter(
        n,
        [
            square_term.reshape((n,) + square.shape[1:]),
            recur_term.reshape((n,) + recur_gates.shape[1:]),
            input_term.reshape((n,) + input_gates.shape[1:]),
            softmax_term.reshape((n,) + softmax_weight.shape),
            deep_blocks,
            loss_blocks,
        ],
        1,
    )
    deep_halves = deep_sum.reshape((2,) + deep_embed.shape)
    both = lax.ppermute(
        jnp.concatenate([deep_halves[0].reshape(-1), loss_sum[:1].reshape(-1)]), "section", [(1, 0)]
    )
    deep_out = jnp.where(is_decoder, deep_halves[1], both[:-128].reshape(deep_embed.shape))
    loss_out = jnp.where(is_decoder, loss_sum[0, 0], both[-1])

    own = (s * n + d) * context_gates.shape[0]
    context_own = lax.dynamic_slice(packed, (0, own), (packed.shape[0], context_gates.shape[0]))
    gates_out = tn(context_own, packed[:, H + 2 * M :])
    context_out = tn(context_own, packed[:, H : H + 2 * M])

    return (
        loss_out,
        table_grad[None],
        input_sum[None],
        recur_sum[None],
        square_sum[None],
        gates_out,
        deep_out,
        context_out,
        softmax_sum,
    )


def in_one_round(
    token_ids,
    resets,
    targets,
    embedding,
    input_gates,
    recur_gates,
    square,
    context_gates,
    deep_embed,
    deep_context,
    softmax_weight,
):
    n = lax.axis_size("dp")
    s = lax.axis_index("section")
    d = lax.axis_index("dp")
    is_decoder = s == 1
    micro, rows, steps = token_ids.shape[1:]
    R = micro * rows
    tokens = R * steps
    H = square.shape[2]
    E = embedding.shape[2]
    M = softmax_weight.shape[1]
    per = embedding.shape[1]
    slots = 512 // n

    def time_major(x):
        return jnp.transpose(x.reshape(R, steps), (1, 0)).reshape(-1)

    ids = time_major(token_ids[0])
    reset_rows = jnp.transpose(resets[0], (2, 0, 1))
    target_rows = jnp.transpose(targets, (2, 0, 1))

    plan = request_slots(ids, n, per, slots)
    asked, hit = round_maps(plan, 0, n, slots)
    lane = jnp.arange(128, dtype=jnp.int32)
    asked = jnp.tile(asked.reshape(n, slots), (1, 128 // slots))
    asked = jnp.where(lane // slots == d % (128 // slots), asked, -1)
    fullest = jnp.max(plan[2]).reshape(1, 1)

    shards = [
        recur_gates[0],
        input_gates[0],
        square[0],
        softmax_weight,
        context_gates,
        deep_embed,
        deep_context,
    ]
    sizes = (R, H, E, M, slots, per, softmax_weight.shape[0])
    results = forward(n, sizes, asked, fullest, hit, embedding[0], reset_rows, target_rows, shards)

    (
        wr,
        wi,
        sq,
        cg,
        de,
        dc,
        softmax_term,
        rec,
        states_low,
        emb,
        deep_pre,
        ctx_tanh,
        context,
        owners,
        smooth_grad,
        loss,
        most,
    ) = results
    blocks = [
        x.shape[-2:]
        for x in (input_gates, recur_gates, square, context_gates, deep_embed, deep_context)
    ]
    table, inputs, recur, squares, gates, deep, contexts, soft, loss, _, _ = backward(
        n,
        sizes,
        blocks,
        [
            deep_pre,
            smooth_grad,
            reset_rows,
            ctx_tanh,
            context,
            loss,
            states_low,
            emb,
            hit,
            owners,
            wr,
            wi,
            sq,
            cg,
            de,
            dc,
            softmax_term,
            rec,
        ],
    )
    def again(carry):
        slow = in_rounds(
            token_ids,
            resets,
            targets,
            embedding,
            input_gates,
            recur_gates,
            square,
            context_gates,
            deep_embed,
            deep_context,
            softmax_weight,
        )
        flat = [x.reshape(x.shape[-2:]) for x in slow[1:]]
        return jnp.int32(0), (jnp.broadcast_to(slow[0], (8, 128)), *flat)

    fast = (loss, table, inputs, recur, squares, gates, deep, contexts, soft)
    done = lax.while_loop(lambda carry: carry[0] > 0, again, (most.reshape(()), fast))[1]
    loss, table, inputs, recur, squares, gates, deep, contexts, soft = finish(*done)
    return (
        loss.reshape(()),
        table[None],
        inputs[None],
        recur[None],
        squares[None],
        gates,
        deep,
        contexts,
        soft,
    )


def per_device(*args):
    n = lax.axis_size("dp")
    blocks = [args[k].shape[-2] for k in (4, 5, 6, 7, 8, 9, 10)]
    aligned = all(rows % 16 == 0 for rows in blocks)
    if aligned and n == 16:
        return in_one_round(*args)
    return in_rounds(*args)


def solution(mesh):
    halves = P("section", "dp", None)
    whole = P(("section", "dp"), None)
    in_specs = (
        P("section", None, "dp", None),
        P("section", None, "dp", None),
        P(None, "dp", None),
        halves,
        halves,
        halves,
        halves,
        whole,
        whole,
        whole,
        whole,
    )
    out_specs = (P(), halves, halves, halves, halves, whole, whole, whole, whole)
    return jax.shard_map(
        per_device, mesh=mesh, in_specs=in_specs, out_specs=out_specs, check_vma=False
    )
```

```python
import functools

import jax
import jax.numpy as jnp
from jax import lax
from jax.experimental import pallas as pl
from jax.experimental.pallas import tpu as pltpu
from jax.sharding import PartitionSpec as P

MESH = pl.DeviceIdType.MESH
ANY = pl.BlockSpec(memory_space=pl.ANY)
VMEM = pl.BlockSpec(memory_space=pltpu.VMEM)
f32 = jnp.float32
bf16 = jnp.bfloat16
VMEM_LIMIT = 62 * 2**20


def nn(a, b):
    return jnp.dot(a, b, preferred_element_type=f32)


def nt(a, b):
    return lax.dot_general(a, b, (((1,), (1,)), ((), ())), preferred_element_type=f32)


def tn(a, b):
    return lax.dot_general(a, b, (((0,), (0,)), ((), ())), preferred_element_type=f32)


def factors(n):
    z = 4 if n % 8 == 0 else 1
    return z, n // (2 * z)


class Place:
    def __init__(self, n):
        self.Z, self.Y = factors(n)
        self.s = lax.axis_index("section")
        d = lax.axis_index("dp")
        self.d = d
        self.c = d % 2
        self.zy = d // 2
        self.y = self.zy % self.Y
        self.z = self.zy // self.Y

    def along_z(self, step):
        return lax.rem(self.z + step + self.Z, self.Z)

    def along_y(self, step):
        return lax.rem(self.y + step + self.Y, self.Y)

    def device(self, z, y, c):
        return (self.s, (z * self.Y + y) * 2 + c)

    def z_near(self):
        return self.z + 1 - 2 * (self.z % 2)

    def z_far(self):
        return lax.rem(self.z + 2, 4)

    def partners(self):
        found = [self.device(self.along_z(k), self.y, self.c) for k in range(1, self.Z)]
        found += [self.device(self.z, self.along_y(k), self.c) for k in range(1, self.Y)]
        return found + [self.device(self.z, self.y, 1 - self.c), (1 - self.s, self.d)]


def greet(devices):
    barrier = pltpu.get_barrier_semaphore()
    for device in devices:
        pl.semaphore_signal(barrier, inc=1, device_id=device, device_id_type=MESH)
    pl.semaphore_wait(barrier, len(devices))


def remote(src, dst, send, recv, device):
    return pltpu.make_async_remote_copy(
        src_ref=src, dst_ref=dst, send_sem=send, recv_sem=recv, device_id=device, device_id_type=MESH
    )


def arrival(ref, sem):
    return pltpu.make_async_copy(ref, ref, sem)


def gather_kernel(n, crossed, *refs):
    count = len(crossed)
    sources, outs = refs[:count], refs[count : 2 * count]
    z_sem, y_sem, c_sem, s_sem, l_sem, x_sem, xs_sem = refs[2 * count :]
    at = Place(n)
    Z, Y = at.Z, at.Y
    greet(at.partners())

    x_copies = []
    for item in range(count):
        if crossed[item]:
            copy = remote(
                sources[item],
                outs[item].at[at.s, at.zy, at.c],
                xs_sem.at[item],
                x_sem.at[item],
                (1 - at.s, at.d),
            )
            copy.start()
            x_copies.append(copy)

    units = []
    for item in range(count):
        if crossed[item]:
            units.append((item, outs[item].at[at.s], sources[item]))
        else:
            units.append((item, outs[item], sources[item]))
    own = len(units)
    for item in range(count):
        if crossed[item]:
            gathered = outs[item].at[1 - at.s]
            units.append((item, gathered, gathered.at[at.zy, at.c]))

    def spread(u, src, zy, z_slot, to_z, to_y):
        gathered = units[u][1]
        dst = gathered.at[zy, at.c]
        if to_z:
            for k in range(1, Z):
                remote(
                    src, dst, s_sem.at[u], z_sem.at[u, k - 1], at.device(at.along_z(k), at.y, at.c)
                ).start()
        if to_y:
            for k in range(1, Y):
                remote(
                    src,
                    dst,
                    s_sem.at[u],
                    y_sem.at[u, z_slot * (Y - 1) + k - 1],
                    at.device(at.z, at.along_y(k), at.c),
                ).start()
        remote(src, dst, s_sem.at[u], c_sem.at[u], at.device(at.z, at.y, 1 - at.c)).start()

    for u, (item, gathered, src) in enumerate(units):
        if u < own:
            pltpu.make_async_copy(src, gathered.at[at.zy, at.c], l_sem.at[u]).start()
        else:
            arrival(src, x_sem.at[item]).wait()
        spread(u, src, at.zy, 0, True, True)
    for u, (item, gathered, _) in enumerate(units):
        for k in range(1, Z):
            zy = at.along_z(-k) * Y + at.y
            block = gathered.at[zy, at.c]
            arrival(block, z_sem.at[u, k - 1]).wait()
            spread(u, block, zy, k, False, True)
        for slot in range(Z):
            for k in range(1, Y):
                zy = at.along_z(-slot) * Y + at.along_y(-k)
                block = gathered.at[zy, at.c]
                arrival(block, y_sem.at[u, slot * (Y - 1) + k - 1]).wait()
                spread(u, block, zy, 0, False, False)
    for u, (item, gathered, src) in enumerate(units):
        if u < own:
            pltpu.make_async_copy(src, gathered.at[at.zy, at.c], l_sem.at[u]).wait()
        theirs = gathered.at[:, 1 - at.c]
        arrival(theirs, c_sem.at[u]).wait()
        most = gathered.at[pl.ds(0, Z * Y - 1)]
        arrival(most, s_sem.at[u]).wait()
        arrival(gathered.at[0, 0], s_sem.at[u]).wait()
    for copy in x_copies:
        copy.wait_send()


def gather(n, arrays, crossed):
    Z, Y = factors(n)
    shapes = []
    for array, over_section in zip(arrays, crossed):
        lead = (2, Z * Y, 2) if over_section else (Z * Y, 2)
        shapes.append(jax.ShapeDtypeStruct(lead + array.shape, array.dtype))
    units = len(arrays) + sum(crossed)
    dma = pltpu.SemaphoreType.DMA
    return pl.pallas_call(
        functools.partial(gather_kernel, n, crossed),
        out_shape=shapes,
        in_specs=[ANY] * len(arrays),
        out_specs=[ANY] * len(arrays),
        scratch_shapes=[
            dma((units, max(Z - 1, 1))),
            dma((units, max(Z * (Y - 1), 1))),
            dma((units,)),
            dma((units,)),
            dma((units,)),
            dma((len(arrays),)),
            dma((len(arrays),)),
        ],
        compiler_params=pltpu.CompilerParams(collective_id=0, has_side_effects=True),
    )(*arrays)


def add_blocks(rows, terms, out, out_type):
    chunk = 16 if rows % 16 == 0 else rows

    def body(i, _):
        part = pl.ds(pl.multiple_of(i * chunk, chunk), chunk)
        total = terms[0][part, :].astype(f32)
        for term in terms[1:]:
            total = total + term[part, :].astype(f32)
        out[part, :] = total.astype(out_type)
        return _

    lax.fori_loop(0, rows // chunk, body, 0)


def scatter_kernel(n, count, *refs):
    sources, outs = refs[:count], refs[count : 2 * count]
    scratch = refs[2 * count :]
    mine, from_c, from_y, from_z = (scratch[k * count : (k + 1) * count] for k in range(4))
    l_sem, cs_sem, cr_sem, ys_sem, yr_sem, zs_sem, zr_sem = scratch[4 * count :]
    at = Place(n)
    Z, Y = at.Z, at.Y
    greet(at.partners()[:-1])

    c_copies, l_copies, y_copies, z_copies = [], [], [], []
    for i in range(count):
        copy = remote(
            sources[i].at[:, 1 - at.c],
            from_c[i],
            cs_sem.at[i],
            cr_sem.at[i],
            at.device(at.z, at.y, 1 - at.c),
        )
        copy.start()
        c_copies.append(copy)
        copy = pltpu.make_async_copy(sources[i].at[:, at.c], mine[i], l_sem.at[i])
        copy.start()
        l_copies.append(copy)

    def after_core(i):
        c_copies[i].wait_recv()
        l_copies[i].wait()
        rows = mine[i].shape[1]
        for k in list(range(1, Y)) + [0]:
            y = at.along_y(k)

            def per_z(z, _):
                zy = z * Y + y
                add_blocks(rows, [mine[i].at[zy], from_c[i].at[zy]], mine[i].at[zy], mine[i].dtype)
                return _

            lax.fori_loop(0, Z, per_z, 0)
            if k:
                for z in range(Z):
                    copy = remote(
                        mine[i].at[z * Y + y],
                        from_y[i].at[k - 1, z],
                        ys_sem.at[i, k - 1, z],
                        yr_sem.at[i, k - 1, z],
                        at.device(at.z, y, at.c),
                    )
                    copy.start()
                    y_copies.append(copy)

    def after_y(i):
        rows = mine[i].shape[1]
        for k in list(range(1, Z)) + [0]:
            z = at.along_z(k)
            block = mine[i].at[z * Y + at.y]
            for j in range(1, Y):
                arrival(from_y[i].at[j - 1, z], yr_sem.at[i, j - 1, z]).wait()
            terms = [block] + [from_y[i].at[j - 1, z] for j in range(1, Y)]
            add_blocks(rows, terms, block, mine[i].dtype)
            if k:
                copy = remote(
                    block,
                    from_z[i].at[k - 1],
                    zs_sem.at[i, k - 1],
                    zr_sem.at[i, k - 1],
                    at.device(z, at.y, at.c),
                )
                copy.start()
                z_copies.append(copy)

    def after_z(i):
        rows = mine[i].shape[1]
        for k in range(1, Z):
            arrival(from_z[i].at[k - 1], zr_sem.at[i, k - 1]).wait()
        terms = [mine[i].at[at.zy]] + [from_z[i].at[k - 1] for k in range(1, Z)]
        add_blocks(rows, terms, outs[i], outs[i].dtype)

    for turn in range(count + 2):
        if turn < count:
            after_core(turn)
        if 0 <= turn - 1 < count:
            after_y(turn - 1)
        if turn - 2 >= 0:
            after_z(turn - 2)
    for copy in c_copies + y_copies + z_copies:
        copy.wait_send()


def scatter(n, arrays, collective_id):
    Z, Y = factors(n)
    count = len(arrays)
    blocks = [a.shape[-2:] for a in arrays]
    arrays = [a.reshape((Z * Y, 2) + b) for a, b in zip(arrays, blocks)]
    dma = pltpu.SemaphoreType.DMA
    scratch = [pltpu.VMEM((Z * Y,) + b, a.dtype) for a, b in zip(arrays, blocks)]
    scratch += [pltpu.VMEM((Z * Y,) + b, a.dtype) for a, b in zip(arrays, blocks)]
    scratch += [pltpu.VMEM((max(Y - 1, 1), Z) + b, a.dtype) for a, b in zip(arrays, blocks)]
    scratch += [pltpu.VMEM((max(Z - 1, 1),) + b, a.dtype) for a, b in zip(arrays, blocks)]
    return pl.pallas_call(
        functools.partial(scatter_kernel, n, count),
        out_shape=[jax.ShapeDtypeStruct(b, f32) for b in blocks],
        in_specs=[ANY] * count,
        out_specs=[VMEM] * count,
        scratch_shapes=scratch
        + [
            dma((count,)),
            dma((count,)),
            dma((count,)),
            dma((count, max(Y - 1, 1), Z)),
            dma((count, max(Y - 1, 1), Z)),
            dma((count, max(Z - 1, 1))),
            dma((count, max(Z - 1, 1))),
        ],
        compiler_params=pltpu.CompilerParams(
            collective_id=collective_id, has_side_effects=True, vmem_limit_bytes=VMEM_LIMIT
        ),
    )(*arrays)


def scan_kernel(emb, wi, wr, ctx, keep, z_o, r_o, n_o, m_o, p_o, h_o, drive):
    R, H = ctx.shape[0], wr.shape[0]
    drive[...] = nt(emb[...], wi[...])

    def step(t, h):
        rows = pl.ds(pl.multiple_of(t * R, R), R)
        p = h * keep[rows, :]
        p_o[rows, :] = p
        rec = nn(p.astype(bf16), wr[...])
        d = drive[rows, :]
        z = jax.nn.sigmoid(d[:, :H] + rec[:, :H] + ctx[:, :H])
        r = jax.nn.sigmoid(d[:, H : 2 * H] + rec[:, H : 2 * H] + ctx[:, H : 2 * H])
        m = rec[:, 2 * H :] + ctx[:, 2 * H :]
        n = jnp.tanh(d[:, 2 * H :] + r * m)
        h = z * p + (1.0 - z) * n
        z_o[rows, :] = z
        r_o[rows, :] = r
        n_o[rows, :] = n
        m_o[rows, :] = m
        h_o[rows, :] = h.astype(bf16)
        return h

    lax.fori_loop(0, emb.shape[0] // R, step, jnp.zeros((R, H), f32))


def gru_forward(emb, wi, wr, ctx, keep):
    tokens, H = emb.shape[0], wr.shape[0]
    shape = jax.ShapeDtypeStruct
    return pl.pallas_call(
        scan_kernel,
        out_shape=[shape((tokens, H), f32)] * 5 + [shape((tokens, H), bf16)],
        in_specs=[VMEM] * 5,
        out_specs=[VMEM] * 6,
        scratch_shapes=[pltpu.VMEM((tokens, 3 * H), f32)],
        compiler_params=pltpu.CompilerParams(vmem_limit_bytes=VMEM_LIMIT),
    )(emb, wi, wr, ctx, keep)


def backward_kernel(sg, carry0, keep, z, r, n, m, p, wr, low_o, cand_o, sum_o):
    R, H = carry0.shape
    steps = sg.shape[0] // R

    def step(i, carry):
        rows = pl.ds(pl.multiple_of((steps - 1 - i) * R, R), R)
        g = sg[rows, :] + carry
        zz = z[rows, :]
        cand = n[rows, :]
        rr = r[rows, :]
        pc = g * (1.0 - zz) * (1.0 - cand * cand)
        pz = g * (p[rows, :] - cand) * zz * (1.0 - zz)
        pr = pc * m[rows, :] * rr * (1.0 - rr)
        rec = jnp.concatenate([pz, pr, pc * rr], axis=1)
        low = rec.astype(bf16)
        low_o[rows, :] = low
        cand_o[rows, :] = pc.astype(bf16)
        sum_o[...] += rec
        return (g * zz + nt(low, wr[...])) * keep[rows, :]

    sum_o[...] = jnp.zeros_like(sum_o)
    lax.fori_loop(0, steps, step, carry0[...])


def gru_backward(sg, carry0, keep, record, wr):
    z, r, n, m, p = record
    tokens, H = sg.shape
    shape = jax.ShapeDtypeStruct
    return pl.pallas_call(
        backward_kernel,
        out_shape=[
            shape((tokens, 3 * H), bf16),
            shape((tokens, H), bf16),
            shape((carry0.shape[0], 3 * H), f32),
        ],
        in_specs=[VMEM] * 9,
        out_specs=[VMEM] * 3,
        compiler_params=pltpu.CompilerParams(vmem_limit_bytes=VMEM_LIMIT),
    )(sg, carry0, keep, z, r, n, m, p, wr)


def finish_kernel(count, *refs):
    loss_in, loss_out = refs[0], refs[count]
    sources, outs, held = refs[1:count], refs[count + 1 : 2 * count], refs[2 * count : 3 * count - 1]
    in_sem, out_sem = refs[-2:]
    ins = [pltpu.make_async_copy(a, b, in_sem.at[k]) for k, (a, b) in enumerate(zip(sources, held))]
    puts = [pltpu.make_async_copy(a, b, out_sem.at[k]) for k, (a, b) in enumerate(zip(held, outs))]
    for copy in ins:
        copy.start()
    loss_out[0, 0] = jnp.max(loss_in[...])
    for copy, put in zip(ins, puts):
        copy.wait()
        put.start()
    for put in puts:
        put.wait()


def finish(loss, *arrays):
    shape = jax.ShapeDtypeStruct
    count = len(arrays)
    return pl.pallas_call(
        functools.partial(finish_kernel, count + 1),
        out_shape=[shape((1, 1), f32)] + [shape(a.shape, a.dtype) for a in arrays],
        in_specs=[VMEM] + [ANY] * count,
        out_specs=[pl.BlockSpec(memory_space=pltpu.SMEM)] + [ANY] * count,
        scratch_shapes=[pltpu.VMEM(a.shape, a.dtype) for a in arrays]
        + [pltpu.SemaphoreType.DMA((count,))] * 2,
        compiler_params=pltpu.CompilerParams(vmem_limit_bytes=16 * 2**20),
    )(loss, *arrays)


def request_slots(ids, n, per, slots):
    count = ids.shape[0]
    index = jnp.arange(count, dtype=jnp.int32)
    same = ids[:, None] == ids[None, :]
    first = jnp.min(jnp.where(same, index[None, :], count), axis=1)
    leads = first == index
    owner = ids // per
    ahead = (owner[:, None] == owner[None, :]) & leads[None, :] & (index[None, :] < first[:, None])
    rank = jnp.sum(ahead.astype(jnp.int32), axis=1)
    return leads, owner, rank, ids - owner * per


def round_maps(plan, turn, n, slots):
    leads, owner, rank, local = plan
    place = rank - turn * slots
    inside = (place >= 0) & (place < slots)
    place = jnp.where(inside, owner * slots + place, -1)
    hit = place[:, None] == jnp.arange(n * slots, dtype=jnp.int32)[None, :]
    asked = jnp.max(jnp.where(hit & leads[:, None], local[:, None], -1), axis=0)
    return asked, hit.astype(bf16)


def swap(x, n):
    shape = x.shape
    return lax.all_to_all(x.reshape((n, -1) + shape[1:]), "dp", 0, 0, tiled=False).reshape(shape)


def owner_map(asked, n, per):
    asked_here = swap(asked, n)
    return (asked_here[:, None] == jnp.arange(per, dtype=jnp.int32)[None, :]).astype(bf16)


def multiple(x, of):
    return pl.multiple_of(x, of)


class Unit:
    def __init__(self, index, src, dst, rows, base, y_first=False, stride=None):
        self.index, self.src, self.dst, self.rows, self.base = index, src, dst, rows, base
        self.y_first, self.stride = y_first, stride or rows

    def block(self, zy, c):
        return self.dst.at[pl.ds(multiple(self.base + (zy * 2 + c) * self.stride, 16), self.rows)]

    def some(self, count):
        return self.dst.at[pl.ds(0, count * self.rows)]


class Gather:
    def __init__(self, at, z_sem, y_sem, c_sem, s_sem):
        self.at, self.z_sem, self.y_sem, self.c_sem, self.s_sem = at, z_sem, y_sem, c_sem, s_sem

    def to_z(self, u, src, dst, z, slot):
        at = self.at
        remote(
            src,
            dst,
            self.s_sem.at[u.index],
            self.z_sem.at[u.index, slot],
            at.device(z, at.y, at.c),
        ).start()

    def to_y(self, u, src, dst, z):
        at = self.at
        remote(
            src,
            dst,
            self.s_sem.at[u.index],
            self.y_sem.at[u.index, z],
            at.device(at.z, at.along_y(1), at.c),
        ).start()

    def to_core(self, u, src, dst):
        at = self.at
        remote(
            src, dst, self.s_sem.at[u.index], self.c_sem.at[u.index], at.device(at.z, at.y, 1 - at.c)
        ).start()

    def begin(self, u):
        at = self.at
        dst = u.block(at.zy, at.c)
        if not u.y_first:
            self.to_z(u, u.src, dst, at.z_far(), 0)
        self.to_y(u, u.src, dst, at.z)
        self.to_core(u, u.src, dst)

    def by_z(self, u, z, y, slot):
        at = self.at
        block = u.block(z * at.Y + y, at.c)
        arrival(block, self.z_sem.at[u.index, slot]).wait()
        return block

    def by_y(self, u, z):
        at = self.at
        block = u.block(z * at.Y + at.along_y(1), at.c)
        arrival(block, self.y_sem.at[u.index, z]).wait()
        return block

    def step1(self, u):
        at = self.at
        far, near = at.z_far(), at.z_near()
        if u.y_first:
            self.to_z(u, u.src, u.block(at.zy, at.c), far, 0)
            block = self.by_y(u, at.z)
            self.to_z(u, block, block, far, 1)
            self.to_core(u, block, block)
            return
        self.to_z(u, u.src, u.block(at.zy, at.c), near, 1)
        block = self.by_z(u, far, at.y, 0)
        self.to_z(u, block, block, near, 2)
        self.to_y(u, block, block, far)
        self.to_core(u, block, block)

    def step2(self, u):
        at = self.at
        far, near = at.z_far(), at.z_near()
        other = at.along_y(1)
        if u.y_first:
            self.to_z(u, u.src, u.block(at.zy, at.c), near, 2)
            block = u.block(at.z * at.Y + other, at.c)
            self.to_z(u, block, block, near, 3)
            for slot, y in ((0, at.y), (1, other)):
                block = self.by_z(u, far, y, slot)
                self.to_z(u, block, block, near, 4 + slot)
                self.to_core(u, block, block)
            return
        for slot, z in ((1, near), (2, lax.rem(near + 2, 4))):
            block = self.by_z(u, z, at.y, slot)
            self.to_y(u, block, block, z)
            self.to_core(u, block, block)

    def step3(self, u):
        at = self.at
        far, near = at.z_far(), at.z_near()
        next_far = lax.rem(near + 2, 4)
        if u.y_first:
            other = at.along_y(1)
            for slot, z, y in (
                (2, near, at.y),
                (3, near, other),
                (4, next_far, at.y),
                (5, next_far, other),
            ):
                block = self.by_z(u, z, y, slot)
                self.to_core(u, block, block)
            return
        for z in (at.z, far, near, next_far):
            block = self.by_y(u, z)
            self.to_core(u, block, block)

    def ready(self, u):
        part = u.some(self.at.Z * self.at.Y)
        arrival(part, self.c_sem.at[u.index]).wait()

    def drain(self, u):
        part = u.some(2 * self.at.Z * self.at.Y - 1)
        arrival(part, self.s_sem.at[u.index]).wait()


class Chain(Gather):
    def on(self, u, src, dst, up, hops):
        at = self.at
        slot = hops - 1 if up else at.Z - 1 + hops - 1

        @pl.when(at.z < at.Z - 1 if up else at.z > 0)
        def _():
            remote(
                src,
                dst,
                self.on_sem.at[u.index],
                self.z_sem.at[u.index, slot],
                at.device(at.z + (1 if up else -1), at.y, at.c),
            ).start()

    def begin(self, u):
        at = self.at
        dst = u.block(at.zy, at.c)
        self.on(u, u.src, dst, True, 1)
        self.on(u, u.src, dst, False, 1)
        self.to_y(u, u.src, dst, at.z)
        self.to_core(u, u.src, dst)

    def pass_z(self, u, k):
        at = self.at
        for up in (True, False):
            z = at.z - k if up else at.z + k

            @pl.when(z >= 0 if up else z < at.Z)
            def _():
                slot = k - 1 if up else at.Z - 1 + k - 1
                block = self.by_z(u, z, at.y, slot)
                if k + 1 < at.Z:
                    self.on(u, block, block, up, k + 1)
                self.to_y(u, block, block, z)
                self.to_core(u, block, block)

    def drain(self, u):
        at = self.at
        part = u.some(2 * at.Z * at.Y - at.Z)
        arrival(part, self.s_sem.at[u.index]).wait()
        for z in range(at.Z):
            sent = (z + 1 if z < at.Z - 1 else 0) + (at.Z - z if z > 0 else 0)

            @pl.when(at.z == z)
            def _():
                part = u.some(sent)
                arrival(part, self.on_sem.at[u.index]).wait()


def column(ref, t):
    rows = ref.shape[2]
    square = (rows, rows)
    diagonal = lax.broadcasted_iota(jnp.int32, square, 0) == lax.broadcasted_iota(jnp.int32, square, 1)
    parts = []
    for k in range(ref.shape[1]):
        line = jnp.broadcast_to(ref[t, k : k + 1, :], square)
        parts.append(jnp.sum(jnp.where(diagonal, line, 0), axis=1, keepdims=True))
    return jnp.concatenate(parts, axis=0)


def forward_kernel(n, sizes, *refs):
    R, H, E, M, slots, per, words = sizes
    (
        asked_rows,
        own_most,
        hit,
        table,
        resets,
        words_in,
        wr_s,
        wi_s,
        sq_s,
        sm_s,
        cg_s,
        de_s,
        dc_s,
    ) = refs[:13]
    (
        wr_o,
        wi_o,
        sq_o,
        cg_o,
        de_o,
        dc_o,
        term_o,
        rec_o,
        h_h,
        emb_h,
        pre_h,
        tanh_h,
        ctx_h,
        owners_h,
        grad_o,
        loss_o,
        most_o,
    ) = refs[13:30]
    (
        asked_in,
        rows_out,
        came,
        wr,
        wi,
        sq,
        sm,
        cg,
        de,
        dc,
        drive,
        rec,
        wrt,
        smooth_in,
        grad_out,
        m_part,
        s_part,
        p_part,
        fullest,
        outer,
        h_o,
        emb_o,
        pre_o,
        tanh_o,
        ctx_o,
        owners_o,
        z_sem,
        y_sem,
        c_sem,
        s_sem,
        l_sem,
        o_sem,
        x_recv,
        x_send,
        as_sem,
        ar_sem,
        rs_sem,
        rr_sem,
        t_send,
        t_recv,
        k_sem,
        on_sem,
        keep,
        labels,
        asked,
    ) = refs[30:]
    at = Place(n)
    tokens = hit.shape[0]
    steps = tokens // R
    is_decoder = at.s == 1
    beside = (1 - at.s, at.d)
    others = [lax.rem(at.d + k, n) for k in range(1, n)]
    for d in range(n):
        asked[d, 0:1, :] = asked_rows[d : d + 1, :]
        asked[d, 1:2, :] = jnp.full((1, 128), own_most[0, 0], jnp.int32)
    greet([(at.s, d) for d in others] + [beside])

    def block_rows(ref, base, rows):
        return ref.at[pl.ds(multiple((base + at.d) * rows, 16), rows)]

    def to_beside(src, dst, k):
        return remote(src, dst, x_send.at[k], x_recv.at[k], beside)

    gather = Gather(at, z_sem, y_sem, c_sem, s_sem)
    chain = Chain(at, z_sem, y_sem, c_sem, s_sem)
    chain.on_sem = on_sem
    u_wi = Unit(1, wi_s, wi, wi_s.shape[0], 0)
    u_wr = Unit(0, wr_s, wr, wr_s.shape[0], 0)
    u_sq = Unit(2, sq_s, sq, sq_s.shape[0], 0)
    own_sm = Unit(3, sm_s, sm, words, 0)
    far_sm = Unit(4, block_rows(sm, n, words), sm, words, n * words)
    crossed = []
    for k, (src, dst) in enumerate([(cg_s, cg), (de_s, de)]):
        rows = src.shape[0]
        crossed.append(
            (
                Unit(3 + 2 * k, src, dst, rows, n * rows),
                Unit(4 + 2 * k, block_rows(dst, 0, rows), dst, rows, 0, k == 0),
            )
        )
    rows = cg_s.shape[0]
    far_block = block_rows(cg, 0, rows)
    cg_halves = [
        Unit(index, far_block.at[pl.ds(k * 16, 16)], cg, 16, k * 16, k == 0, rows)
        for k, index in enumerate((4, 7))
    ]
    rows = dc_s.shape[0]
    own_dc = Unit(5, dc_s, dc, rows, 0)
    far_dc = Unit(6, block_rows(dc, n, rows), dc, rows, n * rows)

    for d in others:
        remote(asked.at[d], asked_in.at[at.d], as_sem, ar_sem, (at.s, d)).start()
    chain.begin(u_wi)
    chain.begin(u_wr)

    @pl.when(is_decoder)
    def _():
        to_beside(dc_s, block_rows(dc, n, dc_s.shape[0]), 3).start()
        to_beside(sm_s, block_rows(sm, n, words), 0).start()

    @pl.when(jnp.logical_not(is_decoder))
    def _():
        for k, (src, dst) in enumerate([(cg_s, cg), (de_s, de)]):
            to_beside(src, block_rows(dst, 0, src.shape[0]), 1 + k).start()

    locals_ = [
        pltpu.make_async_copy(src, block_rows(dst, 0, src.shape[0]), l_sem.at[k])
        for k, (src, dst) in enumerate([(wr_s, wr), (wi_s, wi), (sq_s, sq)])
    ]
    locals_.append(pltpu.make_async_copy(sm_s, block_rows(sm, 0, words), l_sem.at[3]))
    for k, (src, dst) in enumerate([(cg_s, cg), (de_s, de)]):
        locals_.append(pltpu.make_async_copy(src, block_rows(dst, n, src.shape[0]), l_sem.at[4 + k]))
    locals_.append(pltpu.make_async_copy(dc_s, block_rows(dc, 0, dc_s.shape[0]), l_sem.at[6]))
    for copy in locals_:
        copy.start()

    for t in range(steps):
        rows = pl.ds(t * R, R)
        keep[rows, :] = 1.0 - column(resets, t).astype(f32)
        labels[rows, :] = column(words_in, t)

    chain.pass_z(u_wi, 1)
    chain.pass_z(u_wr, 1)
    some_asked = asked_in.at[pl.ds(0, n - 1)]
    arrival(some_asked, ar_sem).wait()
    asked_in[at.d] = asked[at.d]
    group = 128 // slots
    count = lax.broadcasted_iota(jnp.int32, (per, 128), 0)
    most = asked_in[0, 1:2, :]
    for g in range(n // group):
        wanted = asked_in[g * group, 0:1, :]
        for j in range(1, group):
            wanted = jnp.maximum(wanted, asked_in[g * group + j, 0:1, :])
        for j in range(group):
            most = jnp.maximum(most, asked_in[g * group + j, 1:2, :])
        match = (wanted == count).astype(f32).astype(bf16)
        owners_o[:, pl.ds(g * 128, 128)] = match
        rows_out[pl.ds(g * 128, 128), :] = tn(match, table[...]).astype(bf16)
    fullest[0] = jnp.broadcast_to(most, fullest.shape[1:])
    to_beside(fullest.at[0], fullest.at[1], 7).start()

    def slot_rows(ref, d):
        return ref.at[pl.ds(multiple(d * slots, 16), slots)]

    for d in others:
        remote(slot_rows(rows_out, d), slot_rows(came, at.d), rs_sem, rr_sem, (at.s, d)).start()
    cg_own = crossed[0][0]
    far_a, far_b = cg_halves
    de_own, de_far = crossed[1]
    for k in (2, 3):
        if k == 2:

            @pl.when(is_decoder)
            def _():
                arrival(far_block, x_recv.at[1]).wait()
                gather.begin(far_a)

        chain.pass_z(u_wi, k)
        chain.pass_z(u_wr, k)

    gather.step3(u_wi)

    @pl.when(is_decoder)
    def _():
        chain.begin(cg_own)
        chain.begin(far_b)
        gather.step1(far_a)

    @pl.when(jnp.logical_not(is_decoder))
    def _():
        gather.begin(u_sq)

    some_rows = came.at[pl.ds(0, (n - 1) * slots)]
    arrival(some_rows, rr_sem).wait()
    came[pl.ds(multiple(at.d * slots, 16), slots), :] = rows_out[
        pl.ds(multiple(at.d * slots, 16), slots), :
    ]
    emb_o[...] = nn(hit[...], came[...]).astype(bf16)
    to_beside(fullest.at[0], fullest.at[1], 7).wait()
    rank = jnp.max(jnp.maximum(fullest[0], fullest[1]))
    most_o[0, 0] = jnp.where(rank >= slots, 1, 0)
    for copy in locals_:
        copy.wait()
    chain.ready(u_wi)

    def input_drive(i, _):
        cols = pl.ds(multiple(i * 512, 512), 512)
        drive[:, cols] = nt(emb_o[...], wi[cols, :])
        return _

    lax.fori_loop(0, 3 * H // 512, input_drive, 0)
    @pl.when(is_decoder)
    def _():
        chain.pass_z(cg_own, 1)
        chain.pass_z(far_b, 1)

    gather.step3(u_wr)
    chain.ready(u_wr)

    def scan(ctx, service):
        def step(t, h):
            rows = pl.ds(multiple(t * R, R), R)
            p = h * keep[rows, :]
            rec[t, 4] = p
            mix = nn(p.astype(bf16), wr[...])
            d = drive[rows, :]
            z_in = d[:, :H] + mix[:, :H]
            r_in = d[:, H : 2 * H] + mix[:, H : 2 * H]
            m = mix[:, 2 * H :]
            if ctx is not None:
                z_in += ctx[:, :H]
                r_in += ctx[:, H : 2 * H]
                m += ctx[:, 2 * H :]
            z = jax.nn.sigmoid(z_in)
            r = jax.nn.sigmoid(r_in)
            cand = jnp.tanh(d[:, 2 * H :] + r * m)
            h = z * p + (1.0 - z) * cand
            rec[t, 0] = z
            rec[t, 1] = r
            rec[t, 2] = cand
            rec[t, 3] = m
            h_o[rows, :] = h.astype(bf16)
            for when, what in service:
                pl.when(t == when)(what)
            return h

        return lax.fori_loop(0, steps, step, jnp.zeros((R, H), f32))

    def keep_input_gates():
        copy = pltpu.make_async_copy(wi, wi_o, o_sem.at[0])
        copy.start()
        return copy

    def keep_transposed():
        def turn(i, _):
            part = pl.ds(multiple(i * 128, 128), 128)
            wrt[:, part] = wr[part, :].T
            return _

        lax.fori_loop(0, H // 128, turn, 0)
        copy = pltpu.make_async_copy(wrt, wr_o, o_sem.at[1])
        copy.start()
        return copy

    def keep_small(pairs):
        copies = [pltpu.make_async_copy(a, b, k_sem.at[k]) for k, a, b in pairs]
        for copy in copies:
            copy.start()
        return copies

    def end_requests(units, chained=()):
        arrival(some_asked, as_sem).wait()
        arrival(some_rows, rs_sem).wait()
        for u in (u_wi, u_wr) + chained:
            chain.drain(u)
        for u in units:
            gather.drain(u)

    last = pl.ds((steps - 1) * R, R)

    @pl.when(jnp.logical_not(is_decoder))
    def _():
        copies = [keep_input_gates()] + keep_small([(0, emb_o, emb_h), (1, owners_o, owners_h)])
        wide = (own_dc, far_dc, own_sm, far_sm)

        def begin_dc():
            gather.begin(own_dc)
            arrival(far_dc.src, x_recv.at[3]).wait()
            gather.begin(far_dc)

        def begin_far_sm():
            arrival(far_sm.src, x_recv.at[0]).wait()
            gather.begin(far_sm)

        def dc_step1():
            gather.step1(own_dc)
            gather.step1(far_dc)

        scan(
            None,
            [
                (1, lambda: gather.step1(u_sq)),
                (2, begin_dc),
                (5, lambda: gather.begin(own_sm)),
                (7, begin_far_sm),
                (8, lambda: gather.step2(u_sq)),
                (10, dc_step1),
            ],
        )
        gather.step3(u_sq)
        gather.ready(u_sq)
        ctx_tanh = jnp.tanh(nn(h_o[last, :], sq[...]))
        tanh_o[...] = ctx_tanh
        ctx_o[...] = ctx_tanh.astype(bf16)
        sends = [to_beside(ctx_o, ctx_o, 4)]
        sends[0].start()
        copies += [
            pltpu.make_async_copy(rec, rec_o, o_sem.at[2]),
            pltpu.make_async_copy(sq, sq_o, o_sem.at[3]),
        ]
        for copy in copies[-2:]:
            copy.start()
        copies += keep_small([(2, h_o, h_h), (3, tanh_o, tanh_h), (4, ctx_o, ctx_h)])
        gather.step1(own_sm)
        for u in wide[:2]:
            gather.step2(u)
        gather.step1(far_sm)
        gather.step2(own_sm)
        for u in wide[:2]:
            gather.step3(u)
        for u in wide[:2]:
            gather.ready(u)
        outer[...] = nn(ctx_o[...], dc[...])
        sends.append(to_beside(outer, outer, 8))
        sends[1].start()
        copies.append(pltpu.make_async_copy(dc, dc_o, o_sem.at[5]))
        copies[-1].start()
        copies.append(keep_transposed())
        gather.step2(far_sm)
        for u in wide[2:]:
            gather.step3(u)
        for u in wide[2:]:
            gather.ready(u)
        for send in sends:
            send.wait_send()
        for k, (src, dst) in enumerate([(cg_s, cg), (de_s, de)]):
            to_beside(src, block_rows(dst, 0, src.shape[0]), 1 + k).wait_send()
        end_requests((u_sq,) + wide)

        half = n * words
        ZY = at.Z * at.Y
        across = cg.shape[1] // M
        landed = cg.at[pl.ds(0, half // 4), pl.ds(0, 2 * M)]

        def term_block(j, zy, c):
            return sm.at[pl.ds(multiple((j * n + zy * 2 + c) * words, 16), words)]

        def landing(j, zy):
            place = j * ZY + zy
            rows = pl.ds(multiple(place // across * words, 16), words)
            return cg.at[rows, pl.ds(multiple(place % across * M, 128), M)]

        def core_send(j):
            for zy in range(ZY):
                remote(
                    term_block(j, zy, 1 - at.c),
                    landing(j, zy),
                    t_send.at[j],
                    t_recv.at[j],
                    at.device(at.z, at.y, 1 - at.c),
                ).start()

        arrival(smooth_in, x_recv.at[5]).wait()
        tile = half // 5 if half % 640 == 0 else 512
        lanes = lax.broadcasted_iota(jnp.int32, (tokens, 128), 1)
        m_part[...] = jnp.full(m_part.shape, -jnp.inf, f32)
        s_part[...] = jnp.zeros_like(s_part)
        p_part[...] = jnp.zeros_like(p_part)

        def tops(i, _):
            rows = pl.ds(multiple(i * tile, tile), tile)
            logits = nt(smooth_in[...], sm[rows, :])
            parts = [logits[:, k * 128 : (k + 1) * 128] for k in range(tile // 128)]
            before = m_part[...]
            top = before
            for part in parts:
                top = jnp.maximum(top, part)
            total = s_part[...] * jnp.exp(before - top)
            picked = p_part[...]
            for k, part in enumerate(parts):
                total += jnp.exp(part - top)
                picked += jnp.where(lanes == labels[...] - (i * tile + k * 128), part, 0.0)
            m_part[...] = top
            s_part[...] = total
            p_part[...] = picked
            return _

        lax.fori_loop(0, 2 * n * words // tile, tops, 0)
        top = jnp.max(m_part[...], axis=1, keepdims=True)
        total = jnp.sum(s_part[...] * jnp.exp(m_part[...] - top), axis=1, keepdims=True)
        log_norm = top + jnp.log(total)
        picked = jnp.sum(p_part[...], axis=1, keepdims=True)
        scale = 1.0 / (R * n)
        loss = jnp.sum(log_norm - picked, axis=0, keepdims=True) * scale
        loss_o[...] = jnp.broadcast_to(loss, loss_o.shape)
        m_part[...] = jnp.broadcast_to(log_norm, m_part.shape)
        drive[:, pl.ds(0, M)] = jnp.zeros((tokens, M), f32)

        def grads(i, _):
            rows = pl.ds(multiple(i * tile, tile), tile)
            weight = sm[rows, :]
            logits = nt(smooth_in[...], weight)
            low = []
            for k in range(tile // 128):
                part = jnp.exp(logits[:, k * 128 : (k + 1) * 128] - m_part[...])
                hits = lanes == labels[...] - (i * tile + k * 128)
                low.append(((part - jnp.where(hits, 1.0, 0.0)) * scale).astype(bf16))
            low = jnp.concatenate(low, axis=1)
            drive[:, pl.ds(0, M)] += nn(low, weight)
            sm[rows, :] = tn(low, smooth_in[...]).astype(bf16)
            pl.when(i == half // tile)(lambda: core_send(0))
            return _

        lax.fori_loop(0, 2 * n * words // tile, grads, 0)
        grad_out[...] = drive[:, pl.ds(0, M)].astype(bf16)
        send = to_beside(grad_out, grad_o, 6)
        send.start()
        core_send(1)
        for j in (0, 1):
            arrival(landed, t_recv.at[j]).wait()

            def add(zy, _):
                block = term_block(j, zy, at.c)
                add_blocks(words, [block, landing(j, zy)], block, bf16)
                pltpu.make_async_copy(block, term_o.at[j, zy], o_sem.at[4]).start()
                return _

            lax.fori_loop(0, ZY, add, 0)
        for j in (0, 1):
            arrival(landed, t_send.at[j]).wait()
        arrival(term_o, o_sem.at[4]).wait()
        send.wait_send()
        for copy in copies:
            copy.wait()

    @pl.when(is_decoder)
    def _():
        copies = [keep_input_gates()] + keep_small([(0, emb_o, emb_h), (1, owners_o, owners_h)])
        rest = [de_own, de_far]
        chain.pass_z(cg_own, 2)
        chain.pass_z(far_b, 2)
        gather.step2(far_a)
        chain.pass_z(cg_own, 3)
        chain.pass_z(far_b, 3)
        gather.begin(u_sq)
        gather.begin(de_own)
        arrival(de_far.src, x_recv.at[2]).wait()
        gather.begin(de_far)
        gather.step3(far_a)
        gather.step3(cg_own)
        gather.step3(far_b)
        for u in (cg_own, far_a, far_b):
            gather.ready(u)
        copies.append(pltpu.make_async_copy(cg, cg_o, o_sem.at[2]))
        copies[-1].start()
        arrival(ctx_o, x_recv.at[4]).wait()
        service = [
            (1, functools.partial(gather.step1, u_sq)),
            (2, functools.partial(gather.step1, de_own)),
            (3, functools.partial(gather.step1, de_far)),
            (6, functools.partial(gather.step2, u_sq)),
            (8, functools.partial(gather.step2, de_own)),
            (9, functools.partial(gather.step2, de_far)),
        ]
        ctx = nn(ctx_o[...], cg[...])
        scan(ctx, service)
        for u in [u_sq] + rest:
            gather.step3(u)
        for u in [u_sq] + rest:
            gather.ready(u)
        later = [(rec, rec_o), (sq, sq_o), (de, de_o)]
        later = [
            pltpu.make_async_copy(a, b, o_sem.at[3 + k]) for k, (a, b) in enumerate(later)
        ]
        for copy in later:
            copy.start()
        copies += later
        copies += keep_small([(2, h_o, h_h), (4, ctx_o, ctx_h)])
        pre = nn(h_o[...], sq[...]) + nt(emb_o[...], de[...])
        arrival(outer, x_recv.at[8]).wait()
        pre = (pre.reshape(steps, R, 2 * M) + outer[...][None]).reshape(tokens, 2 * M)
        pre_o[...] = pre
        copies += keep_small([(5, pre_o, pre_h)])
        a, b = pre[:, :M], pre[:, M:]
        high = jnp.maximum(a, b)
        smooth = high + jnp.log(jnp.exp(a - high) + jnp.exp(b - high))
        grad_out[...] = smooth.astype(bf16)
        send = to_beside(grad_out, smooth_in, 5)
        send.start()
        copies.append(keep_transposed())
        send.wait_send()
        to_beside(sm_s, block_rows(sm, n, words), 0).wait_send()
        to_beside(dc_s, block_rows(dc, n, dc_s.shape[0]), 3).wait_send()
        end_requests((u_sq, far_a, de_own, de_far), (cg_own, far_b))
        arrival(grad_o, x_recv.at[6]).wait()
        for copy in copies:
            copy.wait()


def forward(n, sizes, asked, fullest, hit, table, resets, targets, shards):
    R, H, E, M, slots, per, words = sizes
    Z, Y = factors(n)
    tokens = hit.shape[0]
    shape = jax.ShapeDtypeStruct
    dma = pltpu.SemaphoreType.DMA
    units = 9
    cg_rows, de_rows, dc_rows = H, 2 * M, H
    return pl.pallas_call(
        functools.partial(forward_kernel, n, sizes),
        out_shape=[
            shape((3 * H, H), bf16),
            shape((3 * H, E), bf16),
            shape((H, H), bf16),
            shape((cg_rows, 3 * H), bf16),
            shape((de_rows, E), bf16),
            shape((dc_rows, 2 * M), bf16),
            shape((2, Z * Y, words, M), bf16),
            shape((tokens // R, 5, R, H), f32),
            shape((tokens, H), bf16),
            shape((tokens, E), bf16),
            shape((tokens, 2 * M), f32),
            shape((R, H), f32),
            shape((R, H), bf16),
            shape((per, n * slots), bf16),
            shape((tokens, M), bf16),
            shape((8, 128), f32),
            shape((1, 1), jnp.int32),
        ],
        in_specs=[VMEM, pl.BlockSpec(memory_space=pltpu.SMEM)] + [VMEM] * 4 + [ANY] * 7,
        out_specs=[ANY] * 14 + [VMEM] * 2 + [pl.BlockSpec(memory_space=pltpu.SMEM)],
        scratch_shapes=[
            pltpu.VMEM((n, 8, 128), jnp.int32),
            pltpu.VMEM((n * slots, E), bf16),
            pltpu.VMEM((n * slots, E), bf16),
            pltpu.VMEM((H, 3 * H), bf16),
            pltpu.VMEM((3 * H, E), bf16),
            pltpu.VMEM((H, H), bf16),
            pltpu.VMEM((2 * n * words, M), bf16),
            pltpu.VMEM((cg_rows, 3 * H), bf16),
            pltpu.VMEM((de_rows, E), bf16),
            pltpu.VMEM((dc_rows, 2 * M), bf16),
            pltpu.VMEM((tokens, 3 * H), f32),
            pltpu.VMEM((tokens // R, 5, R, H), f32),
            pltpu.VMEM((3 * H, H), bf16),
            pltpu.VMEM((tokens, M), bf16),
            pltpu.VMEM((tokens, M), bf16),
            pltpu.VMEM((tokens, 128), f32),
            pltpu.VMEM((tokens, 128), f32),
            pltpu.VMEM((tokens, 128), f32),
            pltpu.VMEM((2, 8, 128), jnp.int32),
            pltpu.VMEM((R, 2 * M), f32),
            pltpu.VMEM((tokens, H), bf16),
            pltpu.VMEM((tokens, E), bf16),
            pltpu.VMEM((tokens, 2 * M), f32),
            pltpu.VMEM((R, H), f32),
            pltpu.VMEM((R, H), bf16),
            pltpu.VMEM((per, n * slots), bf16),
            dma((units, 6)),
            dma((units, Z)),
            dma((units,)),
            dma((units,)),
            dma((7,)),
            dma((7,)),
            dma((10,)),
            dma((10,)),
            dma,
            dma,
            dma,
            dma,
            dma((2,)),
            dma((2,)),
            dma((6,)),
            dma((units,)),
            pltpu.VMEM((tokens, 1), f32),
            pltpu.VMEM((tokens, 1), jnp.int32),
            pltpu.VMEM((n, 8, 128), jnp.int32),
        ],
        compiler_params=pltpu.CompilerParams(
            collective_id=2, has_side_effects=True, vmem_limit_bytes=VMEM_LIMIT
        ),
    )(asked, fullest, hit, table, resets, targets, *shards)


class Sum:
    def __init__(self, at, sems, index, mine, theirs, from_c, from_y, from_z, wholes, rows, out):
        self.at, self.sems, self.index = at, sems, index
        self.mine, self.theirs = mine, theirs
        self.from_c, self.from_y, self.from_z = from_c, from_y, from_z
        self.wholes, self.rows, self.out = wholes, rows, out

    def begin(self):
        at, i = self.at, self.index
        cs, cr = self.sems[:2]
        for zy in range(at.Z * at.Y):
            remote(
                self.theirs(zy), self.from_c(zy), cs.at[i], cr.at[i], at.device(at.z, at.y, 1 - at.c)
            ).start()

    def to_y(self, k, source):
        at, i = self.at, self.index
        ys, yr = self.sems[2:4]
        y = at.along_y(k)
        for z in range(at.Z):
            remote(
                source(z * at.Y + y),
                self.from_y(k, z),
                ys.at[i],
                yr.at[i, k - 1, z],
                at.device(at.z, y, at.c),
            ).start()

    def after_core(self):
        at, i = self.at, self.index
        arrival(self.wholes[0], self.sems[1].at[i]).wait()
        for k in list(range(1, at.Y)) + [0]:
            y = at.along_y(k)

            def per_z(z, _):
                zy = z * at.Y + y
                block = self.mine(zy)
                add_blocks(self.rows, [block, self.from_c(zy)], block, block.dtype)
                return _

            lax.fori_loop(0, at.Z, per_z, 0)
            if k:
                self.to_y(k, self.mine)

    def to_z(self, target, z, slot):
        at, i = self.at, self.index
        zs, zr = self.sems[4:6]
        remote(
            self.mine(target * at.Y + at.y),
            self.from_z(slot),
            zs.at[i],
            zr.at[i, slot],
            at.device(z, at.y, at.c),
        ).start()

    def after_y(self):
        at, i = self.at, self.index
        yr = self.sems[3]

        def per_z(z, _):
            block = self.mine(z * at.Y + at.y)
            came = [self.from_y(j, z) for j in range(1, at.Y)]
            for j, part in enumerate(came):
                arrival(part, yr.at[i, j, z]).wait()
            add_blocks(self.rows, [block] + came, block, block.dtype)
            return _

        lax.fori_loop(0, at.Z, per_z, 0)

        near = at.z_near()
        self.to_z(lax.rem(near + 2, 4), near, 0)
        self.to_z(near, near, 1)

    def add_z(self, target, slot):
        at, i = self.at, self.index
        part = self.from_z(slot)
        arrival(part, self.sems[5].at[i, slot]).wait()
        block = self.mine(target * at.Y + at.y)
        add_blocks(self.rows, [block, part], block, block.dtype)

    def mid_z(self):
        far = self.at.z_far()
        self.add_z(far, 0)
        self.to_z(far, far, 2)

    def after_z(self):
        at, i = self.at, self.index
        cs, _, ys, _, zs, zr = self.sems
        came = [self.from_z(slot) for slot in (1, 2)]
        for slot, part in zip((1, 2), came):
            arrival(part, zr.at[i, slot]).wait()
        add_blocks(self.rows, [self.mine(at.zy)] + came, self.out, self.out.dtype)
        for whole, sem in zip(self.wholes, (cs, ys, zs)):
            if whole is not None:
                arrival(whole, sem.at[i]).wait()


class SumZFirst(Sum):
    def after_core(self):
        at, i = self.at, self.index
        arrival(self.wholes[0], self.sems[1].at[i]).wait()

        def per_zy(zy, _):
            block = self.mine(zy)
            add_blocks(self.rows, [block, self.from_c(zy)], block, block.dtype)
            return _

        lax.fori_loop(0, at.Z * at.Y, per_zy, 0)
        self.to_near(self.mine)

    def to_near(self, source):
        at, i = self.at, self.index
        near = at.z_near()
        ys, yr = self.sems[2:4]
        for k, target in enumerate((lax.rem(near + 2, 4), near)):
            for y in range(at.Y):
                remote(
                    source(target * at.Y + y),
                    self.from_y(1, 2 * k + y),
                    ys.at[i],
                    yr.at[i, 0, 2 * k + y],
                    at.device(near, at.y, at.c),
                ).start()

    def add(self, zy, part, sem):
        arrival(part, sem).wait()
        block = self.mine(zy)
        add_blocks(self.rows, [block, part], block, block.dtype)

    def after_near(self):
        at, i = self.at, self.index
        yr, zs, zr = self.sems[3:6]
        far = at.z_far()
        for k, target in enumerate((far, at.z)):
            for y in range(at.Y):
                self.add(target * at.Y + y, self.from_y(1, 2 * k + y), yr.at[i, 0, 2 * k + y])
                if k == 0:
                    remote(
                        self.mine(far * at.Y + y),
                        self.from_z(y),
                        zs.at[i],
                        zr.at[i, y],
                        at.device(far, at.y, at.c),
                    ).start()

    def after_far(self):
        at, i = self.at, self.index
        zs, zr = self.sems[4:6]
        for y in range(at.Y):
            self.add(at.z * at.Y + y, self.from_z(y), zr.at[i, y])
        other = at.along_y(1)
        remote(
            self.mine(at.z * at.Y + other),
            self.from_z(2),
            zs.at[i],
            zr.at[i, 2],
            at.device(at.z, other, at.c),
        ).start()

    def finish(self):
        at, i = self.at, self.index
        cs, _, ys, _, zs, zr = self.sems
        part = self.from_z(2)
        arrival(part, zr.at[i, 2]).wait()
        add_blocks(self.rows, [self.mine(at.zy), part], self.out, self.out.dtype)
        for whole, sem in zip(self.wholes, (cs, ys, zs)):
            if whole is not None:
                arrival(whole, sem.at[i]).wait()


def backward_kernel_all(n, sizes, *refs):
    R, H, E, M, slots, per, words = sizes
    (
        pre,
        grad,
        resets,
        tanh,
        context,
        loss,
        h_h,
        emb_h,
        hit_h,
        owners_h,
        wr_h,
        wi_h,
        sq_h,
        cg_h,
        de_h,
        dc_h,
        term_h,
        rec_h,
    ) = refs[:18]
    (
        table_h,
        input_h,
        recur_h,
        square_h,
        gates_h,
        deep_h,
        context_h,
        soft_h,
        loss_h,
        early_h,
        late_h,
    ) = refs[18:29]
    (
        wrt,
        wi,
        sq,
        de,
        dc,
        big,
        rec,
        low,
        cand,
        before,
        state_grad,
        total,
        deep_low,
        outer_low,
        early_pack,
        late_pack,
        c_grad,
        c_came,
        pre_low,
        g_out,
        g_in,
        wide_c,
        wide_y,
        wide_z,
        thin_c,
        thin_y,
        thin_z,
        deep_c,
        deep_y,
        deep_z,
        soft_far,
        deep_far,
        far_rows,
        block_rows,
        chunks,
        ctx_cols,
        losses,
        loss_sum,
        cs_sem,
        cr_sem,
        ys_sem,
        yr_sem,
        zs_sem,
        zr_sem,
        pz_sem,
        py_sem,
        pc_sem,
        ps_sem,
        load_sem,
        rec_sem,
        big_sem,
        chunk_sem,
        x_send,
        x_recv,
        ls_sem,
        lr_sem,
        gs_sem,
        gr_sem,
        h,
        emb,
        hit,
        owners,
        small_sem,
        table_o,
        input_o,
        recur_o,
        square_o,
        gates_o,
        deep_o,
        context_o,
        soft_o,
        loss_o,
        put_sem,
        keep,
    ) = refs[29:]
    at = Place(n)
    Z, Y = at.Z, at.Y
    ZY = Z * Y
    tokens = emb.shape[0]
    steps = tokens // R
    is_decoder = at.s == 1
    beside = (1 - at.s, at.d)
    others = [lax.rem(at.d + k, n) for k in range(1, n)]
    sems = (cs_sem, cr_sem, ys_sem, yr_sem, zs_sem, zr_sem)

    loads = [
        pltpu.make_async_copy(a, b, load_sem.at[k])
        for k, (a, b) in enumerate([(sq_h, sq), (wr_h, wrt), (wi_h, wi)])
    ]
    for copy in loads:
        copy.start()
    small = [
        pltpu.make_async_copy(a, b, small_sem.at[k])
        for k, (a, b) in enumerate([(h_h, h), (emb_h, emb), (hit_h, hit), (owners_h, owners)])
    ]
    for copy in small:
        copy.start()
    load_de = pltpu.make_async_copy(de_h, de, load_sem.at[3])
    load_dc = pltpu.make_async_copy(dc_h, dc, load_sem.at[4])

    def load_record(i):
        return pltpu.make_async_copy(
            rec_h.at[steps - 1 - i], rec.at[lax.rem(i, 2)], rec_sem.at[lax.rem(i, 2)]
        )

    load_record(0).start()
    for t in range(steps):
        keep[pl.ds(t * R, R), :] = 1.0 - column(resets, t).astype(f32)
    greet([(at.s, d) for d in others] + [beside])

    def to_beside(src, dst, k):
        return remote(src, dst, x_send.at[k], x_recv.at[k], beside)

    def block_sum(index, term, rows, stride, off, bufs, slot, out, kind=Sum):
        c_buf, y_buf, z_buf = bufs

        def block(zy, c):
            return term.at[pl.ds(multiple(off + (zy * 2 + c) * stride, 16), rows)]

        return kind(
            at,
            sems,
            index,
            lambda zy: block(zy, at.c),
            lambda zy: block(zy, 1 - at.c),
            lambda zy: c_buf.at[slot, zy],
            lambda k, z: y_buf.at[slot, k - 1, z],
            lambda k: z_buf.at[slot, k],
            (c_buf.at[slot], y_buf.at[slot], z_buf.at[slot]),
            rows,
            out,
        )

    wide, thin, deep = (wide_c, wide_y, wide_z), (thin_c, thin_y, thin_z), (deep_c, deep_y, deep_z)
    tall = recur_o.shape[0]
    recur_sums = [
        block_sum(g, wrt, tall, tall, g * H, wide, g, recur_o.at[:, pl.ds(g * H, H)])
        for g in range(3)
    ]
    square_by_y, square_by_z = (
        block_sum(3, sq, tall, tall, 0, wide, 3, square_o, kind) for kind in (Sum, SumZFirst)
    )
    high = input_o.shape[0]
    part = thin_c.shape[2]
    input_sums = [
        block_sum(4 + j, wi, part, high, j * part, thin, j, input_o.at[pl.ds(j * part, part)])
        for j in range(high // part)
    ]
    after = 4 + high // part
    deep_rows = deep_far.shape[0]
    deep_sums = [
        block_sum(
            after + j, de, deep_rows, deep_rows, j * n * deep_rows, deep, j, (deep_far, deep_o)[j]
        )
        for j in range(2)
    ]

    def big_rows(first, count):
        return big.at[pl.ds(multiple(first * words, 16), count * words)]

    def soft_sum(j):
        base_y, base_z = 2 * Z, 2 * Z + 2 * (Y - 1) * Z

        def mine(zy):
            if j == 0:
                apart = zy // Y - at.z
                return big_rows((1 - apart * apart // 4) * Y + zy % Y, 1)
            return big_rows(Z + zy // Y, 1)

        return (SumZFirst, Sum)[j](
            at,
            sems,
            after + 2 + j,
            mine,
            None,
            None,
            lambda k, z: big_rows(base_y + (j * (Y - 1) + k - 1) * Z + z, 1),
            lambda k: big_rows(base_z + j * 3 + k, 1),
            (
                None,
                big_rows(base_y + j * (Y - 1) * Z, (Y - 1) * Z),
                big_rows(base_z + j * 3, 3),
            ),
            words,
            (soft_o, soft_far)[j],
        )

    soft_sums = [soft_sum(0), soft_sum(1)]

    def scan(first, with_state, service):
        def step(i, carry):
            t = steps - 1 - i
            rows = pl.ds(multiple(t * R, R), R)
            slot = lax.rem(i, 2)

            @pl.when(i + 1 < steps)
            def _():
                load_record(i + 1).start()

            load_record(i).wait()
            g = carry + state_grad[rows, :] if with_state else carry
            z, r, c, m, p = (rec[slot, k] for k in range(5))
            pc = g * (1.0 - z) * (1.0 - c * c)
            pz = g * (p - c) * z * (1.0 - z)
            pr = pc * m * r * (1.0 - r)
            pn = pc * r
            parts = [pz, pr, pn]
            back = g * z
            for k, x in enumerate(parts):
                x_low = x.astype(bf16)
                low[rows, pl.ds(k * H, H)] = x_low
                back += nn(x_low, wrt[pl.ds(k * H, H), :])
                if with_state:
                    total[:, pl.ds(k * H, H)] += x
            cand[rows, :] = pc.astype(bf16)
            before[rows, :] = p.astype(bf16)
            for when, what in service:
                pl.when(i == when)(what)
            return back * keep[rows, :]

        lax.fori_loop(0, steps, step, first)

    def recur_term(g):
        cols = pl.ds(g * H, H)

        def body(i, _):
            some = pl.ds(multiple(i * 256, 256), 256)
            rows = pl.ds(multiple(g * H + i * 256, 256), 256)
            wrt[rows, :] = tn(before[:, some], low[:, cols]).astype(bf16)
            return _

        lax.fori_loop(0, H // 256, body, 0)

    def input_term():
        def body(i, _):
            some = pl.ds(multiple(i * 256, 256), 256)
            wi[some, :] = tn(low[:, some], emb[...]).astype(bf16)
            return _

        lax.fori_loop(0, 2 * H // 256, body, 0)

        def last(i, _):
            some = pl.ds(multiple(i * 256, 256), 256)
            rows = pl.ds(multiple(2 * H + i * 256, 256), 256)
            wi[rows, :] = tn(cand[:, some], emb[...]).astype(bf16)
            return _

        lax.fori_loop(0, H // 256, last, 0)

    def slot_rows(ref, d):
        return ref.at[pl.ds(multiple(d * slots, 16), slots)]

    def give(extra):
        grads = nn(low[:, pl.ds(0, 2 * H)], wi[pl.ds(0, 2 * H), :])
        grads += nn(cand[...], wi[pl.ds(2 * H, H), :])
        if extra:
            grads += nn(deep_low[...], de[...])
        g_out[...] = tn(hit[...], grads.astype(bf16)).astype(bf16)
        for d in others:
            remote(slot_rows(g_out, d), slot_rows(g_in, at.d), gs_sem, gr_sem, (at.s, d)).start()

    def take():
        own = pl.ds(multiple(at.d * slots, 16), slots)
        some = g_in.at[pl.ds(0, (n - 1) * slots)]
        arrival(some, gr_sem).wait()
        arrival(some, gs_sem).wait()
        g_in[own, :] = g_out[own, :]
        table_o[...] = nn(owners[...], g_in[...])

    puts = []

    def put(src, dst):
        copy = pltpu.make_async_copy(src, dst, put_sem.at[len(puts)])
        copy.start()
        puts.append(copy)

    def thirds(ref, g):
        return ref.at[:, pl.ds(g * H, H)]

    places = {id(recur_sums[g]): (thirds(recur_o, g), thirds(recur_h, g)) for g in range(3)}
    for j, item in enumerate(input_sums):
        rows = pl.ds(j * part, part)
        places[id(item)] = (input_o.at[rows], input_h.at[rows])

    def end_sums(before, between=None):
        items = list(before) + list(input_sums)
        at_y, at_mid, at_end = len(before), max(len(before) - 1, 0), 0
        while at_end < len(items):
            if at_y < len(items):
                items[at_y].after_y()
                at_y += 1
                if at_y == len(items) and between:
                    between()
            if at_mid < min(at_y - 1, len(items)) or at_y == len(items) > at_mid:
                items[at_mid].mid_z()
                at_mid += 1
            if at_end < at_mid - 1 or at_mid == len(items):
                items[at_end].after_z()
                put(*places[id(items[at_end])])
                at_end += 1

    @pl.when(jnp.logical_not(is_decoder))
    def _():
        puts.clear()
        load_dc.start()
        by_z, by_y = soft_sums
        by_z.to_near(lambda zy: term_h.at[0, zy])
        by_y.to_y(1, lambda zy: term_h.at[1, zy])
        for y in range(Y):
            for z in (at.z_far(), at.z):
                zy = z * Y + y
                pltpu.make_async_copy(term_h.at[0, zy], by_z.mine(zy), big_sem.at[0]).start()
        for z in range(Z):
            zy = z * Y + at.y
            pltpu.make_async_copy(term_h.at[1, zy], by_y.mine(zy), big_sem.at[1]).start()
        losses[at.d] = loss[...]
        for d in others:
            remote(loss, losses.at[at.d], ls_sem, lr_sem, (at.s, d)).start()
        for j, item in enumerate(soft_sums):
            whole = big_rows(j * Z, Z)
            arrival(whole, big_sem.at[j]).wait()
        for copy in loads:
            copy.wait()
        load_dc.wait()
        arrival(outer_low, x_recv.at[6]).wait()
        back = nt(outer_low[...], dc[...])
        arrival(c_came, x_recv.at[0]).wait()
        c = tanh[...]
        c_low = (back + c_came[...].astype(f32)).astype(bf16).astype(f32)
        pre_low[...] = (c_low * (1.0 - c * c)).astype(bf16)
        first = nt(pre_low[...], sq[...])

        def square_term():
            sq[...] = tn(h[pl.ds((steps - 1) * R, R), :], pre_low[...]).astype(bf16)
            square_by_y.begin()

        small[0].wait()
        scan(
            first,
            False,
            [
                (1, square_term),
                (3, by_z.after_near),
                (5, square_by_y.after_core),
                (7, by_y.after_y),
            ],
        )
        for copy in small[1:]:
            copy.wait()
        for g in range(3):
            recur_term(g)
            recur_sums[g].begin()
            if g:
                recur_sums[g - 1].after_core()
        by_z.after_far()
        give(False)
        recur_sums[2].after_core()
        input_term()
        for item in input_sums:
            item.begin()
        square_by_y.after_y()
        for item in input_sums:
            item.after_core()
        by_y.mid_z()
        recur_sums[0].after_y()
        square_by_y.mid_z()
        recur_sums[1].after_y()
        recur_sums[0].mid_z()
        by_y.after_z()
        send = to_beside(soft_far, soft_o, 1)
        send.start()
        some = losses.at[pl.ds(0, n - 1)]
        arrival(some, lr_sem).wait()
        arrival(some, ls_sem).wait()
        all_loss = losses[0]
        for d in range(1, n):
            all_loss += losses[d]
        loss_sum[...] = all_loss
        loss_o[...] = all_loss
        put(loss_o, loss_h)
        loss_send = to_beside(loss_sum, loss_o, 2)
        loss_send.start()
        recur_sums[2].after_y()
        recur_sums[1].mid_z()
        recur_sums[0].after_z()
        put(*places[id(recur_sums[0])])
        take()
        put(table_o, table_h)
        square_by_y.after_z()
        put(square_o, square_h)

        def finish_soft():
            by_z.finish()
            put(soft_o, soft_h)

        end_sums([recur_sums[1], recur_sums[2]], finish_soft)
        send.wait_send()
        loss_send.wait_send()
        arrival(gates_o, x_recv.at[4]).wait()
        put(gates_o, gates_h)
        arrival(context_o, x_recv.at[5]).wait()
        put(context_o, context_h)
        arrival(deep_o, x_recv.at[3]).wait()
        put(deep_o, deep_h)
        for copy in puts:
            copy.wait()

    @pl.when(is_decoder)
    def _():
        puts.clear()
        load_de.start()
        chunk = big.shape[1]
        for k in range(3 * H // chunk):
            pltpu.make_async_copy(
                cg_h.at[:, pl.ds(k * chunk, chunk)], big.at[pl.ds(k * H, H)], big_sem.at[0]
            ).start()
        a, b = pre[:, pl.ds(0, M)], pre[:, pl.ds(M, M)]
        high = jnp.maximum(a, b)
        smooth = high + jnp.log(jnp.exp(a - high) + jnp.exp(b - high))
        sg = grad[...].astype(f32)
        for k, x in enumerate((a, b)):
            cols = pl.ds(k * M, M)
            deep_grad = sg * jnp.exp(x - smooth)
            deep_low[:, cols] = deep_grad.astype(bf16)
            outer_low[:, cols] = jnp.sum(deep_grad.reshape(steps, R, M), axis=0).astype(bf16)
        outer_send = to_beside(outer_low, outer_low, 6)
        outer_send.start()
        for copy in loads:
            copy.wait()
        state_grad[...] = nt(deep_low[...], sq[...])
        total[...] = jnp.zeros_like(total)
        gather = Gather(at, pz_sem, py_sem, pc_sem, ps_sem)
        early = Unit(0, early_pack, early_h, R, 0)
        late = Unit(1, late_pack, late_h, R, 0)
        early_pack[:, pl.ds(0, H)] = context[...]
        early_pack[:, pl.ds(H, 2 * M)] = outer_low[...]
        own_copies = [
            pltpu.make_async_copy(early_pack, early.block(at.zy, at.c), big_sem.at[1]),
            pltpu.make_async_copy(late_pack, late.block(at.zy, at.c), big_sem.at[2]),
        ]
        own_copies[0].start()
        gather.begin(early)
        scan(
            jnp.zeros((R, H), f32),
            True,
            [
                (10, lambda: gather.step1(early)),
            ],
        )
        late_pack[...] = total[...].astype(bf16)
        gates_rows = big.at[pl.ds(0, 3 * H * H // chunk)]
        arrival(gates_rows, big_sem.at[0]).wait()
        for k in range(3 * H // chunk):
            cols = pl.ds(k * chunk, chunk)
            term = nt(late_pack[:, cols], big[pl.ds(k * H, H), :])
            back = term if k == 0 else back + term
        c_grad[...] = back.astype(bf16)
        send = to_beside(c_grad, c_came, 0)
        send.start()
        gather.step2(early)
        own_copies[1].start()
        gather.begin(late)
        for copy in small:
            copy.wait()
        for g in range(3):
            recur_term(g)
            recur_sums[g].begin()
            if g:
                recur_sums[g - 1].after_core()
        gather.step1(late)
        load_de.wait()
        give(True)
        recur_sums[2].after_core()
        sq[...] = tn(h[...], deep_low[...]).astype(bf16)
        square_by_z.begin()
        gather.step2(late)
        de[...] = tn(deep_low[...], emb[...]).astype(bf16)
        for item in deep_sums:
            item.begin()
        input_term()
        for item in input_sums:
            item.begin()
        square_by_z.after_core()
        for item in deep_sums:
            item.after_core()
        for item in input_sums:
            item.after_core()
        gather.step3(early)
        recur_sums[0].after_y()
        square_by_z.after_near()
        recur_sums[1].after_y()
        recur_sums[0].mid_z()
        gather.step3(late)
        recur_sums[2].after_y()
        recur_sums[1].mid_z()
        square_by_z.after_far()
        for u in (early, late):
            gather.ready(u)
        for copy in own_copies:
            copy.wait()
        recur_sums[0].after_z()
        put(*places[id(recur_sums[0])])

        rows = gates_o.shape[0]
        firsts = [(sec * n + at.d) * rows for sec in (0, 1)]
        for k, first in enumerate(firsts):
            lanes = multiple(first // 128 * 128, 128)
            copy = pltpu.make_async_copy(
                early_h.at[:, pl.ds(lanes, 128)], ctx_cols.at[k], big_sem.at[3]
            )
            copy.start()
            copy.wait()
        pieces = (2 * M + 3 * H) // chunk

        def load_chunk(k):
            if k < 2 * M // chunk:
                src = early_h.at[:, pl.ds(H + k * chunk, chunk)]
            else:
                src = late_h.at[:, pl.ds(k * chunk - 2 * M, chunk)]
            return pltpu.make_async_copy(src, chunks.at[k % 2], chunk_sem.at[k % 2])

        load_chunk(0).start()
        for k in range(pieces):
            if k + 1 < pieces:
                load_chunk(k + 1).start()
            load_chunk(k).wait()
            for j, first in enumerate(firsts):
                block_rows[...] = tn(ctx_cols[j], chunks[k % 2])
                product = block_rows[pl.ds(multiple(lax.rem(first, 128), 8), rows), :]
                if k < 2 * M // chunk:
                    dst, cols = context_o, pl.ds(k * chunk, chunk)
                else:
                    dst, cols = gates_o, pl.ds(k * chunk - 2 * M, chunk)
                if j == 0:
                    far_rows[:, pl.ds(k * chunk, chunk)] = product
                else:
                    dst[:, cols] = product
        sends = [
            to_beside(far_rows.at[:, pl.ds(2 * M, 3 * H)], gates_o, 4),
            to_beside(far_rows.at[:, pl.ds(0, 2 * M)], context_o, 5),
        ]
        for copy in sends:
            copy.start()
        put(gates_o, gates_h)
        put(context_o, context_h)
        take()
        put(table_o, table_h)
        recur_sums[2].mid_z()
        for item in deep_sums:
            item.after_y()
        recur_sums[1].after_z()
        put(*places[id(recur_sums[1])])
        for item in deep_sums:
            item.mid_z()
        recur_sums[2].after_z()
        put(*places[id(recur_sums[2])])

        def finish_deep():
            for item in deep_sums:
                item.after_z()
            put(deep_o, deep_h)
            sends.append(to_beside(deep_far, deep_o, 3))
            sends[-1].start()

        end_sums([], finish_deep)
        square_by_z.finish()
        put(square_o, square_h)
        for copy in sends + [send, outer_send]:
            copy.wait_send()
        for u in (early, late):
            gather.drain(u)
        arrival(soft_o, x_recv.at[1]).wait()
        put(soft_o, soft_h)
        arrival(loss_o, x_recv.at[2]).wait()
        put(loss_o, loss_h)
        for copy in puts:
            copy.wait()


def backward(n, sizes, blocks, arrays):
    R, H, E, M, slots, per, words = sizes
    Z, Y = factors(n)
    ZY = Z * Y
    tokens = arrays[0].shape[0]
    shape = jax.ShapeDtypeStruct
    vmem = pltpu.VMEM
    dma = pltpu.SemaphoreType.DMA
    input_b, recur_b, square_b, gates_b, deep_b, context_b = blocks
    tall = recur_b[0]
    part = next(k for k in (64, 48, 32, 16) if input_b[0] % k == 0)
    thin = input_b[0] // part
    units = 4 + thin + 4
    chunk = M
    big_rows = words * (2 * Z + 2 * (Y - 1) * Z + 6)
    big_rows = max(big_rows, 3 * H * H // chunk)
    y1 = max(Y - 1, 1)
    return pl.pallas_call(
        functools.partial(backward_kernel_all, n, sizes),
        out_shape=[
            shape((per, E), f32),
            shape(input_b, f32),
            shape(recur_b, f32),
            shape(square_b, f32),
            shape(gates_b, f32),
            shape(deep_b, f32),
            shape(context_b, f32),
            shape((words, M), f32),
            shape((8, 128), f32),
            shape((n * R, H + 2 * M), bf16),
            shape((n * R, 3 * H), bf16),
        ],
        in_specs=[VMEM] * 6 + [ANY] * 12,
        out_specs=[ANY] * 11,
        scratch_shapes=[
            vmem((3 * H, H), bf16),
            vmem((3 * H, E), bf16),
            vmem((H, H), bf16),
            vmem((2 * M, E), bf16),
            vmem((H, 2 * M), bf16),
            vmem((big_rows, chunk), bf16),
            vmem((2, 5, R, H), f32),
            vmem((tokens, 3 * H), bf16),
            vmem((tokens, H), bf16),
            vmem((tokens, H), bf16),
            vmem((tokens, H), f32),
            vmem((R, 3 * H), f32),
            vmem((tokens, 2 * M), bf16),
            vmem((R, 2 * M), bf16),
            vmem((R, H + 2 * M), bf16),
            vmem((R, 3 * H), bf16),
            vmem((R, H), bf16),
            vmem((R, H), bf16),
            vmem((R, H), bf16),
            vmem((n * slots, E), bf16),
            vmem((n * slots, E), bf16),
            vmem((4, ZY, tall, H), bf16),
            vmem((4, y1, Z, tall, H), bf16),
            vmem((4, 3, tall, H), bf16),
            vmem((thin, ZY, part, E), bf16),
            vmem((thin, y1, Z, part, E), bf16),
            vmem((thin, 3, part, E), bf16),
            vmem((2, ZY) + deep_b, bf16),
            vmem((2, y1, Z) + deep_b, bf16),
            vmem((2, 3) + deep_b, bf16),
            vmem((words, M), f32),
            vmem(deep_b, f32),
            vmem((gates_b[0], 2 * M + 3 * H), f32),
            vmem((128, chunk), f32),
            vmem((2, n * R, chunk), bf16),
            vmem((2, n * R, 128), bf16),
            vmem((n, 8, 128), f32),
            vmem((8, 128), f32),
            dma((units,)),
            dma((units,)),
            dma((units,)),
            dma((units, y1, Z)),
            dma((units,)),
            dma((units, 3)),
            dma((2, 6)),
            dma((2, Z)),
            dma((2,)),
            dma((2,)),
            dma((5,)),
            dma((2,)),
            dma((4,)),
            dma((2,)),
            dma((7,)),
            dma((7,)),
            dma,
            dma,
            dma,
            dma,
            vmem((tokens, H), bf16),
            vmem((tokens, E), bf16),
            vmem((tokens, n * slots), bf16),
            vmem((per, n * slots), bf16),
            dma((4,)),
            vmem((per, E), f32),
            vmem(input_b, f32),
            vmem(recur_b, f32),
            vmem(square_b, f32),
            vmem(gates_b, f32),
            vmem(deep_b, f32),
            vmem(context_b, f32),
            vmem((words, M), f32),
            vmem((8, 128), f32),
            dma((16,)),
            vmem((tokens, 1), f32),
        ],
        compiler_params=pltpu.CompilerParams(
            collective_id=3, has_side_effects=True, vmem_limit_bytes=VMEM_LIMIT
        ),
    )(*arrays)


def in_rounds(
    token_ids,
    resets,
    targets,
    embedding,
    input_gates,
    recur_gates,
    square,
    context_gates,
    deep_embed,
    deep_context,
    softmax_weight,
):
    n = lax.axis_size("dp")
    s = lax.axis_index("section")
    d = lax.axis_index("dp")
    is_decoder = s == 1
    micro, rows, steps = token_ids.shape[1:]
    R = micro * rows
    tokens = R * steps
    H = square.shape[2]
    E = embedding.shape[2]
    M = softmax_weight.shape[1]
    per = embedding.shape[1]
    slots = max(512 // n, 8)
    scale = 1.0 / (R * n)

    def time_major(x):
        return jnp.transpose(x.reshape(R, steps), (1, 0)).reshape(-1)

    ids = time_major(token_ids[0])
    keep = time_major(1 - resets[0]).astype(f32)[:, None]
    labels = time_major(targets)

    plan = request_slots(ids, n, per, slots)
    rounds = lax.pmax(jnp.max(plan[2]) // slots + 1, ("section", "dp"))
    table = embedding[0]

    def fetch(turn):
        asked, hit = round_maps(plan, turn, n, slots)
        owners = owner_map(asked, n, per)
        came = swap(nn(owners, table).astype(bf16), n)
        return owners, hit, nn(hit, came).astype(bf16)

    owners, hit, emb = fetch(0)

    def more(carry):
        turn, emb = carry
        return turn + 1, emb + fetch(turn)[2]

    _, emb = lax.while_loop(lambda c: c[0] < rounds, more, (jnp.int32(1), emb))

    wr, wi, sq, sm, cg, de, dc = gather(
        n,
        [
            recur_gates[0],
            input_gates[0],
            square[0],
            softmax_weight,
            context_gates,
            deep_embed,
            deep_context,
        ],
        (False, False, False, False, True, True, True),
    )
    wr, wi, sq, sm = wr.reshape(H, 3 * H), wi.reshape(3 * H, E), sq.reshape(H, H), sm.reshape(-1, M)
    cg, de, dc = cg.reshape(H, 3 * H), de.reshape(2 * M, E), dc.reshape(H, 2 * M)

    enc = gru_forward(emb, wi, wr, jnp.zeros((R, 3 * H), f32), keep)
    last_low = enc[5][-R:]
    ctx_tanh = jnp.tanh(nn(last_low, sq))
    context = lax.ppermute(ctx_tanh.astype(bf16), "section", [(0, 1)])

    dec = gru_forward(emb, wi, wr, nn(context, cg), keep)
    states_low = dec[5]
    deep_pre = nn(states_low, sq) + nt(emb, de)
    deep_pre = (deep_pre.reshape(steps, R, -1) + nn(context, dc)[None]).reshape(tokens, -1)
    smooth = jnp.logaddexp(deep_pre[:, :M], deep_pre[:, M:])
    smooth_low = smooth.astype(bf16)

    came = lax.ppermute(smooth_low, "section", [(1, 0)])
    head_in = jnp.where(is_decoder, smooth_low, came)
    words = sm.shape[0]
    logits = nt(head_in, sm)
    top = jnp.max(logits, axis=1)
    total = jnp.sum(jnp.exp(logits - top[:, None]), axis=1)
    hits = lax.broadcasted_iota(jnp.int32, logits.shape, 1) == (labels - s * words)[:, None]
    picked = jnp.sum(jnp.where(hits, logits, 0.0), axis=1)
    stats = jnp.stack([top, total, picked])
    other = lax.ppermute(stats, "section", [(0, 1), (1, 0)])
    all_top = jnp.maximum(top, other[0])
    log_norm = all_top + jnp.log(
        total * jnp.exp(top - all_top) + other[1] * jnp.exp(other[0] - all_top)
    )
    loss = jnp.where(is_decoder, jnp.sum(log_norm - picked - other[2]) * scale, 0.0)
    logit_low = ((jnp.exp(logits - log_norm[:, None]) - hits.astype(f32)) * scale).astype(bf16)
    smooth_part = nn(logit_low, sm)
    smooth_grad = smooth_part + lax.ppermute(smooth_part, "section", [(0, 1)])
    softmax_term = tn(logit_low, head_in).astype(bf16)

    deep_grad = jnp.concatenate(
        [
            smooth_grad * jnp.exp(deep_pre[:, :M] - smooth),
            smooth_grad * jnp.exp(deep_pre[:, M:] - smooth),
        ],
        axis=1,
    )
    deep_low = deep_grad.astype(bf16)
    outer_low = jnp.sum(deep_grad.reshape(steps, R, -1), axis=0).astype(bf16)
    state_grad = nt(deep_low, sq)
    dec_low, dec_cand, drive_sum = gru_backward(
        state_grad, jnp.zeros((R, H), f32), keep, dec[:5], wr
    )
    drive_sum_low = drive_sum.astype(bf16)
    context_grad = (nt(outer_low, dc) + nt(drive_sum_low, cg)).astype(bf16)
    packed = lax.all_gather(jnp.concatenate([context, outer_low, drive_sum_low], axis=1), "dp", tiled=True)
    packed_came = lax.ppermute(packed, "section", [(1, 0)])
    packed = jnp.where(is_decoder, packed, packed_came)

    context_back = lax.ppermute(context_grad, "section", [(1, 0)])
    pre_low = (context_back.astype(f32) * (1.0 - ctx_tanh * ctx_tanh)).astype(bf16)
    enc_low, enc_cand, _ = gru_backward(
        jnp.zeros((tokens, H), f32), nt(pre_low, sq), keep, enc[:5], wr
    )

    def pick(of_encoder, of_decoder):
        return jnp.where(is_decoder, of_decoder, of_encoder)

    recur_low = pick(enc_low, dec_low)
    cand_low = pick(enc_cand, dec_cand)
    before_low = pick(enc[4], dec[4]).astype(bf16)
    drive_low = jnp.concatenate([recur_low[:, : 2 * H], cand_low], axis=1)
    recur_term = tn(before_low, recur_low).astype(bf16)
    input_term = tn(drive_low, emb).astype(bf16)
    deep_mask = jnp.where(is_decoder, deep_low, jnp.zeros_like(deep_low))
    input_grad = nn(drive_low, wi) + nn(deep_mask, de)
    rows_pad = jnp.zeros((tokens - R, H), bf16)
    square_term = tn(
        pick(jnp.concatenate([last_low, rows_pad]), states_low),
        pick(jnp.concatenate([pre_low, rows_pad]), deep_low),
    ).astype(bf16)
    deep_term = tn(deep_mask, emb).astype(bf16)

    input_grad_low = input_grad.astype(bf16)

    def give(owners, hit):
        return tn(owners, swap(tn(hit, input_grad_low).astype(bf16), n))

    def give_more(carry):
        turn, grad = carry
        asked, hit = round_maps(plan, turn, n, slots)
        return turn + 1, grad + give(owner_map(asked, n, per), hit)

    table_grad = give(owners, hit)
    _, table_grad = lax.while_loop(
        lambda c: c[0] < rounds, give_more, (jnp.int32(1), table_grad)
    )

    deep_blocks = jnp.stack(
        [x.reshape((n,) + deep_embed.shape) for x in jnp.split(deep_term, 2)], axis=1
    )
    deep_blocks = deep_blocks.reshape(n, 2 * deep_embed.shape[0], E)
    loss_blocks = jnp.broadcast_to(loss, (n, 8, 128))
    square_sum, recur_sum, input_sum, softmax_sum, deep_sum, loss_sum = scatter(
        n,
        [
            square_term.reshape((n,) + square.shape[1:]),
            recur_term.reshape((n,) + recur_gates.shape[1:]),
            input_term.reshape((n,) + input_gates.shape[1:]),
            softmax_term.reshape((n,) + softmax_weight.shape),
            deep_blocks,
            loss_blocks,
        ],
        1,
    )
    deep_halves = deep_sum.reshape((2,) + deep_embed.shape)
    both = lax.ppermute(
        jnp.concatenate([deep_halves[0].reshape(-1), loss_sum[:1].reshape(-1)]), "section", [(1, 0)]
    )
    deep_out = jnp.where(is_decoder, deep_halves[1], both[:-128].reshape(deep_embed.shape))
    loss_out = jnp.where(is_decoder, loss_sum[0, 0], both[-1])

    own = (s * n + d) * context_gates.shape[0]
    context_own = lax.dynamic_slice(packed, (0, own), (packed.shape[0], context_gates.shape[0]))
    gates_out = tn(context_own, packed[:, H + 2 * M :])
    context_out = tn(context_own, packed[:, H : H + 2 * M])

    return (
        loss_out,
        table_grad[None],
        input_sum[None],
        recur_sum[None],
        square_sum[None],
        gates_out,
        deep_out,
        context_out,
        softmax_sum,
    )


def in_one_round(
    token_ids,
    resets,
    targets,
    embedding,
    input_gates,
    recur_gates,
    square,
    context_gates,
    deep_embed,
    deep_context,
    softmax_weight,
):
    n = lax.axis_size("dp")
    s = lax.axis_index("section")
    d = lax.axis_index("dp")
    is_decoder = s == 1
    micro, rows, steps = token_ids.shape[1:]
    R = micro * rows
    tokens = R * steps
    H = square.shape[2]
    E = embedding.shape[2]
    M = softmax_weight.shape[1]
    per = embedding.shape[1]
    slots = 512 // n

    def time_major(x):
        return jnp.transpose(x.reshape(R, steps), (1, 0)).reshape(-1)

    ids = time_major(token_ids[0])
    reset_rows = jnp.transpose(resets[0], (2, 0, 1))
    target_rows = jnp.transpose(targets, (2, 0, 1))

    plan = request_slots(ids, n, per, slots)
    asked, hit = round_maps(plan, 0, n, slots)
    lane = jnp.arange(128, dtype=jnp.int32)
    asked = jnp.tile(asked.reshape(n, slots), (1, 128 // slots))
    asked = jnp.where(lane // slots == d % (128 // slots), asked, -1)
    fullest = jnp.max(plan[2]).reshape(1, 1)

    shards = [
        recur_gates[0],
        input_gates[0],
        square[0],
        softmax_weight,
        context_gates,
        deep_embed,
        deep_context,
    ]
    sizes = (R, H, E, M, slots, per, softmax_weight.shape[0])
    results = forward(n, sizes, asked, fullest, hit, embedding[0], reset_rows, target_rows, shards)

    (
        wr,
        wi,
        sq,
        cg,
        de,
        dc,
        softmax_term,
        rec,
        states_low,
        emb,
        deep_pre,
        ctx_tanh,
        context,
        owners,
        smooth_grad,
        loss,
        most,
    ) = results
    blocks = [
        x.shape[-2:]
        for x in (input_gates, recur_gates, square, context_gates, deep_embed, deep_context)
    ]
    table, inputs, recur, squares, gates, deep, contexts, soft, loss, _, _ = backward(
        n,
        sizes,
        blocks,
        [
            deep_pre,
            smooth_grad,
            reset_rows,
            ctx_tanh,
            context,
            loss,
            states_low,
            emb,
            hit,
            owners,
            wr,
            wi,
            sq,
            cg,
            de,
            dc,
            softmax_term,
            rec,
        ],
    )
    def again(carry):
        slow = in_rounds(
            token_ids,
            resets,
            targets,
            embedding,
            input_gates,
            recur_gates,
            square,
            context_gates,
            deep_embed,
            deep_context,
            softmax_weight,
        )
        flat = [x.reshape(x.shape[-2:]) for x in slow[1:]]
        return jnp.int32(0), (jnp.broadcast_to(slow[0], (8, 128)), *flat)

    fast = (loss, table, inputs, recur, squares, gates, deep, contexts, soft)
    done = lax.while_loop(lambda carry: carry[0] > 0, again, (most.reshape(()), fast))[1]
    loss, table, inputs, recur, squares, gates, deep, contexts, soft = finish(*done)
    return (
        loss.reshape(()),
        table[None],
        inputs[None],
        recur[None],
        squares[None],
        gates,
        deep,
        contexts,
        soft,
    )


def per_device(*args):
    n = lax.axis_size("dp")
    blocks = [args[k].shape[-2] for k in (4, 5, 6, 7, 8, 9, 10)]
    aligned = all(rows % 16 == 0 for rows in blocks)
    if aligned and n == 16:
        return in_one_round(*args)
    return in_rounds(*args)


def solution(mesh):
    halves = P("section", "dp", None)
    whole = P(("section", "dp"), None)
    in_specs = (
        P("section", None, "dp", None),
        P("section", None, "dp", None),
        P(None, "dp", None),
        halves,
        halves,
        halves,
        halves,
        whole,
        whole,
        whole,
        whole,
    )
    out_specs = (P(), halves, halves, halves, halves, whole, whole, whole, whole)
    return jax.shard_map(
        per_device, mesh=mesh, in_specs=in_specs, out_specs=out_specs, check_vma=False
    )
```

```python
import functools

import jax
import jax.numpy as jnp
from jax import lax
from jax.experimental import pallas as pl
from jax.experimental.pallas import tpu as pltpu
from jax.sharding import PartitionSpec as P

MESH = pl.DeviceIdType.MESH
ANY = pl.BlockSpec(memory_space=pl.ANY)
VMEM = pl.BlockSpec(memory_space=pltpu.VMEM)
f32 = jnp.float32
bf16 = jnp.bfloat16
VMEM_LIMIT = 62 * 2**20


def nn(a, b):
    return jnp.dot(a, b, preferred_element_type=f32)


def nt(a, b):
    return lax.dot_general(a, b, (((1,), (1,)), ((), ())), preferred_element_type=f32)


def tn(a, b):
    return lax.dot_general(a, b, (((0,), (0,)), ((), ())), preferred_element_type=f32)


def factors(n):
    z = 4 if n % 8 == 0 else 1
    return z, n // (2 * z)


class Place:
    def __init__(self, n):
        self.Z, self.Y = factors(n)
        self.s = lax.axis_index("section")
        d = lax.axis_index("dp")
        self.d = d
        self.c = d % 2
        self.zy = d // 2
        self.y = self.zy % self.Y
        self.z = self.zy // self.Y

    def along_z(self, step):
        return lax.rem(self.z + step + self.Z, self.Z)

    def along_y(self, step):
        return lax.rem(self.y + step + self.Y, self.Y)

    def device(self, z, y, c):
        return (self.s, (z * self.Y + y) * 2 + c)

    def z_near(self):
        return self.z + 1 - 2 * (self.z % 2)

    def z_far(self):
        return lax.rem(self.z + 2, 4)

    def partners(self):
        found = [self.device(self.along_z(k), self.y, self.c) for k in range(1, self.Z)]
        found += [self.device(self.z, self.along_y(k), self.c) for k in range(1, self.Y)]
        return found + [self.device(self.z, self.y, 1 - self.c), (1 - self.s, self.d)]


def greet(devices):
    barrier = pltpu.get_barrier_semaphore()
    for device in devices:
        pl.semaphore_signal(barrier, inc=1, device_id=device, device_id_type=MESH)
    pl.semaphore_wait(barrier, len(devices))


def remote(src, dst, send, recv, device):
    return pltpu.make_async_remote_copy(
        src_ref=src, dst_ref=dst, send_sem=send, recv_sem=recv, device_id=device, device_id_type=MESH
    )


def arrival(ref, sem):
    return pltpu.make_async_copy(ref, ref, sem)


def gather_kernel(n, crossed, *refs):
    count = len(crossed)
    sources, outs = refs[:count], refs[count : 2 * count]
    z_sem, y_sem, c_sem, s_sem, l_sem, x_sem, xs_sem = refs[2 * count :]
    at = Place(n)
    Z, Y = at.Z, at.Y
    greet(at.partners())

    x_copies = []
    for item in range(count):
        if crossed[item]:
            copy = remote(
                sources[item],
                outs[item].at[at.s, at.zy, at.c],
                xs_sem.at[item],
                x_sem.at[item],
                (1 - at.s, at.d),
            )
            copy.start()
            x_copies.append(copy)

    units = []
    for item in range(count):
        if crossed[item]:
            units.append((item, outs[item].at[at.s], sources[item]))
        else:
            units.append((item, outs[item], sources[item]))
    own = len(units)
    for item in range(count):
        if crossed[item]:
            gathered = outs[item].at[1 - at.s]
            units.append((item, gathered, gathered.at[at.zy, at.c]))

    def spread(u, src, zy, z_slot, to_z, to_y):
        gathered = units[u][1]
        dst = gathered.at[zy, at.c]
        if to_z:
            for k in range(1, Z):
                remote(
                    src, dst, s_sem.at[u], z_sem.at[u, k - 1], at.device(at.along_z(k), at.y, at.c)
                ).start()
        if to_y:
            for k in range(1, Y):
                remote(
                    src,
                    dst,
                    s_sem.at[u],
                    y_sem.at[u, z_slot * (Y - 1) + k - 1],
                    at.device(at.z, at.along_y(k), at.c),
                ).start()
        remote(src, dst, s_sem.at[u], c_sem.at[u], at.device(at.z, at.y, 1 - at.c)).start()

    for u, (item, gathered, src) in enumerate(units):
        if u < own:
            pltpu.make_async_copy(src, gathered.at[at.zy, at.c], l_sem.at[u]).start()
        else:
            arrival(src, x_sem.at[item]).wait()
        spread(u, src, at.zy, 0, True, True)
    for u, (item, gathered, _) in enumerate(units):
        for k in range(1, Z):
            zy = at.along_z(-k) * Y + at.y
            block = gathered.at[zy, at.c]
            arrival(block, z_sem.at[u, k - 1]).wait()
            spread(u, block, zy, k, False, True)
        for slot in range(Z):
            for k in range(1, Y):
                zy = at.along_z(-slot) * Y + at.along_y(-k)
                block = gathered.at[zy, at.c]
                arrival(block, y_sem.at[u, slot * (Y - 1) + k - 1]).wait()
                spread(u, block, zy, 0, False, False)
    for u, (item, gathered, src) in enumerate(units):
        if u < own:
            pltpu.make_async_copy(src, gathered.at[at.zy, at.c], l_sem.at[u]).wait()
        theirs = gathered.at[:, 1 - at.c]
        arrival(theirs, c_sem.at[u]).wait()
        most = gathered.at[pl.ds(0, Z * Y - 1)]
        arrival(most, s_sem.at[u]).wait()
        arrival(gathered.at[0, 0], s_sem.at[u]).wait()
    for copy in x_copies:
        copy.wait_send()


def gather(n, arrays, crossed):
    Z, Y = factors(n)
    shapes = []
    for array, over_section in zip(arrays, crossed):
        lead = (2, Z * Y, 2) if over_section else (Z * Y, 2)
        shapes.append(jax.ShapeDtypeStruct(lead + array.shape, array.dtype))
    units = len(arrays) + sum(crossed)
    dma = pltpu.SemaphoreType.DMA
    return pl.pallas_call(
        functools.partial(gather_kernel, n, crossed),
        out_shape=shapes,
        in_specs=[ANY] * len(arrays),
        out_specs=[ANY] * len(arrays),
        scratch_shapes=[
            dma((units, max(Z - 1, 1))),
            dma((units, max(Z * (Y - 1), 1))),
            dma((units,)),
            dma((units,)),
            dma((units,)),
            dma((len(arrays),)),
            dma((len(arrays),)),
        ],
        compiler_params=pltpu.CompilerParams(collective_id=0, has_side_effects=True),
    )(*arrays)


def add_blocks(rows, terms, out, out_type):
    chunk = 16 if rows % 16 == 0 else rows

    def body(i, _):
        part = pl.ds(pl.multiple_of(i * chunk, chunk), chunk)
        total = terms[0][part, :].astype(f32)
        for term in terms[1:]:
            total = total + term[part, :].astype(f32)
        out[part, :] = total.astype(out_type)
        return _

    lax.fori_loop(0, rows // chunk, body, 0)


def scatter_kernel(n, count, *refs):
    sources, outs = refs[:count], refs[count : 2 * count]
    scratch = refs[2 * count :]
    mine, from_c, from_y, from_z = (scratch[k * count : (k + 1) * count] for k in range(4))
    l_sem, cs_sem, cr_sem, ys_sem, yr_sem, zs_sem, zr_sem = scratch[4 * count :]
    at = Place(n)
    Z, Y = at.Z, at.Y
    greet(at.partners()[:-1])

    c_copies, l_copies, y_copies, z_copies = [], [], [], []
    for i in range(count):
        copy = remote(
            sources[i].at[:, 1 - at.c],
            from_c[i],
            cs_sem.at[i],
            cr_sem.at[i],
            at.device(at.z, at.y, 1 - at.c),
        )
        copy.start()
        c_copies.append(copy)
        copy = pltpu.make_async_copy(sources[i].at[:, at.c], mine[i], l_sem.at[i])
        copy.start()
        l_copies.append(copy)

    def after_core(i):
        c_copies[i].wait_recv()
        l_copies[i].wait()
        rows = mine[i].shape[1]
        for k in list(range(1, Y)) + [0]:
            y = at.along_y(k)

            def per_z(z, _):
                zy = z * Y + y
                add_blocks(rows, [mine[i].at[zy], from_c[i].at[zy]], mine[i].at[zy], mine[i].dtype)
                return _

            lax.fori_loop(0, Z, per_z, 0)
            if k:
                for z in range(Z):
                    copy = remote(
                        mine[i].at[z * Y + y],
                        from_y[i].at[k - 1, z],
                        ys_sem.at[i, k - 1, z],
                        yr_sem.at[i, k - 1, z],
                        at.device(at.z, y, at.c),
                    )
                    copy.start()
                    y_copies.append(copy)

    def after_y(i):
        rows = mine[i].shape[1]
        for k in list(range(1, Z)) + [0]:
            z = at.along_z(k)
            block = mine[i].at[z * Y + at.y]
            for j in range(1, Y):
                arrival(from_y[i].at[j - 1, z], yr_sem.at[i, j - 1, z]).wait()
            terms = [block] + [from_y[i].at[j - 1, z] for j in range(1, Y)]
            add_blocks(rows, terms, block, mine[i].dtype)
            if k:
                copy = remote(
                    block,
                    from_z[i].at[k - 1],
                    zs_sem.at[i, k - 1],
                    zr_sem.at[i, k - 1],
                    at.device(z, at.y, at.c),
                )
                copy.start()
                z_copies.append(copy)

    def after_z(i):
        rows = mine[i].shape[1]
        for k in range(1, Z):
            arrival(from_z[i].at[k - 1], zr_sem.at[i, k - 1]).wait()
        terms = [mine[i].at[at.zy]] + [from_z[i].at[k - 1] for k in range(1, Z)]
        add_blocks(rows, terms, outs[i], outs[i].dtype)

    for turn in range(count + 2):
        if turn < count:
            after_core(turn)
        if 0 <= turn - 1 < count:
            after_y(turn - 1)
        if turn - 2 >= 0:
            after_z(turn - 2)
    for copy in c_copies + y_copies + z_copies:
        copy.wait_send()


def scatter(n, arrays, collective_id):
    Z, Y = factors(n)
    count = len(arrays)
    blocks = [a.shape[-2:] for a in arrays]
    arrays = [a.reshape((Z * Y, 2) + b) for a, b in zip(arrays, blocks)]
    dma = pltpu.SemaphoreType.DMA
    scratch = [pltpu.VMEM((Z * Y,) + b, a.dtype) for a, b in zip(arrays, blocks)]
    scratch += [pltpu.VMEM((Z * Y,) + b, a.dtype) for a, b in zip(arrays, blocks)]
    scratch += [pltpu.VMEM((max(Y - 1, 1), Z) + b, a.dtype) for a, b in zip(arrays, blocks)]
    scratch += [pltpu.VMEM((max(Z - 1, 1),) + b, a.dtype) for a, b in zip(arrays, blocks)]
    return pl.pallas_call(
        functools.partial(scatter_kernel, n, count),
        out_shape=[jax.ShapeDtypeStruct(b, f32) for b in blocks],
        in_specs=[ANY] * count,
        out_specs=[VMEM] * count,
        scratch_shapes=scratch
        + [
            dma((count,)),
            dma((count,)),
            dma((count,)),
            dma((count, max(Y - 1, 1), Z)),
            dma((count, max(Y - 1, 1), Z)),
            dma((count, max(Z - 1, 1))),
            dma((count, max(Z - 1, 1))),
        ],
        compiler_params=pltpu.CompilerParams(
            collective_id=collective_id, has_side_effects=True, vmem_limit_bytes=VMEM_LIMIT
        ),
    )(*arrays)


def scan_kernel(emb, wi, wr, ctx, keep, z_o, r_o, n_o, m_o, p_o, h_o, drive):
    R, H = ctx.shape[0], wr.shape[0]
    drive[...] = nt(emb[...], wi[...])

    def step(t, h):
        rows = pl.ds(pl.multiple_of(t * R, R), R)
        p = h * keep[rows, :]
        p_o[rows, :] = p
        rec = nn(p.astype(bf16), wr[...])
        d = drive[rows, :]
        z = jax.nn.sigmoid(d[:, :H] + rec[:, :H] + ctx[:, :H])
        r = jax.nn.sigmoid(d[:, H : 2 * H] + rec[:, H : 2 * H] + ctx[:, H : 2 * H])
        m = rec[:, 2 * H :] + ctx[:, 2 * H :]
        n = jnp.tanh(d[:, 2 * H :] + r * m)
        h = z * p + (1.0 - z) * n
        z_o[rows, :] = z
        r_o[rows, :] = r
        n_o[rows, :] = n
        m_o[rows, :] = m
        h_o[rows, :] = h.astype(bf16)
        return h

    lax.fori_loop(0, emb.shape[0] // R, step, jnp.zeros((R, H), f32))


def gru_forward(emb, wi, wr, ctx, keep):
    tokens, H = emb.shape[0], wr.shape[0]
    shape = jax.ShapeDtypeStruct
    return pl.pallas_call(
        scan_kernel,
        out_shape=[shape((tokens, H), f32)] * 5 + [shape((tokens, H), bf16)],
        in_specs=[VMEM] * 5,
        out_specs=[VMEM] * 6,
        scratch_shapes=[pltpu.VMEM((tokens, 3 * H), f32)],
        compiler_params=pltpu.CompilerParams(vmem_limit_bytes=VMEM_LIMIT),
    )(emb, wi, wr, ctx, keep)


def backward_kernel(sg, carry0, keep, z, r, n, m, p, wr, low_o, cand_o, sum_o):
    R, H = carry0.shape
    steps = sg.shape[0] // R

    def step(i, carry):
        rows = pl.ds(pl.multiple_of((steps - 1 - i) * R, R), R)
        g = sg[rows, :] + carry
        zz = z[rows, :]
        cand = n[rows, :]
        rr = r[rows, :]
        pc = g * (1.0 - zz) * (1.0 - cand * cand)
        pz = g * (p[rows, :] - cand) * zz * (1.0 - zz)
        pr = pc * m[rows, :] * rr * (1.0 - rr)
        rec = jnp.concatenate([pz, pr, pc * rr], axis=1)
        low = rec.astype(bf16)
        low_o[rows, :] = low
        cand_o[rows, :] = pc.astype(bf16)
        sum_o[...] += rec
        return (g * zz + nt(low, wr[...])) * keep[rows, :]

    sum_o[...] = jnp.zeros_like(sum_o)
    lax.fori_loop(0, steps, step, carry0[...])


def gru_backward(sg, carry0, keep, record, wr):
    z, r, n, m, p = record
    tokens, H = sg.shape
    shape = jax.ShapeDtypeStruct
    return pl.pallas_call(
        backward_kernel,
        out_shape=[
            shape((tokens, 3 * H), bf16),
            shape((tokens, H), bf16),
            shape((carry0.shape[0], 3 * H), f32),
        ],
        in_specs=[VMEM] * 9,
        out_specs=[VMEM] * 3,
        compiler_params=pltpu.CompilerParams(vmem_limit_bytes=VMEM_LIMIT),
    )(sg, carry0, keep, z, r, n, m, p, wr)


def finish_kernel(count, *refs):
    loss_in, loss_out = refs[0], refs[count]
    sources, outs, held = refs[1:count], refs[count + 1 : 2 * count], refs[2 * count : 3 * count - 1]
    in_sem, out_sem = refs[-2:]
    ins = [pltpu.make_async_copy(a, b, in_sem.at[k]) for k, (a, b) in enumerate(zip(sources, held))]
    puts = [pltpu.make_async_copy(a, b, out_sem.at[k]) for k, (a, b) in enumerate(zip(held, outs))]
    for copy in ins:
        copy.start()
    loss_out[0, 0] = jnp.max(loss_in[...])
    for copy, put in zip(ins, puts):
        copy.wait()
        put.start()
    for put in puts:
        put.wait()


def finish(loss, *arrays):
    shape = jax.ShapeDtypeStruct
    count = len(arrays)
    return pl.pallas_call(
        functools.partial(finish_kernel, count + 1),
        out_shape=[shape((1, 1), f32)] + [shape(a.shape, a.dtype) for a in arrays],
        in_specs=[VMEM] + [ANY] * count,
        out_specs=[pl.BlockSpec(memory_space=pltpu.SMEM)] + [ANY] * count,
        scratch_shapes=[pltpu.VMEM(a.shape, a.dtype) for a in arrays]
        + [pltpu.SemaphoreType.DMA((count,))] * 2,
        compiler_params=pltpu.CompilerParams(vmem_limit_bytes=16 * 2**20),
    )(loss, *arrays)


def request_slots(ids, n, per, slots):
    count = ids.shape[0]
    index = jnp.arange(count, dtype=jnp.int32)
    same = ids[:, None] == ids[None, :]
    first = jnp.min(jnp.where(same, index[None, :], count), axis=1)
    leads = first == index
    owner = ids // per
    ahead = (owner[:, None] == owner[None, :]) & leads[None, :] & (index[None, :] < first[:, None])
    rank = jnp.sum(ahead.astype(jnp.int32), axis=1)
    return leads, owner, rank, ids - owner * per


def round_maps(plan, turn, n, slots):
    leads, owner, rank, local = plan
    place = rank - turn * slots
    inside = (place >= 0) & (place < slots)
    place = jnp.where(inside, owner * slots + place, -1)
    hit = place[:, None] == jnp.arange(n * slots, dtype=jnp.int32)[None, :]
    asked = jnp.max(jnp.where(hit & leads[:, None], local[:, None], -1), axis=0)
    return asked, hit.astype(bf16)


def swap(x, n):
    shape = x.shape
    return lax.all_to_all(x.reshape((n, -1) + shape[1:]), "dp", 0, 0, tiled=False).reshape(shape)


def owner_map(asked, n, per):
    asked_here = swap(asked, n)
    return (asked_here[:, None] == jnp.arange(per, dtype=jnp.int32)[None, :]).astype(bf16)


def multiple(x, of):
    return pl.multiple_of(x, of)


class Unit:
    def __init__(self, index, src, dst, rows, base, y_first=False, stride=None):
        self.index, self.src, self.dst, self.rows, self.base = index, src, dst, rows, base
        self.y_first, self.stride = y_first, stride or rows

    def block(self, zy, c):
        return self.dst.at[pl.ds(multiple(self.base + (zy * 2 + c) * self.stride, 16), self.rows)]

    def some(self, count):
        return self.dst.at[pl.ds(0, count * self.rows)]


class Gather:
    def __init__(self, at, z_sem, y_sem, c_sem, s_sem):
        self.at, self.z_sem, self.y_sem, self.c_sem, self.s_sem = at, z_sem, y_sem, c_sem, s_sem

    def to_z(self, u, src, dst, z, slot):
        at = self.at
        remote(
            src,
            dst,
            self.s_sem.at[u.index],
            self.z_sem.at[u.index, slot],
            at.device(z, at.y, at.c),
        ).start()

    def to_y(self, u, src, dst, z):
        at = self.at
        remote(
            src,
            dst,
            self.s_sem.at[u.index],
            self.y_sem.at[u.index, z],
            at.device(at.z, at.along_y(1), at.c),
        ).start()

    def to_core(self, u, src, dst):
        at = self.at
        remote(
            src, dst, self.s_sem.at[u.index], self.c_sem.at[u.index], at.device(at.z, at.y, 1 - at.c)
        ).start()

    def begin(self, u):
        at = self.at
        dst = u.block(at.zy, at.c)
        if not u.y_first:
            self.to_z(u, u.src, dst, at.z_far(), 0)
        self.to_y(u, u.src, dst, at.z)
        self.to_core(u, u.src, dst)

    def by_z(self, u, z, y, slot):
        at = self.at
        block = u.block(z * at.Y + y, at.c)
        arrival(block, self.z_sem.at[u.index, slot]).wait()
        return block

    def by_y(self, u, z):
        at = self.at
        block = u.block(z * at.Y + at.along_y(1), at.c)
        arrival(block, self.y_sem.at[u.index, z]).wait()
        return block

    def step1(self, u):
        at = self.at
        far, near = at.z_far(), at.z_near()
        if u.y_first:
            self.to_z(u, u.src, u.block(at.zy, at.c), far, 0)
            block = self.by_y(u, at.z)
            self.to_z(u, block, block, far, 1)
            self.to_core(u, block, block)
            return
        self.to_z(u, u.src, u.block(at.zy, at.c), near, 1)
        block = self.by_z(u, far, at.y, 0)
        self.to_z(u, block, block, near, 2)
        self.to_y(u, block, block, far)
        self.to_core(u, block, block)

    def step2(self, u):
        at = self.at
        far, near = at.z_far(), at.z_near()
        other = at.along_y(1)
        if u.y_first:
            self.to_z(u, u.src, u.block(at.zy, at.c), near, 2)
            block = u.block(at.z * at.Y + other, at.c)
            self.to_z(u, block, block, near, 3)
            for slot, y in ((0, at.y), (1, other)):
                block = self.by_z(u, far, y, slot)
                self.to_z(u, block, block, near, 4 + slot)
                self.to_core(u, block, block)
            return
        for slot, z in ((1, near), (2, lax.rem(near + 2, 4))):
            block = self.by_z(u, z, at.y, slot)
            self.to_y(u, block, block, z)
            self.to_core(u, block, block)

    def step3(self, u):
        at = self.at
        far, near = at.z_far(), at.z_near()
        next_far = lax.rem(near + 2, 4)
        if u.y_first:
            other = at.along_y(1)
            for slot, z, y in (
                (2, near, at.y),
                (3, near, other),
                (4, next_far, at.y),
                (5, next_far, other),
            ):
                block = self.by_z(u, z, y, slot)
                self.to_core(u, block, block)
            return
        for z in (at.z, far, near, next_far):
            block = self.by_y(u, z)
            self.to_core(u, block, block)

    def ready(self, u):
        part = u.some(self.at.Z * self.at.Y)
        arrival(part, self.c_sem.at[u.index]).wait()

    def drain(self, u):
        part = u.some(2 * self.at.Z * self.at.Y - 1)
        arrival(part, self.s_sem.at[u.index]).wait()


class Chain(Gather):
    def on(self, u, src, dst, up, hops):
        at = self.at
        slot = hops - 1 if up else at.Z - 1 + hops - 1

        @pl.when(at.z < at.Z - 1 if up else at.z > 0)
        def _():
            remote(
                src,
                dst,
                self.on_sem.at[u.index],
                self.z_sem.at[u.index, slot],
                at.device(at.z + (1 if up else -1), at.y, at.c),
            ).start()

    def begin(self, u):
        at = self.at
        dst = u.block(at.zy, at.c)
        self.on(u, u.src, dst, True, 1)
        self.on(u, u.src, dst, False, 1)
        self.to_y(u, u.src, dst, at.z)
        self.to_core(u, u.src, dst)

    def pass_z(self, u, k):
        at = self.at
        for up in (True, False):
            z = at.z - k if up else at.z + k

            @pl.when(z >= 0 if up else z < at.Z)
            def _():
                slot = k - 1 if up else at.Z - 1 + k - 1
                block = self.by_z(u, z, at.y, slot)
                if k + 1 < at.Z:
                    self.on(u, block, block, up, k + 1)
                self.to_y(u, block, block, z)
                self.to_core(u, block, block)

    def drain(self, u):
        at = self.at
        part = u.some(2 * at.Z * at.Y - at.Z)
        arrival(part, self.s_sem.at[u.index]).wait()
        for z in range(at.Z):
            sent = (z + 1 if z < at.Z - 1 else 0) + (at.Z - z if z > 0 else 0)

            @pl.when(at.z == z)
            def _():
                part = u.some(sent)
                arrival(part, self.on_sem.at[u.index]).wait()


def column(ref, t):
    rows = ref.shape[2]
    square = (rows, rows)
    diagonal = lax.broadcasted_iota(jnp.int32, square, 0) == lax.broadcasted_iota(jnp.int32, square, 1)
    parts = []
    for k in range(ref.shape[1]):
        line = jnp.broadcast_to(ref[t, k : k + 1, :], square)
        parts.append(jnp.sum(jnp.where(diagonal, line, 0), axis=1, keepdims=True))
    return jnp.concatenate(parts, axis=0)


def forward_kernel(n, sizes, *refs):
    R, H, E, M, slots, per, words = sizes
    (
        asked_rows,
        own_most,
        hit,
        table,
        resets,
        words_in,
        wr_s,
        wi_s,
        sq_s,
        sm_s,
        cg_s,
        de_s,
        dc_s,
    ) = refs[:13]
    (
        wr_o,
        wi_o,
        sq_o,
        cg_o,
        de_o,
        dc_o,
        term_o,
        rec_o,
        h_h,
        emb_h,
        pre_h,
        tanh_h,
        ctx_h,
        owners_h,
        grad_o,
        loss_o,
        most_o,
    ) = refs[13:30]
    (
        asked_in,
        rows_out,
        came,
        wr,
        wi,
        sq,
        sm,
        cg,
        de,
        dc,
        drive,
        rec,
        wrt,
        smooth_in,
        grad_out,
        m_part,
        s_part,
        p_part,
        fullest,
        outer,
        h_o,
        emb_o,
        pre_o,
        tanh_o,
        ctx_o,
        owners_o,
        z_sem,
        y_sem,
        c_sem,
        s_sem,
        l_sem,
        o_sem,
        x_recv,
        x_send,
        as_sem,
        ar_sem,
        rs_sem,
        rr_sem,
        t_send,
        t_recv,
        k_sem,
        on_sem,
        keep,
        labels,
        asked,
    ) = refs[30:]
    at = Place(n)
    tokens = hit.shape[0]
    steps = tokens // R
    is_decoder = at.s == 1
    beside = (1 - at.s, at.d)
    others = [lax.rem(at.d + k, n) for k in range(1, n)]
    for d in range(n):
        asked[d, 0:1, :] = asked_rows[d : d + 1, :]
        asked[d, 1:2, :] = jnp.full((1, 128), own_most[0, 0], jnp.int32)
    greet([(at.s, d) for d in others] + [beside])

    def block_rows(ref, base, rows):
        return ref.at[pl.ds(multiple((base + at.d) * rows, 16), rows)]

    def to_beside(src, dst, k):
        return remote(src, dst, x_send.at[k], x_recv.at[k], beside)

    gather = Gather(at, z_sem, y_sem, c_sem, s_sem)
    chain = Chain(at, z_sem, y_sem, c_sem, s_sem)
    chain.on_sem = on_sem
    u_wi = Unit(1, wi_s, wi, wi_s.shape[0], 0)
    u_wr = Unit(0, wr_s, wr, wr_s.shape[0], 0)
    u_sq = Unit(2, sq_s, sq, sq_s.shape[0], 0)
    own_sm = Unit(3, sm_s, sm, words, 0)
    far_sm = Unit(4, block_rows(sm, n, words), sm, words, n * words)
    crossed = []
    for k, (src, dst) in enumerate([(cg_s, cg), (de_s, de)]):
        rows = src.shape[0]
        crossed.append(
            (
                Unit(3 + 2 * k, src, dst, rows, n * rows),
                Unit(4 + 2 * k, block_rows(dst, 0, rows), dst, rows, 0, k == 0),
            )
        )
    rows = cg_s.shape[0]
    far_block = block_rows(cg, 0, rows)
    cg_halves = [
        Unit(index, far_block.at[pl.ds(k * 16, 16)], cg, 16, k * 16, k == 0, rows)
        for k, index in enumerate((4, 7))
    ]
    rows = dc_s.shape[0]
    own_dc = Unit(5, dc_s, dc, rows, 0)
    far_dc = Unit(6, block_rows(dc, n, rows), dc, rows, n * rows)

    for d in others:
        remote(asked.at[d], asked_in.at[at.d], as_sem, ar_sem, (at.s, d)).start()
    chain.begin(u_wi)
    chain.begin(u_wr)

    @pl.when(is_decoder)
    def _():
        to_beside(dc_s, block_rows(dc, n, dc_s.shape[0]), 3).start()
        to_beside(sm_s, block_rows(sm, n, words), 0).start()

    @pl.when(jnp.logical_not(is_decoder))
    def _():
        for k, (src, dst) in enumerate([(cg_s, cg), (de_s, de)]):
            to_beside(src, block_rows(dst, 0, src.shape[0]), 1 + k).start()

    locals_ = [
        pltpu.make_async_copy(src, block_rows(dst, 0, src.shape[0]), l_sem.at[k])
        for k, (src, dst) in enumerate([(wr_s, wr), (wi_s, wi), (sq_s, sq)])
    ]
    locals_.append(pltpu.make_async_copy(sm_s, block_rows(sm, 0, words), l_sem.at[3]))
    for k, (src, dst) in enumerate([(cg_s, cg), (de_s, de)]):
        locals_.append(pltpu.make_async_copy(src, block_rows(dst, n, src.shape[0]), l_sem.at[4 + k]))
    locals_.append(pltpu.make_async_copy(dc_s, block_rows(dc, 0, dc_s.shape[0]), l_sem.at[6]))
    for copy in locals_:
        copy.start()

    for t in range(steps):
        rows = pl.ds(t * R, R)
        keep[rows, :] = 1.0 - column(resets, t).astype(f32)
        labels[rows, :] = column(words_in, t)

    chain.pass_z(u_wi, 1)
    chain.pass_z(u_wr, 1)
    some_asked = asked_in.at[pl.ds(0, n - 1)]
    arrival(some_asked, ar_sem).wait()
    asked_in[at.d] = asked[at.d]
    group = 128 // slots
    count = lax.broadcasted_iota(jnp.int32, (per, 128), 0)
    most = asked_in[0, 1:2, :]
    for g in range(n // group):
        wanted = asked_in[g * group, 0:1, :]
        for j in range(1, group):
            wanted = jnp.maximum(wanted, asked_in[g * group + j, 0:1, :])
        for j in range(group):
            most = jnp.maximum(most, asked_in[g * group + j, 1:2, :])
        match = (wanted == count).astype(f32).astype(bf16)
        owners_o[:, pl.ds(g * 128, 128)] = match
        rows_out[pl.ds(g * 128, 128), :] = tn(match, table[...]).astype(bf16)
    fullest[0] = jnp.broadcast_to(most, fullest.shape[1:])
    to_beside(fullest.at[0], fullest.at[1], 7).start()

    def slot_rows(ref, d):
        return ref.at[pl.ds(multiple(d * slots, 16), slots)]

    for d in others:
        remote(slot_rows(rows_out, d), slot_rows(came, at.d), rs_sem, rr_sem, (at.s, d)).start()
    cg_own = crossed[0][0]
    far_a, far_b = cg_halves
    de_own, de_far = crossed[1]
    for k in (2, 3):
        if k == 2:

            @pl.when(is_decoder)
            def _():
                arrival(far_block, x_recv.at[1]).wait()
                gather.begin(far_a)

        chain.pass_z(u_wi, k)
        chain.pass_z(u_wr, k)

    gather.step3(u_wi)

    @pl.when(is_decoder)
    def _():
        chain.begin(cg_own)
        chain.begin(far_b)
        gather.step1(far_a)

    @pl.when(jnp.logical_not(is_decoder))
    def _():
        gather.begin(u_sq)

    some_rows = came.at[pl.ds(0, (n - 1) * slots)]
    arrival(some_rows, rr_sem).wait()
    came[pl.ds(multiple(at.d * slots, 16), slots), :] = rows_out[
        pl.ds(multiple(at.d * slots, 16), slots), :
    ]
    emb_o[...] = nn(hit[...], came[...]).astype(bf16)
    to_beside(fullest.at[0], fullest.at[1], 7).wait()
    rank = jnp.max(jnp.maximum(fullest[0], fullest[1]))
    most_o[0, 0] = jnp.where(rank >= slots, 1, 0)
    for copy in locals_:
        copy.wait()
    chain.ready(u_wi)

    def input_drive(i, _):
        cols = pl.ds(multiple(i * 512, 512), 512)
        drive[:, cols] = nt(emb_o[...], wi[cols, :])
        return _

    lax.fori_loop(0, 3 * H // 512, input_drive, 0)
    @pl.when(is_decoder)
    def _():
        chain.pass_z(cg_own, 1)
        chain.pass_z(far_b, 1)

    gather.step3(u_wr)
    chain.ready(u_wr)

    def scan(ctx, service):
        def step(t, h):
            rows = pl.ds(multiple(t * R, R), R)
            p = h * keep[rows, :]
            rec[t, 4] = p
            mix = nn(p.astype(bf16), wr[...])
            d = drive[rows, :]
            z_in = d[:, :H] + mix[:, :H]
            r_in = d[:, H : 2 * H] + mix[:, H : 2 * H]
            m = mix[:, 2 * H :]
            if ctx is not None:
                z_in += ctx[:, :H]
                r_in += ctx[:, H : 2 * H]
                m += ctx[:, 2 * H :]
            z = jax.nn.sigmoid(z_in)
            r = jax.nn.sigmoid(r_in)
            cand = jnp.tanh(d[:, 2 * H :] + r * m)
            h = z * p + (1.0 - z) * cand
            rec[t, 0] = z
            rec[t, 1] = r
            rec[t, 2] = cand
            rec[t, 3] = m
            h_o[rows, :] = h.astype(bf16)
            for when, what in service:
                pl.when(t == when)(what)
            return h

        return lax.fori_loop(0, steps, step, jnp.zeros((R, H), f32))

    def keep_input_gates():
        copy = pltpu.make_async_copy(wi, wi_o, o_sem.at[0])
        copy.start()
        return copy

    def keep_transposed():
        def turn(i, _):
            part = pl.ds(multiple(i * 128, 128), 128)
            wrt[:, part] = wr[part, :].T
            return _

        lax.fori_loop(0, H // 128, turn, 0)
        copy = pltpu.make_async_copy(wrt, wr_o, o_sem.at[1])
        copy.start()
        return copy

    def keep_small(pairs):
        copies = [pltpu.make_async_copy(a, b, k_sem.at[k]) for k, a, b in pairs]
        for copy in copies:
            copy.start()
        return copies

    def end_requests(units, chained=()):
        arrival(some_asked, as_sem).wait()
        arrival(some_rows, rs_sem).wait()
        for u in (u_wi, u_wr) + chained:
            chain.drain(u)
        for u in units:
            gather.drain(u)

    last = pl.ds((steps - 1) * R, R)

    @pl.when(jnp.logical_not(is_decoder))
    def _():
        copies = [keep_input_gates()] + keep_small([(0, emb_o, emb_h), (1, owners_o, owners_h)])
        wide = (own_dc, far_dc, own_sm, far_sm)

        def begin_dc():
            gather.begin(own_dc)
            arrival(far_dc.src, x_recv.at[3]).wait()
            gather.begin(far_dc)

        def begin_far_sm():
            arrival(far_sm.src, x_recv.at[0]).wait()
            gather.begin(far_sm)

        def dc_step1():
            gather.step1(own_dc)
            gather.step1(far_dc)

        scan(
            None,
            [
                (1, lambda: gather.step1(u_sq)),
                (2, begin_dc),
                (6, lambda: gather.step2(u_sq)),
                (7, lambda: gather.begin(own_sm)),
                (8, begin_far_sm),
                (10, dc_step1),
            ],
        )
        gather.step3(u_sq)
        gather.ready(u_sq)
        ctx_tanh = jnp.tanh(nn(h_o[last, :], sq[...]))
        tanh_o[...] = ctx_tanh
        ctx_o[...] = ctx_tanh.astype(bf16)
        sends = [to_beside(ctx_o, ctx_o, 4)]
        sends[0].start()
        copies += [
            pltpu.make_async_copy(rec, rec_o, o_sem.at[2]),
            pltpu.make_async_copy(sq, sq_o, o_sem.at[3]),
        ]
        for copy in copies[-2:]:
            copy.start()
        copies += keep_small([(2, h_o, h_h), (3, tanh_o, tanh_h), (4, ctx_o, ctx_h)])
        gather.step1(own_sm)
        for u in wide[:2]:
            gather.step2(u)
        gather.step1(far_sm)
        gather.step2(own_sm)
        for u in wide[:2]:
            gather.step3(u)
        for u in wide[:2]:
            gather.ready(u)
        outer[...] = nn(ctx_o[...], dc[...])
        sends.append(to_beside(outer, outer, 8))
        sends[1].start()
        copies.append(pltpu.make_async_copy(dc, dc_o, o_sem.at[5]))
        copies[-1].start()
        copies.append(keep_transposed())
        gather.step2(far_sm)
        for u in wide[2:]:
            gather.step3(u)
        for u in wide[2:]:
            gather.ready(u)
        for send in sends:
            send.wait_send()
        for k, (src, dst) in enumerate([(cg_s, cg), (de_s, de)]):
            to_beside(src, block_rows(dst, 0, src.shape[0]), 1 + k).wait_send()
        end_requests((u_sq,) + wide)

        half = n * words
        ZY = at.Z * at.Y
        across = cg.shape[1] // M
        landed = cg.at[pl.ds(0, half // 4), pl.ds(0, 2 * M)]

        def term_block(j, zy, c):
            return sm.at[pl.ds(multiple((j * n + zy * 2 + c) * words, 16), words)]

        def landing(j, zy):
            place = j * ZY + zy
            rows = pl.ds(multiple(place // across * words, 16), words)
            return cg.at[rows, pl.ds(multiple(place % across * M, 128), M)]

        def core_send(j):
            for zy in range(ZY):
                remote(
                    term_block(j, zy, 1 - at.c),
                    landing(j, zy),
                    t_send.at[j],
                    t_recv.at[j],
                    at.device(at.z, at.y, 1 - at.c),
                ).start()

        arrival(smooth_in, x_recv.at[5]).wait()
        tile = half // 5 if half % 640 == 0 else 512
        lanes = lax.broadcasted_iota(jnp.int32, (tokens, 128), 1)
        m_part[...] = jnp.full(m_part.shape, -jnp.inf, f32)
        s_part[...] = jnp.zeros_like(s_part)
        p_part[...] = jnp.zeros_like(p_part)

        def tops(i, _):
            rows = pl.ds(multiple(i * tile, tile), tile)
            logits = nt(smooth_in[...], sm[rows, :])
            parts = [logits[:, k * 128 : (k + 1) * 128] for k in range(tile // 128)]
            before = m_part[...]
            top = before
            for part in parts:
                top = jnp.maximum(top, part)
            total = s_part[...] * jnp.exp(before - top)
            picked = p_part[...]
            for k, part in enumerate(parts):
                total += jnp.exp(part - top)
                picked += jnp.where(lanes == labels[...] - (i * tile + k * 128), part, 0.0)
            m_part[...] = top
            s_part[...] = total
            p_part[...] = picked
            return _

        lax.fori_loop(0, 2 * n * words // tile, tops, 0)
        top = jnp.max(m_part[...], axis=1, keepdims=True)
        total = jnp.sum(s_part[...] * jnp.exp(m_part[...] - top), axis=1, keepdims=True)
        log_norm = top + jnp.log(total)
        picked = jnp.sum(p_part[...], axis=1, keepdims=True)
        scale = 1.0 / (R * n)
        loss = jnp.sum(log_norm - picked, axis=0, keepdims=True) * scale
        loss_o[...] = jnp.broadcast_to(loss, loss_o.shape)
        m_part[...] = jnp.broadcast_to(log_norm, m_part.shape)
        drive[:, pl.ds(0, M)] = jnp.zeros((tokens, M), f32)

        def grads(i, _):
            rows = pl.ds(multiple(i * tile, tile), tile)
            weight = sm[rows, :]
            logits = nt(smooth_in[...], weight)
            low = []
            for k in range(tile // 128):
                part = jnp.exp(logits[:, k * 128 : (k + 1) * 128] - m_part[...])
                hits = lanes == labels[...] - (i * tile + k * 128)
                low.append(((part - jnp.where(hits, 1.0, 0.0)) * scale).astype(bf16))
            low = jnp.concatenate(low, axis=1)
            drive[:, pl.ds(0, M)] += nn(low, weight)
            sm[rows, :] = tn(low, smooth_in[...]).astype(bf16)
            pl.when(i == half // tile)(lambda: core_send(0))
            return _

        lax.fori_loop(0, 2 * n * words // tile, grads, 0)
        grad_out[...] = drive[:, pl.ds(0, M)].astype(bf16)
        send = to_beside(grad_out, grad_o, 6)
        send.start()
        core_send(1)
        for j in (0, 1):
            arrival(landed, t_recv.at[j]).wait()

            def add(zy, _):
                block = term_block(j, zy, at.c)
                add_blocks(words, [block, landing(j, zy)], block, bf16)
                pltpu.make_async_copy(block, term_o.at[j, zy], o_sem.at[4]).start()
                return _

            lax.fori_loop(0, ZY, add, 0)
        for j in (0, 1):
            arrival(landed, t_send.at[j]).wait()
        arrival(term_o, o_sem.at[4]).wait()
        send.wait_send()
        for copy in copies:
            copy.wait()

    @pl.when(is_decoder)
    def _():
        copies = [keep_input_gates()] + keep_small([(0, emb_o, emb_h), (1, owners_o, owners_h)])
        rest = [de_own, de_far]
        chain.pass_z(cg_own, 2)
        chain.pass_z(far_b, 2)
        gather.step2(far_a)
        chain.pass_z(cg_own, 3)
        chain.pass_z(far_b, 3)
        gather.begin(u_sq)
        gather.begin(de_own)
        arrival(de_far.src, x_recv.at[2]).wait()
        gather.begin(de_far)
        gather.step3(far_a)
        gather.step3(cg_own)
        gather.step3(far_b)
        for u in (cg_own, far_a, far_b):
            gather.ready(u)
        copies.append(pltpu.make_async_copy(cg, cg_o, o_sem.at[2]))
        copies[-1].start()
        arrival(ctx_o, x_recv.at[4]).wait()
        service = [
            (1, functools.partial(gather.step1, u_sq)),
            (2, functools.partial(gather.step1, de_own)),
            (3, functools.partial(gather.step1, de_far)),
            (6, functools.partial(gather.step2, u_sq)),
            (8, functools.partial(gather.step2, de_own)),
            (9, functools.partial(gather.step2, de_far)),
        ]
        ctx = nn(ctx_o[...], cg[...])
        scan(ctx, service)
        for u in [u_sq] + rest:
            gather.step3(u)
        for u in [u_sq] + rest:
            gather.ready(u)
        later = [(rec, rec_o), (sq, sq_o), (de, de_o)]
        later = [
            pltpu.make_async_copy(a, b, o_sem.at[3 + k]) for k, (a, b) in enumerate(later)
        ]
        for copy in later:
            copy.start()
        copies += later
        copies += keep_small([(2, h_o, h_h), (4, ctx_o, ctx_h)])
        pre = nn(h_o[...], sq[...]) + nt(emb_o[...], de[...])
        arrival(outer, x_recv.at[8]).wait()
        pre = (pre.reshape(steps, R, 2 * M) + outer[...][None]).reshape(tokens, 2 * M)
        pre_o[...] = pre
        copies += keep_small([(5, pre_o, pre_h)])
        a, b = pre[:, :M], pre[:, M:]
        high = jnp.maximum(a, b)
        smooth = high + jnp.log(jnp.exp(a - high) + jnp.exp(b - high))
        grad_out[...] = smooth.astype(bf16)
        send = to_beside(grad_out, smooth_in, 5)
        send.start()
        copies.append(keep_transposed())
        send.wait_send()
        to_beside(sm_s, block_rows(sm, n, words), 0).wait_send()
        to_beside(dc_s, block_rows(dc, n, dc_s.shape[0]), 3).wait_send()
        end_requests((u_sq, far_a, de_own, de_far), (cg_own, far_b))
        arrival(grad_o, x_recv.at[6]).wait()
        for copy in copies:
            copy.wait()


def forward(n, sizes, asked, fullest, hit, table, resets, targets, shards):
    R, H, E, M, slots, per, words = sizes
    Z, Y = factors(n)
    tokens = hit.shape[0]
    shape = jax.ShapeDtypeStruct
    dma = pltpu.SemaphoreType.DMA
    units = 9
    cg_rows, de_rows, dc_rows = H, 2 * M, H
    return pl.pallas_call(
        functools.partial(forward_kernel, n, sizes),
        out_shape=[
            shape((3 * H, H), bf16),
            shape((3 * H, E), bf16),
            shape((H, H), bf16),
            shape((cg_rows, 3 * H), bf16),
            shape((de_rows, E), bf16),
            shape((dc_rows, 2 * M), bf16),
            shape((2, Z * Y, words, M), bf16),
            shape((tokens // R, 5, R, H), f32),
            shape((tokens, H), bf16),
            shape((tokens, E), bf16),
            shape((tokens, 2 * M), f32),
            shape((R, H), f32),
            shape((R, H), bf16),
            shape((per, n * slots), bf16),
            shape((tokens, M), bf16),
            shape((8, 128), f32),
            shape((1, 1), jnp.int32),
        ],
        in_specs=[VMEM, pl.BlockSpec(memory_space=pltpu.SMEM)] + [VMEM] * 4 + [ANY] * 7,
        out_specs=[ANY] * 14 + [VMEM] * 2 + [pl.BlockSpec(memory_space=pltpu.SMEM)],
        scratch_shapes=[
            pltpu.VMEM((n, 8, 128), jnp.int32),
            pltpu.VMEM((n * slots, E), bf16),
            pltpu.VMEM((n * slots, E), bf16),
            pltpu.VMEM((H, 3 * H), bf16),
            pltpu.VMEM((3 * H, E), bf16),
            pltpu.VMEM((H, H), bf16),
            pltpu.VMEM((2 * n * words, M), bf16),
            pltpu.VMEM((cg_rows, 3 * H), bf16),
            pltpu.VMEM((de_rows, E), bf16),
            pltpu.VMEM((dc_rows, 2 * M), bf16),
            pltpu.VMEM((tokens, 3 * H), f32),
            pltpu.VMEM((tokens // R, 5, R, H), f32),
            pltpu.VMEM((3 * H, H), bf16),
            pltpu.VMEM((tokens, M), bf16),
            pltpu.VMEM((tokens, M), bf16),
            pltpu.VMEM((tokens, 128), f32),
            pltpu.VMEM((tokens, 128), f32),
            pltpu.VMEM((tokens, 128), f32),
            pltpu.VMEM((2, 8, 128), jnp.int32),
            pltpu.VMEM((R, 2 * M), f32),
            pltpu.VMEM((tokens, H), bf16),
            pltpu.VMEM((tokens, E), bf16),
            pltpu.VMEM((tokens, 2 * M), f32),
            pltpu.VMEM((R, H), f32),
            pltpu.VMEM((R, H), bf16),
            pltpu.VMEM((per, n * slots), bf16),
            dma((units, 6)),
            dma((units, Z)),
            dma((units,)),
            dma((units,)),
            dma((7,)),
            dma((7,)),
            dma((10,)),
            dma((10,)),
            dma,
            dma,
            dma,
            dma,
            dma((2,)),
            dma((2,)),
            dma((6,)),
            dma((units,)),
            pltpu.VMEM((tokens, 1), f32),
            pltpu.VMEM((tokens, 1), jnp.int32),
            pltpu.VMEM((n, 8, 128), jnp.int32),
        ],
        compiler_params=pltpu.CompilerParams(
            collective_id=2, has_side_effects=True, vmem_limit_bytes=VMEM_LIMIT
        ),
    )(asked, fullest, hit, table, resets, targets, *shards)


class Sum:
    def __init__(self, at, sems, index, mine, theirs, from_c, from_y, from_z, wholes, rows, out):
        self.at, self.sems, self.index = at, sems, index
        self.mine, self.theirs = mine, theirs
        self.from_c, self.from_y, self.from_z = from_c, from_y, from_z
        self.wholes, self.rows, self.out = wholes, rows, out

    def begin(self):
        at, i = self.at, self.index
        cs, cr = self.sems[:2]
        for zy in range(at.Z * at.Y):
            remote(
                self.theirs(zy), self.from_c(zy), cs.at[i], cr.at[i], at.device(at.z, at.y, 1 - at.c)
            ).start()

    def to_y(self, k, source):
        at, i = self.at, self.index
        ys, yr = self.sems[2:4]
        y = at.along_y(k)
        for z in range(at.Z):
            remote(
                source(z * at.Y + y),
                self.from_y(k, z),
                ys.at[i],
                yr.at[i, k - 1, z],
                at.device(at.z, y, at.c),
            ).start()

    def after_core(self):
        at, i = self.at, self.index
        arrival(self.wholes[0], self.sems[1].at[i]).wait()
        for k in list(range(1, at.Y)) + [0]:
            y = at.along_y(k)

            def per_z(z, _):
                zy = z * at.Y + y
                block = self.mine(zy)
                add_blocks(self.rows, [block, self.from_c(zy)], block, block.dtype)
                return _

            lax.fori_loop(0, at.Z, per_z, 0)
            if k:
                self.to_y(k, self.mine)

    def to_z(self, target, z, slot):
        at, i = self.at, self.index
        zs, zr = self.sems[4:6]
        remote(
            self.mine(target * at.Y + at.y),
            self.from_z(slot),
            zs.at[i],
            zr.at[i, slot],
            at.device(z, at.y, at.c),
        ).start()

    def after_y(self):
        at, i = self.at, self.index
        yr = self.sems[3]

        def per_z(z, _):
            block = self.mine(z * at.Y + at.y)
            came = [self.from_y(j, z) for j in range(1, at.Y)]
            for j, part in enumerate(came):
                arrival(part, yr.at[i, j, z]).wait()
            add_blocks(self.rows, [block] + came, block, block.dtype)
            return _

        lax.fori_loop(0, at.Z, per_z, 0)

        near = at.z_near()
        self.to_z(lax.rem(near + 2, 4), near, 0)
        self.to_z(near, near, 1)

    def add_z(self, target, slot):
        at, i = self.at, self.index
        part = self.from_z(slot)
        arrival(part, self.sems[5].at[i, slot]).wait()
        block = self.mine(target * at.Y + at.y)
        add_blocks(self.rows, [block, part], block, block.dtype)

    def mid_z(self):
        far = self.at.z_far()
        self.add_z(far, 0)
        self.to_z(far, far, 2)

    def after_z(self):
        at, i = self.at, self.index
        cs, _, ys, _, zs, zr = self.sems
        came = [self.from_z(slot) for slot in (1, 2)]
        for slot, part in zip((1, 2), came):
            arrival(part, zr.at[i, slot]).wait()
        add_blocks(self.rows, [self.mine(at.zy)] + came, self.out, self.out.dtype)
        for whole, sem in zip(self.wholes, (cs, ys, zs)):
            if whole is not None:
                arrival(whole, sem.at[i]).wait()


class SumZFirst(Sum):
    def after_core(self):
        at, i = self.at, self.index
        arrival(self.wholes[0], self.sems[1].at[i]).wait()

        def per_zy(zy, _):
            block = self.mine(zy)
            add_blocks(self.rows, [block, self.from_c(zy)], block, block.dtype)
            return _

        lax.fori_loop(0, at.Z * at.Y, per_zy, 0)
        self.to_near(self.mine)

    def to_near(self, source):
        at, i = self.at, self.index
        near = at.z_near()
        ys, yr = self.sems[2:4]
        for k, target in enumerate((lax.rem(near + 2, 4), near)):
            for y in range(at.Y):
                remote(
                    source(target * at.Y + y),
                    self.from_y(1, 2 * k + y),
                    ys.at[i],
                    yr.at[i, 0, 2 * k + y],
                    at.device(near, at.y, at.c),
                ).start()

    def add(self, zy, part, sem):
        arrival(part, sem).wait()
        block = self.mine(zy)
        add_blocks(self.rows, [block, part], block, block.dtype)

    def after_near(self):
        at, i = self.at, self.index
        yr, zs, zr = self.sems[3:6]
        far = at.z_far()
        for k, target in enumerate((far, at.z)):
            for y in range(at.Y):
                self.add(target * at.Y + y, self.from_y(1, 2 * k + y), yr.at[i, 0, 2 * k + y])
                if k == 0:
                    remote(
                        self.mine(far * at.Y + y),
                        self.from_z(y),
                        zs.at[i],
                        zr.at[i, y],
                        at.device(far, at.y, at.c),
                    ).start()

    def after_far(self):
        at, i = self.at, self.index
        zs, zr = self.sems[4:6]
        for y in range(at.Y):
            self.add(at.z * at.Y + y, self.from_z(y), zr.at[i, y])
        other = at.along_y(1)
        remote(
            self.mine(at.z * at.Y + other),
            self.from_z(2),
            zs.at[i],
            zr.at[i, 2],
            at.device(at.z, other, at.c),
        ).start()

    def finish(self):
        at, i = self.at, self.index
        cs, _, ys, _, zs, zr = self.sems
        part = self.from_z(2)
        arrival(part, zr.at[i, 2]).wait()
        add_blocks(self.rows, [self.mine(at.zy), part], self.out, self.out.dtype)
        for whole, sem in zip(self.wholes, (cs, ys, zs)):
            if whole is not None:
                arrival(whole, sem.at[i]).wait()


def backward_kernel_all(n, sizes, *refs):
    R, H, E, M, slots, per, words = sizes
    (
        pre,
        grad,
        resets,
        tanh,
        context,
        loss,
        h_h,
        emb_h,
        hit_h,
        owners_h,
        wr_h,
        wi_h,
        sq_h,
        cg_h,
        de_h,
        dc_h,
        term_h,
        rec_h,
    ) = refs[:18]
    (
        table_h,
        input_h,
        recur_h,
        square_h,
        gates_h,
        deep_h,
        context_h,
        soft_h,
        loss_h,
        early_h,
        late_h,
    ) = refs[18:29]
    (
        wrt,
        wi,
        sq,
        de,
        dc,
        big,
        rec,
        low,
        cand,
        before,
        state_grad,
        total,
        deep_low,
        outer_low,
        early_pack,
        late_pack,
        c_grad,
        c_came,
        pre_low,
        g_out,
        g_in,
        wide_c,
        wide_y,
        wide_z,
        thin_c,
        thin_y,
        thin_z,
        deep_c,
        deep_y,
        deep_z,
        soft_far,
        deep_far,
        far_rows,
        block_rows,
        chunks,
        ctx_cols,
        losses,
        loss_sum,
        cs_sem,
        cr_sem,
        ys_sem,
        yr_sem,
        zs_sem,
        zr_sem,
        pz_sem,
        py_sem,
        pc_sem,
        ps_sem,
        load_sem,
        rec_sem,
        big_sem,
        chunk_sem,
        x_send,
        x_recv,
        ls_sem,
        lr_sem,
        gs_sem,
        gr_sem,
        h,
        emb,
        hit,
        owners,
        small_sem,
        table_o,
        input_o,
        recur_o,
        square_o,
        gates_o,
        deep_o,
        context_o,
        soft_o,
        loss_o,
        put_sem,
        keep,
    ) = refs[29:]
    at = Place(n)
    Z, Y = at.Z, at.Y
    ZY = Z * Y
    tokens = emb.shape[0]
    steps = tokens // R
    is_decoder = at.s == 1
    beside = (1 - at.s, at.d)
    others = [lax.rem(at.d + k, n) for k in range(1, n)]
    sems = (cs_sem, cr_sem, ys_sem, yr_sem, zs_sem, zr_sem)

    loads = [
        pltpu.make_async_copy(a, b, load_sem.at[k])
        for k, (a, b) in enumerate([(sq_h, sq), (wr_h, wrt), (wi_h, wi)])
    ]
    for copy in loads:
        copy.start()
    small = [
        pltpu.make_async_copy(a, b, small_sem.at[k])
        for k, (a, b) in enumerate([(h_h, h), (emb_h, emb), (hit_h, hit), (owners_h, owners)])
    ]
    for copy in small:
        copy.start()
    load_de = pltpu.make_async_copy(de_h, de, load_sem.at[3])
    load_dc = pltpu.make_async_copy(dc_h, dc, load_sem.at[4])

    def load_record(i):
        return pltpu.make_async_copy(
            rec_h.at[steps - 1 - i], rec.at[lax.rem(i, 2)], rec_sem.at[lax.rem(i, 2)]
        )

    load_record(0).start()
    for t in range(steps):
        keep[pl.ds(t * R, R), :] = 1.0 - column(resets, t).astype(f32)
    greet([(at.s, d) for d in others] + [beside])

    def to_beside(src, dst, k):
        return remote(src, dst, x_send.at[k], x_recv.at[k], beside)

    def block_sum(index, term, rows, stride, off, bufs, slot, out, kind=Sum):
        c_buf, y_buf, z_buf = bufs

        def block(zy, c):
            return term.at[pl.ds(multiple(off + (zy * 2 + c) * stride, 16), rows)]

        return kind(
            at,
            sems,
            index,
            lambda zy: block(zy, at.c),
            lambda zy: block(zy, 1 - at.c),
            lambda zy: c_buf.at[slot, zy],
            lambda k, z: y_buf.at[slot, k - 1, z],
            lambda k: z_buf.at[slot, k],
            (c_buf.at[slot], y_buf.at[slot], z_buf.at[slot]),
            rows,
            out,
        )

    wide, thin, deep = (wide_c, wide_y, wide_z), (thin_c, thin_y, thin_z), (deep_c, deep_y, deep_z)
    tall = recur_o.shape[0]
    recur_sums = [
        block_sum(g, wrt, tall, tall, g * H, wide, g, recur_o.at[:, pl.ds(g * H, H)])
        for g in range(3)
    ]
    square_by_y, square_by_z = (
        block_sum(3, sq, tall, tall, 0, wide, 3, square_o, kind) for kind in (Sum, SumZFirst)
    )
    high = input_o.shape[0]
    part = thin_c.shape[2]
    input_sums = [
        block_sum(4 + j, wi, part, high, j * part, thin, j, input_o.at[pl.ds(j * part, part)])
        for j in range(high // part)
    ]
    after = 4 + high // part
    deep_rows = deep_far.shape[0]
    deep_sums = [
        block_sum(
            after + j, de, deep_rows, deep_rows, j * n * deep_rows, deep, j, (deep_far, deep_o)[j]
        )
        for j in range(2)
    ]

    def big_rows(first, count):
        return big.at[pl.ds(multiple(first * words, 16), count * words)]

    def soft_sum(j):
        base_y, base_z = 2 * Z, 2 * Z + 2 * (Y - 1) * Z

        def mine(zy):
            if j == 0:
                apart = zy // Y - at.z
                return big_rows((1 - apart * apart // 4) * Y + zy % Y, 1)
            return big_rows(Z + zy // Y, 1)

        return (SumZFirst, Sum)[j](
            at,
            sems,
            after + 2 + j,
            mine,
            None,
            None,
            lambda k, z: big_rows(base_y + (j * (Y - 1) + k - 1) * Z + z, 1),
            lambda k: big_rows(base_z + j * 3 + k, 1),
            (
                None,
                big_rows(base_y + j * (Y - 1) * Z, (Y - 1) * Z),
                big_rows(base_z + j * 3, 3),
            ),
            words,
            (soft_o, soft_far)[j],
        )

    soft_sums = [soft_sum(0), soft_sum(1)]

    def scan(first, with_state, service):
        def step(i, carry):
            t = steps - 1 - i
            rows = pl.ds(multiple(t * R, R), R)
            slot = lax.rem(i, 2)

            @pl.when(i + 1 < steps)
            def _():
                load_record(i + 1).start()

            load_record(i).wait()
            g = carry + state_grad[rows, :] if with_state else carry
            z, r, c, m, p = (rec[slot, k] for k in range(5))
            pc = g * (1.0 - z) * (1.0 - c * c)
            pz = g * (p - c) * z * (1.0 - z)
            pr = pc * m * r * (1.0 - r)
            pn = pc * r
            parts = [pz, pr, pn]
            back = g * z
            for k, x in enumerate(parts):
                x_low = x.astype(bf16)
                low[rows, pl.ds(k * H, H)] = x_low
                back += nn(x_low, wrt[pl.ds(k * H, H), :])
                if with_state:
                    total[:, pl.ds(k * H, H)] += x
            cand[rows, :] = pc.astype(bf16)
            before[rows, :] = p.astype(bf16)
            for when, what in service:
                pl.when(i == when)(what)
            return back * keep[rows, :]

        lax.fori_loop(0, steps, step, first)

    def recur_term(g):
        cols = pl.ds(g * H, H)

        def body(i, _):
            some = pl.ds(multiple(i * 256, 256), 256)
            rows = pl.ds(multiple(g * H + i * 256, 256), 256)
            wrt[rows, :] = tn(before[:, some], low[:, cols]).astype(bf16)
            return _

        lax.fori_loop(0, H // 256, body, 0)

    def input_term():
        def body(i, _):
            some = pl.ds(multiple(i * 256, 256), 256)
            wi[some, :] = tn(low[:, some], emb[...]).astype(bf16)
            return _

        lax.fori_loop(0, 2 * H // 256, body, 0)

        def last(i, _):
            some = pl.ds(multiple(i * 256, 256), 256)
            rows = pl.ds(multiple(2 * H + i * 256, 256), 256)
            wi[rows, :] = tn(cand[:, some], emb[...]).astype(bf16)
            return _

        lax.fori_loop(0, H // 256, last, 0)

    def slot_rows(ref, d):
        return ref.at[pl.ds(multiple(d * slots, 16), slots)]

    def give(extra):
        grads = nn(low[:, pl.ds(0, 2 * H)], wi[pl.ds(0, 2 * H), :])
        grads += nn(cand[...], wi[pl.ds(2 * H, H), :])
        if extra:
            grads += nn(deep_low[...], de[...])
        g_out[...] = tn(hit[...], grads.astype(bf16)).astype(bf16)
        for d in others:
            remote(slot_rows(g_out, d), slot_rows(g_in, at.d), gs_sem, gr_sem, (at.s, d)).start()

    def take():
        own = pl.ds(multiple(at.d * slots, 16), slots)
        some = g_in.at[pl.ds(0, (n - 1) * slots)]
        arrival(some, gr_sem).wait()
        arrival(some, gs_sem).wait()
        g_in[own, :] = g_out[own, :]
        table_o[...] = nn(owners[...], g_in[...])

    puts = []

    def put(src, dst):
        copy = pltpu.make_async_copy(src, dst, put_sem.at[len(puts)])
        copy.start()
        puts.append(copy)

    def thirds(ref, g):
        return ref.at[:, pl.ds(g * H, H)]

    places = {id(recur_sums[g]): (thirds(recur_o, g), thirds(recur_h, g)) for g in range(3)}
    for j, item in enumerate(input_sums):
        rows = pl.ds(j * part, part)
        places[id(item)] = (input_o.at[rows], input_h.at[rows])

    def end_sums(before, between=None):
        items = list(before) + list(input_sums)
        at_y, at_mid, at_end = len(before), max(len(before) - 1, 0), 0
        while at_end < len(items):
            if at_y < len(items):
                items[at_y].after_y()
                at_y += 1
                if at_y == len(items) and between:
                    between()
            if at_mid < min(at_y - 1, len(items)) or at_y == len(items) > at_mid:
                items[at_mid].mid_z()
                at_mid += 1
            if at_end < at_mid - 1 or at_mid == len(items):
                items[at_end].after_z()
                put(*places[id(items[at_end])])
                at_end += 1

    @pl.when(jnp.logical_not(is_decoder))
    def _():
        puts.clear()
        load_dc.start()
        by_z, by_y = soft_sums
        by_z.to_near(lambda zy: term_h.at[0, zy])
        by_y.to_y(1, lambda zy: term_h.at[1, zy])
        for y in range(Y):
            for z in (at.z_far(), at.z):
                zy = z * Y + y
                pltpu.make_async_copy(term_h.at[0, zy], by_z.mine(zy), big_sem.at[0]).start()
        for z in range(Z):
            zy = z * Y + at.y
            pltpu.make_async_copy(term_h.at[1, zy], by_y.mine(zy), big_sem.at[1]).start()
        losses[at.d] = loss[...]
        for d in others:
            remote(loss, losses.at[at.d], ls_sem, lr_sem, (at.s, d)).start()
        for j, item in enumerate(soft_sums):
            whole = big_rows(j * Z, Z)
            arrival(whole, big_sem.at[j]).wait()
        for copy in loads:
            copy.wait()
        load_dc.wait()
        arrival(outer_low, x_recv.at[6]).wait()
        back = nt(outer_low[...], dc[...])
        arrival(c_came, x_recv.at[0]).wait()
        c = tanh[...]
        c_low = (back + c_came[...].astype(f32)).astype(bf16).astype(f32)
        pre_low[...] = (c_low * (1.0 - c * c)).astype(bf16)
        first = nt(pre_low[...], sq[...])

        def square_term():
            sq[...] = tn(h[pl.ds((steps - 1) * R, R), :], pre_low[...]).astype(bf16)
            square_by_y.begin()

        small[0].wait()
        scan(
            first,
            False,
            [
                (1, square_term),
                (3, by_z.after_near),
                (5, square_by_y.after_core),
                (7, by_y.after_y),
            ],
        )
        for copy in small[1:]:
            copy.wait()
        for g in range(3):
            recur_term(g)
            recur_sums[g].begin()
            if g:
                recur_sums[g - 1].after_core()
        by_z.after_far()
        give(False)
        recur_sums[2].after_core()
        input_term()
        for item in input_sums:
            item.begin()
        square_by_y.after_y()
        for item in input_sums:
            item.after_core()
        by_y.mid_z()
        recur_sums[0].after_y()
        square_by_y.mid_z()
        recur_sums[1].after_y()
        recur_sums[0].mid_z()
        by_y.after_z()
        send = to_beside(soft_far, soft_o, 1)
        send.start()
        some = losses.at[pl.ds(0, n - 1)]
        arrival(some, lr_sem).wait()
        arrival(some, ls_sem).wait()
        all_loss = losses[0]
        for d in range(1, n):
            all_loss += losses[d]
        loss_sum[...] = all_loss
        loss_o[...] = all_loss
        put(loss_o, loss_h)
        loss_send = to_beside(loss_sum, loss_o, 2)
        loss_send.start()
        recur_sums[2].after_y()
        recur_sums[1].mid_z()
        recur_sums[0].after_z()
        put(*places[id(recur_sums[0])])
        take()
        put(table_o, table_h)
        square_by_y.after_z()
        put(square_o, square_h)

        def finish_soft():
            by_z.finish()
            put(soft_o, soft_h)

        end_sums([recur_sums[1], recur_sums[2]], finish_soft)
        send.wait_send()
        loss_send.wait_send()
        arrival(gates_o, x_recv.at[4]).wait()
        put(gates_o, gates_h)
        arrival(context_o, x_recv.at[5]).wait()
        put(context_o, context_h)
        arrival(deep_o, x_recv.at[3]).wait()
        put(deep_o, deep_h)
        for copy in puts:
            copy.wait()

    @pl.when(is_decoder)
    def _():
        puts.clear()
        load_de.start()
        chunk = big.shape[1]
        for k in range(3 * H // chunk):
            pltpu.make_async_copy(
                cg_h.at[:, pl.ds(k * chunk, chunk)], big.at[pl.ds(k * H, H)], big_sem.at[0]
            ).start()
        a, b = pre[:, pl.ds(0, M)], pre[:, pl.ds(M, M)]
        high = jnp.maximum(a, b)
        smooth = high + jnp.log(jnp.exp(a - high) + jnp.exp(b - high))
        sg = grad[...].astype(f32)
        for k, x in enumerate((a, b)):
            cols = pl.ds(k * M, M)
            deep_grad = sg * jnp.exp(x - smooth)
            deep_low[:, cols] = deep_grad.astype(bf16)
            outer_low[:, cols] = jnp.sum(deep_grad.reshape(steps, R, M), axis=0).astype(bf16)
        outer_send = to_beside(outer_low, outer_low, 6)
        outer_send.start()
        for copy in loads:
            copy.wait()
        state_grad[...] = nt(deep_low[...], sq[...])
        total[...] = jnp.zeros_like(total)
        gather = Gather(at, pz_sem, py_sem, pc_sem, ps_sem)
        early = Unit(0, early_pack, early_h, R, 0)
        late = Unit(1, late_pack, late_h, R, 0)
        early_pack[:, pl.ds(0, H)] = context[...]
        early_pack[:, pl.ds(H, 2 * M)] = outer_low[...]
        own_copies = [
            pltpu.make_async_copy(early_pack, early.block(at.zy, at.c), big_sem.at[1]),
            pltpu.make_async_copy(late_pack, late.block(at.zy, at.c), big_sem.at[2]),
        ]
        own_copies[0].start()
        gather.begin(early)
        scan(
            jnp.zeros((R, H), f32),
            True,
            [
                (7, lambda: gather.step1(early)),
            ],
        )
        late_pack[...] = total[...].astype(bf16)
        gates_rows = big.at[pl.ds(0, 3 * H * H // chunk)]
        arrival(gates_rows, big_sem.at[0]).wait()
        for k in range(3 * H // chunk):
            cols = pl.ds(k * chunk, chunk)
            term = nt(late_pack[:, cols], big[pl.ds(k * H, H), :])
            back = term if k == 0 else back + term
        c_grad[...] = back.astype(bf16)
        send = to_beside(c_grad, c_came, 0)
        send.start()
        gather.step2(early)
        own_copies[1].start()
        gather.begin(late)
        for copy in small:
            copy.wait()
        for g in range(3):
            recur_term(g)
            recur_sums[g].begin()
            if g:
                recur_sums[g - 1].after_core()
        gather.step1(late)
        load_de.wait()
        give(True)
        recur_sums[2].after_core()
        sq[...] = tn(h[...], deep_low[...]).astype(bf16)
        square_by_z.begin()
        gather.step2(late)
        de[...] = tn(deep_low[...], emb[...]).astype(bf16)
        for item in deep_sums:
            item.begin()
        input_term()
        for item in input_sums:
            item.begin()
        square_by_z.after_core()
        for item in deep_sums:
            item.after_core()
        for item in input_sums:
            item.after_core()
        gather.step3(early)
        recur_sums[0].after_y()
        square_by_z.after_near()
        recur_sums[1].after_y()
        recur_sums[0].mid_z()
        gather.step3(late)
        recur_sums[2].after_y()
        recur_sums[1].mid_z()
        square_by_z.after_far()
        for u in (early, late):
            gather.ready(u)
        for copy in own_copies:
            copy.wait()
        recur_sums[0].after_z()
        put(*places[id(recur_sums[0])])

        rows = gates_o.shape[0]
        firsts = [(sec * n + at.d) * rows for sec in (0, 1)]
        for k, first in enumerate(firsts):
            lanes = multiple(first // 128 * 128, 128)
            copy = pltpu.make_async_copy(
                early_h.at[:, pl.ds(lanes, 128)], ctx_cols.at[k], big_sem.at[3]
            )
            copy.start()
            copy.wait()
        pieces = (2 * M + 3 * H) // chunk

        def load_chunk(k):
            if k < 2 * M // chunk:
                src = early_h.at[:, pl.ds(H + k * chunk, chunk)]
            else:
                src = late_h.at[:, pl.ds(k * chunk - 2 * M, chunk)]
            return pltpu.make_async_copy(src, chunks.at[k % 2], chunk_sem.at[k % 2])

        load_chunk(0).start()
        for k in range(pieces):
            if k + 1 < pieces:
                load_chunk(k + 1).start()
            load_chunk(k).wait()
            for j, first in enumerate(firsts):
                block_rows[...] = tn(ctx_cols[j], chunks[k % 2])
                product = block_rows[pl.ds(multiple(lax.rem(first, 128), 8), rows), :]
                if k < 2 * M // chunk:
                    dst, cols = context_o, pl.ds(k * chunk, chunk)
                else:
                    dst, cols = gates_o, pl.ds(k * chunk - 2 * M, chunk)
                if j == 0:
                    far_rows[:, pl.ds(k * chunk, chunk)] = product
                else:
                    dst[:, cols] = product
        sends = [
            to_beside(far_rows.at[:, pl.ds(2 * M, 3 * H)], gates_o, 4),
            to_beside(far_rows.at[:, pl.ds(0, 2 * M)], context_o, 5),
        ]
        for copy in sends:
            copy.start()
        put(gates_o, gates_h)
        put(context_o, context_h)
        take()
        put(table_o, table_h)
        recur_sums[2].mid_z()
        for item in deep_sums:
            item.after_y()
        recur_sums[1].after_z()
        put(*places[id(recur_sums[1])])
        for item in deep_sums:
            item.mid_z()
        recur_sums[2].after_z()
        put(*places[id(recur_sums[2])])

        def finish_deep():
            for item in deep_sums:
                item.after_z()
            put(deep_o, deep_h)
            sends.append(to_beside(deep_far, deep_o, 3))
            sends[-1].start()

        end_sums([], finish_deep)
        square_by_z.finish()
        put(square_o, square_h)
        for copy in sends + [send, outer_send]:
            copy.wait_send()
        for u in (early, late):
            gather.drain(u)
        arrival(soft_o, x_recv.at[1]).wait()
        put(soft_o, soft_h)
        arrival(loss_o, x_recv.at[2]).wait()
        put(loss_o, loss_h)
        for copy in puts:
            copy.wait()


def backward(n, sizes, blocks, arrays):
    R, H, E, M, slots, per, words = sizes
    Z, Y = factors(n)
    ZY = Z * Y
    tokens = arrays[0].shape[0]
    shape = jax.ShapeDtypeStruct
    vmem = pltpu.VMEM
    dma = pltpu.SemaphoreType.DMA
    input_b, recur_b, square_b, gates_b, deep_b, context_b = blocks
    tall = recur_b[0]
    part = next(k for k in (64, 48, 32, 16) if input_b[0] % k == 0)
    thin = input_b[0] // part
    units = 4 + thin + 4
    chunk = M
    big_rows = words * (2 * Z + 2 * (Y - 1) * Z + 6)
    big_rows = max(big_rows, 3 * H * H // chunk)
    y1 = max(Y - 1, 1)
    return pl.pallas_call(
        functools.partial(backward_kernel_all, n, sizes),
        out_shape=[
            shape((per, E), f32),
            shape(input_b, f32),
            shape(recur_b, f32),
            shape(square_b, f32),
            shape(gates_b, f32),
            shape(deep_b, f32),
            shape(context_b, f32),
            shape((words, M), f32),
            shape((8, 128), f32),
            shape((n * R, H + 2 * M), bf16),
            shape((n * R, 3 * H), bf16),
        ],
        in_specs=[VMEM] * 6 + [ANY] * 12,
        out_specs=[ANY] * 11,
        scratch_shapes=[
            vmem((3 * H, H), bf16),
            vmem((3 * H, E), bf16),
            vmem((H, H), bf16),
            vmem((2 * M, E), bf16),
            vmem((H, 2 * M), bf16),
            vmem((big_rows, chunk), bf16),
            vmem((2, 5, R, H), f32),
            vmem((tokens, 3 * H), bf16),
            vmem((tokens, H), bf16),
            vmem((tokens, H), bf16),
            vmem((tokens, H), f32),
            vmem((R, 3 * H), f32),
            vmem((tokens, 2 * M), bf16),
            vmem((R, 2 * M), bf16),
            vmem((R, H + 2 * M), bf16),
            vmem((R, 3 * H), bf16),
            vmem((R, H), bf16),
            vmem((R, H), bf16),
            vmem((R, H), bf16),
            vmem((n * slots, E), bf16),
            vmem((n * slots, E), bf16),
            vmem((4, ZY, tall, H), bf16),
            vmem((4, y1, Z, tall, H), bf16),
            vmem((4, 3, tall, H), bf16),
            vmem((thin, ZY, part, E), bf16),
            vmem((thin, y1, Z, part, E), bf16),
            vmem((thin, 3, part, E), bf16),
            vmem((2, ZY) + deep_b, bf16),
            vmem((2, y1, Z) + deep_b, bf16),
            vmem((2, 3) + deep_b, bf16),
            vmem((words, M), f32),
            vmem(deep_b, f32),
            vmem((gates_b[0], 2 * M + 3 * H), f32),
            vmem((128, chunk), f32),
            vmem((2, n * R, chunk), bf16),
            vmem((2, n * R, 128), bf16),
            vmem((n, 8, 128), f32),
            vmem((8, 128), f32),
            dma((units,)),
            dma((units,)),
            dma((units,)),
            dma((units, y1, Z)),
            dma((units,)),
            dma((units, 3)),
            dma((2, 6)),
            dma((2, Z)),
            dma((2,)),
            dma((2,)),
            dma((5,)),
            dma((2,)),
            dma((4,)),
            dma((2,)),
            dma((7,)),
            dma((7,)),
            dma,
            dma,
            dma,
            dma,
            vmem((tokens, H), bf16),
            vmem((tokens, E), bf16),
            vmem((tokens, n * slots), bf16),
            vmem((per, n * slots), bf16),
            dma((4,)),
            vmem((per, E), f32),
            vmem(input_b, f32),
            vmem(recur_b, f32),
            vmem(square_b, f32),
            vmem(gates_b, f32),
            vmem(deep_b, f32),
            vmem(context_b, f32),
            vmem((words, M), f32),
            vmem((8, 128), f32),
            dma((16,)),
            vmem((tokens, 1), f32),
        ],
        compiler_params=pltpu.CompilerParams(
            collective_id=3, has_side_effects=True, vmem_limit_bytes=VMEM_LIMIT
        ),
    )(*arrays)


def in_rounds(
    token_ids,
    resets,
    targets,
    embedding,
    input_gates,
    recur_gates,
    square,
    context_gates,
    deep_embed,
    deep_context,
    softmax_weight,
):
    n = lax.axis_size("dp")
    s = lax.axis_index("section")
    d = lax.axis_index("dp")
    is_decoder = s == 1
    micro, rows, steps = token_ids.shape[1:]
    R = micro * rows
    tokens = R * steps
    H = square.shape[2]
    E = embedding.shape[2]
    M = softmax_weight.shape[1]
    per = embedding.shape[1]
    slots = max(512 // n, 8)
    scale = 1.0 / (R * n)

    def time_major(x):
        return jnp.transpose(x.reshape(R, steps), (1, 0)).reshape(-1)

    ids = time_major(token_ids[0])
    keep = time_major(1 - resets[0]).astype(f32)[:, None]
    labels = time_major(targets)

    plan = request_slots(ids, n, per, slots)
    rounds = lax.pmax(jnp.max(plan[2]) // slots + 1, ("section", "dp"))
    table = embedding[0]

    def fetch(turn):
        asked, hit = round_maps(plan, turn, n, slots)
        owners = owner_map(asked, n, per)
        came = swap(nn(owners, table).astype(bf16), n)
        return owners, hit, nn(hit, came).astype(bf16)

    owners, hit, emb = fetch(0)

    def more(carry):
        turn, emb = carry
        return turn + 1, emb + fetch(turn)[2]

    _, emb = lax.while_loop(lambda c: c[0] < rounds, more, (jnp.int32(1), emb))

    wr, wi, sq, sm, cg, de, dc = gather(
        n,
        [
            recur_gates[0],
            input_gates[0],
            square[0],
            softmax_weight,
            context_gates,
            deep_embed,
            deep_context,
        ],
        (False, False, False, False, True, True, True),
    )
    wr, wi, sq, sm = wr.reshape(H, 3 * H), wi.reshape(3 * H, E), sq.reshape(H, H), sm.reshape(-1, M)
    cg, de, dc = cg.reshape(H, 3 * H), de.reshape(2 * M, E), dc.reshape(H, 2 * M)

    enc = gru_forward(emb, wi, wr, jnp.zeros((R, 3 * H), f32), keep)
    last_low = enc[5][-R:]
    ctx_tanh = jnp.tanh(nn(last_low, sq))
    context = lax.ppermute(ctx_tanh.astype(bf16), "section", [(0, 1)])

    dec = gru_forward(emb, wi, wr, nn(context, cg), keep)
    states_low = dec[5]
    deep_pre = nn(states_low, sq) + nt(emb, de)
    deep_pre = (deep_pre.reshape(steps, R, -1) + nn(context, dc)[None]).reshape(tokens, -1)
    smooth = jnp.logaddexp(deep_pre[:, :M], deep_pre[:, M:])
    smooth_low = smooth.astype(bf16)

    came = lax.ppermute(smooth_low, "section", [(1, 0)])
    head_in = jnp.where(is_decoder, smooth_low, came)
    words = sm.shape[0]
    logits = nt(head_in, sm)
    top = jnp.max(logits, axis=1)
    total = jnp.sum(jnp.exp(logits - top[:, None]), axis=1)
    hits = lax.broadcasted_iota(jnp.int32, logits.shape, 1) == (labels - s * words)[:, None]
    picked = jnp.sum(jnp.where(hits, logits, 0.0), axis=1)
    stats = jnp.stack([top, total, picked])
    other = lax.ppermute(stats, "section", [(0, 1), (1, 0)])
    all_top = jnp.maximum(top, other[0])
    log_norm = all_top + jnp.log(
        total * jnp.exp(top - all_top) + other[1] * jnp.exp(other[0] - all_top)
    )
    loss = jnp.where(is_decoder, jnp.sum(log_norm - picked - other[2]) * scale, 0.0)
    logit_low = ((jnp.exp(logits - log_norm[:, None]) - hits.astype(f32)) * scale).astype(bf16)
    smooth_part = nn(logit_low, sm)
    smooth_grad = smooth_part + lax.ppermute(smooth_part, "section", [(0, 1)])
    softmax_term = tn(logit_low, head_in).astype(bf16)

    deep_grad = jnp.concatenate(
        [
            smooth_grad * jnp.exp(deep_pre[:, :M] - smooth),
            smooth_grad * jnp.exp(deep_pre[:, M:] - smooth),
        ],
        axis=1,
    )
    deep_low = deep_grad.astype(bf16)
    outer_low = jnp.sum(deep_grad.reshape(steps, R, -1), axis=0).astype(bf16)
    state_grad = nt(deep_low, sq)
    dec_low, dec_cand, drive_sum = gru_backward(
        state_grad, jnp.zeros((R, H), f32), keep, dec[:5], wr
    )
    drive_sum_low = drive_sum.astype(bf16)
    context_grad = (nt(outer_low, dc) + nt(drive_sum_low, cg)).astype(bf16)
    packed = lax.all_gather(jnp.concatenate([context, outer_low, drive_sum_low], axis=1), "dp", tiled=True)
    packed_came = lax.ppermute(packed, "section", [(1, 0)])
    packed = jnp.where(is_decoder, packed, packed_came)

    context_back = lax.ppermute(context_grad, "section", [(1, 0)])
    pre_low = (context_back.astype(f32) * (1.0 - ctx_tanh * ctx_tanh)).astype(bf16)
    enc_low, enc_cand, _ = gru_backward(
        jnp.zeros((tokens, H), f32), nt(pre_low, sq), keep, enc[:5], wr
    )

    def pick(of_encoder, of_decoder):
        return jnp.where(is_decoder, of_decoder, of_encoder)

    recur_low = pick(enc_low, dec_low)
    cand_low = pick(enc_cand, dec_cand)
    before_low = pick(enc[4], dec[4]).astype(bf16)
    drive_low = jnp.concatenate([recur_low[:, : 2 * H], cand_low], axis=1)
    recur_term = tn(before_low, recur_low).astype(bf16)
    input_term = tn(drive_low, emb).astype(bf16)
    deep_mask = jnp.where(is_decoder, deep_low, jnp.zeros_like(deep_low))
    input_grad = nn(drive_low, wi) + nn(deep_mask, de)
    rows_pad = jnp.zeros((tokens - R, H), bf16)
    square_term = tn(
        pick(jnp.concatenate([last_low, rows_pad]), states_low),
        pick(jnp.concatenate([pre_low, rows_pad]), deep_low),
    ).astype(bf16)
    deep_term = tn(deep_mask, emb).astype(bf16)

    input_grad_low = input_grad.astype(bf16)

    def give(owners, hit):
        return tn(owners, swap(tn(hit, input_grad_low).astype(bf16), n))

    def give_more(carry):
        turn, grad = carry
        asked, hit = round_maps(plan, turn, n, slots)
        return turn + 1, grad + give(owner_map(asked, n, per), hit)

    table_grad = give(owners, hit)
    _, table_grad = lax.while_loop(
        lambda c: c[0] < rounds, give_more, (jnp.int32(1), table_grad)
    )

    deep_blocks = jnp.stack(
        [x.reshape((n,) + deep_embed.shape) for x in jnp.split(deep_term, 2)], axis=1
    )
    deep_blocks = deep_blocks.reshape(n, 2 * deep_embed.shape[0], E)
    loss_blocks = jnp.broadcast_to(loss, (n, 8, 128))
    square_sum, recur_sum, input_sum, softmax_sum, deep_sum, loss_sum = scatter(
        n,
        [
            square_term.reshape((n,) + square.shape[1:]),
            recur_term.reshape((n,) + recur_gates.shape[1:]),
            input_term.reshape((n,) + input_gates.shape[1:]),
            softmax_term.reshape((n,) + softmax_weight.shape),
            deep_blocks,
            loss_blocks,
        ],
        1,
    )
    deep_halves = deep_sum.reshape((2,) + deep_embed.shape)
    both = lax.ppermute(
        jnp.concatenate([deep_halves[0].reshape(-1), loss_sum[:1].reshape(-1)]), "section", [(1, 0)]
    )
    deep_out = jnp.where(is_decoder, deep_halves[1], both[:-128].reshape(deep_embed.shape))
    loss_out = jnp.where(is_decoder, loss_sum[0, 0], both[-1])

    own = (s * n + d) * context_gates.shape[0]
    context_own = lax.dynamic_slice(packed, (0, own), (packed.shape[0], context_gates.shape[0]))
    gates_out = tn(context_own, packed[:, H + 2 * M :])
    context_out = tn(context_own, packed[:, H : H + 2 * M])

    return (
        loss_out,
        table_grad[None],
        input_sum[None],
        recur_sum[None],
        square_sum[None],
        gates_out,
        deep_out,
        context_out,
        softmax_sum,
    )


def in_one_round(
    token_ids,
    resets,
    targets,
    embedding,
    input_gates,
    recur_gates,
    square,
    context_gates,
    deep_embed,
    deep_context,
    softmax_weight,
):
    n = lax.axis_size("dp")
    s = lax.axis_index("section")
    d = lax.axis_index("dp")
    is_decoder = s == 1
    micro, rows, steps = token_ids.shape[1:]
    R = micro * rows
    tokens = R * steps
    H = square.shape[2]
    E = embedding.shape[2]
    M = softmax_weight.shape[1]
    per = embedding.shape[1]
    slots = 512 // n

    def time_major(x):
        return jnp.transpose(x.reshape(R, steps), (1, 0)).reshape(-1)

    ids = time_major(token_ids[0])
    reset_rows = jnp.transpose(resets[0], (2, 0, 1))
    target_rows = jnp.transpose(targets, (2, 0, 1))

    plan = request_slots(ids, n, per, slots)
    asked, hit = round_maps(plan, 0, n, slots)
    lane = jnp.arange(128, dtype=jnp.int32)
    asked = jnp.tile(asked.reshape(n, slots), (1, 128 // slots))
    asked = jnp.where(lane // slots == d % (128 // slots), asked, -1)
    fullest = jnp.max(plan[2]).reshape(1, 1)

    shards = [
        recur_gates[0],
        input_gates[0],
        square[0],
        softmax_weight,
        context_gates,
        deep_embed,
        deep_context,
    ]
    sizes = (R, H, E, M, slots, per, softmax_weight.shape[0])
    results = forward(n, sizes, asked, fullest, hit, embedding[0], reset_rows, target_rows, shards)

    (
        wr,
        wi,
        sq,
        cg,
        de,
        dc,
        softmax_term,
        rec,
        states_low,
        emb,
        deep_pre,
        ctx_tanh,
        context,
        owners,
        smooth_grad,
        loss,
        most,
    ) = results
    blocks = [
        x.shape[-2:]
        for x in (input_gates, recur_gates, square, context_gates, deep_embed, deep_context)
    ]
    table, inputs, recur, squares, gates, deep, contexts, soft, loss, _, _ = backward(
        n,
        sizes,
        blocks,
        [
            deep_pre,
            smooth_grad,
            reset_rows,
            ctx_tanh,
            context,
            loss,
            states_low,
            emb,
            hit,
            owners,
            wr,
            wi,
            sq,
            cg,
            de,
            dc,
            softmax_term,
            rec,
        ],
    )
    def again(carry):
        slow = in_rounds(
            token_ids,
            resets,
            targets,
            embedding,
            input_gates,
            recur_gates,
            square,
            context_gates,
            deep_embed,
            deep_context,
            softmax_weight,
        )
        flat = [x.reshape(x.shape[-2:]) for x in slow[1:]]
        return jnp.int32(0), (jnp.broadcast_to(slow[0], (8, 128)), *flat)

    fast = (loss, table, inputs, recur, squares, gates, deep, contexts, soft)
    done = lax.while_loop(lambda carry: carry[0] > 0, again, (most.reshape(()), fast))[1]
    loss, table, inputs, recur, squares, gates, deep, contexts, soft = finish(*done)
    return (
        loss.reshape(()),
        table[None],
        inputs[None],
        recur[None],
        squares[None],
        gates,
        deep,
        contexts,
        soft,
    )


def per_device(*args):
    n = lax.axis_size("dp")
    blocks = [args[k].shape[-2] for k in (4, 5, 6, 7, 8, 9, 10)]
    aligned = all(rows % 16 == 0 for rows in blocks)
    if aligned and n == 16:
        return in_one_round(*args)
    return in_rounds(*args)


def solution(mesh):
    halves = P("section", "dp", None)
    whole = P(("section", "dp"), None)
    in_specs = (
        P("section", None, "dp", None),
        P("section", None, "dp", None),
        P(None, "dp", None),
        halves,
        halves,
        halves,
        halves,
        whole,
        whole,
        whole,
        whole,
    )
    out_specs = (P(), halves, halves, halves, halves, whole, whole, whole, whole)
    return jax.shard_map(
        per_device, mesh=mesh, in_specs=in_specs, out_specs=out_specs, check_vma=False
    )
```
